32 devices in a mesh: fsdp: 16 (over z, y, x), tensor: 2 (over core).
Axes of the slice: x: 2, y: 2, z: 4, core: 2. Of those that a mesh axis runs over, the one named last changes fastest.
Arguments:
- inputs: float32 [20480, 1024], P(('fsdp', 'tensor')), may hold values from -6 to 6
- cotangent: bfloat16 [20480, 1024], P(('fsdp', 'tensor')), may hold values from -6 to 6
- token_mask: int32 [32, 640], P('fsdp'), may hold values from 0 to 1, as said below
- w_qkv: float32 [3, 1024, 1024], P(None, 'fsdp', 'tensor'), may hold values from -0.1875 to 0.1875
- w_out: float32 [1024, 1024], P('tensor', 'fsdp'), may hold values from -2 to 2
- w_fc1: float32 [1024, 4096], P('fsdp', 'tensor'), may hold values from -0.1875 to 0.1875
- w_fc2: float32 [4096, 1024], P('tensor', 'fsdp'), may hold values from -0.09375 to 0.09375
- vectors: float32 [12, 1024], P(None, 'fsdp'), may hold values from -1 to 2.1
- qkv_row: float32 [3, 1024], P(None, 'fsdp'), may hold values from 461.6 to 1846.4
- qkv_col: float32 [3, 1024], P(None, 'tensor'), may hold values from 461.6 to 1846.4
- out_row: float32 [1024], P('tensor'), may hold values from 7.2125 to 28.85
- out_col: float32 [1024], P('fsdp'), may hold values from 7.2125 to 28.85
- fc1_row: float32 [1024], P('fsdp'), may hold values from 57.7 to 230.8
- fc1_col: float32 [4096], P('tensor'), may hold values from 57.7 to 230.8
- fc2_row: float32 [4096], P('tensor'), may hold values from 230.8 to 923.2
- fc2_col: float32 [1024], P('fsdp'), may hold values from 230.8 to 923.2
- vec_second: float32 [12, 1024], P(None, 'fsdp'), may hold values from 36.928 to 5908.48
Outputs:
- block_out: float32 [20480, 1024], P(('fsdp', 'tensor'))
- input_grad: float32 [20480, 1024], P(('fsdp', 'tensor'))
- grad_qkv: float32 [3, 1024, 1024], P(None, 'fsdp', 'tensor')
- grad_out: float32 [1024, 1024], P('tensor', 'fsdp')
- grad_fc1: float32 [1024, 4096], P('fsdp', 'tensor')
- grad_fc2: float32 [4096, 1024], P('tensor', 'fsdp')
- grad_vectors: float32 [12, 1024], P(None, 'fsdp')
- new_qkv: float32 [3, 1024, 1024], P(None, 'fsdp', 'tensor')
- new_out: float32 [1024, 1024], P('tensor', 'fsdp')
- new_fc1: float32 [1024, 4096], P('fsdp', 'tensor')
- new_fc2: float32 [4096, 1024], P('tensor', 'fsdp')
- new_vectors: float32 [12, 1024], P(None, 'fsdp')
- qkv_row_new: float32 [3, 1024], P(None, 'fsdp')
- qkv_col_new: float32 [3, 1024], P(None, 'tensor')
- out_row_new: float32 [1024], P('tensor')
- out_col_new: float32 [1024], P('fsdp')
- fc1_row_new: float32 [1024], P('fsdp')
- fc1_col_new: float32 [4096], P('tensor')
- fc2_row_new: float32 [4096], P('tensor')
- fc2_col_new: float32 [1024], P('fsdp')
- vec_second_new: float32 [12, 1024], P(None, 'fsdp')
The draws below stay inside these ranges and needn't reach their ends.
Inputs may be any that keep to these rules, and one draw needn't show every extreme that they name: `token_mask`: 1 marks a token that takes part, 0 a dropped patch or padding; row 0 of every image is 1 and rows 577 to 639 are 0.
All inputs are finite; a program needn't handle non-finite values.
Results may differ from the reference program's by a relative error of at most 0.009.
The reference program's roundings to bfloat16 on the way count: a program that leaves them out, or rounds other values in their place, can miss the bound.
Values may be sent and summed in bfloat16 or wider, within the bound.
A program may use at most 192 MiB of HBM per device.

```python
import math
import jax
import jax.numpy as jnp
from jax import lax

D = 1024
HEADS = 16
HEAD_DIM = 64
FF = 4096
SEQ = 577
SLOT = 640
STEP = 20
IMG_GRP = 2
IMAGES = 32
ROWS = 20480
VEC = 12


def draw_token_mask(key, part):
    key = jax.random.fold_in(key, 11)
    image_index = lax.broadcasted_iota(jnp.int32, (IMAGES, SLOT), 0)
    position = lax.broadcasted_iota(jnp.int32, (IMAGES, SLOT), 1)
    group_index = image_index // IMG_GRP
    inner_index = image_index % IMG_GRP
    threshold = 300 + 300 * group_index // max(IMAGES // IMG_GRP - 1, 1) + 300 * inner_index // max(IMG_GRP - 1, 1)
    rolled = jax.random.randint(key, (IMAGES, SLOT), 0, 1000)
    chosen = (rolled < threshold) | (position == 0)
    chosen = chosen & (position < SEQ)
    return chosen.astype(jnp.int32)


def draw_vectors(key, part):
    key = jax.random.fold_in(key, 5)
    key_gain, key_shift = jax.random.split(key)
    ramp_up = lax.broadcasted_iota(jnp.float32, (VEC, D), 1) / D
    gain_rows = (0.5 + ramp_up) * jax.random.uniform(key_gain, (VEC, D), jnp.float32, 0.8, 1.2)
    shifts = jnp.clip(0.2 * jax.random.normal(key_shift, (VEC, D), jnp.float32), -1.0, 1.0)
    row_index = lax.broadcasted_iota(jnp.int32, (VEC, D), 0)
    return jnp.where((row_index == 0) | (row_index == 5), gain_rows, shifts)


def draw_vec_second(key, part):
    key = jax.random.fold_in(key, 7)
    factor = jnp.concatenate([jnp.array([0.8, 0.8, 0.25, 0.25, 0.3, 0.08, 0.08], jnp.float32), jnp.full((FF // D,), 0.02, jnp.float32), jnp.array([0.25], jnp.float32)])
    spread = jnp.exp(jax.random.uniform(key, (VEC, D), jnp.float32, 0.0, math.log(4.0)))
    return 0.1 * SEQ * IMAGES * factor[:, None] * spread


def block_scale(stream_key, extent, cuts, low, largest):
    def one(axis_at, shards_of):
        heights = jax.random.uniform(jax.random.fold_in(jax.random.fold_in(stream_key, 6), axis_at), (shards_of,), jnp.float32, low / len(cuts), largest / len(cuts))
        return jnp.repeat(jnp.exp(heights), extent[axis_at] // shards_of).reshape((-1,) + (1,) * (len(extent) - axis_at - 1))

    level = one(*cuts[0])
    for cut in cuts[1:]:
        level = level * one(*cut)
    return level


def gaussian(key, dims, scale, bound, cuts=(), kind=jnp.bfloat16):
    drawn = scale * jax.random.normal(key, dims, jnp.float32)
    if cuts:
        drawn = drawn * block_scale(key, dims, cuts, -0.22, 0.18)
    return jnp.clip(drawn, -bound, bound).astype(kind)


def setup_inputs(seed: int = 0) -> dict:
    arg_keys = jax.random.split(jax.random.key(seed), 18)
    return {
        "inputs": gaussian(arg_keys[0], (ROWS, D), 1.0, 6.0, ((0, 32),), jnp.float32),
        "cotangent": gaussian(arg_keys[1], (ROWS, D), 1.0, 6.0, ((0, 32),)),
        "token_mask": draw_token_mask(jax.random.fold_in(arg_keys[17], 71), 0),
        "w_qkv": gaussian(arg_keys[3], (3, D, D), D ** -0.5, 0.1875, ((1, 16), (2, 2)), jnp.float32),
        "w_out": gaussian(arg_keys[4], (D, D), (4 * D // SEQ) ** -0.5, 2.0, ((0, 2), (1, 16)), jnp.float32),
        "w_fc1": gaussian(arg_keys[5], (D, FF), D ** -0.5, 0.1875, ((0, 16), (1, 2)), jnp.float32),
        "w_fc2": gaussian(arg_keys[6], (FF, D), FF ** -0.5, 0.09375, ((0, 2), (1, 16)), jnp.float32),
        "vectors": draw_vectors(jax.random.fold_in(arg_keys[17], 71), 0),
        "qkv_row": jnp.clip(jnp.exp(math.log(1846.4) - 1.3862944 * jax.random.uniform(arg_keys[8], (3, D), jnp.float32) ** block_scale(arg_keys[8], (3, D), ((1, 16),), -0.2, 0.2)), 461.6, 1846.4),
        "qkv_col": jnp.clip(jnp.exp(math.log(1846.4) - 1.3862944 * jax.random.uniform(arg_keys[9], (3, D), jnp.float32) ** block_scale(arg_keys[9], (3, D), ((1, 2),), -0.2, 0.2)), 461.6, 1846.4),
        "out_row": jnp.clip(jnp.exp(math.log(28.85) - 1.3862944 * jax.random.uniform(arg_keys[10], (D,), jnp.float32) ** block_scale(arg_keys[10], (D,), ((0, 2),), -0.2, 0.2)), 7.2125, 28.85),
        "out_col": jnp.clip(jnp.exp(math.log(28.85) - 1.3862944 * jax.random.uniform(arg_keys[11], (D,), jnp.float32) ** block_scale(arg_keys[11], (D,), ((0, 16),), -0.2, 0.2)), 7.2125, 28.85),
        "fc1_row": jnp.clip(jnp.exp(math.log(230.8) - 1.3862944 * jax.random.uniform(arg_keys[12], (D,), jnp.float32) ** block_scale(arg_keys[12], (D,), ((0, 16),), -0.2, 0.2)), 57.7, 230.8),
        "fc1_col": jnp.clip(jnp.exp(math.log(230.8) - 1.3862944 * jax.random.uniform(arg_keys[13], (FF,), jnp.float32) ** block_scale(arg_keys[13], (FF,), ((0, 2),), -0.2, 0.2)), 57.7, 230.8),
        "fc2_row": jnp.clip(jnp.exp(math.log(923.2) - 1.3862944 * jax.random.uniform(arg_keys[14], (FF,), jnp.float32) ** block_scale(arg_keys[14], (FF,), ((0, 2),), -0.2, 0.2)), 230.8, 923.2),
        "fc2_col": jnp.clip(jnp.exp(math.log(923.2) - 1.3862944 * jax.random.uniform(arg_keys[15], (D,), jnp.float32) ** block_scale(arg_keys[15], (D,), ((0, 16),), -0.2, 0.2)), 230.8, 923.2),
        "vec_second": draw_vec_second(jax.random.fold_in(arg_keys[17], 71), 0),
    }


EPS_NORM = 1e-05
EPS_ONE = 1e-30
CLIP_LEVEL = 1.0
LEARN_RATE = 0.5
HIGHEST = lax.Precision.HIGHEST

@jax.custom_vjp
def low(v):
    return lax.optimization_barrier(v.astype(jnp.bfloat16)).astype(jnp.float32)

@jax.custom_vjp
def low_back(v):
    return v

def low_keep(v):
    return (low(v), None)

def low_pass(kept, grad):
    return (grad,)

def back_keep(v):
    return (v, None)

def back_low(kept, grad):
    return (low(grad),)
low.defvjp(low_keep, low_pass)
low_back.defvjp(back_keep, back_low)

def layer_norm(values, gain, shift):
    average = lax.optimization_barrier(jnp.mean(values, axis=-1, keepdims=True))
    center = values - average
    spread = lax.optimization_barrier(jnp.mean(center * center, axis=-1, keepdims=True))
    return center * lax.rsqrt(spread + EPS_NORM) * gain + shift

def image_forward(inputs, params, valid_row):
    w_qkv, w_out, w_fc1, w_fc2, vectors = [low(weight) for weight in params]
    keep_rows = valid_row.astype(jnp.float32)[:, None]
    normed = low(layer_norm(inputs, vectors[0], vectors[1]))
    biases = jnp.stack([vectors[2], jnp.zeros_like(vectors[2]), vectors[3]])[:, None, :]
    projected = jnp.einsum('sd,cde->cse', normed, w_qkv, precision=HIGHEST) + biases
    projected = low(low_back(projected)).reshape(3, SLOT, HEADS, HEAD_DIM)
    scores = low_back(jnp.einsum('qhd,khd->hqk', projected[0], projected[1], precision=HIGHEST)) * HEAD_DIM ** (-0.5)
    scores = jnp.where(valid_row[None, None, :] > 0, scores, -1e+30)
    highest = lax.optimization_barrier(jnp.max(scores, axis=-1, keepdims=True))
    raised = jnp.exp(scores - highest)
    attention = raised / lax.optimization_barrier(jnp.sum(raised, axis=-1, keepdims=True))
    mixed_heads = jnp.einsum('hqk,khd->qhd', low(attention), projected[2], precision=HIGHEST)
    mixed_heads = low(low_back(mixed_heads.reshape(SLOT, D)))
    branch = low_back(jnp.dot(mixed_heads, w_out, precision=HIGHEST))
    middle = inputs + (branch + vectors[4]) * keep_rows
    normed_two = low(layer_norm(middle, vectors[5], vectors[6]))
    hidden_bias = vectors[7:VEC - 1].reshape(FF)
    preact = low_back(jnp.dot(normed_two, w_fc1, precision=HIGHEST) + hidden_bias)
    active = low(preact * jax.nn.sigmoid(1.702 * preact))
    branch_two = low_back(jnp.dot(active, w_fc2, precision=HIGHEST))
    return middle + (branch_two + vectors[VEC - 1]) * keep_rows

def factored(grad, weight, row_old, col_old):
    decay_rate = 1.0 - STEP ** (-0.8)
    square = grad * grad + EPS_ONE
    row_new = decay_rate * row_old + (1.0 - decay_rate) * lax.optimization_barrier(jnp.mean(square, axis=-1))
    col_new = decay_rate * col_old + (1.0 - decay_rate) * lax.optimization_barrier(jnp.mean(square, axis=-2))
    row_mean = lax.optimization_barrier(jnp.mean(row_new, axis=-1, keepdims=True))
    scaled = row_new[..., :, None] * col_new[..., None, :] / row_mean[..., None]
    update = grad * lax.rsqrt(scaled)
    update_norm = jnp.sqrt(jnp.mean(update * update) + 1e-06)
    update = update / jnp.maximum(1.0, update_norm / CLIP_LEVEL)
    size_weight = jnp.sqrt(jnp.mean(weight * weight) + 1e-06)
    return (row_new, col_new, weight - LEARN_RATE * size_weight * update)

def group_total(per_row):
    wide_sum = lax.optimization_barrier(jnp.sum(per_row[7:VEC - 1], keepdims=True))
    return jnp.concatenate([per_row[:7], jnp.broadcast_to(wide_sum, (VEC - 8,)), per_row[VEC - 1:]])

def row_counts():
    return jnp.concatenate([jnp.full((7,), D, jnp.float32), jnp.full((VEC - 8,), FF, jnp.float32), jnp.full((1,), D, jnp.float32)])

def vector_step(grad, weight, second_old):
    decay_rate = 1.0 - STEP ** (-0.8)
    second = decay_rate * second_old + (1.0 - decay_rate) * (grad * grad + EPS_ONE)
    update = grad * lax.rsqrt(second)
    counts = row_counts()
    update_norm = jnp.sqrt(group_total(lax.optimization_barrier(jnp.sum(update * update, axis=1))) / counts + 1e-06)
    update = update / jnp.maximum(1.0, update_norm / CLIP_LEVEL)[:, None]
    size_weight = jnp.sqrt(group_total(lax.optimization_barrier(jnp.sum(weight * weight, axis=1))) / counts + 1e-06)
    return (second, weight - LEARN_RATE * size_weight[:, None] * update)

def reference(inputs, cotangent, token_mask, w_qkv, w_out, w_fc1, w_fc2, vectors, qkv_row, qkv_col, out_row, out_col, fc1_row, fc1_col, fc2_row, fc2_col, vec_second):
    params = (w_qkv, w_out, w_fc1, w_fc2, vectors)
    image_rows = inputs.reshape(IMAGES, SLOT, D)
    grads_in = cotangent.astype(jnp.float32).reshape(IMAGES, SLOT, D)

    def one_image(totals, item_all):
        rows_now, grad_rows, valid_row = item_all

        def forward(values, weights):
            return image_forward(values, weights, valid_row)
        output, pullback = jax.vjp(forward, rows_now, params)
        grad_values, grad_params = pullback(grad_rows)
        return (jax.tree.map(jnp.add, totals, grad_params), (output, grad_values))
    zero_grads = jax.tree.map(jnp.zeros_like, params)
    totals, (outputs, grads_values) = lax.scan(one_image, zero_grads, (image_rows, grads_in, token_mask))
    grad_qkv, grad_out, grad_fc1, grad_fc2, grad_vectors = totals
    qkv_row_new, qkv_col_new, new_qkv = factored(grad_qkv, w_qkv, qkv_row, qkv_col)
    out_row_new, out_col_new, new_out = factored(grad_out, w_out, out_row, out_col)
    fc1_row_new, fc1_col_new, new_fc1 = factored(grad_fc1, w_fc1, fc1_row, fc1_col)
    fc2_row_new, fc2_col_new, new_fc2 = factored(grad_fc2, w_fc2, fc2_row, fc2_col)
    vec_second_new, new_vectors = vector_step(grad_vectors, vectors, vec_second)
    return (outputs.reshape(ROWS, D), grads_values.reshape(ROWS, D), grad_qkv, grad_out, grad_fc1, grad_fc2, grad_vectors, new_qkv, new_out, new_fc1, new_fc2, new_vectors, qkv_row_new, qkv_col_new, out_row_new, out_col_new, fc1_row_new, fc1_col_new, fc2_row_new, fc2_col_new, vec_second_new)
```

```python
import functools

import jax
import jax.numpy as jnp
from jax import lax
from jax.experimental import pallas as pl
from jax.experimental.pallas import tpu as pltpu
from jax.sharding import PartitionSpec as P

HEAD_DIM = 64
FF = 4096
STEP = 20
VEC = 12
LANES = 128

EPS_NORM = 1e-05
EPS_ONE = 1e-30
CLIP_LEVEL = 1.0
LEARN_RATE = 0.5
MESH = pl.DeviceIdType.MESH
LOG2E = 1.4426950408889634


def grid_of(count):
    return {16: (4, 2, 2), 32: (2, 4, 4)}.get(count, (count, 1, 1))


def norm_parts(values):
    average = jnp.mean(values, axis=-1, keepdims=True)
    center = values - average
    inverse = lax.rsqrt(jnp.mean(center * center, axis=-1, keepdims=True) + EPS_NORM)
    return (center * inverse, inverse)


def norm_back(grad_normed, normed, inverse, gain):
    scaled = grad_normed * gain
    first_mean = jnp.mean(scaled, axis=-1, keepdims=True)
    second_mean = jnp.mean(scaled * normed, axis=-1, keepdims=True)
    return inverse * (scaled - first_mean - normed * second_mean)


class Place:
    def __init__(self, dims, tensor):
        self.dims = dims
        self.tensor = tensor
        fsdp = lax.axis_index("fsdp")
        _, ny, nx = dims
        self.at = (fsdp // (ny * nx), (fsdp // nx) % ny, fsdp % nx)
        self.rank = lax.axis_index("tensor")

    def moved(self, axis, step):
        place = list(self.at) + [self.rank]
        size = (*self.dims, self.tensor)[axis]
        place[axis] = lax.rem(place[axis] + step + size, size)
        return tuple(place)

    def device(self, place):
        z, y, x, rank = place
        return {"fsdp": (z * self.dims[1] + y) * self.dims[2] + x, "tensor": rank}

    def size(self, axis):
        return (*self.dims, self.tensor)[axis]

    def barrier(self):
        sem = pltpu.get_barrier_semaphore()
        count = 0
        for axis in range(4):
            for step in range(1, self.size(axis)):
                pl.semaphore_signal(
                    sem,
                    inc=1,
                    device_id=self.device(self.moved(axis, step)),
                    device_id_type=MESH,
                )
                count += 1
        if count:
            pl.semaphore_wait(sem, count)


def axis_order(half):
    return (0, 1, 2) if half == 0 else (0, 2, 1)


def gather_kernel(dims, tensor, parts, pack_ref, *refs):
    outs, (local_sem, send_sem, recv_sem) = refs[: len(parts)], refs[len(parts) :]
    here = Place(dims, tensor)
    rows_all = pack_ref.shape[0]
    half_rows = rows_all // 2

    def rows(half):
        return pl.ds(half * half_rows, half_rows)

    def columns(item, place):
        _, _, out, start, width, shared = parts_items[item]
        total = widths[out]
        base = 0 if shared else place[3] * total
        return pl.ds(pl.multiple_of(base + start, LANES), width)

    parts_items = []
    widths = []
    for out, (offset, width, chunks, shared) in enumerate(parts):
        widths.append(width)
        for chunk in range(chunks):
            size = width // chunks
            parts_items.append((offset + chunk * size, size, out, chunk * size, size, shared))
    count = len(parts_items)

    def region(item, half, place, free):
        out = outs[parts_items[item][2]]
        index = tuple(slice(None) if a in free else place[a] for a in range(3))
        return out.at[(*index, rows(half), columns(item, place))]

    def shard(item, half):
        start, width = parts_items[item][:2]
        return pack_ref.at[rows(half), pl.ds(start, width)]

    def axes(item, half):
        order = axis_order(half)
        return order if parts_items[item][5] else (*order, 3)

    own_place = (*here.at, here.rank)

    def copies(item, half, phase, landing):
        order = axes(item, half)
        axis, free = order[phase], order[:phase]
        found = []
        for step in range(1, here.size(axis)):
            own = region(item, half, own_place, free)
            if landing:
                src = dst = region(item, half, here.moved(axis, -step), free)
            else:
                src, dst = (shard(item, half) if phase == 0 else own), own
            found.append(
                pltpu.make_async_remote_copy(
                    src_ref=src,
                    dst_ref=dst,
                    send_sem=send_sem.at[item, half, phase, step - 1],
                    recv_sem=recv_sem.at[item, half, phase, step - 1],
                    device_id=here.device(here.moved(axis, step)),
                    device_id_type=MESH,
                )
            )
        return found

    here.barrier()
    local = []
    sent = []
    for item in range(count):
        for half in range(2):
            copy = pltpu.make_async_copy(
                shard(item, half), region(item, half, own_place, ()), local_sem.at[item, half]
            )
            copy.start()
            local.append(copy)
    phases = 4
    for wave in range(count + phases):
        for phase in reversed(range(phases + 1)):
            item = wave - phase
            if not 0 <= item < count:
                continue
            for half in range(2):
                order = axes(item, half)
                if 0 < phase <= len(order):
                    for copy in copies(item, half, phase - 1, True):
                        copy.wait_recv()
                if phase == 1:
                    local[2 * item + half].wait()
                if phase < len(order):
                    for copy in copies(item, half, phase, False):
                        copy.start()
                        sent.append(copy)
    for copy in sent:
        copy.wait_send()


def gather_weights(dims, tensor, pack, parts):
    rows = pack.shape[0]
    shapes = [
        jax.ShapeDtypeStruct(
            (*dims, rows, width * (1 if shared else tensor)), jnp.bfloat16
        )
        for _, width, _, shared in parts
    ]
    count = sum(chunks for _, _, chunks, _ in parts)
    peers = max(2, *dims, tensor) - 1
    anywhere = pl.BlockSpec(memory_space=pl.ANY)
    return pl.pallas_call(
        functools.partial(gather_kernel, dims, tensor, parts),
        out_shape=shapes,
        in_specs=[anywhere],
        out_specs=[anywhere] * len(parts),
        scratch_shapes=[
            pltpu.SemaphoreType.DMA((count, 2)),
            pltpu.SemaphoreType.DMA((count, 2, 4, peers)),
            pltpu.SemaphoreType.DMA((count, 2, 4, peers)),
        ],
        compiler_params=pltpu.CompilerParams(collective_id=0, has_side_effects=True),
    )(pack)


def reduce_kernel(dims, tensor, items, *refs):
    n_grads = 1 + max(item[0] for item in items)
    grads = refs[:n_grads]
    total_ref = refs[n_grads]
    own, from_core, one_x, one_y, two_y, two_x, from_z, local_sem, send_sem, recv_sem = refs[n_grads + 1 :]
    here = Place(dims, tensor)
    nz, ny, nx = dims
    half_rows = own.shape[4]
    own_place = (*here.at, here.rank)
    count = len(items)

    def columns(item):
        _, _, width, _, offset = items[item]
        return pl.ds(offset, width)

    def grad(item, half, rank):
        which, start, width, total, _ = items[item]
        column = pl.ds(pl.multiple_of(rank * total + start, LANES), width)
        return grads[which].at[:, :, :, pl.ds(half * half_rows, half_rows), column]

    def order(half):
        return (3, 2, 1, 0) if half == 0 else (3, 1, 2, 0)

    def part(item, half, place, fixed):
        index = tuple(place[a] if a in fixed else slice(None) for a in range(3))
        return own.at[(half, *index, slice(None), columns(item))]

    def slot(item, half, phase, step):
        if phase == 0:
            return from_core.at[half, step - 1, :, :, :, :, columns(item)]
        if phase == 3:
            return from_z.at[half, step - 1, :, columns(item)]
        if phase == 1:
            buffer = one_x if half == 0 else one_y
            return buffer.at[step - 1, :, :, :, columns(item)]
        buffer = two_y if half == 0 else two_x
        return buffer.at[step - 1, :, :, columns(item)]

    def copies(item, half, phase):
        axes = order(half)
        axis, fixed = axes[phase], axes[1 : phase + 1]
        found = []
        for step in range(1, here.size(axis)):
            target = here.moved(axis, step)
            src = grad(item, half, target[3]) if phase == 0 else part(item, half, target, fixed)
            found.append(
                pltpu.make_async_remote_copy(
                    src_ref=src,
                    dst_ref=slot(item, half, phase, step),
                    send_sem=send_sem.at[item, half, phase, step - 1],
                    recv_sem=recv_sem.at[item, half, phase, step - 1],
                    device_id=here.device(target),
                    device_id_type=MESH,
                )
            )
        return found

    def add_in(item, half, phase):
        axes = order(half)
        axis, fixed = axes[phase], axes[1 : phase + 1]
        column = columns(item)
        steps = here.size(axis) - 1
        if phase == 3:
            value = own[(half, *here.at, slice(None), column)].astype(jnp.float32)
            for step in range(steps):
                value = value + from_z[half, step, :, column].astype(jnp.float32)
            total_ref[pl.ds(half * half_rows, half_rows), column] = value
            return
        if steps == 0:
            return
        free = [a for a in range(3) if a not in fixed]
        sizes = [dims[a] for a in free]
        loops = 1
        for size in sizes:
            loops *= size

        def body(at, carry):
            place = list(here.at)
            inner = []
            rest = at
            for axis_at, size in reversed(list(zip(free, sizes))):
                place[axis_at] = rest % size
                inner.insert(0, rest % size)
                rest = rest // size
            where = (half, *place, slice(None), column)
            value = own[where]
            for step in range(steps):
                if phase == 0:
                    piece = from_core[(half, step, *inner, slice(None), column)]
                elif phase == 1:
                    piece = (one_x if half == 0 else one_y)[(step, *inner, slice(None), column)]
                else:
                    piece = (two_y if half == 0 else two_x)[(step, *inner, slice(None), column)]
                value = value + piece
            own[where] = value
            return carry

        lax.fori_loop(0, loops, body, 0)

    here.barrier()
    local = {}
    sent = []
    for item in range(count):
        for half in range(2):
            copy = pltpu.make_async_copy(
                grad(item, half, here.rank), part(item, half, own_place, ()), local_sem.at[item, half]
            )
            copy.start()
            local[item, half] = copy
    phases = 4
    for wave in range(count + phases):
        for phase in reversed(range(phases + 1)):
            item = wave - phase
            if not 0 <= item < count:
                continue
            for half in range(2):
                if phase:
                    if phase == 1:
                        local[item, half].wait()
                    for copy in copies(item, half, phase - 1):
                        copy.wait_recv()
                    add_in(item, half, phase - 1)
                if phase < phases:
                    for copy in copies(item, half, phase):
                        copy.start()
                        sent.append(copy)
    for copy in sent:
        copy.wait_send()


def reduce_grads(dims, tensor, grads, widths, chunks):
    rows = grads[0].shape[3]
    half_rows = rows // 2
    items = []
    offset = 0
    for which, (width, pieces) in enumerate(zip(widths, chunks)):
        size = width // pieces
        for piece in range(pieces):
            items.append((which, piece * size, size, width, offset))
            offset += size
    nz, ny, nx = dims
    peers = max(2, *dims, tensor) - 1
    low = jnp.bfloat16
    anywhere = pl.BlockSpec(memory_space=pl.ANY)

    def hold(*shape):
        return pltpu.VMEM(tuple(max(1, size) for size in shape), low)

    return pl.pallas_call(
        functools.partial(reduce_kernel, dims, tensor, tuple(items)),
        out_shape=jax.ShapeDtypeStruct((rows, offset), jnp.float32),
        in_specs=[anywhere] * len(grads),
        out_specs=pl.BlockSpec(memory_space=pltpu.VMEM),
        scratch_shapes=[
            hold(2, nz, ny, nx, half_rows, offset),
            hold(2, tensor - 1, nz, ny, nx, half_rows, offset),
            hold(nx - 1, nz, ny, half_rows, offset),
            hold(ny - 1, nz, nx, half_rows, offset),
            hold(ny - 1, nz, half_rows, offset),
            hold(nx - 1, nz, half_rows, offset),
            hold(2, nz - 1, half_rows, offset),
            pltpu.SemaphoreType.DMA((len(items), 2)),
            pltpu.SemaphoreType.DMA((len(items), 2, 4, peers)),
            pltpu.SemaphoreType.DMA((len(items), 2, 4, peers)),
        ],
        compiler_params=pltpu.CompilerParams(
            collective_id=1, has_side_effects=True, vmem_limit_bytes=60 << 20
        ),
    )(*grads)


def attend_kernel(query_ref, key_ref, value_ref, bias_ref, mixed_ref):
    bias = bias_ref[...]
    for head in range(2):
        part = slice(head * HEAD_DIM, (head + 1) * HEAD_DIM)
        scores = lax.dot_general(
            query_ref[:, part], key_ref[:, part], (((1,), (1,)), ((), ())), preferred_element_type=jnp.float32
        )
        scores = scores * (HEAD_DIM ** (-0.5) * LOG2E) + bias
        raised = jnp.exp2(scores - jnp.max(scores, axis=1, keepdims=True))
        summed = jnp.sum(raised, axis=1, keepdims=True)
        attention = (raised * (1.0 / summed)).astype(jnp.bfloat16)
        mixed = jnp.dot(attention, value_ref[:, part], preferred_element_type=jnp.float32)
        mixed_ref[:, part] = mixed.astype(jnp.bfloat16)


def attend_back_kernel(query_ref, key_ref, value_ref, bias_ref, grad_ref, out_ref):
    bias = bias_ref[...]
    contract_last = (((1,), (1,)), ((), ()))
    for head in range(2):
        part = slice(head * HEAD_DIM, (head + 1) * HEAD_DIM)
        query, key, value, grad = (r[:, part] for r in (query_ref, key_ref, value_ref, grad_ref))
        scores = lax.dot_general(key, query, contract_last, preferred_element_type=jnp.float32)
        scores = scores * (HEAD_DIM ** (-0.5) * LOG2E) + bias
        raised = jnp.exp2(scores - jnp.max(scores, axis=0, keepdims=True))
        attention = raised * (1.0 / jnp.sum(raised, axis=0, keepdims=True))
        grad_value = jnp.dot(attention.astype(jnp.bfloat16), grad, preferred_element_type=jnp.float32)
        grad_attention = lax.dot_general(value, grad, contract_last, preferred_element_type=jnp.float32)
        weighted = jnp.sum(attention * grad_attention, axis=0, keepdims=True)
        grad_scores = (attention * (grad_attention - weighted) * HEAD_DIM ** (-0.5)).astype(jnp.bfloat16)
        grad_key = jnp.dot(grad_scores, query, preferred_element_type=jnp.float32)
        grad_query = jnp.dot(key.T, grad_scores, preferred_element_type=jnp.float32).T
        out_ref[0, :, part] = grad_query.astype(jnp.bfloat16)
        out_ref[1, :, part] = grad_key.astype(jnp.bfloat16)
        out_ref[2, :, part] = grad_value.astype(jnp.bfloat16)


def pair_column(kind, columns):
    per_rank = columns // LANES

    def index(pair):
        return (0, (pair // per_rank) * 3 * per_rank + kind * per_rank + pair % per_rank)

    return index


def attend(projected, bias_row, columns, width):
    rows = projected.shape[0]
    blocks = [pl.BlockSpec((rows, LANES), pair_column(kind, columns)) for kind in range(3)]
    return pl.pallas_call(
        attend_kernel,
        grid=(width // LANES,),
        out_shape=jax.ShapeDtypeStruct((rows, width), jnp.bfloat16),
        in_specs=[*blocks, pl.BlockSpec((1, rows), lambda pair: (0, 0))],
        out_specs=pl.BlockSpec((rows, LANES), lambda pair: (0, pair)),
        compiler_params=pltpu.CompilerParams(vmem_limit_bytes=40 << 20),
    )(projected, projected, projected, bias_row)


def attend_back(projected, bias_column, grad_mixed, columns, width):
    rows = projected.shape[0]
    blocks = [pl.BlockSpec((rows, LANES), pair_column(kind, columns)) for kind in range(3)]
    plain = pl.BlockSpec((rows, LANES), lambda pair: (0, pair))
    return pl.pallas_call(
        attend_back_kernel,
        grid=(width // LANES,),
        out_shape=jax.ShapeDtypeStruct((3, rows, width), jnp.bfloat16),
        in_specs=[*blocks, pl.BlockSpec((rows, 1), lambda pair: (0, 0)), plain],
        out_specs=pl.BlockSpec((3, rows, LANES), lambda pair: (0, 0, pair)),
        compiler_params=pltpu.CompilerParams(vmem_limit_bytes=40 << 20),
    )(projected, projected, projected, bias_column, grad_mixed)


def group_total(per_row):
    wide_sum = jnp.sum(per_row[7 : VEC - 1], keepdims=True)
    return jnp.concatenate(
        [per_row[:7], jnp.broadcast_to(wide_sum, (VEC - 8,)), per_row[VEC - 1 :]]
    )


def on_device(
    inputs,
    cotangent,
    token_mask,
    w_qkv,
    w_out,
    w_fc1,
    w_fc2,
    vectors,
    qkv_row,
    qkv_col,
    out_row,
    out_col,
    fc1_row,
    fc1_col,
    fc2_row,
    fc2_col,
    vec_second,
):
    tensor_count = lax.axis_size("tensor")
    fsdp_count = lax.axis_size("fsdp")
    dims = grid_of(fsdp_count)
    tensor_rank = lax.axis_index("tensor")
    rows_here, width = inputs.shape
    own_rows, columns = w_qkv.shape[1:]
    hidden = w_fc1.shape[1]
    low = jnp.bfloat16

    keep = lax.dynamic_slice_in_dim(token_mask, tensor_rank, 1, 0)
    keep_rows = keep.reshape(rows_here, 1).astype(jnp.float32)
    bias = jnp.where(keep > 0, 0.0, -1e30).astype(jnp.float32)

    widths = (3 * columns, columns, hidden, hidden, LANES)
    offsets = [sum(widths[:at]) for at in range(5)]
    pack = jnp.concatenate(
        [
            w_qkv.transpose(1, 0, 2).reshape(own_rows, 3 * columns),
            w_out.T,
            w_fc1,
            w_fc2.T,
            jnp.pad(vectors.T, ((0, 0), (0, LANES - VEC))),
        ],
        axis=1,
    ).astype(low)
    parts = (
        (offsets[0], widths[0], 1, False),
        (offsets[4], widths[4], 1, True),
        (offsets[1], widths[1], 1, False),
        (offsets[2], widths[2], 2, False),
        (offsets[3], widths[3], 2, False),
    )
    weight_qkv, table, weight_out, weight_one, weight_two = (
        array.reshape(width, array.shape[-1])
        for array in gather_weights(dims, tensor_count, pack, parts)
    )
    table = table[:, :VEC].T.astype(jnp.float32)
    head_bias = jnp.stack(
        [
            table[2].reshape(tensor_count, columns),
            jnp.zeros((tensor_count, columns), jnp.float32),
            table[3].reshape(tensor_count, columns),
        ],
        axis=1,
    ).reshape(1, 3 * width)
    bias_hidden = table[7 : VEC - 1].reshape(1, FF)

    def dot(left, right, left_dim, right_dim):
        return lax.dot_general(
            left, right, (((left_dim,), (right_dim,)), ((), ())), preferred_element_type=jnp.float32
        )

    normed_one, inverse_one = norm_parts(inputs)
    low_one = (normed_one * table[0] + table[1]).astype(low)
    projected = (dot(low_one, weight_qkv, 1, 0) + head_bias).astype(low)
    mixed_rows = attend(projected, bias, columns, width)
    middle = inputs + (dot(mixed_rows, weight_out, 1, 1) + table[4]) * keep_rows
    normed_two, inverse_two = norm_parts(middle)
    low_two = (normed_two * table[5] + table[6]).astype(low)
    preact = dot(low_two, weight_one, 1, 0) + bias_hidden
    sigmoid_pre = jax.nn.sigmoid(1.702 * preact)
    active = (preact * sigmoid_pre).astype(low)
    block_out = middle + (dot(active, weight_two, 1, 1) + table[VEC - 1]) * keep_rows

    grad_top = cotangent.astype(jnp.float32)
    grad_masked = grad_top * keep_rows
    back_two = grad_masked.astype(low)
    grad_two = dot(back_two, active, 0, 0).astype(low)
    grad_active = dot(back_two, weight_two, 1, 0)
    derivative = sigmoid_pre + 1.702 * preact * sigmoid_pre * (1.0 - sigmoid_pre)
    grad_pre = (grad_active * derivative).astype(low)
    grad_one = dot(low_two, grad_pre, 0, 0).astype(low)
    grad_low_two = dot(grad_pre, weight_one, 1, 1)
    grad_middle = grad_top + norm_back(grad_low_two, normed_two, inverse_two, table[5])
    grad_masked_one = grad_middle * keep_rows
    back_one = grad_masked_one.astype(low)
    grad_out_weight = dot(back_one, mixed_rows, 0, 0).astype(low)
    grad_mixed = dot(back_one, weight_out, 1, 0).astype(low)
    grad_heads = attend_back(projected, bias.reshape(rows_here, 1), grad_mixed, columns, width)
    grad_proj = (
        grad_heads.reshape(3, rows_here, tensor_count, columns)
        .transpose(1, 2, 0, 3)
        .reshape(rows_here, 3 * width)
    )
    grad_qkv = dot(low_one, grad_proj, 0, 0).astype(low)
    grad_low_one = dot(grad_proj, weight_qkv, 1, 1)
    input_grad = grad_middle + norm_back(grad_low_one, normed_one, inverse_one, table[0])

    def column_sum(values):
        return jnp.sum(values, axis=0, dtype=jnp.float32)

    grad_table = jnp.concatenate(
        [
            jnp.stack(
                [
                    column_sum(grad_low_one * normed_one),
                    column_sum(grad_low_one),
                    column_sum(grad_heads[0]),
                    column_sum(grad_heads[2]),
                    column_sum(grad_masked_one),
                    column_sum(grad_low_two * normed_two),
                    column_sum(grad_low_two),
                ]
            ),
            column_sum(grad_pre).reshape(FF // width, width),
            column_sum(grad_masked)[None],
        ],
        0,
    )
    table_block = jnp.pad(grad_table.T.astype(low), ((0, 0), (0, LANES - VEC)))
    grad_arrays = [
        array.reshape(*dims, own_rows, array.shape[1])
        for array in (
            grad_two,
            grad_one,
            grad_out_weight,
            grad_qkv,
            jnp.concatenate([table_block] * tensor_count, axis=1),
        )
    ]
    reduced = reduce_grads(
        dims, tensor_count, grad_arrays, (hidden, hidden, columns, 3 * columns, LANES), (2, 2, 1, 1, 1)
    )
    own_two = reduced[:, :hidden].T
    own_one = reduced[:, hidden : 2 * hidden]
    own_out = reduced[:, 2 * hidden : 2 * hidden + columns].T
    own_qkv = (
        reduced[:, 2 * hidden + columns : 2 * hidden + 4 * columns]
        .reshape(own_rows, 3, columns)
        .transpose(1, 0, 2)
    )
    table_grad = reduced[:, 2 * hidden + 4 * columns :][:, :VEC].T

    squares_qkv = own_qkv * own_qkv
    squares_out = own_out * own_out
    squares_one = own_one * own_one
    squares_two = own_two * own_two
    tensor_part = jnp.concatenate(
        [
            jnp.sum(squares_qkv, axis=2),
            jnp.sum(squares_out, axis=0)[None],
            jnp.sum(squares_one, axis=1)[None],
            jnp.sum(squares_two, axis=0)[None],
        ],
        0,
    )
    fsdp_part = (
        jnp.sum(squares_qkv, axis=1),
        jnp.sum(squares_out, axis=1),
        jnp.sum(squares_one, axis=0),
        jnp.sum(squares_two, axis=1),
    )
    tensor_total = lax.psum(tensor_part, "tensor")
    fsdp_total = lax.psum((fsdp_part[0], fsdp_part[1], fsdp_part[2], fsdp_part[3]), "fsdp")
    decay_rate = 1.0 - STEP ** (-0.8)
    keep_old = 1.0 - decay_rate
    qkv_row_new = decay_rate * qkv_row + keep_old * (tensor_total[0:3] / width + EPS_ONE)
    qkv_col_new = decay_rate * qkv_col + keep_old * (fsdp_total[0] / width + EPS_ONE)
    out_row_new = decay_rate * out_row + keep_old * (fsdp_total[1] / width + EPS_ONE)
    out_col_new = decay_rate * out_col + keep_old * (tensor_total[3] / width + EPS_ONE)
    fc1_row_new = decay_rate * fc1_row + keep_old * (tensor_total[4] / FF + EPS_ONE)
    fc1_col_new = decay_rate * fc1_col + keep_old * (fsdp_total[2] / width + EPS_ONE)
    fc2_row_new = decay_rate * fc2_row + keep_old * (fsdp_total[3] / width + EPS_ONE)
    fc2_col_new = decay_rate * fc2_col + keep_old * (tensor_total[5] / FF + EPS_ONE)
    vec_second_new = decay_rate * vec_second + keep_old * (table_grad * table_grad + EPS_ONE)
    vector_update = table_grad * lax.rsqrt(vec_second_new)
    ratio_qkv = jnp.sum(
        squares_qkv / (qkv_row_new[:, :, None] * qkv_col_new[:, None, :]), axis=(1, 2)
    )
    ratio_out = jnp.sum(squares_out / (out_row_new[:, None] * out_col_new[None, :]))
    ratio_one = jnp.sum(squares_one / (fc1_row_new[:, None] * fc1_col_new[None, :]))
    ratio_two = jnp.sum(squares_two / (fc2_row_new[:, None] * fc2_col_new[None, :]))
    ratios = jnp.concatenate([ratio_qkv, jnp.stack([ratio_out, ratio_one, ratio_two])])
    row_sums = jnp.concatenate(
        [
            jnp.sum(qkv_row_new, axis=1) / tensor_count,
            jnp.stack(
                [
                    jnp.sum(out_row_new) / fsdp_count,
                    jnp.sum(fc1_row_new) / tensor_count,
                    jnp.sum(fc2_row_new) / fsdp_count,
                ]
            ),
        ]
    )
    weight_sums = jnp.stack(
        [
            jnp.sum(w_qkv * w_qkv),
            jnp.sum(w_out * w_out),
            jnp.sum(w_fc1 * w_fc1),
            jnp.sum(w_fc2 * w_fc2),
        ]
    )
    vector_sums = jnp.sum(vector_update * vector_update, axis=1) / tensor_count
    vector_weight = jnp.sum(vectors * vectors, axis=1) / tensor_count
    sums = jnp.concatenate([ratios, row_sums, weight_sums, vector_sums, vector_weight])
    sums = lax.psum(sums, ("fsdp", "tensor"))
    ratios, row_sums, weight_sums, vector_sums, vector_weight = jnp.split(
        sums, [6, 12, 16, 16 + VEC]
    )
    row_means = row_sums / jnp.array([width, width, width, width, width, FF], jnp.float32)
    update_sq = jnp.stack(
        [
            jnp.sum(row_means[:3] * ratios[:3]),
            row_means[3] * ratios[3],
            row_means[4] * ratios[4],
            row_means[5] * ratios[5],
        ]
    )
    entries = jnp.array([3 * width * width, width * width, width * FF, FF * width], jnp.float32)
    damping = 1.0 / jnp.maximum(1.0, jnp.sqrt(update_sq / entries + 1e-06) / CLIP_LEVEL)
    step_size = LEARN_RATE * jnp.sqrt(weight_sums / entries + 1e-06) * damping
    update_qkv = own_qkv * lax.rsqrt(
        qkv_row_new[:, :, None] * qkv_col_new[:, None, :] / row_means[:3, None, None]
    )
    update_out = own_out * lax.rsqrt(out_row_new[:, None] * out_col_new[None, :] / row_means[3])
    update_one = own_one * lax.rsqrt(fc1_row_new[:, None] * fc1_col_new[None, :] / row_means[4])
    update_two = own_two * lax.rsqrt(fc2_row_new[:, None] * fc2_col_new[None, :] / row_means[5])
    new_qkv = w_qkv - step_size[0] * update_qkv
    new_out = w_out - step_size[1] * update_out
    new_fc1 = w_fc1 - step_size[2] * update_one
    new_fc2 = w_fc2 - step_size[3] * update_two
    counts = jnp.concatenate(
        [
            jnp.full((7,), width, jnp.float32),
            jnp.full((VEC - 8,), FF, jnp.float32),
            jnp.full((1,), width, jnp.float32),
        ]
    )
    vector_norm = jnp.sqrt(group_total(vector_sums) / counts + 1e-06)
    vector_size = jnp.sqrt(group_total(vector_weight) / counts + 1e-06)
    new_vectors = (
        vectors
        - (LEARN_RATE * vector_size / jnp.maximum(1.0, vector_norm / CLIP_LEVEL))[:, None]
        * vector_update
    )
    return (
        block_out,
        input_grad,
        own_qkv,
        own_out,
        own_one,
        own_two,
        table_grad,
        new_qkv,
        new_out,
        new_fc1,
        new_fc2,
        new_vectors,
        qkv_row_new,
        qkv_col_new,
        out_row_new,
        out_col_new,
        fc1_row_new,
        fc1_col_new,
        fc2_row_new,
        fc2_col_new,
        vec_second_new,
    )


def solution(mesh):
    in_specs = (
        P(("fsdp", "tensor"), None),
        P(("fsdp", "tensor"), None),
        P("fsdp", None),
        P(None, "fsdp", "tensor"),
        P("tensor", "fsdp"),
        P("fsdp", "tensor"),
        P("tensor", "fsdp"),
        P(None, "fsdp"),
        P(None, "fsdp"),
        P(None, "tensor"),
        P("tensor"),
        P("fsdp"),
        P("fsdp"),
        P("tensor"),
        P("tensor"),
        P("fsdp"),
        P(None, "fsdp"),
    )
    out_specs = (
        P(("fsdp", "tensor"), None),
        P(("fsdp", "tensor"), None),
        P(None, "fsdp", "tensor"),
        P("tensor", "fsdp"),
        P("fsdp", "tensor"),
        P("tensor", "fsdp"),
        P(None, "fsdp"),
        P(None, "fsdp", "tensor"),
        P("tensor", "fsdp"),
        P("fsdp", "tensor"),
        P("tensor", "fsdp"),
        P(None, "fsdp"),
        P(None, "fsdp"),
        P(None, "tensor"),
        P("tensor"),
        P("fsdp"),
        P("fsdp"),
        P("tensor"),
        P("tensor"),
        P("fsdp"),
        P(None, "fsdp"),
    )
    return jax.shard_map(
        on_device, mesh=mesh, in_specs=in_specs, out_specs=out_specs, check_vma=False
    )
```

```python
import functools

import jax
import jax.numpy as jnp
from jax import lax
from jax.experimental import pallas as pl
from jax.experimental.pallas import tpu as pltpu
from jax.sharding import PartitionSpec as P

HEAD_DIM = 64
FF = 4096
STEP = 20
VEC = 12
LANES = 128

EPS_NORM = 1e-05
EPS_ONE = 1e-30
CLIP_LEVEL = 1.0
LEARN_RATE = 0.5
MESH = pl.DeviceIdType.MESH
LOG2E = 1.4426950408889634
CONTRACT_LAST = (((1,), (1,)), ((), ()))


def grid_of(count):
    return {16: (4, 2, 2), 32: (2, 4, 4)}.get(count, (count, 1, 1))


def norm_parts(values):
    average = jnp.mean(values, axis=-1, keepdims=True)
    center = values - average
    inverse = lax.rsqrt(jnp.mean(center * center, axis=-1, keepdims=True) + EPS_NORM)
    return (center * inverse, inverse)


def norm_back(grad_normed, normed, inverse, gain):
    scaled = grad_normed * gain
    first_mean = jnp.mean(scaled, axis=-1, keepdims=True)
    second_mean = jnp.mean(scaled * normed, axis=-1, keepdims=True)
    return inverse * (scaled - first_mean - normed * second_mean)


class Place:
    def __init__(self, dims, tensor):
        self.dims = dims
        self.tensor = tensor
        fsdp = lax.axis_index("fsdp")
        _, ny, nx = dims
        self.at = (fsdp // (ny * nx), (fsdp // nx) % ny, fsdp % nx)
        self.rank = lax.axis_index("tensor")

    def moved(self, axis, step):
        place = list(self.at) + [self.rank]
        size = (*self.dims, self.tensor)[axis]
        place[axis] = lax.rem(place[axis] + step + size, size)
        return tuple(place)

    def device(self, place):
        z, y, x, rank = place
        return {"fsdp": (z * self.dims[1] + y) * self.dims[2] + x, "tensor": rank}

    def size(self, axis):
        return (*self.dims, self.tensor)[axis]

    def barrier(self):
        sem = pltpu.get_barrier_semaphore()
        count = 0
        for axis in range(4):
            for step in range(1, self.size(axis)):
                pl.semaphore_signal(
                    sem,
                    inc=1,
                    device_id=self.device(self.moved(axis, step)),
                    device_id_type=MESH,
                )
                count += 1
        if count:
            pl.semaphore_wait(sem, count)


def axis_order(half):
    return (0, 1, 2) if half == 0 else (0, 2, 1)


def gather_kernel(dims, tensor, parts, pack_ref, *refs):
    outs, (local_sem, send_sem, recv_sem) = refs[: len(parts)], refs[len(parts) :]
    here = Place(dims, tensor)
    rows_all = pack_ref.shape[0]
    half_rows = rows_all // 2

    def rows(half):
        return pl.ds(half * half_rows, half_rows)

    def columns(item, place):
        _, _, out, start, width, shared = parts_items[item]
        total = widths[out]
        base = 0 if shared else place[3] * total
        return pl.ds(pl.multiple_of(base + start, LANES), width)

    parts_items = []
    widths = []
    for out, (offset, width, chunks, shared) in enumerate(parts):
        widths.append(width)
        for chunk in range(chunks):
            size = width // chunks
            parts_items.append((offset + chunk * size, size, out, chunk * size, size, shared))
    count = len(parts_items)

    def region(item, half, place, free):
        out = outs[parts_items[item][2]]
        index = tuple(slice(None) if a in free else place[a] for a in range(3))
        return out.at[(*index, rows(half), columns(item, place))]

    def shard(item, half):
        start, width = parts_items[item][:2]
        return pack_ref.at[rows(half), pl.ds(start, width)]

    def axes(item, half):
        order = axis_order(half)
        return order if parts_items[item][5] else (*order, 3)

    own_place = (*here.at, here.rank)

    def copies(item, half, phase, landing):
        order = axes(item, half)
        axis, free = order[phase], order[:phase]
        found = []
        for step in range(1, here.size(axis)):
            own = region(item, half, own_place, free)
            if landing:
                src = dst = region(item, half, here.moved(axis, -step), free)
            else:
                src, dst = (shard(item, half) if phase == 0 else own), own
            found.append(
                pltpu.make_async_remote_copy(
                    src_ref=src,
                    dst_ref=dst,
                    send_sem=send_sem.at[item, half, phase, step - 1],
                    recv_sem=recv_sem.at[item, half, phase, step - 1],
                    device_id=here.device(here.moved(axis, step)),
                    device_id_type=MESH,
                )
            )
        return found

    here.barrier()
    local = []
    sent = []
    for item in range(count):
        for half in range(2):
            copy = pltpu.make_async_copy(
                shard(item, half), region(item, half, own_place, ()), local_sem.at[item, half]
            )
            copy.start()
            local.append(copy)
    phases = 4
    for wave in range(count + phases):
        for phase in reversed(range(phases + 1)):
            item = wave - phase
            if not 0 <= item < count:
                continue
            for half in range(2):
                order = axes(item, half)
                if 0 < phase <= len(order):
                    for copy in copies(item, half, phase - 1, True):
                        copy.wait_recv()
                if phase == 1:
                    local[2 * item + half].wait()
                if phase < len(order):
                    for copy in copies(item, half, phase, False):
                        copy.start()
                        sent.append(copy)
    for copy in sent:
        copy.wait_send()


def gather_weights(dims, tensor, pack, parts):
    rows = pack.shape[0]
    shapes = [
        jax.ShapeDtypeStruct(
            (*dims, rows, width * (1 if shared else tensor)), jnp.bfloat16
        )
        for _, width, _, shared in parts
    ]
    count = sum(chunks for _, _, chunks, _ in parts)
    peers = max(2, *dims, tensor) - 1
    anywhere = pl.BlockSpec(memory_space=pl.ANY)
    return pl.pallas_call(
        functools.partial(gather_kernel, dims, tensor, parts),
        name="gather_weights",
        out_shape=shapes,
        in_specs=[anywhere],
        out_specs=[anywhere] * len(parts),
        scratch_shapes=[
            pltpu.SemaphoreType.DMA((count, 2)),
            pltpu.SemaphoreType.DMA((count, 2, 4, peers)),
            pltpu.SemaphoreType.DMA((count, 2, 4, peers)),
        ],
        compiler_params=pltpu.CompilerParams(collective_id=0, has_side_effects=True),
    )(pack)


class Layout:
    def __init__(self, columns, hidden, order):
        sizes = {"qkv": 3 * columns, "out": columns, "one": hidden, "two": hidden, "vec": LANES}
        self.order = order
        self.sizes = sizes
        self.start = {}
        at = 0
        for name in order:
            self.start[name] = at
            at += sizes[name]
        self.total = at
        self.columns = columns

    def span(self, name):
        return (self.start[name], self.sizes[name])

    def matrices(self):
        base = self.start["qkv"]
        pairs = range(self.columns // LANES)
        spans = [[(base + (pair * 3 + at) * LANES, LANES) for pair in pairs] for at in range(3)]
        return spans + [[self.span(name)] for name in ("out", "one", "two")]


def pick(values, lane):
    row = jnp.zeros((1, LANES), jnp.float32)
    for at, value in enumerate(values):
        row = jnp.where(lane == at, value, row)
    return row


def total_of(values):
    return jnp.sum(jnp.sum(values, axis=1, keepdims=True), axis=0, keepdims=True)


def reduce_kernel(dims, tensor, items, layout, *refs):
    n_grads = 1 + max(item[0] for item in items)
    grads = refs[:n_grads]
    weights = refs[n_grads : n_grads + 4]
    state_col, state_row, second_ref, vector_ref = refs[n_grads + 4 : n_grads + 8]
    total_ref, col_new_ref, row_new_ref, second_new_ref, sums_ref = refs[n_grads + 8 : n_grads + 13]
    (
        own,
        from_core,
        one_x,
        one_y,
        two_y,
        two_x,
        from_z,
        col_sum,
        col_in,
        row_sum,
        row_in,
        small,
        small_in,
        local_sem,
        send_sem,
        recv_sem,
        sum_send,
        sum_recv,
    ) = refs[n_grads + 13 :]
    here = Place(dims, tensor)
    nz, ny, nx = dims
    half_rows = own.shape[4]
    own_place = (*here.at, here.rank)
    count = len(items)

    def columns(item):
        _, _, width, _, offset = items[item]
        return pl.ds(offset, width)

    def grad(item, half, rank):
        which, start, width, total, _ = items[item]
        column = pl.ds(pl.multiple_of(rank * total + start, LANES), width)
        return grads[which].at[:, :, :, pl.ds(half * half_rows, half_rows), column]

    def order(half):
        return (3, 2, 1, 0) if half == 0 else (3, 1, 2, 0)

    def part(item, half, place, fixed):
        index = tuple(place[a] if a in fixed else slice(None) for a in range(3))
        return own.at[(half, *index, slice(None), columns(item))]

    def slot(item, half, phase, step):
        if phase == 0:
            return from_core.at[half, step - 1, :, :, :, :, columns(item)]
        if phase == 3:
            return from_z.at[half, step - 1, :, columns(item)]
        if phase == 1:
            buffer = one_x if half == 0 else one_y
            return buffer.at[step - 1, :, :, :, columns(item)]
        buffer = two_y if half == 0 else two_x
        return buffer.at[step - 1, :, :, columns(item)]

    def copies(item, half, phase):
        axes = order(half)
        axis, fixed = axes[phase], axes[1 : phase + 1]
        found = []
        for step in range(1, here.size(axis)):
            target = here.moved(axis, step)
            src = grad(item, half, target[3]) if phase == 0 else part(item, half, target, fixed)
            found.append(
                pltpu.make_async_remote_copy(
                    src_ref=src,
                    dst_ref=slot(item, half, phase, step),
                    send_sem=send_sem.at[item, half, phase, step - 1],
                    recv_sem=recv_sem.at[item, half, phase, step - 1],
                    device_id=here.device(target),
                    device_id_type=MESH,
                )
            )
        return found

    def add_in(item, half, phase):
        axes = order(half)
        axis, fixed = axes[phase], axes[1 : phase + 1]
        column = columns(item)
        steps = here.size(axis) - 1
        if phase == 3:
            value = own[(half, *here.at, slice(None), column)].astype(jnp.float32)
            for step in range(steps):
                value = value + from_z[half, step, :, column].astype(jnp.float32)
            total_ref[pl.ds(half * half_rows, half_rows), column] = value
            return
        if steps == 0:
            return
        free = [a for a in range(3) if a not in fixed]
        sizes = [dims[a] for a in free]
        loops = 1
        for size in sizes:
            loops *= size

        def body(at, carry):
            place = list(here.at)
            inner = []
            rest = at
            for axis_at, size in reversed(list(zip(free, sizes))):
                place[axis_at] = rest % size
                inner.insert(0, rest % size)
                rest = rest // size
            where = (half, *place, slice(None), column)
            value = own[where]
            for step in range(steps):
                if phase == 0:
                    piece = from_core[(half, step, *inner, slice(None), column)]
                elif phase == 1:
                    piece = (one_x if half == 0 else one_y)[(step, *inner, slice(None), column)]
                else:
                    piece = (two_y if half == 0 else two_x)[(step, *inner, slice(None), column)]
                value = value + piece
            own[where] = value
            return carry

        lax.fori_loop(0, loops, body, 0)

    sent = []

    def exchange(kind, phase, axis, buffer, landing):
        moved = []
        for step in range(1, here.size(axis)):
            copy = pltpu.make_async_remote_copy(
                src_ref=buffer.at[phase],
                dst_ref=landing.at[phase, step - 1],
                send_sem=sum_send.at[kind, phase, step - 1],
                recv_sem=sum_recv.at[kind, phase, step - 1],
                device_id=here.device(here.moved(axis, step)),
                device_id_type=MESH,
            )
            copy.start()
            moved.append(copy)
        sent.extend(moved)

        def finish():
            value = buffer[phase]
            for step, copy in enumerate(moved):
                copy.wait_recv()
                value = value + landing[phase, step]
            buffer[phase + 1] = value

        return finish

    here.barrier()
    local = {}
    for item in range(count):
        for half in range(2):
            copy = pltpu.make_async_copy(
                grad(item, half, here.rank), part(item, half, own_place, ()), local_sem.at[item, half]
            )
            copy.start()
            local[item, half] = copy
    phases = 4
    for wave in range(count + phases):
        for phase in reversed(range(phases + 1)):
            item = wave - phase
            if not 0 <= item < count:
                continue
            for half in range(2):
                if phase:
                    if phase == 1:
                        local[item, half].wait()
                    for copy in copies(item, half, phase - 1):
                        copy.wait_recv()
                    add_in(item, half, phase - 1)
                if phase < phases:
                    for copy in copies(item, half, phase):
                        copy.start()
                        sent.append(copy)

    decay_rate = 1.0 - STEP ** (-0.8)
    keep_old = 1.0 - decay_rate
    rows = total_ref.shape[0]
    width = rows * nz * ny * nx
    long = layout.sizes["one"] * tensor
    matrices = layout.matrices()
    lane = lax.broadcasted_iota(jnp.int32, (1, LANES), 1)
    row_parts = []
    for spans in matrices:
        row_part = 0.0
        for start, size in spans:
            value = total_ref[:, pl.ds(start, size)]
            square = value * value
            col_sum[0, :, pl.ds(start, size)] = jnp.sum(square, axis=0, keepdims=True)
            row_part = row_part + jnp.sum(square, axis=1, keepdims=True)
        row_parts.append(row_part)
    row_sum[0] = pick(row_parts, lane)
    finish_row = exchange(0, 0, 3, row_sum, row_in)
    finish_col = exchange(1, 0, 0, col_sum, col_in)
    vec_start = layout.start["vec"]
    table_grad = total_ref[:, pl.ds(vec_start, LANES)]
    second_new = decay_rate * second_ref[...] + keep_old * (table_grad * table_grad + EPS_ONE)
    second_new_ref[...] = second_new
    vector_update = table_grad * lax.rsqrt(second_new)
    vector_sums = jnp.sum(vector_update * vector_update, axis=0, keepdims=True) / tensor
    vector_weight = jnp.sum(vector_ref[...] * vector_ref[...], axis=0, keepdims=True) / tensor
    weight_sums = [total_of(jnp.sum(weights[0][...] * weights[0][...], axis=0))]
    weight_sums += [total_of(ref[...] * ref[...]) for ref in weights[1:]]
    finish_row()
    row_counts = pick([jnp.full((1, 1), 1.0 / size, jnp.float32) for size in (width, width, width, width, long, long)], lane)
    row_new = decay_rate * state_row[...] + keep_old * (row_sum[1] * row_counts + EPS_ONE)
    row_new_ref[...] = row_new
    finish_col()
    exchange(1, 1, 1, col_sum, col_in)()
    exchange(1, 2, 2, col_sum, col_in)()
    col_new = decay_rate * state_col[...] + keep_old * (col_sum[3] / width + EPS_ONE)
    col_new_ref[...] = col_new
    ratios = []
    means = []
    for at, spans in enumerate(matrices):
        row_at = row_new[:, at : at + 1]
        ratio = 0.0
        for start, size in spans:
            value = total_ref[:, pl.ds(start, size)]
            col_at = col_new_ref[:, pl.ds(start, size)]
            ratio = ratio + total_of(value * value / (row_at * col_at))
        ratios.append(ratio)
        if at in (3, 5):
            means.append(jnp.sum(col_at, axis=1, keepdims=True) / (nz * ny * nx))
        else:
            means.append(jnp.sum(row_at, axis=0, keepdims=True) / tensor)
    small[0] = jnp.concatenate(
        [pick(ratios + means + weight_sums, lane), vector_sums, vector_weight, jnp.zeros((5, LANES), jnp.float32)], axis=0
    )
    for phase in range(4):
        exchange(2, phase, phase, small, small_in)()
    sums_ref[...] = small[4]
    for copy in sent:
        copy.wait_send()


def reduce_grads(dims, tensor, layout, grads, chunks, weights, states):
    rows = grads[0].shape[3]
    half_rows = rows // 2
    items = []
    offset = 0
    for which, (name, pieces) in enumerate(zip(layout.order, chunks)):
        width = layout.sizes[name]
        size = width // pieces
        for piece in range(pieces):
            items.append((which, piece * size, size, width, offset))
            offset += size
    nz, ny, nx = dims
    peers = max(2, *dims, tensor) - 1
    low = jnp.bfloat16
    full = jnp.float32
    anywhere = pl.BlockSpec(memory_space=pl.ANY)
    inside = pl.BlockSpec(memory_space=pltpu.VMEM)

    def hold(*shape):
        return pltpu.VMEM(tuple(max(1, size) for size in shape), low)

    sums = offset - LANES
    return pl.pallas_call(
        functools.partial(reduce_kernel, dims, tensor, tuple(items), layout),
        name="reduce_grads",
        out_shape=[
            jax.ShapeDtypeStruct((rows, offset), full),
            jax.ShapeDtypeStruct((1, sums), full),
            jax.ShapeDtypeStruct((rows, LANES), full),
            jax.ShapeDtypeStruct((rows, LANES), full),
            jax.ShapeDtypeStruct((8, LANES), full),
        ],
        in_specs=[anywhere] * len(grads) + [inside] * 8,
        out_specs=[inside] * 5,
        scratch_shapes=[
            hold(2, nz, ny, nx, half_rows, offset),
            hold(2, tensor - 1, nz, ny, nx, half_rows, offset),
            hold(nx - 1, nz, ny, half_rows, offset),
            hold(ny - 1, nz, nx, half_rows, offset),
            hold(ny - 1, nz, half_rows, offset),
            hold(nx - 1, nz, half_rows, offset),
            hold(2, nz - 1, half_rows, offset),
            pltpu.VMEM((4, 1, sums), full),
            pltpu.VMEM((3, peers, 1, sums), full),
            pltpu.VMEM((2, rows, LANES), full),
            pltpu.VMEM((1, peers, rows, LANES), full),
            pltpu.VMEM((5, 8, LANES), full),
            pltpu.VMEM((4, peers, 8, LANES), full),
            pltpu.SemaphoreType.DMA((len(items), 2)),
            pltpu.SemaphoreType.DMA((len(items), 2, 4, peers)),
            pltpu.SemaphoreType.DMA((len(items), 2, 4, peers)),
            pltpu.SemaphoreType.DMA((3, 4, peers)),
            pltpu.SemaphoreType.DMA((3, 4, peers)),
        ],
        compiler_params=pltpu.CompilerParams(
            collective_id=1, has_side_effects=True, vmem_limit_bytes=60 << 20
        ),
    )(*grads, *weights, *states)


def update_kernel(layout, width, long, *refs):
    total_ref, col_ref, row_ref, second_ref, sums_ref, vector_ref = refs[:6]
    weights = refs[6:10]
    own_qkv, own_out, own_one, own_two, own_table = refs[10:15]
    new_qkv, new_out, new_one, new_two, new_vectors, second_new = refs[15:21]
    qkv_row, qkv_col, out_row, out_col, one_row, one_col, two_row, two_col = refs[21:]
    lane = lax.broadcasted_iota(jnp.int32, (1, LANES), 1)

    def at(index):
        return sums_ref[0:1, index : index + 1]

    lengths = (width, width, width, width, width, long)
    means = [at(6 + m) / lengths[m] for m in range(6)]
    squares = [means[m] * at(m) for m in range(6)]
    squares = [squares[0] + squares[1] + squares[2], *squares[3:]]
    entries = (3 * width * width, width * width, width * long, width * long)
    step_size = []
    for m in range(4):
        damping = 1.0 / jnp.maximum(1.0, jnp.sqrt(squares[m] / entries[m] + 1e-06) / CLIP_LEVEL)
        step_size.append(LEARN_RATE * jnp.sqrt(at(12 + m) / entries[m] + 1e-06) * damping)
    spread = [(m, place, *span) for m, spans in enumerate(layout.matrices()) for place, span in enumerate(spans)]
    for m, place, start, size in spread:
        grad = total_ref[:, pl.ds(start, size)]
        col = col_ref[:, pl.ds(start, size)]
        step = step_size[max(0, m - 2)] * grad * lax.rsqrt(row_ref[:, m : m + 1] * col / means[m])
        if m < 3:
            part = slice(place * LANES, (place + 1) * LANES)
            own_qkv[m, :, part] = grad
            new_qkv[m, :, part] = weights[0][m, :, part] - step
            qkv_col[m : m + 1, part] = col
        elif m == 4:
            own_one[...] = grad
            new_one[...] = weights[2][...] - step
            one_col[...] = col
        else:
            own, new, weight = (own_out, new_out, weights[1]) if m == 3 else (own_two, new_two, weights[3])
            own[...] = grad.T
            new[...] = weight[...] - step.T
            (out_row if m == 3 else two_row)[...] = col
    row_flat = row_ref[...].T
    qkv_row[...] = row_flat[0:3]
    out_col[...] = row_flat[3:4]
    one_row[...] = row_flat[4:5]
    two_col[...] = row_flat[5:6]

    wide = (lane >= 7) & (lane < VEC - 1)
    counts = jnp.where(wide, float(long), float(width))

    def grouped(values):
        inside = jnp.sum(jnp.where(wide, values, 0.0), axis=1, keepdims=True)
        return jnp.where(wide, inside, values)

    table_grad = total_ref[:, pl.ds(layout.start["vec"], LANES)]
    update = table_grad * lax.rsqrt(second_ref[...])
    norm = jnp.sqrt(grouped(sums_ref[1:2, :]) / counts + 1e-06)
    size = jnp.sqrt(grouped(sums_ref[2:3, :]) / counts + 1e-06)
    fresh = vector_ref[...] - LEARN_RATE * size / jnp.maximum(1.0, norm / CLIP_LEVEL) * update
    own_table[...] = table_grad.T[:VEC]
    new_vectors[...] = fresh.T[:VEC]
    second_new[...] = second_ref[...].T[:VEC]


def update_weights(layout, width, long, columns, hidden, rows, values, vectors, weights):
    full = jnp.float32
    shapes = [
        (3, rows, columns),
        (columns, rows),
        (rows, hidden),
        (hidden, rows),
        (VEC, rows),
        (3, rows, columns),
        (columns, rows),
        (rows, hidden),
        (hidden, rows),
        (VEC, rows),
        (VEC, rows),
        (3, rows),
        (3, columns),
        (1, columns),
        (1, rows),
        (1, rows),
        (1, hidden),
        (1, hidden),
        (1, rows),
    ]
    return pl.pallas_call(
        functools.partial(update_kernel, layout, width, long),
        name="update_weights",
        out_shape=[jax.ShapeDtypeStruct(shape, full) for shape in shapes],
        compiler_params=pltpu.CompilerParams(vmem_limit_bytes=48 << 20),
    )(*values, vectors, *weights)


def attend_kernel(heads_ref, bias_ref, mixed_ref):
    bias = bias_ref[...]
    for head in range(2):
        query, key, value = head_parts(heads_ref, head)
        scores = lax.dot_general(query, key, CONTRACT_LAST, preferred_element_type=jnp.float32)
        scores = scores * (HEAD_DIM ** (-0.5) * LOG2E) + bias
        raised = jnp.exp2(scores - jnp.max(scores, axis=1, keepdims=True))
        summed = jnp.sum(raised, axis=1, keepdims=True)
        attention = (raised * (1.0 / summed)).astype(jnp.bfloat16)
        mixed = jnp.dot(attention, value, preferred_element_type=jnp.float32)
        mixed_ref[:, pl.ds(head * HEAD_DIM, HEAD_DIM)] = mixed.astype(jnp.bfloat16)


def head_parts(heads_ref, head):
    return [heads_ref[:, pl.ds(kind * LANES + head * HEAD_DIM, HEAD_DIM)] for kind in range(3)]


def attend_back_kernel(heads_ref, bias_ref, grad_ref, out_ref):
    bias = bias_ref[...]
    for head in range(2):
        query, key, value = head_parts(heads_ref, head)
        grad = grad_ref[:, pl.ds(head * HEAD_DIM, HEAD_DIM)]
        scores = lax.dot_general(key, query, CONTRACT_LAST, preferred_element_type=jnp.float32)
        scores = scores * (HEAD_DIM ** (-0.5) * LOG2E) + bias
        raised = jnp.exp2(scores - jnp.max(scores, axis=0, keepdims=True))
        attention = raised * (1.0 / jnp.sum(raised, axis=0, keepdims=True))
        grad_value = jnp.dot(attention.astype(jnp.bfloat16), grad, preferred_element_type=jnp.float32)
        grad_attention = lax.dot_general(value, grad, CONTRACT_LAST, preferred_element_type=jnp.float32)
        weighted = jnp.sum(attention * grad_attention, axis=0, keepdims=True)
        grad_scores = (attention * (grad_attention - weighted) * HEAD_DIM ** (-0.5)).astype(jnp.bfloat16)
        grad_key = jnp.dot(grad_scores, query, preferred_element_type=jnp.float32)
        grad_query = jnp.dot(key.T, grad_scores, preferred_element_type=jnp.float32).T
        for kind, value in enumerate((grad_query, grad_key, grad_value)):
            out_ref[:, pl.ds(kind * LANES + head * HEAD_DIM, HEAD_DIM)] = value.astype(jnp.bfloat16)


def attend(projected, bias_row, width):
    rows = projected.shape[0]
    return pl.pallas_call(
        attend_kernel,
        name="attend",
        grid=(width // LANES,),
        out_shape=jax.ShapeDtypeStruct((rows, width), jnp.bfloat16),
        in_specs=[
            pl.BlockSpec((rows, 3 * LANES), lambda pair: (0, pair)),
            pl.BlockSpec((1, rows), lambda pair: (0, 0)),
        ],
        out_specs=pl.BlockSpec((rows, LANES), lambda pair: (0, pair)),
        compiler_params=pltpu.CompilerParams(vmem_limit_bytes=40 << 20),
    )(projected, bias_row)


def attend_back(projected, bias_column, grad_mixed, width):
    rows = projected.shape[0]
    return pl.pallas_call(
        attend_back_kernel,
        name="attend_back",
        grid=(width // LANES,),
        out_shape=jax.ShapeDtypeStruct((rows, 3 * width), jnp.bfloat16),
        in_specs=[
            pl.BlockSpec((rows, 3 * LANES), lambda pair: (0, pair)),
            pl.BlockSpec((rows, 1), lambda pair: (0, 0)),
            pl.BlockSpec((rows, LANES), lambda pair: (0, pair)),
        ],
        out_specs=pl.BlockSpec((rows, 3 * LANES), lambda pair: (0, pair)),
        compiler_params=pltpu.CompilerParams(vmem_limit_bytes=40 << 20),
    )(projected, bias_column, grad_mixed)


def paired(array, axis):
    moved = jnp.moveaxis(array, axis, -2)
    lead = moved.shape[:-2]
    blocks = moved.reshape(*lead, 3, moved.shape[-1] // LANES, LANES)
    return jnp.swapaxes(blocks, -3, -2).reshape(*lead, 3 * moved.shape[-1])


def on_device(
    inputs,
    cotangent,
    token_mask,
    w_qkv,
    w_out,
    w_fc1,
    w_fc2,
    vectors,
    qkv_row,
    qkv_col,
    out_row,
    out_col,
    fc1_row,
    fc1_col,
    fc2_row,
    fc2_col,
    vec_second,
):
    tensor_count = lax.axis_size("tensor")
    dims = grid_of(lax.axis_size("fsdp"))
    tensor_rank = lax.axis_index("tensor")
    rows_here, width = inputs.shape
    own_rows, columns = w_qkv.shape[1:]
    hidden = w_fc1.shape[1]
    low = jnp.bfloat16

    keep = lax.dynamic_slice_in_dim(token_mask, tensor_rank, 1, 0)
    keep_rows = keep.reshape(rows_here, 1).astype(jnp.float32)
    bias = jnp.where(keep > 0, 0.0, -1e30).astype(jnp.float32)

    widths = (3 * columns, columns, hidden, hidden, LANES)
    offsets = [sum(widths[:at]) for at in range(5)]
    pack = jnp.concatenate(
        [
            paired(w_qkv, 0),
            w_out.T,
            w_fc1,
            w_fc2.T,
            jnp.pad(vectors.T, ((0, 0), (0, LANES - VEC))),
        ],
        axis=1,
    ).astype(low)
    parts = (
        (offsets[0], widths[0], 1, False),
        (offsets[4], widths[4], 1, True),
        (offsets[1], widths[1], 1, False),
        (offsets[2], widths[2], 2, False),
        (offsets[3], widths[3], 2, False),
    )
    weight_qkv, table, weight_out, weight_one, weight_two = (
        array.reshape(width, array.shape[-1])
        for array in gather_weights(dims, tensor_count, pack, parts)
    )
    table = table[:, :VEC].T.astype(jnp.float32)
    head_bias = paired(jnp.stack([table[2], jnp.zeros_like(table[2]), table[3]]), 0)[None]
    bias_hidden = table[7 : VEC - 1].reshape(1, FF)

    def dot(left, right, left_dim, right_dim):
        return lax.dot_general(
            left, right, (((left_dim,), (right_dim,)), ((), ())), preferred_element_type=jnp.float32
        )

    normed_one, inverse_one = norm_parts(inputs)
    low_one = (normed_one * table[0] + table[1]).astype(low)
    projected = (dot(low_one, weight_qkv, 1, 0) + head_bias).astype(low)
    mixed_rows = attend(projected, bias, width)
    middle = inputs + (dot(mixed_rows, weight_out, 1, 1) + table[4]) * keep_rows
    normed_two, inverse_two = norm_parts(middle)
    low_two = (normed_two * table[5] + table[6]).astype(low)
    preact = dot(low_two, weight_one, 1, 0) + bias_hidden
    sigmoid_pre = jax.nn.sigmoid(1.702 * preact)
    active = (preact * sigmoid_pre).astype(low)
    block_out = middle + (dot(active, weight_two, 1, 1) + table[VEC - 1]) * keep_rows

    grad_top = cotangent.astype(jnp.float32)
    grad_masked = grad_top * keep_rows
    back_two = grad_masked.astype(low)
    grad_two = dot(back_two, active, 0, 0).astype(low)
    grad_active = dot(back_two, weight_two, 1, 0)
    derivative = sigmoid_pre + 1.702 * preact * sigmoid_pre * (1.0 - sigmoid_pre)
    grad_pre = (grad_active * derivative).astype(low)
    grad_one = dot(low_two, grad_pre, 0, 0).astype(low)
    grad_low_two = dot(grad_pre, weight_one, 1, 1)
    grad_middle = grad_top + norm_back(grad_low_two, normed_two, inverse_two, table[5])
    grad_masked_one = grad_middle * keep_rows
    back_one = grad_masked_one.astype(low)
    grad_out_weight = dot(back_one, mixed_rows, 0, 0).astype(low)
    grad_mixed = dot(back_one, weight_out, 1, 0).astype(low)
    grad_proj = attend_back(projected, bias.reshape(rows_here, 1), grad_mixed, width)
    grad_qkv = dot(low_one, grad_proj, 0, 0).astype(low)
    grad_low_one = dot(grad_proj, weight_qkv, 1, 1)
    input_grad = grad_middle + norm_back(grad_low_one, normed_one, inverse_one, table[0])

    def column_sum(values):
        return jnp.sum(values, axis=0, dtype=jnp.float32)

    head_sums = column_sum(grad_proj).reshape(width // LANES, 3, LANES)
    grad_table = jnp.concatenate(
        [
            jnp.stack(
                [
                    column_sum(grad_low_one * normed_one),
                    column_sum(grad_low_one),
                    head_sums[:, 0].reshape(width),
                    head_sums[:, 2].reshape(width),
                    column_sum(grad_masked_one),
                    column_sum(grad_low_two * normed_two),
                    column_sum(grad_low_two),
                ]
            ),
            column_sum(grad_pre).reshape(FF // width, width),
            column_sum(grad_masked)[None],
        ],
        0,
    )
    table_block = jnp.pad(grad_table.T.astype(low), ((0, 0), (0, LANES - VEC)))
    layout = Layout(columns, hidden, ("two", "one", "out", "qkv", "vec"))
    grad_arrays = [
        array.reshape(*dims, own_rows, array.shape[1])
        for array in (
            grad_two,
            grad_one,
            grad_out_weight,
            grad_qkv,
            jnp.concatenate([table_block] * tensor_count, axis=1),
        )
    ]
    col_state = {"qkv": paired(qkv_col, 0), "out": out_row, "one": fc1_col, "two": fc2_row}
    state_col = jnp.concatenate([col_state[name] for name in layout.order[:4]])[None]
    state_row = jnp.concatenate([qkv_row, out_col[None], fc1_row[None], fc2_col[None]], axis=0)
    state_row = jnp.pad(state_row.T, ((0, 0), (0, LANES - 6)))
    second = jnp.pad(vec_second.T, ((0, 0), (0, LANES - VEC)), constant_values=1.0)
    vectors_turned = jnp.pad(vectors.T, ((0, 0), (0, LANES - VEC)))
    weights = (w_qkv, w_out, w_fc1, w_fc2)
    values = reduce_grads(
        dims,
        tensor_count,
        layout,
        grad_arrays,
        (2, 2, 1, 1, 1),
        weights,
        (state_col, state_row, second, vectors_turned),
    )
    outs = update_weights(
        layout, width, FF, columns, hidden, own_rows, values, vectors_turned, weights
    )
    outs = [out.reshape(-1) if out.shape[0] == 1 else out for out in outs]
    return (block_out, input_grad, *outs[:10], *outs[11:], outs[10])


def solution(mesh):
    in_specs = (
        P(("fsdp", "tensor"), None),
        P(("fsdp", "tensor"), None),
        P("fsdp", None),
        P(None, "fsdp", "tensor"),
        P("tensor", "fsdp"),
        P("fsdp", "tensor"),
        P("tensor", "fsdp"),
        P(None, "fsdp"),
        P(None, "fsdp"),
        P(None, "tensor"),
        P("tensor"),
        P("fsdp"),
        P("fsdp"),
        P("tensor"),
        P("tensor"),
        P("fsdp"),
        P(None, "fsdp"),
    )
    out_specs = (
        P(("fsdp", "tensor"), None),
        P(("fsdp", "tensor"), None),
        P(None, "fsdp", "tensor"),
        P("tensor", "fsdp"),
        P("fsdp", "tensor"),
        P("tensor", "fsdp"),
        P(None, "fsdp"),
        P(None, "fsdp", "tensor"),
        P("tensor", "fsdp"),
        P("fsdp", "tensor"),
        P("tensor", "fsdp"),
        P(None, "fsdp"),
        P(None, "fsdp"),
        P(None, "tensor"),
        P("tensor"),
        P("fsdp"),
        P("fsdp"),
        P("tensor"),
        P("tensor"),
        P("fsdp"),
        P(None, "fsdp"),
    )
    return jax.shard_map(
        on_device, mesh=mesh, in_specs=in_specs, out_specs=out_specs, check_vma=False
    )
```

```python
import functools

import jax
import jax.numpy as jnp
from jax import lax
from jax.experimental import pallas as pl
from jax.experimental.pallas import tpu as pltpu
from jax.sharding import PartitionSpec as P

HEAD_DIM = 64
FF = 4096
STEP = 20
VEC = 12
LANES = 128

EPS_NORM = 1e-05
EPS_ONE = 1e-30
CLIP_LEVEL = 1.0
LEARN_RATE = 0.5
MESH = pl.DeviceIdType.MESH
LOG2E = 1.4426950408889634
CONTRACT_LAST = (((1,), (1,)), ((), ()))


def grid_of(count):
    return {16: (4, 2, 2), 32: (2, 4, 4)}.get(count, (count, 1, 1))


def norm_parts(values):
    average = jnp.mean(values, axis=-1, keepdims=True)
    center = values - average
    inverse = lax.rsqrt(jnp.mean(center * center, axis=-1, keepdims=True) + EPS_NORM)
    return (center * inverse, inverse)


def norm_back(grad_normed, normed, inverse, gain):
    scaled = grad_normed * gain
    first_mean = jnp.mean(scaled, axis=-1, keepdims=True)
    second_mean = jnp.mean(scaled * normed, axis=-1, keepdims=True)
    return inverse * (scaled - first_mean - normed * second_mean)


class Place:
    def __init__(self, dims, tensor):
        self.dims = dims
        self.tensor = tensor
        fsdp = lax.axis_index("fsdp")
        _, ny, nx = dims
        self.at = (fsdp // (ny * nx), (fsdp // nx) % ny, fsdp % nx)
        self.rank = lax.axis_index("tensor")

    def moved(self, axis, step):
        place = list(self.at) + [self.rank]
        size = (*self.dims, self.tensor)[axis]
        place[axis] = lax.rem(place[axis] + step + size, size)
        return tuple(place)

    def device(self, place):
        z, y, x, rank = place
        return {"fsdp": (z * self.dims[1] + y) * self.dims[2] + x, "tensor": rank}

    def size(self, axis):
        return (*self.dims, self.tensor)[axis]

    def barrier(self):
        sem = pltpu.get_barrier_semaphore()
        count = 0
        for axis in range(4):
            for step in range(1, self.size(axis)):
                pl.semaphore_signal(
                    sem,
                    inc=1,
                    device_id=self.device(self.moved(axis, step)),
                    device_id_type=MESH,
                )
                count += 1
        if count:
            pl.semaphore_wait(sem, count)


def axis_order(half):
    return (0, 1, 2) if half == 0 else (0, 2, 1)


def norm_rows(values):
    average = jnp.mean(values, axis=1, keepdims=True)
    center = values - average
    inverse = lax.rsqrt(jnp.mean(center * center, axis=1, keepdims=True) + EPS_NORM)
    return center * inverse, inverse


def dot(left, right, dims=(((1,), (0,)), ((), ()))):
    return lax.dot_general(left, right, dims, preferred_element_type=jnp.float32)


def turn(source, target):
    for start in range(0, source.shape[1], LANES):
        target[pl.ds(start, LANES), :] = source[:, pl.ds(start, LANES)].T


def attend_pair(heads, bias):
    mixed = []
    for head in range(2):
        query, key, value = (
            heads[:, kind * LANES + head * HEAD_DIM : kind * LANES + (head + 1) * HEAD_DIM] for kind in range(3)
        )
        scores = dot(query, key, CONTRACT_LAST) * (HEAD_DIM ** (-0.5) * LOG2E) + bias
        raised = jnp.exp2(scores - jnp.max(scores, axis=1, keepdims=True))
        summed = jnp.sum(raised, axis=1, keepdims=True)
        attention = (raised * (1.0 / summed)).astype(jnp.bfloat16)
        mixed.append(dot(attention, value).astype(jnp.bfloat16))
    return jnp.concatenate(mixed, axis=1)


class Gather:
    def __init__(self, here, pack_ref, outs, parts, local_sem, send_sem, recv_sem):
        self.here = here
        self.pack = pack_ref
        self.outs = outs
        self.half_rows = pack_ref.shape[0] // 2
        self.parts = parts
        self.sems = (local_sem, send_sem, recv_sem)
        self.own = (*here.at, here.rank)
        self.sent = []
        self.local = {}

    def rows(self, half):
        return pl.ds(half * self.half_rows, self.half_rows)

    def region(self, item, half, place, free):
        out, _, start, size, total, shared = self.parts[item]
        base = 0 if shared else place[3] * total
        column = pl.ds(pl.multiple_of(base + start, LANES), size)
        index = tuple(slice(None) if a in free else place[a] for a in range(3))
        return self.outs[out].at[(*index, self.rows(half), column)]

    def shard(self, item, half):
        _, offset, _, size, _, _ = self.parts[item]
        return self.pack.at[self.rows(half), pl.ds(offset, size)]

    def axes(self, item, half):
        order = axis_order(half)
        return order if self.parts[item][5] else (*order, 3)

    def copies(self, item, half, phase, landing):
        here = self.here
        order = self.axes(item, half)
        axis, free = order[phase], order[:phase]
        found = []
        for step in range(1, here.size(axis)):
            own = self.region(item, half, self.own, free)
            if landing:
                src = dst = self.region(item, half, here.moved(axis, -step), free)
            else:
                src, dst = (self.shard(item, half) if phase == 0 else own), own
            found.append(
                pltpu.make_async_remote_copy(
                    src_ref=src,
                    dst_ref=dst,
                    send_sem=self.sems[1].at[item, half, phase, step - 1],
                    recv_sem=self.sems[2].at[item, half, phase, step - 1],
                    device_id=here.device(here.moved(axis, step)),
                    device_id_type=MESH,
                )
            )
        return found

    def start(self):
        for item in range(len(self.parts)):
            for half in range(2):
                copy = pltpu.make_async_copy(
                    self.shard(item, half), self.region(item, half, self.own, ()), self.sems[0].at[item, half]
                )
                copy.start()
                self.local[item, half] = copy

    def advance(self, item, phase):
        for half in range(2):
            order = self.axes(item, half)
            if 0 < phase <= len(order):
                for copy in self.copies(item, half, phase - 1, True):
                    copy.wait_recv()
            if phase == 1:
                self.local[item, half].wait()
            if phase < len(order):
                for copy in self.copies(item, half, phase, False):
                    copy.start()
                    self.sent.append(copy)

    def finish(self):
        for copy in self.sent:
            copy.wait_send()


PHASES = 4
BLOCK = 512


def forward_kernel(dims, tensor, parts, plan, pack_ref, input_ref, top_ref, keep_ref, bias_ref, *refs):
    outs = refs[:5]
    weight_qkv, weight_vec, weight_out, weight_one, weight_two = outs
    (
        block_out,
        grad_middle,
        back_one,
        projected,
        mixed,
        low_one,
        grad_one,
        grad_two,
        table,
        vec_sums,
        pre_sums,
    ) = refs[5:16]
    (
        vec_buf,
        qkv_buf,
        out_buf,
        one_buf,
        two_buf,
        low_two,
        low_two_turned,
        back_two,
        back_two_turned,
        grad_low_two,
        hidden_bias,
        head_bias,
        one_stage,
        two_stage,
        load_sem,
        store_sem,
        local_sem,
        send_sem,
        recv_sem,
    ) = refs[16:]
    here = Place(dims, tensor)
    gather = Gather(here, pack_ref, outs, parts, local_sem, send_sem, recv_sem)
    rows, width = input_ref.shape
    low = jnp.bfloat16
    step_rows = LANES

    def row_steps(body, carry):
        return lax.fori_loop(
            0, rows // step_rows, lambda at, c: body(pl.ds(pl.multiple_of(at * step_rows, step_rows), step_rows), c), carry
        )

    def load(source, buffer, sem):
        return pltpu.make_async_copy(source, buffer, sem)

    def first_norm():
        copy = load(weight_vec, vec_buf, load_sem.at[0])
        copy.start()
        copy.wait()
        whole = vec_buf[...].reshape(width, LANES).astype(jnp.float32).T
        table[...] = whole[:16]
        for at in range(VEC - 8):
            hidden_bias[:, pl.ds(at * width, width)] = whole[7 + at : 8 + at]
        for pair in range(width // LANES):
            for kind, row in ((0, 2), (2, 3)):
                head_bias[:, pl.ds((pair * 3 + kind) * LANES, LANES)] = whole[
                    row : row + 1, pair * LANES : (pair + 1) * LANES
                ]
            head_bias[:, pl.ds((pair * 3 + 1) * LANES, LANES)] = jnp.zeros((1, LANES), jnp.float32)

        def body(part, carry):
            normed, _ = norm_rows(input_ref[part, :])
            low_one[part, :] = (normed * table[0:1, :] + table[1:2, :]).astype(low)
            back_two[part, :] = (top_ref[part, :].astype(jnp.float32) * keep_ref[part, :]).astype(low)
            return carry

        row_steps(body, 0)
        turn(back_two, back_two_turned)

    def heads(first, count, per_rank):
        def pair_of(at):
            return lax.rem(here.rank + at // count, tensor) * per_rank + first + lax.rem(at, count)

        def weights(at):
            column = pl.multiple_of(pair_of(at) * 3 * LANES, LANES)
            slot = lax.rem(at, 2)
            return load(
                weight_qkv.at[:, :, :, :, pl.ds(column, 3 * LANES)], qkv_buf.at[slot], load_sem.at[slot]
            )

        weights(0).start()

        def body(at, carry):
            weights(at).wait()

            @pl.when(at + 1 < tensor * count)
            def _():
                weights(at + 1).start()

            pair = pair_of(at)
            column = pl.ds(pl.multiple_of(pair * 3 * LANES, LANES), 3 * LANES)
            weight = qkv_buf[lax.rem(at, 2)].reshape(width, 3 * LANES)
            value = (dot(low_one[...], weight) + head_bias[:, column]).astype(low)
            projected[:, column] = value
            mixed[:, pl.ds(pl.multiple_of(pair * LANES, LANES), LANES)] = attend_pair(value, bias_ref[...])
            return carry

        lax.fori_loop(0, tensor * count, body, 0)

    def second_norm():
        copy = load(weight_out, out_buf, load_sem.at[0])
        copy.start()
        copy.wait()
        term = dot(mixed[...], out_buf[...].reshape(width, width), CONTRACT_LAST)
        grad_middle[...] = term

        def body(part, carry):
            middle = input_ref[part, :] + (grad_middle[part, :] + table[4:5, :]) * keep_ref[part, :]
            grad_middle[part, :] = middle
            normed, _ = norm_rows(middle)
            low_two[part, :] = (normed * table[5:6, :] + table[6:7, :]).astype(low)
            return carry

        row_steps(body, 0)
        turn(low_two, low_two_turned)

    def stores(column, slot):
        return [
            pltpu.make_async_copy(stage.at[slot], out.at[:, column], store_sem.at[which, slot])
            for which, (stage, out) in enumerate(((one_stage, grad_one), (two_stage, grad_two)))
        ]

    def hidden(first, total, opening):
        def column_of(at):
            base = lax.rem(here.rank + at, tensor) * total + first
            return pl.ds(pl.multiple_of(base, LANES), BLOCK)

        def weights(at):
            slot = lax.rem(at, 2)
            column = column_of(at)
            return [
                load(source.at[:, :, :, :, column], buffer.at[slot], load_sem.at[2 * which + slot])
                for which, (source, buffer) in enumerate(((weight_one, one_buf), (weight_two, two_buf)))
            ]

        for copy in weights(0):
            copy.start()

        def body(at, carry):
            slot = lax.rem(at, 2)
            column = column_of(at)
            for copy in weights(at):
                copy.wait()

            @pl.when(at + 1 < tensor)
            def _():
                for copy in weights(at + 1):
                    copy.start()

            one = one_buf[slot].reshape(width, BLOCK)
            two = two_buf[slot].reshape(width, BLOCK)
            preact = dot(low_two[...], one) + hidden_bias[:, column]
            gate = jax.nn.sigmoid(1.702 * preact)
            active = (preact * gate).astype(low)
            derivative = gate + 1.702 * preact * gate * (1.0 - gate)
            grad_pre = (dot(back_two[...], two) * derivative).astype(low)
            pre_sums[:, column] = jnp.sum(grad_pre.astype(jnp.float32), axis=0, keepdims=True)
            out_term = dot(active, two, CONTRACT_LAST)
            back_term = dot(grad_pre, one, CONTRACT_LAST)
            if opening:

                @pl.when(at == 0)
                def _():
                    block_out[...] = out_term
                    grad_low_two[...] = back_term

                @pl.when(at > 0)
                def _():
                    block_out[...] += out_term
                    grad_low_two[...] += back_term

                @pl.when(at > 1)
                def _():
                    for copy in stores(column, slot):
                        copy.wait()

            else:
                block_out[...] += out_term
                grad_low_two[...] += back_term
                for copy in stores(column, slot):
                    copy.wait()
            one_stage[slot] = dot(low_two_turned[...], grad_pre).astype(low)
            two_stage[slot] = dot(back_two_turned[...], active).astype(low)
            for copy in stores(column, slot):
                copy.start()
            return carry

        lax.fori_loop(0, tensor, body, 0)

    def last_norm():
        def body(part, sums):
            middle = grad_middle[part, :]
            keep = keep_ref[part, :]
            top = top_ref[part, :].astype(jnp.float32)
            block_out[part, :] = middle + (block_out[part, :] + table[VEC - 1 : VEC, :]) * keep
            normed, inverse = norm_rows(middle)
            grad_low = grad_low_two[part, :]
            scaled = grad_low * table[5:6, :]
            first = jnp.mean(scaled, axis=1, keepdims=True)
            second = jnp.mean(scaled * normed, axis=1, keepdims=True)
            grad = top + inverse * (scaled - first - normed * second)
            grad_middle[part, :] = grad
            masked = grad * keep
            back_one[part, :] = masked.astype(low)
            terms = (masked, grad_low * normed, grad_low, top * keep)
            return tuple(old + jnp.sum(term, axis=0, keepdims=True) for old, term in zip(sums, terms))

        zero = jnp.zeros((1, width), jnp.float32)
        for at, value in enumerate(row_steps(body, (zero,) * 4)):
            vec_sums[at : at + 1, :] = value

    here.barrier()
    gather.start()
    count = len(parts)
    for wave in range(count + PHASES):
        for phase in reversed(range(PHASES + 1)):
            item = wave - phase
            if 0 <= item < count:
                gather.advance(item, phase)
        task = plan[wave - PHASES] if wave >= PHASES else None
        if task is None:
            continue
        if task[0] == "norm":
            first_norm()
        elif task[0] == "heads":
            heads(*task[1:])
        elif task[0] == "out":
            second_norm()
        else:
            hidden(*task[1:])
    last_norm()
    for slot in range(2):
        for copy in stores(pl.ds(0, BLOCK), slot):
            copy.wait()
    gather.finish()


def forward(dims, tensor, pack, inputs, cotangent, keep_rows, bias, columns, hidden):
    own_rows = pack.shape[0]
    rows, width = inputs.shape
    low, full = jnp.bfloat16, jnp.float32
    widths = (3 * columns, LANES, columns, hidden, hidden)
    offsets = [sum(widths[:at]) for at in range(5)]
    per_rank = columns // LANES
    parts = [(1, offsets[1], 0, LANES, LANES, True)]
    plan = [("norm",)]
    groups = max(1, per_rank // 2)
    each = per_rank // groups
    for at in range(groups):
        size = each * 3 * LANES
        parts.append((0, offsets[0] + at * size, at * size, size, widths[0], False))
        plan.append(("heads", at * each, each, per_rank))
    parts.append((2, offsets[2], 0, columns, columns, False))
    plan.append(("out",))
    for start in range(0, hidden, BLOCK):
        for which in (3, 4):
            parts.append((which, offsets[which] + start, start, BLOCK, hidden, False))
        plan += [None, ("hidden", start, hidden, start == 0)]
    count = len(parts)
    peers = max(2, *dims, tensor) - 1
    anywhere = pl.BlockSpec(memory_space=pl.ANY)
    inside = pl.BlockSpec(memory_space=pltpu.VMEM)

    def shape(kind, *size):
        return jax.ShapeDtypeStruct(size, kind)

    return pl.pallas_call(
        functools.partial(forward_kernel, dims, tensor, tuple(parts), tuple(plan)),
        name="forward",
        out_shape=[
            *(shape(low, *dims, own_rows, w * (1 if at == 1 else tensor)) for at, w in enumerate(widths)),
            shape(full, rows, width),
            shape(full, rows, width),
            shape(low, rows, width),
            shape(low, rows, 3 * width),
            shape(low, rows, width),
            shape(low, rows, width),
            shape(low, width, hidden * tensor),
            shape(low, width, hidden * tensor),
            shape(full, 16, width),
            shape(full, 8, width),
            shape(full, 1, hidden * tensor),
        ],
        in_specs=[anywhere] + [inside] * 4,
        out_specs=[anywhere] * 5 + [inside] * 6 + [anywhere] * 2 + [inside] * 3,
        scratch_shapes=[
            pltpu.VMEM((*dims, own_rows, LANES), low),
            pltpu.VMEM((2, *dims, own_rows, 3 * LANES), low),
            pltpu.VMEM((*dims, own_rows, width), low),
            pltpu.VMEM((2, *dims, own_rows, BLOCK), low),
            pltpu.VMEM((2, *dims, own_rows, BLOCK), low),
            pltpu.VMEM((rows, width), low),
            pltpu.VMEM((width, rows), low),
            pltpu.VMEM((rows, width), low),
            pltpu.VMEM((width, rows), low),
            pltpu.VMEM((rows, width), full),
            pltpu.VMEM((1, hidden * tensor), full),
            pltpu.VMEM((1, 3 * width), full),
            pltpu.VMEM((2, width, BLOCK), low),
            pltpu.VMEM((2, width, BLOCK), low),
            pltpu.SemaphoreType.DMA((4,)),
            pltpu.SemaphoreType.DMA((2, 2)),
            pltpu.SemaphoreType.DMA((count, 2)),
            pltpu.SemaphoreType.DMA((count, 2, 4, peers)),
            pltpu.SemaphoreType.DMA((count, 2, 4, peers)),
        ],
        compiler_params=pltpu.CompilerParams(
            collective_id=0, has_side_effects=True, vmem_limit_bytes=62 << 20
        ),
    )(pack, inputs, cotangent, keep_rows, bias)


class Layout:
    def __init__(self, columns, hidden, order):
        sizes = {"qkv": 3 * columns, "out": columns, "one": hidden, "two": hidden, "vec": LANES}
        self.order = order
        self.sizes = sizes
        self.start = {}
        at = 0
        for name in order:
            self.start[name] = at
            at += sizes[name]
        self.total = at
        self.columns = columns

    def span(self, name):
        return (self.start[name], self.sizes[name])

    def matrices(self):
        base = self.start["qkv"]
        pairs = range(self.columns // LANES)
        spans = [[(base + (pair * 3 + at) * LANES, LANES) for pair in pairs] for at in range(3)]
        return spans + [[self.span(name)] for name in ("out", "one", "two")]


def pick(values, lane):
    row = jnp.zeros((1, LANES), jnp.float32)
    for at, value in enumerate(values):
        row = jnp.where(lane == at, value, row)
    return row


def total_of(values):
    return jnp.sum(jnp.sum(values, axis=1, keepdims=True), axis=0, keepdims=True)


def reduce_kernel(dims, tensor, items, layout, *refs):
    n_grads = 1 + max(item[0] for item in items)
    grads = refs[:n_grads]
    weights = refs[n_grads : n_grads + 4]
    state_col, state_row, second_ref, vector_ref = refs[n_grads + 4 : n_grads + 8]
    total_ref, col_new_ref, row_new_ref, second_new_ref, sums_ref = refs[n_grads + 8 : n_grads + 13]
    (
        own,
        from_core,
        one_x,
        one_y,
        two_y,
        two_x,
        from_z,
        col_sum,
        col_in,
        row_sum,
        row_in,
        small,
        small_in,
        local_sem,
        send_sem,
        recv_sem,
        sum_send,
        sum_recv,
    ) = refs[n_grads + 13 :]
    here = Place(dims, tensor)
    nz, ny, nx = dims
    half_rows = own.shape[4]
    own_place = (*here.at, here.rank)
    count = len(items)

    def columns(item):
        _, _, width, _, offset = items[item]
        return pl.ds(offset, width)

    def grad(item, half, rank):
        which, start, width, total, _ = items[item]
        column = pl.ds(pl.multiple_of(rank * total + start, LANES), width)
        return grads[which].at[:, :, :, pl.ds(half * half_rows, half_rows), column]

    def order(half):
        return (3, 2, 1, 0) if half == 0 else (3, 1, 2, 0)

    def part(item, half, place, fixed):
        index = tuple(place[a] if a in fixed else slice(None) for a in range(3))
        return own.at[(half, *index, slice(None), columns(item))]

    def slot(item, half, phase, step):
        if phase == 0:
            return from_core.at[half, step - 1, :, :, :, :, columns(item)]
        if phase == 3:
            return from_z.at[half, step - 1, :, columns(item)]
        if phase == 1:
            buffer = one_x if half == 0 else one_y
            return buffer.at[step - 1, :, :, :, columns(item)]
        buffer = two_y if half == 0 else two_x
        return buffer.at[step - 1, :, :, columns(item)]

    def copies(item, half, phase):
        axes = order(half)
        axis, fixed = axes[phase], axes[1 : phase + 1]
        found = []
        for step in range(1, here.size(axis)):
            target = here.moved(axis, step)
            src = grad(item, half, target[3]) if phase == 0 else part(item, half, target, fixed)
            found.append(
                pltpu.make_async_remote_copy(
                    src_ref=src,
                    dst_ref=slot(item, half, phase, step),
                    send_sem=send_sem.at[item, half, phase, step - 1],
                    recv_sem=recv_sem.at[item, half, phase, step - 1],
                    device_id=here.device(target),
                    device_id_type=MESH,
                )
            )
        return found

    def add_in(item, half, phase):
        axes = order(half)
        axis, fixed = axes[phase], axes[1 : phase + 1]
        column = columns(item)
        steps = here.size(axis) - 1
        if phase == 3:
            value = own[(half, *here.at, slice(None), column)].astype(jnp.float32)
            for step in range(steps):
                value = value + from_z[half, step, :, column].astype(jnp.float32)
            total_ref[pl.ds(half * half_rows, half_rows), column] = value
            return
        if steps == 0:
            return
        free = [a for a in range(3) if a not in fixed]
        sizes = [dims[a] for a in free]
        loops = 1
        for size in sizes:
            loops *= size

        def body(at, carry):
            place = list(here.at)
            inner = []
            rest = at
            for axis_at, size in reversed(list(zip(free, sizes))):
                place[axis_at] = rest % size
                inner.insert(0, rest % size)
                rest = rest // size
            where = (half, *place, slice(None), column)
            value = own[where]
            for step in range(steps):
                if phase == 0:
                    piece = from_core[(half, step, *inner, slice(None), column)]
                elif phase == 1:
                    piece = (one_x if half == 0 else one_y)[(step, *inner, slice(None), column)]
                else:
                    piece = (two_y if half == 0 else two_x)[(step, *inner, slice(None), column)]
                value = value + piece
            own[where] = value
            return carry

        lax.fori_loop(0, loops, body, 0)

    sent = []

    def exchange(kind, phase, axis, buffer, landing):
        moved = []
        for step in range(1, here.size(axis)):
            copy = pltpu.make_async_remote_copy(
                src_ref=buffer.at[phase],
                dst_ref=landing.at[phase, step - 1],
                send_sem=sum_send.at[kind, phase, step - 1],
                recv_sem=sum_recv.at[kind, phase, step - 1],
                device_id=here.device(here.moved(axis, step)),
                device_id_type=MESH,
            )
            copy.start()
            moved.append(copy)
        sent.extend(moved)

        def finish():
            value = buffer[phase]
            for step, copy in enumerate(moved):
                copy.wait_recv()
                value = value + landing[phase, step]
            buffer[phase + 1] = value

        return finish

    here.barrier()
    local = {}
    for item in range(count):
        for half in range(2):
            copy = pltpu.make_async_copy(
                grad(item, half, here.rank), part(item, half, own_place, ()), local_sem.at[item, half]
            )
            copy.start()
            local[item, half] = copy
    phases = 4
    for wave in range(count + phases):
        for phase in reversed(range(phases + 1)):
            item = wave - phase
            if not 0 <= item < count:
                continue
            for half in range(2):
                if phase:
                    if phase == 1:
                        local[item, half].wait()
                    for copy in copies(item, half, phase - 1):
                        copy.wait_recv()
                    add_in(item, half, phase - 1)
                if phase < phases:
                    for copy in copies(item, half, phase):
                        copy.start()
                        sent.append(copy)

    decay_rate = 1.0 - STEP ** (-0.8)
    keep_old = 1.0 - decay_rate
    rows = total_ref.shape[0]
    width = rows * nz * ny * nx
    long = layout.sizes["one"] * tensor
    matrices = layout.matrices()
    lane = lax.broadcasted_iota(jnp.int32, (1, LANES), 1)
    row_parts = []
    for spans in matrices:
        row_part = 0.0
        for start, size in spans:
            value = total_ref[:, pl.ds(start, size)]
            square = value * value
            col_sum[0, :, pl.ds(start, size)] = jnp.sum(square, axis=0, keepdims=True)
            row_part = row_part + jnp.sum(square, axis=1, keepdims=True)
        row_parts.append(row_part)
    row_sum[0] = pick(row_parts, lane)
    finish_row = exchange(0, 0, 3, row_sum, row_in)
    finish_col = exchange(1, 0, 0, col_sum, col_in)
    vec_start = layout.start["vec"]
    table_grad = total_ref[:, pl.ds(vec_start, LANES)]
    second_new = decay_rate * second_ref[...] + keep_old * (table_grad * table_grad + EPS_ONE)
    second_new_ref[...] = second_new
    vector_update = table_grad * lax.rsqrt(second_new)
    vector_sums = jnp.sum(vector_update * vector_update, axis=0, keepdims=True) / tensor
    vector_weight = jnp.sum(vector_ref[...] * vector_ref[...], axis=0, keepdims=True) / tensor
    weight_sums = [total_of(jnp.sum(weights[0][...] * weights[0][...], axis=0))]
    weight_sums += [total_of(ref[...] * ref[...]) for ref in weights[1:]]
    finish_row()
    row_counts = pick([jnp.full((1, 1), 1.0 / size, jnp.float32) for size in (width, width, width, width, long, long)], lane)
    row_new = decay_rate * state_row[...] + keep_old * (row_sum[1] * row_counts + EPS_ONE)
    row_new_ref[...] = row_new
    finish_col()
    exchange(1, 1, 1, col_sum, col_in)()
    exchange(1, 2, 2, col_sum, col_in)()
    col_new = decay_rate * state_col[...] + keep_old * (col_sum[3] / width + EPS_ONE)
    col_new_ref[...] = col_new
    ratios = []
    means = []
    for at, spans in enumerate(matrices):
        row_at = row_new[:, at : at + 1]
        ratio = 0.0
        for start, size in spans:
            value = total_ref[:, pl.ds(start, size)]
            col_at = col_new_ref[:, pl.ds(start, size)]
            ratio = ratio + total_of(value * value / (row_at * col_at))
        ratios.append(ratio)
        if at in (3, 5):
            means.append(jnp.sum(col_at, axis=1, keepdims=True) / (nz * ny * nx))
        else:
            means.append(jnp.sum(row_at, axis=0, keepdims=True) / tensor)
    small[0] = jnp.concatenate(
        [pick(ratios + means + weight_sums, lane), vector_sums, vector_weight, jnp.zeros((5, LANES), jnp.float32)], axis=0
    )
    for phase in range(4):
        exchange(2, phase, phase, small, small_in)()
    sums_ref[...] = small[4]
    for copy in sent:
        copy.wait_send()


def reduce_grads(dims, tensor, layout, grads, chunks, weights, states):
    rows = grads[0].shape[3]
    half_rows = rows // 2
    items = []
    offset = 0
    for which, (name, pieces) in enumerate(zip(layout.order, chunks)):
        width = layout.sizes[name]
        size = width // pieces
        for piece in range(pieces):
            items.append((which, piece * size, size, width, offset))
            offset += size
    nz, ny, nx = dims
    peers = max(2, *dims, tensor) - 1
    low = jnp.bfloat16
    full = jnp.float32
    anywhere = pl.BlockSpec(memory_space=pl.ANY)
    inside = pl.BlockSpec(memory_space=pltpu.VMEM)

    def hold(*shape):
        return pltpu.VMEM(tuple(max(1, size) for size in shape), low)

    sums = offset - LANES
    return pl.pallas_call(
        functools.partial(reduce_kernel, dims, tensor, tuple(items), layout),
        name="reduce_grads",
        out_shape=[
            jax.ShapeDtypeStruct((rows, offset), full),
            jax.ShapeDtypeStruct((1, sums), full),
            jax.ShapeDtypeStruct((rows, LANES), full),
            jax.ShapeDtypeStruct((rows, LANES), full),
            jax.ShapeDtypeStruct((8, LANES), full),
        ],
        in_specs=[anywhere] * len(grads) + [inside] * 8,
        out_specs=[inside] * 5,
        scratch_shapes=[
            hold(2, nz, ny, nx, half_rows, offset),
            hold(2, tensor - 1, nz, ny, nx, half_rows, offset),
            hold(nx - 1, nz, ny, half_rows, offset),
            hold(ny - 1, nz, nx, half_rows, offset),
            hold(ny - 1, nz, half_rows, offset),
            hold(nx - 1, nz, half_rows, offset),
            hold(2, nz - 1, half_rows, offset),
            pltpu.VMEM((4, 1, sums), full),
            pltpu.VMEM((3, peers, 1, sums), full),
            pltpu.VMEM((2, rows, LANES), full),
            pltpu.VMEM((1, peers, rows, LANES), full),
            pltpu.VMEM((5, 8, LANES), full),
            pltpu.VMEM((4, peers, 8, LANES), full),
            pltpu.SemaphoreType.DMA((len(items), 2)),
            pltpu.SemaphoreType.DMA((len(items), 2, 4, peers)),
            pltpu.SemaphoreType.DMA((len(items), 2, 4, peers)),
            pltpu.SemaphoreType.DMA((3, 4, peers)),
            pltpu.SemaphoreType.DMA((3, 4, peers)),
        ],
        compiler_params=pltpu.CompilerParams(
            collective_id=1, has_side_effects=True, vmem_limit_bytes=60 << 20
        ),
    )(*grads, *weights, *states)


def update_kernel(layout, width, long, *refs):
    total_ref, col_ref, row_ref, second_ref, sums_ref, vector_ref = refs[:6]
    weights = refs[6:10]
    own_qkv, own_out, own_one, own_two, own_table = refs[10:15]
    new_qkv, new_out, new_one, new_two, new_vectors, second_new = refs[15:21]
    qkv_row, qkv_col, out_row, out_col, one_row, one_col, two_row, two_col = refs[21:]
    lane = lax.broadcasted_iota(jnp.int32, (1, LANES), 1)

    def at(index):
        return sums_ref[0:1, index : index + 1]

    lengths = (width, width, width, width, width, long)
    means = [at(6 + m) / lengths[m] for m in range(6)]
    squares = [means[m] * at(m) for m in range(6)]
    squares = [squares[0] + squares[1] + squares[2], *squares[3:]]
    entries = (3 * width * width, width * width, width * long, width * long)
    step_size = []
    for m in range(4):
        damping = 1.0 / jnp.maximum(1.0, jnp.sqrt(squares[m] / entries[m] + 1e-06) / CLIP_LEVEL)
        step_size.append(LEARN_RATE * jnp.sqrt(at(12 + m) / entries[m] + 1e-06) * damping)
    spread = [(m, place, *span) for m, spans in enumerate(layout.matrices()) for place, span in enumerate(spans)]
    for m, place, start, size in spread:
        grad = total_ref[:, pl.ds(start, size)]
        col = col_ref[:, pl.ds(start, size)]
        step = step_size[max(0, m - 2)] * grad * lax.rsqrt(row_ref[:, m : m + 1] * col / means[m])
        if m < 3:
            part = slice(place * LANES, (place + 1) * LANES)
            own_qkv[m, :, part] = grad
            new_qkv[m, :, part] = weights[0][m, :, part] - step
            qkv_col[m : m + 1, part] = col
        elif m == 4:
            own_one[...] = grad
            new_one[...] = weights[2][...] - step
            one_col[...] = col
        else:
            own, new, weight = (own_out, new_out, weights[1]) if m == 3 else (own_two, new_two, weights[3])
            own[...] = grad.T
            new[...] = weight[...] - step.T
            (out_row if m == 3 else two_row)[...] = col
    row_flat = row_ref[...].T
    qkv_row[...] = row_flat[0:3]
    out_col[...] = row_flat[3:4]
    one_row[...] = row_flat[4:5]
    two_col[...] = row_flat[5:6]

    wide = (lane >= 7) & (lane < VEC - 1)
    counts = jnp.where(wide, float(long), float(width))

    def grouped(values):
        inside = jnp.sum(jnp.where(wide, values, 0.0), axis=1, keepdims=True)
        return jnp.where(wide, inside, values)

    table_grad = total_ref[:, pl.ds(layout.start["vec"], LANES)]
    update = table_grad * lax.rsqrt(second_ref[...])
    norm = jnp.sqrt(grouped(sums_ref[1:2, :]) / counts + 1e-06)
    size = jnp.sqrt(grouped(sums_ref[2:3, :]) / counts + 1e-06)
    fresh = vector_ref[...] - LEARN_RATE * size / jnp.maximum(1.0, norm / CLIP_LEVEL) * update
    own_table[...] = table_grad.T[:VEC]
    new_vectors[...] = fresh.T[:VEC]
    second_new[...] = second_ref[...].T[:VEC]


def update_weights(layout, width, long, columns, hidden, rows, values, vectors, weights):
    full = jnp.float32
    shapes = [
        (3, rows, columns),
        (columns, rows),
        (rows, hidden),
        (hidden, rows),
        (VEC, rows),
        (3, rows, columns),
        (columns, rows),
        (rows, hidden),
        (hidden, rows),
        (VEC, rows),
        (VEC, rows),
        (3, rows),
        (3, columns),
        (1, columns),
        (1, rows),
        (1, rows),
        (1, hidden),
        (1, hidden),
        (1, rows),
    ]
    return pl.pallas_call(
        functools.partial(update_kernel, layout, width, long),
        name="update_weights",
        out_shape=[jax.ShapeDtypeStruct(shape, full) for shape in shapes],
        compiler_params=pltpu.CompilerParams(vmem_limit_bytes=48 << 20),
    )(*values, vectors, *weights)


def head_parts(heads_ref, head):
    return [heads_ref[:, pl.ds(kind * LANES + head * HEAD_DIM, HEAD_DIM)] for kind in range(3)]


def attend_back_kernel(heads_ref, bias_ref, grad_ref, out_ref):
    bias = bias_ref[...]
    for head in range(2):
        query, key, value = head_parts(heads_ref, head)
        grad = grad_ref[:, pl.ds(head * HEAD_DIM, HEAD_DIM)]
        scores = lax.dot_general(key, query, CONTRACT_LAST, preferred_element_type=jnp.float32)
        scores = scores * (HEAD_DIM ** (-0.5) * LOG2E) + bias
        raised = jnp.exp2(scores - jnp.max(scores, axis=0, keepdims=True))
        attention = raised * (1.0 / jnp.sum(raised, axis=0, keepdims=True))
        grad_value = jnp.dot(attention.astype(jnp.bfloat16), grad, preferred_element_type=jnp.float32)
        grad_attention = lax.dot_general(value, grad, CONTRACT_LAST, preferred_element_type=jnp.float32)
        weighted = jnp.sum(attention * grad_attention, axis=0, keepdims=True)
        grad_scores = (attention * (grad_attention - weighted) * HEAD_DIM ** (-0.5)).astype(jnp.bfloat16)
        grad_key = jnp.dot(grad_scores, query, preferred_element_type=jnp.float32)
        grad_query = jnp.dot(key.T, grad_scores, preferred_element_type=jnp.float32).T
        for kind, value in enumerate((grad_query, grad_key, grad_value)):
            out_ref[:, pl.ds(kind * LANES + head * HEAD_DIM, HEAD_DIM)] = value.astype(jnp.bfloat16)


def attend_back(projected, bias_column, grad_mixed, width):
    rows = projected.shape[0]
    return pl.pallas_call(
        attend_back_kernel,
        name="attend_back",
        grid=(width // LANES,),
        out_shape=jax.ShapeDtypeStruct((rows, 3 * width), jnp.bfloat16),
        in_specs=[
            pl.BlockSpec((rows, 3 * LANES), lambda pair: (0, pair)),
            pl.BlockSpec((rows, 1), lambda pair: (0, 0)),
            pl.BlockSpec((rows, LANES), lambda pair: (0, pair)),
        ],
        out_specs=pl.BlockSpec((rows, 3 * LANES), lambda pair: (0, pair)),
        compiler_params=pltpu.CompilerParams(vmem_limit_bytes=40 << 20),
    )(projected, bias_column, grad_mixed)


def paired(array, axis):
    moved = jnp.moveaxis(array, axis, -2)
    lead = moved.shape[:-2]
    blocks = moved.reshape(*lead, 3, moved.shape[-1] // LANES, LANES)
    return jnp.swapaxes(blocks, -3, -2).reshape(*lead, 3 * moved.shape[-1])


def on_device(
    inputs,
    cotangent,
    token_mask,
    w_qkv,
    w_out,
    w_fc1,
    w_fc2,
    vectors,
    qkv_row,
    qkv_col,
    out_row,
    out_col,
    fc1_row,
    fc1_col,
    fc2_row,
    fc2_col,
    vec_second,
):
    tensor_count = lax.axis_size("tensor")
    dims = grid_of(lax.axis_size("fsdp"))
    tensor_rank = lax.axis_index("tensor")
    rows_here, width = inputs.shape
    own_rows, columns = w_qkv.shape[1:]
    hidden = w_fc1.shape[1]
    low = jnp.bfloat16

    keep = lax.dynamic_slice_in_dim(token_mask, tensor_rank, 1, 0)
    keep_rows = keep.reshape(rows_here, 1).astype(jnp.float32)
    bias = jnp.where(keep > 0, 0.0, -1e30).astype(jnp.float32)

    pack = jnp.concatenate(
        [
            paired(w_qkv, 0),
            jnp.pad(vectors.T, ((0, 0), (0, LANES - VEC))),
            w_out.T,
            w_fc1,
            w_fc2.T,
        ],
        axis=1,
    ).astype(low)
    (
        weight_qkv,
        _,
        weight_out,
        _,
        _,
        block_out,
        grad_middle,
        back_one,
        projected,
        mixed_rows,
        low_one,
        grad_one,
        grad_two,
        table,
        vec_sums,
        pre_sums,
    ) = forward(dims, tensor_count, pack, inputs, cotangent, keep_rows, bias, columns, hidden)
    weight_qkv = weight_qkv.reshape(width, 3 * width)
    weight_out = weight_out.reshape(width, width)
    normed_one, inverse_one = norm_parts(inputs)
    grad_out_weight = dot(back_one, mixed_rows, (((0,), (0,)), ((), ()))).astype(low)
    grad_mixed = dot(back_one, weight_out).astype(low)
    grad_proj = attend_back(projected, bias.reshape(rows_here, 1), grad_mixed, width)
    grad_qkv = dot(low_one, grad_proj, (((0,), (0,)), ((), ()))).astype(low)
    grad_low_one = dot(grad_proj, weight_qkv, CONTRACT_LAST)
    input_grad = grad_middle + norm_back(grad_low_one, normed_one, inverse_one, table[0])

    def column_sum(values):
        return jnp.sum(values, axis=0, dtype=jnp.float32)

    head_sums = column_sum(grad_proj).reshape(width // LANES, 3, LANES)
    grad_table = jnp.concatenate(
        [
            jnp.stack(
                [
                    column_sum(grad_low_one * normed_one),
                    column_sum(grad_low_one),
                    head_sums[:, 0].reshape(width),
                    head_sums[:, 2].reshape(width),
                    vec_sums[0],
                    vec_sums[1],
                    vec_sums[2],
                ]
            ),
            pre_sums.reshape(FF // width, width),
            vec_sums[3:4],
        ],
        0,
    )
    table_block = jnp.pad(grad_table.T.astype(low), ((0, 0), (0, LANES - VEC)))
    layout = Layout(columns, hidden, ("two", "one", "out", "qkv", "vec"))
    grad_arrays = [
        array.reshape(*dims, own_rows, array.shape[1])
        for array in (
            grad_two,
            grad_one,
            grad_out_weight,
            grad_qkv,
            jnp.concatenate([table_block] * tensor_count, axis=1),
        )
    ]
    col_state = {"qkv": paired(qkv_col, 0), "out": out_row, "one": fc1_col, "two": fc2_row}
    state_col = jnp.concatenate([col_state[name] for name in layout.order[:4]])[None]
    state_row = jnp.concatenate([qkv_row, out_col[None], fc1_row[None], fc2_col[None]], axis=0)
    state_row = jnp.pad(state_row.T, ((0, 0), (0, LANES - 6)))
    second = jnp.pad(vec_second.T, ((0, 0), (0, LANES - VEC)), constant_values=1.0)
    vectors_turned = jnp.pad(vectors.T, ((0, 0), (0, LANES - VEC)))
    weights = (w_qkv, w_out, w_fc1, w_fc2)
    values = reduce_grads(
        dims,
        tensor_count,
        layout,
        grad_arrays,
        (2, 2, 1, 1, 1),
        weights,
        (state_col, state_row, second, vectors_turned),
    )
    outs = update_weights(
        layout, width, FF, columns, hidden, own_rows, values, vectors_turned, weights
    )
    outs = [out.reshape(-1) if out.shape[0] == 1 else out for out in outs]
    return (block_out, input_grad, *outs[:10], *outs[11:], outs[10])


def solution(mesh):
    in_specs = (
        P(("fsdp", "tensor"), None),
        P(("fsdp", "tensor"), None),
        P("fsdp", None),
        P(None, "fsdp", "tensor"),
        P("tensor", "fsdp"),
        P("fsdp", "tensor"),
        P("tensor", "fsdp"),
        P(None, "fsdp"),
        P(None, "fsdp"),
        P(None, "tensor"),
        P("tensor"),
        P("fsdp"),
        P("fsdp"),
        P("tensor"),
        P("tensor"),
        P("fsdp"),
        P(None, "fsdp"),
    )
    out_specs = (
        P(("fsdp", "tensor"), None),
        P(("fsdp", "tensor"), None),
        P(None, "fsdp", "tensor"),
        P("tensor", "fsdp"),
        P("fsdp", "tensor"),
        P("tensor", "fsdp"),
        P(None, "fsdp"),
        P(None, "fsdp", "tensor"),
        P("tensor", "fsdp"),
        P("fsdp", "tensor"),
        P("tensor", "fsdp"),
        P(None, "fsdp"),
        P(None, "fsdp"),
        P(None, "tensor"),
        P("tensor"),
        P("fsdp"),
        P("fsdp"),
        P("tensor"),
        P("tensor"),
        P("fsdp"),
        P(None, "fsdp"),
    )
    return jax.shard_map(
        on_device, mesh=mesh, in_specs=in_specs, out_specs=out_specs, check_vma=False
    )
```

```python
import functools

import jax
import jax.numpy as jnp
from jax import lax
from jax.experimental import pallas as pl
from jax.experimental.pallas import tpu as pltpu
from jax.sharding import PartitionSpec as P

HEAD_DIM = 64
FF = 4096
STEP = 20
VEC = 12
LANES = 128

EPS_NORM = 1e-05
EPS_ONE = 1e-30
CLIP_LEVEL = 1.0
LEARN_RATE = 0.5
MESH = pl.DeviceIdType.MESH
LOG2E = 1.4426950408889634
CONTRACT_LAST = (((1,), (1,)), ((), ()))


def grid_of(count):
    return {16: (4, 2, 2), 32: (2, 4, 4)}.get(count, (count, 1, 1))


class Place:
    def __init__(self, dims, tensor):
        self.dims = dims
        self.tensor = tensor
        fsdp = lax.axis_index("fsdp")
        _, ny, nx = dims
        self.at = (fsdp // (ny * nx), (fsdp // nx) % ny, fsdp % nx)
        self.rank = lax.axis_index("tensor")

    def moved(self, axis, step):
        place = list(self.at) + [self.rank]
        size = (*self.dims, self.tensor)[axis]
        place[axis] = lax.rem(place[axis] + step + size, size)
        return tuple(place)

    def device(self, place):
        z, y, x, rank = place
        return {"fsdp": (z * self.dims[1] + y) * self.dims[2] + x, "tensor": rank}

    def size(self, axis):
        return (*self.dims, self.tensor)[axis]

    def barrier(self):
        sem = pltpu.get_barrier_semaphore()
        count = 0
        for axis in range(4):
            for step in range(1, self.size(axis)):
                pl.semaphore_signal(
                    sem,
                    inc=1,
                    device_id=self.device(self.moved(axis, step)),
                    device_id_type=MESH,
                )
                count += 1
        if count:
            pl.semaphore_wait(sem, count)


def axis_order(half):
    return (0, 1, 2) if half == 0 else (0, 2, 1)


def norm_rows(values):
    average = jnp.mean(values, axis=1, keepdims=True)
    center = values - average
    inverse = lax.rsqrt(jnp.mean(center * center, axis=1, keepdims=True) + EPS_NORM)
    return center * inverse, inverse


def dot(left, right, dims=(((1,), (0,)), ((), ()))):
    return lax.dot_general(left, right, dims, preferred_element_type=jnp.float32)


def turn(source, target):
    for start in range(0, source.shape[1], LANES):
        target[pl.ds(start, LANES), :] = source[:, pl.ds(start, LANES)].T


def attend_pair(heads, bias):
    mixed = []
    for head in range(2):
        query, key, value = (
            heads[:, kind * LANES + head * HEAD_DIM : kind * LANES + (head + 1) * HEAD_DIM] for kind in range(3)
        )
        scores = dot(query, key, CONTRACT_LAST) * (HEAD_DIM ** (-0.5) * LOG2E) + bias
        raised = jnp.exp2(scores - jnp.max(scores, axis=1, keepdims=True))
        summed = jnp.sum(raised, axis=1, keepdims=True)
        attention = (raised * (1.0 / summed)).astype(jnp.bfloat16)
        mixed.append(dot(attention, value).astype(jnp.bfloat16))
    return jnp.concatenate(mixed, axis=1)


class Gather:
    def __init__(self, here, pack_ref, outs, parts, local_sem, send_sem, recv_sem):
        self.here = here
        self.pack = pack_ref
        self.outs = outs
        self.half_rows = pack_ref.shape[0] // 2
        self.parts = parts
        self.sems = (local_sem, send_sem, recv_sem)
        self.own = (*here.at, here.rank)
        self.sent = []
        self.local = {}

    def rows(self, half):
        return pl.ds(half * self.half_rows, self.half_rows)

    def region(self, item, half, place, free):
        out, _, start, size, total, shared = self.parts[item]
        base = 0 if shared else place[3] * total
        column = pl.ds(pl.multiple_of(base + start, LANES), size)
        index = tuple(slice(None) if a in free else place[a] for a in range(3))
        return self.outs[out].at[(*index, self.rows(half), column)]

    def shard(self, item, half):
        _, offset, _, size, _, _ = self.parts[item]
        return self.pack.at[self.rows(half), pl.ds(offset, size)]

    def axes(self, item, half):
        order = axis_order(half)
        return order if self.parts[item][5] else (*order, 3)

    def copies(self, item, half, phase, landing):
        here = self.here
        order = self.axes(item, half)
        axis, free = order[phase], order[:phase]
        found = []
        for step in range(1, here.size(axis)):
            own = self.region(item, half, self.own, free)
            if landing:
                src = dst = self.region(item, half, here.moved(axis, -step), free)
            else:
                src, dst = (self.shard(item, half) if phase == 0 else own), own
            found.append(
                pltpu.make_async_remote_copy(
                    src_ref=src,
                    dst_ref=dst,
                    send_sem=self.sems[1].at[item, half, phase, step - 1],
                    recv_sem=self.sems[2].at[item, half, phase, step - 1],
                    device_id=here.device(here.moved(axis, step)),
                    device_id_type=MESH,
                )
            )
        return found

    def start(self):
        for item in range(len(self.parts)):
            for half in range(2):
                copy = pltpu.make_async_copy(
                    self.shard(item, half), self.region(item, half, self.own, ()), self.sems[0].at[item, half]
                )
                copy.start()
                self.local[item, half] = copy

    def advance(self, item, phase):
        for half in range(2):
            order = self.axes(item, half)
            if 0 < phase <= len(order):
                for copy in self.copies(item, half, phase - 1, True):
                    copy.wait_recv()
            if phase == 1:
                self.local[item, half].wait()
            if phase < len(order):
                for copy in self.copies(item, half, phase, False):
                    copy.start()
                    self.sent.append(copy)

    def finish(self):
        for copy in self.sent:
            copy.wait_send()


PHASES = 4
BLOCK = 512
PIECE = 256
LAG = 2
TASK_RATE = 0.6


def forward_kernel(dims, tensor, parts, plan, pack_ref, input_ref, top_ref, keep_ref, bias_ref, *refs):
    outs, land = refs[:5], refs[5:7]
    weight_qkv, weight_vec, weight_out, weight_one, weight_two = outs
    (
        block_out,
        grad_middle,
        back_one,
        projected,
        mixed,
        low_one,
        grad_one,
        grad_two,
        table,
        vec_sums,
        pre_sums,
    ) = refs[7:18]
    (
        vec_buf,
        qkv_buf,
        head_stage,
        out_buf,
        one_buf,
        two_buf,
        low_two,
        low_two_turned,
        back_two,
        back_two_turned,
        grad_low_two,
        hidden_bias,
        head_bias,
        one_stage,
        two_stage,
        other,
        load_sem,
        store_sem,
        head_sem,
        land_sem,
        local_sem,
        send_sem,
        recv_sem,
    ) = refs[18:]
    here = Place(dims, tensor)
    gather = Gather(here, pack_ref, outs, parts, local_sem, send_sem, recv_sem)
    rows, width = input_ref.shape
    low = jnp.bfloat16
    step_rows = LANES

    def row_steps(body, carry):
        return lax.fori_loop(
            0, rows // step_rows, lambda at, c: body(pl.ds(pl.multiple_of(at * step_rows, step_rows), step_rows), c), carry
        )

    def load(source, buffer, sem):
        return pltpu.make_async_copy(source, buffer, sem)

    def first_norm():
        copy = load(weight_vec, vec_buf, load_sem.at[0])
        copy.start()
        copy.wait()
        whole = vec_buf[...].reshape(width, LANES).astype(jnp.float32).T
        table[...] = whole[:16]
        for at in range(VEC - 8):
            hidden_bias[:, pl.ds(at * width, width)] = whole[7 + at : 8 + at]
        for pair in range(width // LANES):
            for kind, row in ((0, 2), (2, 3)):
                head_bias[:, pl.ds((pair * 3 + kind) * LANES, LANES)] = whole[
                    row : row + 1, pair * LANES : (pair + 1) * LANES
                ]
            head_bias[:, pl.ds((pair * 3 + 1) * LANES, LANES)] = jnp.zeros((1, LANES), jnp.float32)

        def body(part, carry):
            normed, _ = norm_rows(input_ref[part, :])
            low_one[part, :] = (normed * table[0:1, :] + table[1:2, :]).astype(low)
            back_two[part, :] = (top_ref[part, :].astype(jnp.float32) * keep_ref[part, :]).astype(low)
            return carry

        row_steps(body, 0)
        turn(back_two, back_two_turned)

    def head_store(pair, slot):
        column = pl.ds(pl.multiple_of(pair * 3 * LANES, LANES), 3 * LANES)
        return pltpu.make_async_copy(head_stage.at[slot], projected.at[:, column], head_sem.at[slot])

    def heads(first, per_rank):
        def pair_of(at):
            return lax.rem(here.rank + at, tensor) * per_rank + first

        def weights(at):
            column = pl.multiple_of(pair_of(at) * 3 * LANES, LANES)
            slot = lax.rem(at, 2)
            return load(
                weight_qkv.at[:, :, :, :, pl.ds(column, 3 * LANES)], qkv_buf.at[slot], load_sem.at[slot]
            )

        weights(0).start()

        def body(at, carry):
            weights(at).wait()

            @pl.when(at + 1 < tensor)
            def _():
                weights(at + 1).start()

            pair = pair_of(at)
            slot = lax.rem(at, 2)
            column = pl.ds(pl.multiple_of(pair * 3 * LANES, LANES), 3 * LANES)
            weight = qkv_buf[slot].reshape(width, 3 * LANES)
            value = (dot(low_one[...], weight) + head_bias[:, column]).astype(low)
            if first:
                head_store(pair, slot).wait()
            else:

                @pl.when(at > 1)
                def _():
                    head_store(pair, slot).wait()

            head_stage[slot] = value
            head_store(pair, slot).start()
            mixed[:, pl.ds(pl.multiple_of(pair * LANES, LANES), LANES)] = attend_pair(value, bias_ref[...])
            return carry

        lax.fori_loop(0, tensor, body, 0)

    def second_norm():
        copy = load(weight_out, out_buf, load_sem.at[0])
        copy.start()
        copy.wait()
        term = dot(mixed[...], out_buf[...].reshape(width, width), CONTRACT_LAST)
        grad_middle[...] = term

        def body(part, carry):
            middle = input_ref[part, :] + (grad_middle[part, :] + table[4:5, :]) * keep_ref[part, :]
            grad_middle[part, :] = middle
            normed, _ = norm_rows(middle)
            low_two[part, :] = (normed * table[5:6, :] + table[6:7, :]).astype(low)
            return carry

        row_steps(body, 0)
        turn(low_two, low_two_turned)

    stages = (one_stage, two_stage)

    def hand_over(at, slot, chunk):
        place = (*here.at, lax.rem(here.rank + at + 1, tensor))
        return [
            pltpu.make_async_remote_copy(
                src_ref=stages[which].at[slot],
                dst_ref=land[which].at[at, chunk],
                send_sem=store_sem.at[which, slot],
                recv_sem=land_sem.at[which, at, chunk],
                device_id=here.device(place),
                device_id_type=MESH,
            )
            for which in range(2)
        ]

    def stores(start, slot):
        return [
            pltpu.make_async_copy(
                stages[which].at[slot],
                out.at[:, :, :, :, pl.ds(start, BLOCK)],
                store_sem.at[which, slot],
            )
            for which, out in enumerate((grad_one, grad_two))
        ]

    def hidden(first, total):
        chunk = first // BLOCK

        def column_of(at):
            base = lax.rem(here.rank + at + 1, tensor) * total + first
            return pl.ds(pl.multiple_of(base, LANES), BLOCK)

        def weights(at):
            slot = lax.rem(at, 2)
            column = column_of(at)
            return [
                load(source.at[:, :, :, :, column], buffer.at[slot], load_sem.at[2 * which + slot])
                for which, (source, buffer) in enumerate(((weight_one, one_buf), (weight_two, two_buf)))
            ]

        for copy in weights(0):
            copy.start()

        def body(at, carry):
            slot = lax.rem(at, 2)
            column = column_of(at)
            for copy in weights(at):
                copy.wait()

            @pl.when(at + 1 < tensor)
            def _():
                for copy in weights(at + 1):
                    copy.start()

            one = one_buf[slot].reshape(width, BLOCK)
            two = two_buf[slot].reshape(width, BLOCK)
            preact = dot(low_two[...], one) + hidden_bias[:, column]
            gate = jax.nn.sigmoid(1.702 * preact)
            active = (preact * gate).astype(low)
            derivative = gate + 1.702 * preact * gate * (1.0 - gate)
            grad_pre = (dot(back_two[...], two) * derivative).astype(low)
            pre_sums[:, column] = jnp.sum(grad_pre.astype(jnp.float32), axis=0, keepdims=True)
            out_term = dot(active, two, CONTRACT_LAST)
            back_term = dot(grad_pre, one, CONTRACT_LAST)
            if chunk == 0:

                @pl.when(at == 0)
                def _():
                    block_out[...] = out_term
                    grad_low_two[...] = back_term

                @pl.when(at > 0)
                def _():
                    block_out[...] += out_term
                    grad_low_two[...] += back_term

                @pl.when(at > 1)
                def _():
                    for copy in hand_over(at - 2, slot, chunk):
                        copy.wait_send()

            else:
                block_out[...] += out_term
                grad_low_two[...] += back_term

                @pl.when(at == 1)
                def _():
                    for copy in stores(0, slot):
                        copy.wait()

                @pl.when(at != 1)
                def _():
                    for copy in hand_over(0, slot, chunk):
                        copy.wait_send()

            for stage, left, right in (
                (one_stage, low_two_turned, grad_pre),
                (two_stage, back_two_turned, active),
            ):
                value = dot(left[...], right).astype(low)
                stage[slot] = value.reshape(*stage.shape[1:])

            @pl.when(at < tensor - 1)
            def _():
                for copy in hand_over(at, slot, chunk):
                    copy.start()

            @pl.when(at == tensor - 1)
            def _():
                for step in range(tensor - 1):
                    for which, copy in enumerate(hand_over(step, slot, chunk)):
                        copy.wait_recv()
                        fetch = load(land[which].at[step, chunk], other, load_sem.at[0])
                        fetch.start()
                        fetch.wait()
                        stages[which][slot] = stages[which][slot] + other[...]
                for copy in stores(first, slot):
                    copy.start()

            return carry

        lax.fori_loop(0, tensor, body, 0)

    def last_norm():
        def body(part, sums):
            middle = grad_middle[part, :]
            keep = keep_ref[part, :]
            top = top_ref[part, :].astype(jnp.float32)
            block_out[part, :] = middle + (block_out[part, :] + table[VEC - 1 : VEC, :]) * keep
            normed, inverse = norm_rows(middle)
            grad_low = grad_low_two[part, :]
            scaled = grad_low * table[5:6, :]
            first = jnp.mean(scaled, axis=1, keepdims=True)
            second = jnp.mean(scaled * normed, axis=1, keepdims=True)
            grad = top + inverse * (scaled - first - normed * second)
            grad_middle[part, :] = grad
            masked = grad * keep
            back_one[part, :] = masked.astype(low)
            terms = (masked, grad_low * normed, grad_low, top * keep)
            return tuple(old + jnp.sum(term, axis=0, keepdims=True) for old, term in zip(sums, terms))

        zero = jnp.zeros((1, width), jnp.float32)
        for at, value in enumerate(row_steps(body, (zero,) * 4)):
            vec_sums[at : at + 1, :] = value

    here.barrier()
    gather.start()
    count = len(parts)
    for wave in range(count + LAG * PHASES):
        for phase in reversed(range(PHASES + 1)):
            item = wave - LAG * phase
            if 0 <= item < count:
                gather.advance(item, phase)
        task = plan[wave - LAG * PHASES] if wave >= LAG * PHASES else None
        if task is None:
            continue
        if task[0] == "norm":
            first_norm()
        elif task[0] == "heads":
            heads(*task[1:])
        elif task[0] == "out":
            second_norm()
        else:
            hidden(*task[1:])
    last_norm()
    slots = range(min(2, tensor))
    for slot in slots:
        head_store(0, slot).wait()
        if slot == (tensor - 1) % 2:
            for copy in stores(0, slot):
                copy.wait()
        else:
            for copy in hand_over(0, slot, 0):
                copy.wait_send()
    gather.finish()


def forward(dims, tensor, pack, inputs, cotangent, keep_rows, bias, columns, hidden):
    own_rows = pack.shape[0]
    rows, width = inputs.shape
    low, full = jnp.bfloat16, jnp.float32
    widths = (3 * columns, LANES, columns, hidden, hidden)
    offsets = [sum(widths[:at]) for at in range(5)]
    per_rank = columns // LANES
    parts = [(1, offsets[1], 0, LANES, LANES, True)]
    plan = [("norm",)]
    for at in range(per_rank):
        size = 3 * LANES
        parts.append((0, offsets[0] + at * size, at * size, size, widths[0], False))
        plan.append(("heads", at, per_rank))
    for start in range(0, columns, PIECE):
        size = min(PIECE, columns - start)
        parts.append((2, offsets[2] + start, start, size, columns, False))
        plan.append(("out",) if start + size == columns else None)
    for start in range(0, hidden, PIECE):
        for which in (3, 4):
            parts.append((which, offsets[which] + start, start, PIECE, hidden, False))
            full_block = which == 4 and (start + PIECE) % BLOCK == 0
            plan.append(("hidden", start + PIECE - BLOCK, hidden) if full_block else None)
    count = len(parts)
    peers = max(2, *dims, tensor) - 1
    anywhere = pl.BlockSpec(memory_space=pl.ANY)
    inside = pl.BlockSpec(memory_space=pltpu.VMEM)

    def shape(kind, *size):
        return jax.ShapeDtypeStruct(size, kind)

    return pl.pallas_call(
        functools.partial(forward_kernel, dims, tensor, tuple(parts), tuple(plan)),
        name="forward",
        out_shape=[
            *(shape(low, *dims, own_rows, w * (1 if at == 1 else tensor)) for at, w in enumerate(widths)),
            *[shape(low, max(1, tensor - 1), hidden // BLOCK, *dims, own_rows, BLOCK)] * 2,
            shape(full, rows, width),
            shape(full, rows, width),
            shape(low, rows, width),
            shape(low, rows, 3 * width),
            shape(low, rows, width),
            shape(low, rows, width),
            *[shape(low, *dims, own_rows, hidden)] * 2,
            shape(full, 16, width),
            shape(full, 8, width),
            shape(full, 1, hidden * tensor),
        ],
        in_specs=[anywhere] + [inside] * 4,
        out_specs=[anywhere] * 7 + [inside] * 3 + [anywhere] + [inside] * 2 + [anywhere] * 2 + [inside] * 3,
        scratch_shapes=[
            pltpu.VMEM((*dims, own_rows, LANES), low),
            pltpu.VMEM((2, *dims, own_rows, 3 * LANES), low),
            pltpu.VMEM((2, rows, 3 * LANES), low),
            pltpu.VMEM((*dims, own_rows, width), low),
            pltpu.VMEM((2, *dims, own_rows, BLOCK), low),
            pltpu.VMEM((2, *dims, own_rows, BLOCK), low),
            pltpu.VMEM((rows, width), low),
            pltpu.VMEM((width, rows), low),
            pltpu.VMEM((rows, width), low),
            pltpu.VMEM((width, rows), low),
            pltpu.VMEM((rows, width), full),
            pltpu.VMEM((1, hidden * tensor), full),
            pltpu.VMEM((1, 3 * width), full),
            pltpu.VMEM((2, *dims, own_rows, BLOCK), low),
            pltpu.VMEM((2, *dims, own_rows, BLOCK), low),
            pltpu.VMEM((*dims, own_rows, BLOCK), low),
            pltpu.SemaphoreType.DMA((4,)),
            pltpu.SemaphoreType.DMA((2, 2)),
            pltpu.SemaphoreType.DMA((2,)),
            pltpu.SemaphoreType.DMA((2, max(1, tensor - 1), hidden // BLOCK)),
            pltpu.SemaphoreType.DMA((count, 2)),
            pltpu.SemaphoreType.DMA((count, 2, 4, peers)),
            pltpu.SemaphoreType.DMA((count, 2, 4, peers)),
        ],
        compiler_params=pltpu.CompilerParams(
            collective_id=0, has_side_effects=True, vmem_limit_bytes=62 << 20
        ),
    )(pack, inputs, cotangent, keep_rows, bias)


class Layout:
    def __init__(self, columns, hidden, order):
        sizes = {"qkv": 3 * columns, "out": columns, "one": hidden, "two": hidden, "vec": LANES}
        self.order = order
        self.sizes = sizes
        self.start = {}
        at = 0
        for name in order:
            self.start[name] = at
            at += sizes[name]
        self.total = at
        self.columns = columns

    def span(self, name):
        return (self.start[name], self.sizes[name])

    def matrices(self):
        base = self.start["qkv"]
        pairs = range(self.columns // LANES)
        spans = [[(base + (pair * 3 + at) * LANES, LANES) for pair in pairs] for at in range(3)]
        return spans + [[self.span(name)] for name in ("out", "one", "two")]


def pick(values, lane):
    row = jnp.zeros((1, LANES), jnp.float32)
    for at, value in enumerate(values):
        row = jnp.where(lane == at, value, row)
    return row


def total_of(values):
    return jnp.sum(jnp.sum(values, axis=1, keepdims=True), axis=0, keepdims=True)


def attend_pair_back(heads, bias, grads):
    parts = ([], [], [])
    for head in range(2):
        query, key, value = (
            heads[:, kind * LANES + head * HEAD_DIM : kind * LANES + (head + 1) * HEAD_DIM] for kind in range(3)
        )
        grad = grads[:, head * HEAD_DIM : (head + 1) * HEAD_DIM]
        scores = dot(key, query, CONTRACT_LAST) * (HEAD_DIM ** (-0.5) * LOG2E) + bias
        raised = jnp.exp2(scores - jnp.max(scores, axis=0, keepdims=True))
        attention = raised * (1.0 / jnp.sum(raised, axis=0, keepdims=True))
        grad_value = dot(attention.astype(jnp.bfloat16), grad)
        grad_attention = dot(value, grad, CONTRACT_LAST)
        weighted = jnp.sum(attention * grad_attention, axis=0, keepdims=True)
        grad_scores = (attention * (grad_attention - weighted) * HEAD_DIM ** (-0.5)).astype(jnp.bfloat16)
        grad_key = dot(grad_scores, query)
        grad_query = dot(key.T, grad_scores).T
        for kind, part in enumerate((grad_query, grad_key, grad_value)):
            parts[kind].append(part.astype(jnp.bfloat16))
    return jnp.concatenate([piece for kind in parts for piece in kind], axis=1)


def backward_kernel(dims, tensor, items, layout, *refs):
    (
        sum_two,
        sum_one,
        weight_qkv,
        weight_out,
        projected,
        input_ref,
        middle_ref,
        mixed,
        low_one,
        back_one,
        bias_ref,
        table,
        vec_sums,
        pre_sums,
    ) = refs[:14]
    weights = refs[14:18]
    state_col, state_row, second_ref, vector_ref = refs[18:22]
    input_grad, total_ref, col_new_ref, row_new_ref, second_new_ref, sums_ref = refs[22:28]
    (
        own,
        from_core,
        one_x,
        one_y,
        two_y,
        two_x,
        from_z,
        col_sum,
        col_in,
        row_sum,
        row_in,
        small,
        small_in,
        low_turned,
        back_turned,
        grad_mixed,
        out_buf,
        qkv_buf,
        head_buf,
        row_buf,
        out_stage,
        qkv_stage,
        vec_stage,
        head_sums,
        table_grad_ref,
        load_sem,
        stage_sem,
        core_sem,
        local_sem,
        send_sem,
        recv_sem,
        sum_send,
        sum_recv,
    ) = refs[28:]
    here = Place(dims, tensor)
    nz, ny, nx = dims
    low = jnp.bfloat16
    half_rows = own.shape[4]
    own_rows = 2 * half_rows
    rows, width = input_grad.shape
    own_place = (*here.at, here.rank)
    count = len(items)
    core_start = layout.start["out"]

    def columns(item):
        _, start, size, _ = items[item]
        return pl.ds(start, size)

    def core_columns(item):
        _, start, size, _ = items[item]
        return pl.ds(start - core_start, size)

    def order(half):
        return (3, 2, 1, 0) if half == 0 else (3, 1, 2, 0)

    def part(item, half, place, fixed):
        index = tuple(place[a] if a in fixed else slice(None) for a in range(3))
        return own.at[(half, *index, slice(None), columns(item))]

    def slot(item, half, phase, step):
        if phase == 3:
            return from_z.at[half, step - 1, :, columns(item)]
        if phase == 1:
            buffer = one_x if half == 0 else one_y
            return buffer.at[step - 1, :, :, :, columns(item)]
        buffer = two_y if half == 0 else two_x
        return buffer.at[step - 1, :, :, columns(item)]

    def copies(item, half, phase):
        axes = order(half)
        axis, fixed = axes[phase], axes[1 : phase + 1]
        found = []
        for step in range(1, here.size(axis)):
            target = here.moved(axis, step)
            found.append(
                pltpu.make_async_remote_copy(
                    src_ref=part(item, half, target, fixed),
                    dst_ref=slot(item, half, phase, step),
                    send_sem=send_sem.at[item, half, phase, step - 1],
                    recv_sem=recv_sem.at[item, half, phase, step - 1],
                    device_id=here.device(target),
                    device_id_type=MESH,
                )
            )
        return found

    def add_in(item, half, phase):
        axes = order(half)
        axis, fixed = axes[phase], axes[1 : phase + 1]
        column = columns(item)
        steps = here.size(axis) - 1
        if phase == 3:
            value = own[(half, *here.at, slice(None), column)].astype(jnp.float32)
            for step in range(steps):
                value = value + from_z[half, step, :, column].astype(jnp.float32)
            total_ref[pl.ds(half * half_rows, half_rows), column] = value
            return
        if steps == 0:
            return
        free = [a for a in range(3) if a not in fixed]
        sizes = [dims[a] for a in free]
        loops = 1
        for size in sizes:
            loops *= size

        def body(at, carry):
            place = list(here.at)
            inner = []
            rest = at
            for axis_at, size in reversed(list(zip(free, sizes))):
                place[axis_at] = rest % size
                inner.insert(0, rest % size)
                rest = rest // size
            where = (half, *place, slice(None), column)
            value = own[where]
            for step in range(steps):
                if phase == 0:
                    near = (step, *inner, pl.ds(half * half_rows, half_rows), core_columns(item))
                    piece = from_core[near]
                elif phase == 1:
                    piece = (one_x if half == 0 else one_y)[(step, *inner, slice(None), column)]
                else:
                    piece = (two_y if half == 0 else two_x)[(step, *inner, slice(None), column)]
                value = value + piece
            own[where] = value
            return carry

        lax.fori_loop(0, loops, body, 0)

    sent = []

    def exchange(kind, phase, axis, buffer, landing):
        moved = []
        for step in range(1, here.size(axis)):
            copy = pltpu.make_async_remote_copy(
                src_ref=buffer.at[phase],
                dst_ref=landing.at[phase, step - 1],
                send_sem=sum_send.at[kind, phase, step - 1],
                recv_sem=sum_recv.at[kind, phase, step - 1],
                device_id=here.device(here.moved(axis, step)),
                device_id_type=MESH,
            )
            copy.start()
            moved.append(copy)
        sent.extend(moved)

        def finish():
            value = buffer[phase]
            for step, copy in enumerate(moved):
                copy.wait_recv()
                value = value + landing[phase, step]
            buffer[phase + 1] = value

        return finish

    def hand_over(item, step, source, sem):
        return pltpu.make_async_remote_copy(
            src_ref=source,
            dst_ref=from_core.at[step - 1, :, :, :, :, core_columns(item)],
            send_sem=sem,
            recv_sem=core_sem.at[item, step - 1],
            device_id=here.device(here.moved(3, step)),
            device_id_type=MESH,
        )

    arriving = {}

    def keep_own(item, value, start=0, size=None):
        block = value.reshape(nz, ny, nx, own_rows, value.shape[1])
        size = value.shape[1] if size is None else size
        column = pl.ds(items[item][1], size)
        for half in range(2):
            own[half, :, :, :, :, column] = block[
                :, :, :, half * half_rows : (half + 1) * half_rows, start : start + size
            ]

    out_items = [at for at, item in enumerate(items) if item[0] == "out"]
    qkv_items = [at for at, item in enumerate(items) if item[0] == "qkv"]
    vec_item = count - 1
    per_rank = len(qkv_items)
    steps_in_all = per_rank * tensor

    def rank_at(step):
        return lax.rem(here.rank + step, tensor)

    def pair_loads(at):
        turn_at, place = divmod(at, tensor)
        pair = rank_at(place + 1) * per_rank + turn_at
        column = pl.ds(pl.multiple_of(pair * 3 * LANES, LANES), 3 * LANES)
        near = at % 2
        return pair, column, [
            pltpu.make_async_copy(
                weight_qkv.at[:, :, :, :, column], qkv_buf.at[near], load_sem.at[0, near]
            ),
            pltpu.make_async_copy(projected.at[:, column], head_buf.at[near], load_sem.at[1, near]),
        ]

    def out_task():
        fetch = pltpu.make_async_copy(weight_out, out_buf, load_sem.at[2, 0])
        fetch.start()
        turn(back_one, back_turned)
        for copy in pair_loads(0)[2]:
            copy.start()
        size = out_stage.shape[5]
        for step in range(1, tensor + 1):
            column = pl.ds(pl.multiple_of(rank_at(step) * size, LANES), size)
            value = dot(back_turned[...], mixed[:, column]).astype(low)
            if step < tensor:
                out_stage[step - 1] = value.reshape(nz, ny, nx, own_rows, size)
                for item in out_items:
                    start = items[item][1] - core_start
                    source = out_stage.at[step - 1, :, :, :, :, pl.ds(start, items[item][2])]
                    copy = hand_over(item, step, source, stage_sem.at[item, step - 1])
                    copy.start()
                    sent.append(copy)
                    arriving.setdefault(item, []).append(copy)
            else:
                for item in out_items:
                    keep_own(item, value, items[item][1] - core_start, items[item][2])
        fetch.wait()
        grad_mixed[...] = dot(back_one[...], out_buf[...].reshape(width, width)).astype(low)
        turn(low_one, low_turned)

    staged = {}

    def pair_task(at):
        turn_at, place = divmod(at, tensor)
        pair, column, loads = pair_loads(at)
        for copy in loads:
            copy.wait()
        if at + 1 < steps_in_all:
            for copy in pair_loads(at + 1)[2]:
                copy.start()
        near = at % 2
        grads = grad_mixed[:, pl.ds(pl.multiple_of(pair * LANES, LANES), LANES)]
        value = attend_pair_back(head_buf[near], bias_ref[...], grads)
        head_sums[:, column] = jnp.sum(value.astype(jnp.float32), axis=0, keepdims=True)
        weight = qkv_buf[near].reshape(width, 3 * LANES)
        term = dot(value, weight, CONTRACT_LAST)
        if at == 0:
            input_grad[...] = term
        else:
            input_grad[...] += term
        item = qkv_items[turn_at]
        grad = dot(low_turned[...], value).astype(low)
        if place + 1 < tensor:
            if near in staged:
                staged[near].wait_send()
            qkv_stage[near] = grad.reshape(nz, ny, nx, own_rows, 3 * LANES)
            copy = hand_over(item, place + 1, qkv_stage.at[near], stage_sem.at[item, place])
            copy.start()
            staged[near] = copy
            arriving.setdefault(item, []).append(copy)
        else:
            keep_own(item, grad)

    def last_task():
        step_rows = LANES

        def fetch(at):
            near = lax.rem(at, 2)
            part = pl.ds(pl.multiple_of(at * step_rows, step_rows), step_rows)
            return [
                pltpu.make_async_copy(source.at[part, :], row_buf.at[which, near], load_sem.at[which, near])
                for which, source in enumerate((input_ref, middle_ref))
            ]

        for copy in fetch(0):
            copy.start()

        def body(at, sums):
            for copy in fetch(at):
                copy.wait()

            @pl.when(at + 1 < rows // step_rows)
            def _():
                for copy in fetch(at + 1):
                    copy.start()

            near = lax.rem(at, 2)
            part = pl.ds(pl.multiple_of(at * step_rows, step_rows), step_rows)
            normed, inverse = norm_rows(row_buf[0, near])
            grad_low = input_grad[part, :]
            scaled = grad_low * table[0:1, :]
            first = jnp.mean(scaled, axis=1, keepdims=True)
            second = jnp.mean(scaled * normed, axis=1, keepdims=True)
            input_grad[part, :] = row_buf[1, near] + inverse * (scaled - first - normed * second)
            terms = (grad_low * normed, grad_low)
            return tuple(old + jnp.sum(term, axis=0, keepdims=True) for old, term in zip(sums, terms))

        zero = jnp.zeros((1, width), jnp.float32)
        found = lax.fori_loop(0, rows // step_rows, body, (zero, zero))
        table_grad_ref[...] = jnp.zeros_like(table_grad_ref)
        for at in range(2):
            table_grad_ref[at : at + 1, :] = found[at]
        for pair in range(width // LANES):
            for kind, row in ((0, 2), (2, 3)):
                table_grad_ref[row : row + 1, pl.ds(pair * LANES, LANES)] = head_sums[
                    :, pl.ds((pair * 3 + kind) * LANES, LANES)
                ]
        for at, row in enumerate((4, 5, 6, VEC - 1)):
            table_grad_ref[row : row + 1, :] = vec_sums[at : at + 1, :]
        for at in range(VEC - 8):
            table_grad_ref[7 + at : 8 + at, :] = pre_sums[:, pl.ds(at * width, width)]
        value = table_grad_ref[...].T.astype(low)
        vec_stage[...] = value.reshape(nz, ny, nx, own_rows, LANES)
        for step in range(1, tensor):
            copy = hand_over(vec_item, step, vec_stage, stage_sem.at[vec_item, step - 1])
            copy.start()
            sent.append(copy)
            arriving.setdefault(vec_item, []).append(copy)
        keep_own(vec_item, value)

    tasks = [out_task]
    tasks += [functools.partial(pair_task, at) for at in range(steps_in_all)]
    tasks.append(last_task)
    needs = {item: 1 for item in out_items}
    needs |= {item: 1 + tensor * (at + 1) for at, item in enumerate(qkv_items)}
    needs[vec_item] = len(tasks)
    done = 0

    here.barrier()
    local = {}
    for item, (name, start, size, source) in enumerate(items):
        if name in ("one", "two"):
            array = sum_one if name == "one" else sum_two
            for half in range(2):
                copy = pltpu.make_async_copy(
                    array.at[:, :, :, pl.ds(half * half_rows, half_rows), pl.ds(source, size)],
                    part(item, half, own_place, ()),
                    local_sem.at[item, half],
                )
                copy.start()
                local[item, half] = copy
    for wave in range(count + LAG * 3):
        if wave < count:
            while done < needs.get(wave, 0):
                tasks[done]()
                done += 1
        for phase in reversed(range(1, 5)):
            item = wave - LAG * (phase - 1)
            if not 0 <= item < count:
                continue
            for half in range(2):
                if phase > 1:
                    for copy in copies(item, half, phase - 1):
                        copy.wait_recv()
                    add_in(item, half, phase - 1)
                elif (item, half) in local:
                    local[item, half].wait()
                else:
                    if half == 0:
                        for copy in arriving.get(item, ()):
                            copy.wait_recv()
                    add_in(item, half, 0)
                if phase < 4:
                    for copy in copies(item, half, phase):
                        copy.start()
                        sent.append(copy)
        while done < min(len(tasks), TASK_RATE * (wave + 1)):
            tasks[done]()
            done += 1
    sent.extend(staged.values())

    decay_rate = 1.0 - STEP ** (-0.8)
    keep_old = 1.0 - decay_rate
    long = layout.sizes["one"] * tensor
    matrices = layout.matrices()
    lane = lax.broadcasted_iota(jnp.int32, (1, LANES), 1)
    row_parts = []
    for spans in matrices:
        row_part = 0.0
        for start, size in spans:
            value = total_ref[:, pl.ds(start, size)]
            square = value * value
            col_sum[0, :, pl.ds(start, size)] = jnp.sum(square, axis=0, keepdims=True)
            row_part = row_part + jnp.sum(square, axis=1, keepdims=True)
        row_parts.append(row_part)
    row_sum[0] = pick(row_parts, lane)
    finish_row = exchange(0, 0, 3, row_sum, row_in)
    finish_col = exchange(1, 0, 0, col_sum, col_in)
    vec_start = layout.start["vec"]
    table_grad = total_ref[:, pl.ds(vec_start, LANES)]
    second_new = decay_rate * second_ref[...] + keep_old * (table_grad * table_grad + EPS_ONE)
    second_new_ref[...] = second_new
    vector_update = table_grad * lax.rsqrt(second_new)
    vector_sums = jnp.sum(vector_update * vector_update, axis=0, keepdims=True) / tensor
    vector_weight = jnp.sum(vector_ref[...] * vector_ref[...], axis=0, keepdims=True) / tensor
    weight_sums = [total_of(jnp.sum(weights[0][...] * weights[0][...], axis=0))]
    weight_sums += [total_of(ref[...] * ref[...]) for ref in weights[1:]]
    finish_row()
    row_counts = pick([jnp.full((1, 1), 1.0 / size, jnp.float32) for size in (width, width, width, width, long, long)], lane)
    row_new = decay_rate * state_row[...] + keep_old * (row_sum[1] * row_counts + EPS_ONE)
    row_new_ref[...] = row_new
    finish_col()
    exchange(1, 1, 1, col_sum, col_in)()
    exchange(1, 2, 2, col_sum, col_in)()
    col_new = decay_rate * state_col[...] + keep_old * (col_sum[3] / width + EPS_ONE)
    col_new_ref[...] = col_new
    ratios = []
    means = []
    for at, spans in enumerate(matrices):
        row_at = row_new[:, at : at + 1]
        ratio = 0.0
        for start, size in spans:
            value = total_ref[:, pl.ds(start, size)]
            col_at = col_new_ref[:, pl.ds(start, size)]
            ratio = ratio + total_of(value * value / (row_at * col_at))
        ratios.append(ratio)
        if at in (3, 5):
            means.append(jnp.sum(col_at, axis=1, keepdims=True) / (nz * ny * nx))
        else:
            means.append(jnp.sum(row_at, axis=0, keepdims=True) / tensor)
    small[0] = jnp.concatenate(
        [pick(ratios + means + weight_sums, lane), vector_sums, vector_weight, jnp.zeros((5, LANES), jnp.float32)], axis=0
    )
    for phase in range(4):
        exchange(2, phase, phase, small, small_in)()
    sums_ref[...] = small[4]
    for copy in sent:
        copy.wait_send()


def backward(dims, tensor, layout, large, near, weights, states):
    rows, width = near[0].shape
    own_rows = width // (dims[0] * dims[1] * dims[2])
    half_rows = own_rows // 2
    columns = layout.columns
    items = []
    for start in range(0, layout.sizes["one"], PIECE):
        for name in ("two", "one"):
            items.append((name, layout.start[name] + start, PIECE, start))
    for start in range(0, columns, PIECE):
        items.append(("out", layout.start["out"] + start, min(PIECE, columns - start), start))
    for start in range(0, 3 * columns, 3 * LANES):
        items.append(("qkv", layout.start["qkv"] + start, 3 * LANES, start))
    items.append(("vec", layout.start["vec"], LANES, 0))
    nz, ny, nx = dims
    peers = max(2, *dims, tensor) - 1
    others = max(1, tensor - 1)
    offset = layout.total
    from_here = offset - layout.start["out"]
    low, full = jnp.bfloat16, jnp.float32
    anywhere = pl.BlockSpec(memory_space=pl.ANY)
    inside = pl.BlockSpec(memory_space=pltpu.VMEM)

    def hold(*shape):
        return pltpu.VMEM(tuple(max(1, size) for size in shape), low)

    sums = offset - LANES
    count = len(items)
    return pl.pallas_call(
        functools.partial(backward_kernel, dims, tensor, tuple(items), layout),
        name="backward",
        out_shape=[
            jax.ShapeDtypeStruct((rows, width), full),
            jax.ShapeDtypeStruct((own_rows, offset), full),
            jax.ShapeDtypeStruct((1, sums), full),
            jax.ShapeDtypeStruct((own_rows, LANES), full),
            jax.ShapeDtypeStruct((own_rows, LANES), full),
            jax.ShapeDtypeStruct((8, LANES), full),
        ],
        in_specs=[anywhere] * len(large) + [inside] * (len(near) + 8),
        out_specs=[inside] * 6,
        scratch_shapes=[
            hold(2, nz, ny, nx, half_rows, offset),
            hold(others, nz, ny, nx, own_rows, from_here),
            hold(nx - 1, nz, ny, half_rows, offset),
            hold(ny - 1, nz, nx, half_rows, offset),
            hold(ny - 1, nz, half_rows, offset),
            hold(nx - 1, nz, half_rows, offset),
            hold(2, nz - 1, half_rows, offset),
            pltpu.VMEM((4, 1, sums), full),
            pltpu.VMEM((3, peers, 1, sums), full),
            pltpu.VMEM((2, own_rows, LANES), full),
            pltpu.VMEM((1, peers, own_rows, LANES), full),
            pltpu.VMEM((5, 8, LANES), full),
            pltpu.VMEM((4, peers, 8, LANES), full),
            hold(width, rows),
            hold(width, rows),
            hold(rows, width),
            hold(*dims, own_rows, width),
            hold(2, *dims, own_rows, 3 * LANES),
            hold(2, rows, 3 * LANES),
            pltpu.VMEM((2, 2, LANES, width), full),
            hold(others, *dims, own_rows, columns),
            hold(2, *dims, own_rows, 3 * LANES),
            hold(*dims, own_rows, LANES),
            pltpu.VMEM((1, 3 * width), full),
            pltpu.VMEM((LANES, width), full),
            pltpu.SemaphoreType.DMA((3, 2)),
            pltpu.SemaphoreType.DMA((count, others)),
            pltpu.SemaphoreType.DMA((count, others)),
            pltpu.SemaphoreType.DMA((count, 2)),
            pltpu.SemaphoreType.DMA((count, 2, 4, peers)),
            pltpu.SemaphoreType.DMA((count, 2, 4, peers)),
            pltpu.SemaphoreType.DMA((3, 4, peers)),
            pltpu.SemaphoreType.DMA((3, 4, peers)),
        ],
        compiler_params=pltpu.CompilerParams(
            collective_id=1, has_side_effects=True, vmem_limit_bytes=63 << 20
        ),
    )(*large, *near, *weights, *states)


def update_kernel(layout, width, long, *refs):
    total_ref, col_ref, row_ref, second_ref, sums_ref, vector_ref = refs[:6]
    weights = refs[6:10]
    own_qkv, own_out, own_one, own_two, own_table = refs[10:15]
    new_qkv, new_out, new_one, new_two, new_vectors, second_new = refs[15:21]
    qkv_row, qkv_col, out_row, out_col, one_row, one_col, two_row, two_col = refs[21:]
    lane = lax.broadcasted_iota(jnp.int32, (1, LANES), 1)

    def at(index):
        return sums_ref[0:1, index : index + 1]

    lengths = (width, width, width, width, width, long)
    means = [at(6 + m) / lengths[m] for m in range(6)]
    squares = [means[m] * at(m) for m in range(6)]
    squares = [squares[0] + squares[1] + squares[2], *squares[3:]]
    entries = (3 * width * width, width * width, width * long, width * long)
    step_size = []
    for m in range(4):
        damping = 1.0 / jnp.maximum(1.0, jnp.sqrt(squares[m] / entries[m] + 1e-06) / CLIP_LEVEL)
        step_size.append(LEARN_RATE * jnp.sqrt(at(12 + m) / entries[m] + 1e-06) * damping)
    spread = [(m, place, *span) for m, spans in enumerate(layout.matrices()) for place, span in enumerate(spans)]
    for m, place, start, size in spread:
        grad = total_ref[:, pl.ds(start, size)]
        col = col_ref[:, pl.ds(start, size)]
        step = step_size[max(0, m - 2)] * grad * lax.rsqrt(row_ref[:, m : m + 1] * col / means[m])
        if m < 3:
            part = slice(place * LANES, (place + 1) * LANES)
            own_qkv[m, :, part] = grad
            new_qkv[m, :, part] = weights[0][m, :, part] - step
            qkv_col[m : m + 1, part] = col
        elif m == 4:
            own_one[...] = grad
            new_one[...] = weights[2][...] - step
            one_col[...] = col
        else:
            own, new, weight = (own_out, new_out, weights[1]) if m == 3 else (own_two, new_two, weights[3])
            own[...] = grad.T
            new[...] = weight[...] - step.T
            (out_row if m == 3 else two_row)[...] = col
    row_flat = row_ref[...].T
    qkv_row[...] = row_flat[0:3]
    out_col[...] = row_flat[3:4]
    one_row[...] = row_flat[4:5]
    two_col[...] = row_flat[5:6]

    wide = (lane >= 7) & (lane < VEC - 1)
    counts = jnp.where(wide, float(long), float(width))

    def grouped(values):
        inside = jnp.sum(jnp.where(wide, values, 0.0), axis=1, keepdims=True)
        return jnp.where(wide, inside, values)

    table_grad = total_ref[:, pl.ds(layout.start["vec"], LANES)]
    update = table_grad * lax.rsqrt(second_ref[...])
    norm = jnp.sqrt(grouped(sums_ref[1:2, :]) / counts + 1e-06)
    size = jnp.sqrt(grouped(sums_ref[2:3, :]) / counts + 1e-06)
    fresh = vector_ref[...] - LEARN_RATE * size / jnp.maximum(1.0, norm / CLIP_LEVEL) * update
    own_table[...] = table_grad.T[:VEC]
    new_vectors[...] = fresh.T[:VEC]
    second_new[...] = second_ref[...].T[:VEC]


def update_weights(layout, width, long, columns, hidden, rows, values, vectors, weights):
    full = jnp.float32
    shapes = [
        (3, rows, columns),
        (columns, rows),
        (rows, hidden),
        (hidden, rows),
        (VEC, rows),
        (3, rows, columns),
        (columns, rows),
        (rows, hidden),
        (hidden, rows),
        (VEC, rows),
        (VEC, rows),
        (3, rows),
        (3, columns),
        (1, columns),
        (1, rows),
        (1, rows),
        (1, hidden),
        (1, hidden),
        (1, rows),
    ]
    return pl.pallas_call(
        functools.partial(update_kernel, layout, width, long),
        name="update_weights",
        out_shape=[jax.ShapeDtypeStruct(shape, full) for shape in shapes],
        compiler_params=pltpu.CompilerParams(vmem_limit_bytes=48 << 20),
    )(*values, vectors, *weights)


def paired(array, axis):
    moved = jnp.moveaxis(array, axis, -2)
    lead = moved.shape[:-2]
    blocks = moved.reshape(*lead, 3, moved.shape[-1] // LANES, LANES)
    return jnp.swapaxes(blocks, -3, -2).reshape(*lead, 3 * moved.shape[-1])


def on_device(
    inputs,
    cotangent,
    token_mask,
    w_qkv,
    w_out,
    w_fc1,
    w_fc2,
    vectors,
    qkv_row,
    qkv_col,
    out_row,
    out_col,
    fc1_row,
    fc1_col,
    fc2_row,
    fc2_col,
    vec_second,
):
    tensor_count = lax.axis_size("tensor")
    dims = grid_of(lax.axis_size("fsdp"))
    tensor_rank = lax.axis_index("tensor")
    rows_here, width = inputs.shape
    own_rows, columns = w_qkv.shape[1:]
    hidden = w_fc1.shape[1]
    low = jnp.bfloat16

    keep = lax.dynamic_slice_in_dim(token_mask, tensor_rank, 1, 0)
    keep_rows = keep.reshape(rows_here, 1).astype(jnp.float32)
    bias = jnp.where(keep > 0, 0.0, -1e30).astype(jnp.float32)

    pack = jnp.concatenate(
        [
            paired(w_qkv, 0),
            jnp.pad(vectors.T, ((0, 0), (0, LANES - VEC))),
            w_out.T,
            w_fc1,
            w_fc2.T,
        ],
        axis=1,
    ).astype(low)
    (
        weight_qkv,
        _,
        weight_out,
        *_,
        block_out,
        grad_middle,
        back_one,
        projected,
        mixed_rows,
        low_one,
        grad_one,
        grad_two,
        table,
        vec_sums,
        pre_sums,
    ) = forward(dims, tensor_count, pack, inputs, cotangent, keep_rows, bias, columns, hidden)
    layout = Layout(columns, hidden, ("two", "one", "out", "qkv", "vec"))
    col_state = {"qkv": paired(qkv_col, 0), "out": out_row, "one": fc1_col, "two": fc2_row}
    state_col = jnp.concatenate([col_state[name] for name in layout.order[:4]])[None]
    state_row = jnp.concatenate([qkv_row, out_col[None], fc1_row[None], fc2_col[None]], axis=0)
    state_row = jnp.pad(state_row.T, ((0, 0), (0, LANES - 6)))
    second = jnp.pad(vec_second.T, ((0, 0), (0, LANES - VEC)), constant_values=1.0)
    vectors_turned = jnp.pad(vectors.T, ((0, 0), (0, LANES - VEC)))
    weights = (w_qkv, w_out, w_fc1, w_fc2)
    input_grad, *values = backward(
        dims,
        tensor_count,
        layout,
        (grad_two, grad_one, weight_qkv, weight_out, projected, inputs, grad_middle),
        (mixed_rows, low_one, back_one, bias.reshape(rows_here, 1), table, vec_sums, pre_sums),
        weights,
        (state_col, state_row, second, vectors_turned),
    )
    outs = update_weights(
        layout, width, FF, columns, hidden, own_rows, values, vectors_turned, weights
    )
    outs = [out.reshape(-1) if out.shape[0] == 1 else out for out in outs]
    return (block_out, input_grad, *outs[:10], *outs[11:], outs[10])


def solution(mesh):
    in_specs = (
        P(("fsdp", "tensor"), None),
        P(("fsdp", "tensor"), None),
        P("fsdp", None),
        P(None, "fsdp", "tensor"),
        P("tensor", "fsdp"),
        P("fsdp", "tensor"),
        P("tensor", "fsdp"),
        P(None, "fsdp"),
        P(None, "fsdp"),
        P(None, "tensor"),
        P("tensor"),
        P("fsdp"),
        P("fsdp"),
        P("tensor"),
        P("tensor"),
        P("fsdp"),
        P(None, "fsdp"),
    )
    out_specs = (
        P(("fsdp", "tensor"), None),
        P(("fsdp", "tensor"), None),
        P(None, "fsdp", "tensor"),
        P("tensor", "fsdp"),
        P("fsdp", "tensor"),
        P("tensor", "fsdp"),
        P(None, "fsdp"),
        P(None, "fsdp", "tensor"),
        P("tensor", "fsdp"),
        P("fsdp", "tensor"),
        P("tensor", "fsdp"),
        P(None, "fsdp"),
        P(None, "fsdp"),
        P(None, "tensor"),
        P("tensor"),
        P("fsdp"),
        P("fsdp"),
        P("tensor"),
        P("tensor"),
        P("fsdp"),
        P(None, "fsdp"),
    )
    return jax.shard_map(
        on_device, mesh=mesh, in_specs=in_specs, out_specs=out_specs, check_vma=False
    )
```

```python
import functools

import jax
import jax.numpy as jnp
from jax import lax
from jax.experimental import pallas as pl
from jax.experimental.pallas import tpu as pltpu
from jax.sharding import PartitionSpec as P

HEAD_DIM = 64
FF = 4096
STEP = 20
VEC = 12
LANES = 128

EPS_NORM = 1e-05
EPS_ONE = 1e-30
CLIP_LEVEL = 1.0
LEARN_RATE = 0.5
MESH = pl.DeviceIdType.MESH
LOG2E = 1.4426950408889634
CONTRACT_LAST = (((1,), (1,)), ((), ()))


def grid_of(count):
    return {16: (4, 2, 2), 32: (2, 4, 4)}.get(count, (count, 1, 1))


class Place:
    def __init__(self, dims, tensor):
        self.dims = dims
        self.tensor = tensor
        fsdp = lax.axis_index("fsdp")
        _, ny, nx = dims
        self.at = (fsdp // (ny * nx), (fsdp // nx) % ny, fsdp % nx)
        self.rank = lax.axis_index("tensor")

    def moved(self, axis, step):
        place = list(self.at) + [self.rank]
        size = (*self.dims, self.tensor)[axis]
        place[axis] = lax.rem(place[axis] + step + size, size)
        return tuple(place)

    def device(self, place):
        z, y, x, rank = place
        return {"fsdp": (z * self.dims[1] + y) * self.dims[2] + x, "tensor": rank}

    def size(self, axis):
        return (*self.dims, self.tensor)[axis]

    def barrier(self):
        sem = pltpu.get_barrier_semaphore()
        count = 0
        for axis in range(4):
            for step in range(1, self.size(axis)):
                pl.semaphore_signal(
                    sem,
                    inc=1,
                    device_id=self.device(self.moved(axis, step)),
                    device_id_type=MESH,
                )
                count += 1
        if count:
            pl.semaphore_wait(sem, count)


def axis_order(half):
    return (0, 1, 2) if half == 0 else (0, 2, 1)


def norm_rows(values):
    average = jnp.mean(values, axis=1, keepdims=True)
    center = values - average
    inverse = lax.rsqrt(jnp.mean(center * center, axis=1, keepdims=True) + EPS_NORM)
    return center * inverse, inverse


def dot(left, right, dims=(((1,), (0,)), ((), ()))):
    return lax.dot_general(left, right, dims, preferred_element_type=jnp.float32)


def turn(source, target):
    for start in range(0, source.shape[1], LANES):
        target[pl.ds(start, LANES), :] = source[:, pl.ds(start, LANES)].T


def attend_pair(heads, bias):
    mixed = []
    for head in range(2):
        query, key, value = (
            heads[:, kind * LANES + head * HEAD_DIM : kind * LANES + (head + 1) * HEAD_DIM] for kind in range(3)
        )
        scores = dot(query, key, CONTRACT_LAST) * (HEAD_DIM ** (-0.5) * LOG2E) + bias
        raised = jnp.exp2(scores - jnp.max(scores, axis=1, keepdims=True))
        summed = jnp.sum(raised, axis=1, keepdims=True)
        attention = (raised * (1.0 / summed)).astype(jnp.bfloat16)
        mixed.append(dot(attention, value).astype(jnp.bfloat16))
    return jnp.concatenate(mixed, axis=1)


class Steps:
    def __init__(self):
        self.steps = {}

    def add(self, name, run, time, rank, after=(), waits=(), starts=()):
        self.steps[name] = (run, time, rank, tuple(after), tuple(waits), tuple(starts))

    def arrange(self):
        now, free, arrival, done, order = 0.0, {}, {}, set(), []
        left = list(self.steps)
        while left:
            best, soonest = None, None
            for name in left:
                _, time, rank, after, waits, _ = self.steps[name]
                if any(other not in done for other in after) or any(wait not in arrival for wait in waits):
                    continue
                ready = max([arrival[wait] for wait in waits], default=0.0)
                if ready <= now:
                    if best is None or rank < self.steps[best][2]:
                        best = name
                elif soonest is None or ready < soonest:
                    soonest = ready
            if best is None:
                now = soonest
                continue
            _, time, _, _, _, starts = self.steps[best]
            now += time
            for transfer, link, length in starts:
                begin = max(now, free.get(link, 0.0))
                free[link] = begin + length
                arrival[transfer] = begin + length + LATENCY
            done.add(best)
            left.remove(best)
            order.append(best)
        return order, now

    def run(self):
        for name in self.arrange()[0]:
            self.steps[name][0]()


class Gather:
    def __init__(self, here, pack_ref, outs, parts, local_sem, send_sem, recv_sem):
        self.here = here
        self.pack = pack_ref
        self.outs = outs
        self.half_rows = pack_ref.shape[0] // 2
        self.parts = parts
        self.sems = (local_sem, send_sem, recv_sem)
        self.own = (*here.at, here.rank)
        self.sent = []
        self.local = {}

    def rows(self, half):
        return pl.ds(half * self.half_rows, self.half_rows)

    def region(self, item, half, place, free):
        out, _, start, size, total, shared = self.parts[item]
        base = 0 if shared else place[3] * total
        column = pl.ds(pl.multiple_of(base + start, LANES), size)
        index = tuple(slice(None) if a in free else place[a] for a in range(3))
        return self.outs[out].at[(*index, self.rows(half), column)]

    def shard(self, item, half):
        _, offset, _, size, _, _ = self.parts[item]
        return self.pack.at[self.rows(half), pl.ds(offset, size)]

    def axes(self, item, half):
        order = axis_order(half)
        return order if self.parts[item][5] else (*order, 3)

    def copies(self, item, half, phase, landing):
        here = self.here
        order = self.axes(item, half)
        axis, free = order[phase], order[:phase]
        found = []
        for step in range(1, here.size(axis)):
            own = self.region(item, half, self.own, free)
            if landing:
                src = dst = self.region(item, half, here.moved(axis, -step), free)
            else:
                src, dst = (self.shard(item, half) if phase == 0 else own), own
            found.append(
                pltpu.make_async_remote_copy(
                    src_ref=src,
                    dst_ref=dst,
                    send_sem=self.sems[1].at[item, half, phase, step - 1],
                    recv_sem=self.sems[2].at[item, half, phase, step - 1],
                    device_id=here.device(here.moved(axis, step)),
                    device_id_type=MESH,
                )
            )
        return found

    def start(self):
        for item in range(len(self.parts)):
            for half in range(2):
                copy = pltpu.make_async_copy(
                    self.shard(item, half), self.region(item, half, self.own, ()), self.sems[0].at[item, half]
                )
                copy.start()
                self.local[item, half] = copy

    def advance(self, item, phase):
        for half in range(2):
            order = self.axes(item, half)
            if 0 < phase <= len(order):
                for copy in self.copies(item, half, phase - 1, True):
                    copy.wait_recv()
            if phase == 1:
                self.local[item, half].wait()
            if phase < len(order):
                for copy in self.copies(item, half, phase, False):
                    copy.start()
                    self.sent.append(copy)

    def finish(self):
        for copy in self.sent:
            copy.wait_send()


BLOCK = 512
PIECE = 256
DEPTH = 3
LATENCY = 1.5
UNIT = 16.0
CORE_UNIT = 40.0
PUMP = 0.4


def forward_kernel(dims, tensor, parts, tasks, per_rank, hidden_total, pack_ref, input_ref, top_ref, keep_ref, bias_ref, *refs):
    outs, land = refs[:5], refs[5:7]
    weight_qkv, weight_vec, weight_out, weight_one, weight_two = outs
    (
        block_out,
        grad_middle,
        back_one,
        projected,
        mixed,
        low_one,
        grad_one,
        grad_two,
        table,
        vec_sums,
        pre_sums,
    ) = refs[7:18]
    (
        vec_buf,
        qkv_buf,
        head_stage,
        out_buf,
        one_buf,
        two_buf,
        low_two,
        low_two_turned,
        back_two,
        back_two_turned,
        grad_low_two,
        hidden_bias,
        head_bias,
        one_stage,
        two_stage,
        one_keep,
        two_keep,
        other,
        load_sem,
        store_sem,
        keep_sem,
        head_sem,
        land_sem,
        local_sem,
        send_sem,
        recv_sem,
    ) = refs[18:]
    here = Place(dims, tensor)
    gather = Gather(here, pack_ref, outs, parts, local_sem, send_sem, recv_sem)
    rows, width = input_ref.shape
    low = jnp.bfloat16
    step_rows = LANES

    def row_steps(body, carry):
        return lax.fori_loop(
            0, rows // step_rows, lambda at, c: body(pl.ds(pl.multiple_of(at * step_rows, step_rows), step_rows), c), carry
        )

    def load(source, buffer, sem):
        return pltpu.make_async_copy(source, buffer, sem)

    def first_norm():
        copy = load(weight_vec, vec_buf, load_sem.at[7])
        copy.start()
        copy.wait()
        whole = vec_buf[...].reshape(width, LANES).astype(jnp.float32).T
        table[...] = whole[:16]
        for at in range(VEC - 8):
            hidden_bias[:, pl.ds(at * width, width)] = whole[7 + at : 8 + at]
        for pair in range(width // LANES):
            for kind, row in ((0, 2), (2, 3)):
                head_bias[:, pl.ds((pair * 3 + kind) * LANES, LANES)] = whole[
                    row : row + 1, pair * LANES : (pair + 1) * LANES
                ]
            head_bias[:, pl.ds((pair * 3 + 1) * LANES, LANES)] = jnp.zeros((1, LANES), jnp.float32)

        def body(part, carry):
            normed, _ = norm_rows(input_ref[part, :])
            low_one[part, :] = (normed * table[0:1, :] + table[1:2, :]).astype(low)
            back_two[part, :] = (top_ref[part, :].astype(jnp.float32) * keep_ref[part, :]).astype(low)
            return carry

        row_steps(body, 0)
        turn(back_two, back_two_turned)

    def head_store(pair, slot):
        column = pl.ds(pl.multiple_of(pair * 3 * LANES, LANES), 3 * LANES)
        return pltpu.make_async_copy(head_stage.at[slot], projected.at[:, column], head_sem.at[slot])

    def pair_of(at):
        turn_at, place = divmod(at, tensor)
        return lax.rem(here.rank + place, tensor) * per_rank + turn_at

    def head_load(at):
        column = pl.multiple_of(pair_of(at) * 3 * LANES, LANES)
        return load(
            weight_qkv.at[:, :, :, :, pl.ds(column, 3 * LANES)], qkv_buf.at[at % 2], load_sem.at[at % 2]
        )

    def heads(at):
        head_load(at).wait()
        pair = pair_of(at)
        slot = at % 2
        column = pl.ds(pl.multiple_of(pair * 3 * LANES, LANES), 3 * LANES)
        weight = qkv_buf[slot].reshape(width, 3 * LANES)
        value = (dot(low_one[...], weight) + head_bias[:, column]).astype(low)
        if at > 1:
            head_store(pair, slot).wait()
        head_stage[slot] = value
        head_store(pair, slot).start()
        mixed[:, pl.ds(pl.multiple_of(pair * LANES, LANES), LANES)] = attend_pair(value, bias_ref[...])

    def out_load():
        return load(weight_out, out_buf, load_sem.at[2])

    def second_norm():
        out_load().wait()
        term = dot(mixed[...], out_buf[...].reshape(width, width), CONTRACT_LAST)
        grad_middle[...] = term

        def body(part, carry):
            middle = input_ref[part, :] + (grad_middle[part, :] + table[4:5, :]) * keep_ref[part, :]
            grad_middle[part, :] = middle
            normed, _ = norm_rows(middle)
            low_two[part, :] = (normed * table[5:6, :] + table[6:7, :]).astype(low)
            return carry

        row_steps(body, 0)
        turn(low_two, low_two_turned)

    stages = (one_stage, two_stage)
    keeps = (one_keep, two_keep)

    def hand_over(at):
        chunk, place = divmod(at, tensor)
        target = (*here.at, lax.rem(here.rank + place + 1, tensor))
        return [
            pltpu.make_async_remote_copy(
                src_ref=stages[which].at[at % 2],
                dst_ref=land[which].at[place, chunk],
                send_sem=store_sem.at[which, at % 2],
                recv_sem=land_sem.at[which, place, chunk],
                device_id=here.device(target),
                device_id_type=MESH,
            )
            for which in range(2)
        ]

    def keep_store(chunk):
        return [
            pltpu.make_async_copy(
                keeps[which].at[chunk % 2],
                out.at[:, :, :, :, pl.ds(chunk * BLOCK, BLOCK)],
                keep_sem.at[which, chunk % 2],
            )
            for which, out in enumerate((grad_one, grad_two))
        ]

    def hidden_column(at):
        chunk, place = divmod(at, tensor)
        base = lax.rem(here.rank + place + 1, tensor) * hidden_total + chunk * BLOCK
        return pl.ds(pl.multiple_of(base, LANES), BLOCK)

    def hidden_load(at):
        column = hidden_column(at)
        return [
            load(source.at[:, :, :, :, column], buffer.at[at % 2], load_sem.at[3 + 2 * which + at % 2])
            for which, (source, buffer) in enumerate(((weight_one, one_buf), (weight_two, two_buf)))
        ]

    staged = {}

    def hidden(at):
        chunk, place = divmod(at, tensor)
        column = hidden_column(at)
        for copy in hidden_load(at):
            copy.wait()
        one = one_buf[at % 2].reshape(width, BLOCK)
        two = two_buf[at % 2].reshape(width, BLOCK)
        preact = dot(low_two[...], one) + hidden_bias[:, column]
        gate = jax.nn.sigmoid(1.702 * preact)
        active = (preact * gate).astype(low)
        derivative = gate + 1.702 * preact * gate * (1.0 - gate)
        grad_pre = (dot(back_two[...], two) * derivative).astype(low)
        pre_sums[:, column] = jnp.sum(grad_pre.astype(jnp.float32), axis=0, keepdims=True)
        if at == 0:
            block_out[...] = dot(active, two, CONTRACT_LAST)
            grad_low_two[...] = dot(grad_pre, one, CONTRACT_LAST)
        else:
            block_out[...] += dot(active, two, CONTRACT_LAST)
            grad_low_two[...] += dot(grad_pre, one, CONTRACT_LAST)
        mine = place == tensor - 1
        if mine:
            targets = [ref.at[chunk % 2] for ref in keeps]
            if chunk > 1:
                for copy in keep_store(chunk):
                    copy.wait()
        else:
            targets = [ref.at[at % 2] for ref in stages]
            for copy in staged.pop(at % 2, ()):
                copy.wait_send()
        for target, left, right in (
            (targets[0], low_two_turned, grad_pre),
            (targets[1], back_two_turned, active),
        ):
            target[...] = dot(left[...], right).astype(low).reshape(*target.shape)
        if not mine:
            staged[at % 2] = hand_over(at)
            for copy in staged[at % 2]:
                copy.start()

    def combine(chunk):
        for place in range(tensor - 1):
            for which, copy in enumerate(hand_over(chunk * tensor + place)):
                copy.wait_recv()
                fetch = load(land[which].at[place, chunk], other, load_sem.at[7])
                fetch.start()
                fetch.wait()
                keeps[which][chunk % 2] = keeps[which][chunk % 2] + other[...]
        for copy in keep_store(chunk):
            copy.start()

    def last_norm():
        def body(part, sums):
            middle = grad_middle[part, :]
            keep = keep_ref[part, :]
            top = top_ref[part, :].astype(jnp.float32)
            block_out[part, :] = middle + (block_out[part, :] + table[VEC - 1 : VEC, :]) * keep
            normed, inverse = norm_rows(middle)
            grad_low = grad_low_two[part, :]
            scaled = grad_low * table[5:6, :]
            first = jnp.mean(scaled, axis=1, keepdims=True)
            second = jnp.mean(scaled * normed, axis=1, keepdims=True)
            grad = top + inverse * (scaled - first - normed * second)
            grad_middle[part, :] = grad
            masked = grad * keep
            back_one[part, :] = masked.astype(low)
            terms = (masked, grad_low * normed, grad_low, top * keep)
            return tuple(old + jnp.sum(term, axis=0, keepdims=True) for old, term in zip(sums, terms))

        zero = jnp.zeros((1, width), jnp.float32)
        for at, value in enumerate(row_steps(body, (zero,) * 4)):
            vec_sums[at : at + 1, :] = value

    here.barrier()
    gather.start()
    steps = Steps()
    whole = sum(part[3] for part in parts)
    nz, ny, nx = dims

    def lengths(item, phase):
        share = parts[item][3] / whole
        return (
            (share * UNIT * nz, "z"),
            (share * UNIT * nz / 2, "xy"),
            (share * UNIT * nz, "xy"),
            (share * CORE_UNIT, "core"),
        )[phase]

    for item, part in enumerate(parts):
        phases = 3 if part[5] else 4
        for phase in range(phases + 1):
            after = [("copy", item, phase - 1)] if phase else []
            if phase == 0 and item >= DEPTH:
                after = [("copy", item - DEPTH, 1)]
            length, link = lengths(item, min(phase, 3))
            steps.add(
                ("copy", item, phase),
                functools.partial(gather.advance, item, phase),
                PUMP,
                0.5 if phase == 0 else 0.0,
                after,
                [(item, phase - 1)] if phase else [],
                [((item, phase), link, length)] if phase < phases else [],
            )

    def landed(items):
        return [("copy", item, 3 if parts[item][5] else 4) for item in items]

    def start(copies):
        for copy in copies:
            copy.start()

    previous = None
    head_count, block_count = per_rank * tensor, FF // BLOCK
    for name, at, items in tasks:
        after = landed(items) + ([previous] if previous else [])
        begin, run, time = {
            "norm": (None, first_norm, 5.0),
            "heads": (lambda at=at: head_load(at).start(), lambda at=at: heads(at), 3.0),
            "out": (lambda: out_load().start(), second_norm, 5.0),
            "hidden": (lambda at=at: start(hidden_load(at)), lambda at=at: hidden(at), 5.5),
        }[name]
        if begin is not None:
            first = landed(items)
            if at > 1:
                first.append((name, at - 2))
            steps.add(("load", name, at), begin, 0.1, 0.2, first)
            after.append(("load", name, at))
        mine = name == "hidden" and at % tensor == tensor - 1
        chunk = at // tensor
        if mine and chunk > 1:
            after.append(("combine", chunk - 2))
        starts = []
        if name == "hidden" and not mine:
            starts = [(("hand", at), "core", CORE_UNIT / len(parts))]
        steps.add((name, at), run, time, 1.0, after, (), starts)
        if mine:
            waits = [("hand", chunk * tensor + place) for place in range(tensor - 1)]
            steps.add(
                ("combine", chunk), functools.partial(combine, chunk), 2.0, 0.8, [(name, at)], waits
            )
        previous = (name, at)
    steps.add(("last", 0), last_norm, 4.0, 0.9, [previous])
    steps.run()
    for slot in range(min(2, head_count)):
        head_store(0, slot).wait()
    for chunk in range(min(2, block_count // tensor)):
        for copy in keep_store(chunk):
            copy.wait()
    for copies in staged.values():
        for copy in copies:
            copy.wait_send()
    gather.finish()


def forward(dims, tensor, pack, inputs, cotangent, keep_rows, bias, columns, hidden):
    own_rows = pack.shape[0]
    rows, width = inputs.shape
    low, full = jnp.bfloat16, jnp.float32
    widths = (3 * columns, LANES, columns, hidden, hidden)
    offsets = [sum(widths[:at]) for at in range(5)]
    per_rank = columns // LANES
    parts = [(1, offsets[1], 0, LANES, LANES, True)]
    tasks = [("norm", 0, (0,))]
    for at in range(per_rank):
        size = 3 * LANES
        parts.append((0, offsets[0] + at * size, at * size, size, widths[0], False))
        tasks += [("heads", at * tensor + place, (len(parts) - 1,)) for place in range(tensor)]
    needed = []
    for start in range(0, columns, PIECE):
        size = min(PIECE, columns - start)
        needed.append(len(parts))
        parts.append((2, offsets[2] + start, start, size, columns, False))
    tasks.append(("out", 0, tuple(needed)))
    for block in range(hidden // BLOCK):
        needed = []
        for start in range(block * BLOCK, (block + 1) * BLOCK, PIECE):
            for which in (3, 4):
                needed.append(len(parts))
                parts.append((which, offsets[which] + start, start, PIECE, hidden, False))
        tasks += [("hidden", block * tensor + place, tuple(needed)) for place in range(tensor)]
    count = len(parts)
    peers = max(2, *dims, tensor) - 1
    anywhere = pl.BlockSpec(memory_space=pl.ANY)
    inside = pl.BlockSpec(memory_space=pltpu.VMEM)

    def shape(kind, *size):
        return jax.ShapeDtypeStruct(size, kind)

    return pl.pallas_call(
        functools.partial(forward_kernel, dims, tensor, tuple(parts), tuple(tasks), per_rank, hidden),
        name="forward",
        out_shape=[
            *(shape(low, *dims, own_rows, w * (1 if at == 1 else tensor)) for at, w in enumerate(widths)),
            *[shape(low, max(1, tensor - 1), hidden // BLOCK, *dims, own_rows, BLOCK)] * 2,
            shape(full, rows, width),
            shape(full, rows, width),
            shape(low, rows, width),
            shape(low, rows, 3 * width),
            shape(low, rows, width),
            shape(low, rows, width),
            *[shape(low, *dims, own_rows, hidden)] * 2,
            shape(full, 16, width),
            shape(full, 8, width),
            shape(full, 1, hidden * tensor),
        ],
        in_specs=[anywhere] + [inside] * 4,
        out_specs=[anywhere] * 7 + [inside] * 3 + [anywhere] + [inside] * 2 + [anywhere] * 2 + [inside] * 3,
        scratch_shapes=[
            pltpu.VMEM((*dims, own_rows, LANES), low),
            pltpu.VMEM((2, *dims, own_rows, 3 * LANES), low),
            pltpu.VMEM((2, rows, 3 * LANES), low),
            pltpu.VMEM((*dims, own_rows, width), low),
            pltpu.VMEM((2, *dims, own_rows, BLOCK), low),
            pltpu.VMEM((2, *dims, own_rows, BLOCK), low),
            pltpu.VMEM((rows, width), low),
            pltpu.VMEM((width, rows), low),
            pltpu.VMEM((rows, width), low),
            pltpu.VMEM((width, rows), low),
            pltpu.VMEM((rows, width), full),
            pltpu.VMEM((1, hidden * tensor), full),
            pltpu.VMEM((1, 3 * width), full),
            pltpu.VMEM((2, *dims, own_rows, BLOCK), low),
            pltpu.VMEM((2, *dims, own_rows, BLOCK), low),
            pltpu.VMEM((2, *dims, own_rows, BLOCK), low),
            pltpu.VMEM((2, *dims, own_rows, BLOCK), low),
            pltpu.VMEM((*dims, own_rows, BLOCK), low),
            pltpu.SemaphoreType.DMA((8,)),
            pltpu.SemaphoreType.DMA((2, 2)),
            pltpu.SemaphoreType.DMA((2, 2)),
            pltpu.SemaphoreType.DMA((2,)),
            pltpu.SemaphoreType.DMA((2, max(1, tensor - 1), hidden // BLOCK)),
            pltpu.SemaphoreType.DMA((count, 2)),
            pltpu.SemaphoreType.DMA((count, 2, 4, peers)),
            pltpu.SemaphoreType.DMA((count, 2, 4, peers)),
        ],
        compiler_params=pltpu.CompilerParams(
            collective_id=0, has_side_effects=True, vmem_limit_bytes=62 << 20
        ),
    )(pack, inputs, cotangent, keep_rows, bias)


class Layout:
    def __init__(self, columns, hidden, order):
        sizes = {"qkv": 3 * columns, "out": columns, "one": hidden, "two": hidden, "vec": LANES}
        self.order = order
        self.sizes = sizes
        self.start = {}
        at = 0
        for name in order:
            self.start[name] = at
            at += sizes[name]
        self.total = at
        self.columns = columns

    def span(self, name):
        return (self.start[name], self.sizes[name])

    def matrices(self):
        base = self.start["qkv"]
        pairs = range(self.columns // LANES)
        spans = [[(base + (pair * 3 + at) * LANES, LANES) for pair in pairs] for at in range(3)]
        return spans + [[self.span(name)] for name in ("out", "one", "two")]


def pick(values, lane):
    row = jnp.zeros((1, LANES), jnp.float32)
    for at, value in enumerate(values):
        row = jnp.where(lane == at, value, row)
    return row


def total_of(values):
    return jnp.sum(jnp.sum(values, axis=1, keepdims=True), axis=0, keepdims=True)


def attend_pair_back(heads, bias, grads):
    parts = ([], [], [])
    for head in range(2):
        query, key, value = (
            heads[:, kind * LANES + head * HEAD_DIM : kind * LANES + (head + 1) * HEAD_DIM] for kind in range(3)
        )
        grad = grads[:, head * HEAD_DIM : (head + 1) * HEAD_DIM]
        scores = dot(key, query, CONTRACT_LAST) * (HEAD_DIM ** (-0.5) * LOG2E) + bias
        raised = jnp.exp2(scores - jnp.max(scores, axis=0, keepdims=True))
        attention = raised * (1.0 / jnp.sum(raised, axis=0, keepdims=True))
        grad_value = dot(attention.astype(jnp.bfloat16), grad)
        grad_attention = dot(value, grad, CONTRACT_LAST)
        weighted = jnp.sum(attention * grad_attention, axis=0, keepdims=True)
        grad_scores = (attention * (grad_attention - weighted) * HEAD_DIM ** (-0.5)).astype(jnp.bfloat16)
        grad_key = dot(grad_scores, query)
        grad_query = dot(key.T, grad_scores).T
        for kind, part in enumerate((grad_query, grad_key, grad_value)):
            parts[kind].append(part.astype(jnp.bfloat16))
    return jnp.concatenate([piece for kind in parts for piece in kind], axis=1)


def backward_kernel(dims, tensor, items, layout, *refs):
    (
        sum_two,
        sum_one,
        weight_qkv,
        weight_out,
        projected,
        input_ref,
        middle_ref,
        mixed,
        low_one,
        back_one,
        bias_ref,
        table,
        vec_sums,
        pre_sums,
    ) = refs[:14]
    weights = refs[14:18]
    state_col, state_row, second_ref, vector_ref = refs[18:22]
    input_grad, total_ref, col_new_ref, row_new_ref, second_new_ref, sums_ref = refs[22:28]
    (
        own,
        from_core,
        one_x,
        one_y,
        two_y,
        two_x,
        from_z,
        col_sum,
        col_in,
        row_sum,
        row_in,
        small,
        small_in,
        low_turned,
        back_turned,
        grad_mixed,
        out_buf,
        qkv_buf,
        head_buf,
        row_buf,
        out_stage,
        qkv_stage,
        vec_stage,
        head_sums,
        table_grad_ref,
        load_sem,
        stage_sem,
        core_sem,
        local_sem,
        send_sem,
        recv_sem,
        sum_send,
        sum_recv,
    ) = refs[28:]
    here = Place(dims, tensor)
    nz, ny, nx = dims
    low = jnp.bfloat16
    half_rows = own.shape[4]
    own_rows = 2 * half_rows
    rows, width = input_grad.shape
    own_place = (*here.at, here.rank)
    count = len(items)
    core_start = layout.start["out"]

    def columns(item):
        _, start, size, _ = items[item]
        return pl.ds(start, size)

    def core_columns(item):
        _, start, size, _ = items[item]
        return pl.ds(start - core_start, size)

    def order(half):
        return (3, 2, 1, 0) if half == 0 else (3, 1, 2, 0)

    def part(item, half, place, fixed):
        index = tuple(place[a] if a in fixed else slice(None) for a in range(3))
        return own.at[(half, *index, slice(None), columns(item))]

    def slot(item, half, phase, step):
        if phase == 3:
            return from_z.at[half, step - 1, :, columns(item)]
        if phase == 1:
            buffer = one_x if half == 0 else one_y
            return buffer.at[step - 1, :, :, :, columns(item)]
        buffer = two_y if half == 0 else two_x
        return buffer.at[step - 1, :, :, columns(item)]

    def copies(item, half, phase):
        axes = order(half)
        axis, fixed = axes[phase], axes[1 : phase + 1]
        found = []
        for step in range(1, here.size(axis)):
            target = here.moved(axis, step)
            found.append(
                pltpu.make_async_remote_copy(
                    src_ref=part(item, half, target, fixed),
                    dst_ref=slot(item, half, phase, step),
                    send_sem=send_sem.at[item, half, phase, step - 1],
                    recv_sem=recv_sem.at[item, half, phase, step - 1],
                    device_id=here.device(target),
                    device_id_type=MESH,
                )
            )
        return found

    def add_in(item, half, phase):
        axes = order(half)
        axis, fixed = axes[phase], axes[1 : phase + 1]
        column = columns(item)
        steps = here.size(axis) - 1
        if phase == 3:
            value = own[(half, *here.at, slice(None), column)].astype(jnp.float32)
            for step in range(steps):
                value = value + from_z[half, step, :, column].astype(jnp.float32)
            total_ref[pl.ds(half * half_rows, half_rows), column] = value
            return
        if steps == 0:
            return
        free = [a for a in range(3) if a not in fixed]
        sizes = [dims[a] for a in free]
        loops = 1
        for size in sizes:
            loops *= size

        def body(at, carry):
            place = list(here.at)
            inner = []
            rest = at
            for axis_at, size in reversed(list(zip(free, sizes))):
                place[axis_at] = rest % size
                inner.insert(0, rest % size)
                rest = rest // size
            where = (half, *place, slice(None), column)
            value = own[where]
            for step in range(steps):
                if phase == 0:
                    near = (step, *inner, pl.ds(half * half_rows, half_rows), core_columns(item))
                    piece = from_core[near]
                elif phase == 1:
                    piece = (one_x if half == 0 else one_y)[(step, *inner, slice(None), column)]
                else:
                    piece = (two_y if half == 0 else two_x)[(step, *inner, slice(None), column)]
                value = value + piece
            own[where] = value
            return carry

        lax.fori_loop(0, loops, body, 0)

    sent = []

    def exchange(kind, phase, axis, buffer, landing):
        moved = []
        for step in range(1, here.size(axis)):
            copy = pltpu.make_async_remote_copy(
                src_ref=buffer.at[phase],
                dst_ref=landing.at[phase, step - 1],
                send_sem=sum_send.at[kind, phase, step - 1],
                recv_sem=sum_recv.at[kind, phase, step - 1],
                device_id=here.device(here.moved(axis, step)),
                device_id_type=MESH,
            )
            copy.start()
            moved.append(copy)
        sent.extend(moved)

        def finish():
            value = buffer[phase]
            for step, copy in enumerate(moved):
                copy.wait_recv()
                value = value + landing[phase, step]
            buffer[phase + 1] = value

        return finish

    def hand_over(item, step, source, sem):
        return pltpu.make_async_remote_copy(
            src_ref=source,
            dst_ref=from_core.at[step - 1, :, :, :, :, core_columns(item)],
            send_sem=sem,
            recv_sem=core_sem.at[item, step - 1],
            device_id=here.device(here.moved(3, step)),
            device_id_type=MESH,
        )

    arriving = {}

    def keep_own(item, value, start=0, size=None):
        block = value.reshape(nz, ny, nx, own_rows, value.shape[1])
        size = value.shape[1] if size is None else size
        column = pl.ds(items[item][1], size)
        for half in range(2):
            own[half, :, :, :, :, column] = block[
                :, :, :, half * half_rows : (half + 1) * half_rows, start : start + size
            ]

    out_items = [at for at, item in enumerate(items) if item[0] == "out"]
    qkv_items = [at for at, item in enumerate(items) if item[0] == "qkv"]
    vec_item = count - 1
    per_rank = len(qkv_items)
    steps_in_all = per_rank * tensor

    def rank_at(step):
        return lax.rem(here.rank + step, tensor)

    def pair_loads(at):
        turn_at, place = divmod(at, tensor)
        pair = rank_at(place + 1) * per_rank + turn_at
        column = pl.ds(pl.multiple_of(pair * 3 * LANES, LANES), 3 * LANES)
        near = at % 2
        return pair, column, [
            pltpu.make_async_copy(
                weight_qkv.at[:, :, :, :, column], qkv_buf.at[near], load_sem.at[0, near]
            ),
            pltpu.make_async_copy(projected.at[:, column], head_buf.at[near], load_sem.at[1, near]),
        ]

    def out_task():
        fetch = pltpu.make_async_copy(weight_out, out_buf, load_sem.at[2, 0])
        fetch.start()
        turn(back_one, back_turned)
        for copy in pair_loads(0)[2]:
            copy.start()
        size = out_stage.shape[5]
        for step in range(1, tensor + 1):
            column = pl.ds(pl.multiple_of(rank_at(step) * size, LANES), size)
            value = dot(back_turned[...], mixed[:, column]).astype(low)
            if step < tensor:
                out_stage[step - 1] = value.reshape(nz, ny, nx, own_rows, size)
                for item in out_items:
                    start = items[item][1] - core_start
                    source = out_stage.at[step - 1, :, :, :, :, pl.ds(start, items[item][2])]
                    copy = hand_over(item, step, source, stage_sem.at[item, step - 1])
                    copy.start()
                    sent.append(copy)
                    arriving.setdefault(item, []).append(copy)
            else:
                for item in out_items:
                    keep_own(item, value, items[item][1] - core_start, items[item][2])
        fetch.wait()
        grad_mixed[...] = dot(back_one[...], out_buf[...].reshape(width, width)).astype(low)
        turn(low_one, low_turned)

    staged = {}

    def pair_task(at):
        turn_at, place = divmod(at, tensor)
        pair, column, loads = pair_loads(at)
        for copy in loads:
            copy.wait()
        if at + 1 < steps_in_all:
            for copy in pair_loads(at + 1)[2]:
                copy.start()
        near = at % 2
        grads = grad_mixed[:, pl.ds(pl.multiple_of(pair * LANES, LANES), LANES)]
        value = attend_pair_back(head_buf[near], bias_ref[...], grads)
        head_sums[:, column] = jnp.sum(value.astype(jnp.float32), axis=0, keepdims=True)
        weight = qkv_buf[near].reshape(width, 3 * LANES)
        term = dot(value, weight, CONTRACT_LAST)
        if at == 0:
            input_grad[...] = term
        else:
            input_grad[...] += term
        item = qkv_items[turn_at]
        grad = dot(low_turned[...], value).astype(low)
        if place + 1 < tensor:
            if near in staged:
                staged[near].wait_send()
            qkv_stage[near] = grad.reshape(nz, ny, nx, own_rows, 3 * LANES)
            copy = hand_over(item, place + 1, qkv_stage.at[near], stage_sem.at[item, place])
            copy.start()
            staged[near] = copy
            arriving.setdefault(item, []).append(copy)
        else:
            keep_own(item, grad)

    def last_task():
        step_rows = LANES

        def fetch(at):
            near = lax.rem(at, 2)
            part = pl.ds(pl.multiple_of(at * step_rows, step_rows), step_rows)
            return [
                pltpu.make_async_copy(source.at[part, :], row_buf.at[which, near], load_sem.at[which, near])
                for which, source in enumerate((input_ref, middle_ref))
            ]

        for copy in fetch(0):
            copy.start()

        def body(at, sums):
            for copy in fetch(at):
                copy.wait()

            @pl.when(at + 1 < rows // step_rows)
            def _():
                for copy in fetch(at + 1):
                    copy.start()

            near = lax.rem(at, 2)
            part = pl.ds(pl.multiple_of(at * step_rows, step_rows), step_rows)
            normed, inverse = norm_rows(row_buf[0, near])
            grad_low = input_grad[part, :]
            scaled = grad_low * table[0:1, :]
            first = jnp.mean(scaled, axis=1, keepdims=True)
            second = jnp.mean(scaled * normed, axis=1, keepdims=True)
            input_grad[part, :] = row_buf[1, near] + inverse * (scaled - first - normed * second)
            terms = (grad_low * normed, grad_low)
            return tuple(old + jnp.sum(term, axis=0, keepdims=True) for old, term in zip(sums, terms))

        zero = jnp.zeros((1, width), jnp.float32)
        found = lax.fori_loop(0, rows // step_rows, body, (zero, zero))
        table_grad_ref[...] = jnp.zeros_like(table_grad_ref)
        for at in range(2):
            table_grad_ref[at : at + 1, :] = found[at]
        for pair in range(width // LANES):
            for kind, row in ((0, 2), (2, 3)):
                table_grad_ref[row : row + 1, pl.ds(pair * LANES, LANES)] = head_sums[
                    :, pl.ds((pair * 3 + kind) * LANES, LANES)
                ]
        for at, row in enumerate((4, 5, 6, VEC - 1)):
            table_grad_ref[row : row + 1, :] = vec_sums[at : at + 1, :]
        for at in range(VEC - 8):
            table_grad_ref[7 + at : 8 + at, :] = pre_sums[:, pl.ds(at * width, width)]
        value = table_grad_ref[...].T.astype(low)
        vec_stage[...] = value.reshape(nz, ny, nx, own_rows, LANES)
        for step in range(1, tensor):
            copy = hand_over(vec_item, step, vec_stage, stage_sem.at[vec_item, step - 1])
            copy.start()
            sent.append(copy)
            arriving.setdefault(vec_item, []).append(copy)
        keep_own(vec_item, value)

    here.barrier()
    local = {}
    for item, (name, start, size, source) in enumerate(items):
        if name in ("one", "two"):
            array = sum_one if name == "one" else sum_two
            for half in range(2):
                copy = pltpu.make_async_copy(
                    array.at[:, :, :, pl.ds(half * half_rows, half_rows), pl.ds(source, size)],
                    part(item, half, own_place, ()),
                    local_sem.at[item, half],
                )
                copy.start()
                local[item, half] = copy
    def advance(item, phase):
        for half in range(2):
            if phase > 1:
                for copy in copies(item, half, phase - 1):
                    copy.wait_recv()
                add_in(item, half, phase - 1)
            elif (item, half) in local:
                local[item, half].wait()
            else:
                if half == 0:
                    for copy in arriving.get(item, ()):
                        copy.wait_recv()
                add_in(item, half, 0)
            if phase < 4:
                for copy in copies(item, half, phase):
                    copy.start()
                    sent.append(copy)

    steps = Steps()
    owner = {item: ("out", 0) for item in out_items}
    owner |= {item: ("pair", tensor * (at + 1) - 1) for at, item in enumerate(qkv_items)}
    owner[vec_item] = ("last", 0)
    for item, (name, _, size, _) in enumerate(items):
        share = size / layout.total
        length = {1: share * UNIT * nz, 2: share * UNIT * nz / 2, 3: share * UNIT * nz}
        early = item not in owner
        for phase in range(1, 5):
            after = [("copy", item, phase - 1)] if phase > 1 else []
            waits = [(item, phase - 1)] if phase > 1 else []
            if phase == 1 and early and item >= DEPTH:
                after = [("copy", item - DEPTH, 2)]
            if phase == 1 and not early:
                after, waits = [owner[item]], [("core", owner[item])]
            steps.add(
                ("copy", item, phase),
                functools.partial(advance, item, phase),
                PUMP * (1.5 if phase == 2 else 1.0),
                (0.5 if phase == 1 and early else 0.0),
                after,
                waits,
                [((item, phase), "z" if phase == 3 else "xy", length[phase])] if phase < 4 else [],
            )
    steps.add(("out", 0), out_task, 8.0, 1.0, (), (), [(("core", ("out", 0)), "core", CORE_UNIT / 12)])
    for at in range(steps_in_all):
        after = [("pair", at - 1) if at else ("out", 0)]
        starts = [(("core", ("pair", at)), "core", CORE_UNIT / 24)]
        steps.add(("pair", at), functools.partial(pair_task, at), 6.0, 1.0, after, (), starts)
    steps.add(
        ("last", 0), last_task, 4.0, 1.0, [("pair", steps_in_all - 1)], (), [(("core", ("last", 0)), "core", 1.0)]
    )
    steps.run()
    sent.extend(staged.values())

    decay_rate = 1.0 - STEP ** (-0.8)
    keep_old = 1.0 - decay_rate
    long = layout.sizes["one"] * tensor
    matrices = layout.matrices()
    lane = lax.broadcasted_iota(jnp.int32, (1, LANES), 1)
    row_parts = []
    for spans in matrices:
        row_part = 0.0
        for start, size in spans:
            value = total_ref[:, pl.ds(start, size)]
            square = value * value
            col_sum[0, :, pl.ds(start, size)] = jnp.sum(square, axis=0, keepdims=True)
            row_part = row_part + jnp.sum(square, axis=1, keepdims=True)
        row_parts.append(row_part)
    row_sum[0] = pick(row_parts, lane)
    finish_row = exchange(0, 0, 3, row_sum, row_in)
    finish_col = exchange(1, 0, 0, col_sum, col_in)
    vec_start = layout.start["vec"]
    table_grad = total_ref[:, pl.ds(vec_start, LANES)]
    second_new = decay_rate * second_ref[...] + keep_old * (table_grad * table_grad + EPS_ONE)
    second_new_ref[...] = second_new
    vector_update = table_grad * lax.rsqrt(second_new)
    vector_sums = jnp.sum(vector_update * vector_update, axis=0, keepdims=True) / tensor
    vector_weight = jnp.sum(vector_ref[...] * vector_ref[...], axis=0, keepdims=True) / tensor
    weight_sums = [total_of(jnp.sum(weights[0][...] * weights[0][...], axis=0))]
    weight_sums += [total_of(ref[...] * ref[...]) for ref in weights[1:]]
    finish_row()
    row_counts = pick([jnp.full((1, 1), 1.0 / size, jnp.float32) for size in (width, width, width, width, long, long)], lane)
    row_new = decay_rate * state_row[...] + keep_old * (row_sum[1] * row_counts + EPS_ONE)
    row_new_ref[...] = row_new
    finish_col()
    exchange(1, 1, 1, col_sum, col_in)()
    exchange(1, 2, 2, col_sum, col_in)()
    col_new = decay_rate * state_col[...] + keep_old * (col_sum[3] / width + EPS_ONE)
    col_new_ref[...] = col_new
    ratios = []
    means = []
    for at, spans in enumerate(matrices):
        row_at = row_new[:, at : at + 1]
        ratio = 0.0
        for start, size in spans:
            value = total_ref[:, pl.ds(start, size)]
            col_at = col_new_ref[:, pl.ds(start, size)]
            ratio = ratio + total_of(value * value / (row_at * col_at))
        ratios.append(ratio)
        if at in (3, 5):
            means.append(jnp.sum(col_at, axis=1, keepdims=True) / (nz * ny * nx))
        else:
            means.append(jnp.sum(row_at, axis=0, keepdims=True) / tensor)
    small[0] = jnp.concatenate(
        [pick(ratios + means + weight_sums, lane), vector_sums, vector_weight, jnp.zeros((5, LANES), jnp.float32)], axis=0
    )
    for phase in range(4):
        exchange(2, phase, phase, small, small_in)()
    sums_ref[...] = small[4]
    for copy in sent:
        copy.wait_send()


def backward(dims, tensor, layout, large, near, weights, states):
    rows, width = near[0].shape
    own_rows = width // (dims[0] * dims[1] * dims[2])
    half_rows = own_rows // 2
    columns = layout.columns
    items = []
    for start in range(0, layout.sizes["one"], PIECE):
        for name in ("two", "one"):
            items.append((name, layout.start[name] + start, PIECE, start))
    for start in range(0, columns, PIECE):
        items.append(("out", layout.start["out"] + start, min(PIECE, columns - start), start))
    for start in range(0, 3 * columns, 3 * LANES):
        items.append(("qkv", layout.start["qkv"] + start, 3 * LANES, start))
    items.append(("vec", layout.start["vec"], LANES, 0))
    nz, ny, nx = dims
    peers = max(2, *dims, tensor) - 1
    others = max(1, tensor - 1)
    offset = layout.total
    from_here = offset - layout.start["out"]
    low, full = jnp.bfloat16, jnp.float32
    anywhere = pl.BlockSpec(memory_space=pl.ANY)
    inside = pl.BlockSpec(memory_space=pltpu.VMEM)

    def hold(*shape):
        return pltpu.VMEM(tuple(max(1, size) for size in shape), low)

    sums = offset - LANES
    count = len(items)
    return pl.pallas_call(
        functools.partial(backward_kernel, dims, tensor, tuple(items), layout),
        name="backward",
        out_shape=[
            jax.ShapeDtypeStruct((rows, width), full),
            jax.ShapeDtypeStruct((own_rows, offset), full),
            jax.ShapeDtypeStruct((1, sums), full),
            jax.ShapeDtypeStruct((own_rows, LANES), full),
            jax.ShapeDtypeStruct((own_rows, LANES), full),
            jax.ShapeDtypeStruct((8, LANES), full),
        ],
        in_specs=[anywhere] * len(large) + [inside] * (len(near) + 8),
        out_specs=[inside] * 6,
        scratch_shapes=[
            hold(2, nz, ny, nx, half_rows, offset),
            hold(others, nz, ny, nx, own_rows, from_here),
            hold(nx - 1, nz, ny, half_rows, offset),
            hold(ny - 1, nz, nx, half_rows, offset),
            hold(ny - 1, nz, half_rows, offset),
            hold(nx - 1, nz, half_rows, offset),
            hold(2, nz - 1, half_rows, offset),
            pltpu.VMEM((4, 1, sums), full),
            pltpu.VMEM((3, peers, 1, sums), full),
            pltpu.VMEM((2, own_rows, LANES), full),
            pltpu.VMEM((1, peers, own_rows, LANES), full),
            pltpu.VMEM((5, 8, LANES), full),
            pltpu.VMEM((4, peers, 8, LANES), full),
            hold(width, rows),
            hold(width, rows),
            hold(rows, width),
            hold(*dims, own_rows, width),
            hold(2, *dims, own_rows, 3 * LANES),
            hold(2, rows, 3 * LANES),
            pltpu.VMEM((2, 2, LANES, width), full),
            hold(others, *dims, own_rows, columns),
            hold(2, *dims, own_rows, 3 * LANES),
            hold(*dims, own_rows, LANES),
            pltpu.VMEM((1, 3 * width), full),
            pltpu.VMEM((LANES, width), full),
            pltpu.SemaphoreType.DMA((3, 2)),
            pltpu.SemaphoreType.DMA((count, others)),
            pltpu.SemaphoreType.DMA((count, others)),
            pltpu.SemaphoreType.DMA((count, 2)),
            pltpu.SemaphoreType.DMA((count, 2, 4, peers)),
            pltpu.SemaphoreType.DMA((count, 2, 4, peers)),
            pltpu.SemaphoreType.DMA((3, 4, peers)),
            pltpu.SemaphoreType.DMA((3, 4, peers)),
        ],
        compiler_params=pltpu.CompilerParams(
            collective_id=1, has_side_effects=True, vmem_limit_bytes=63 << 20
        ),
    )(*large, *near, *weights, *states)


def update_kernel(layout, width, long, *refs):
    total_ref, col_ref, row_ref, second_ref, sums_ref, vector_ref = refs[:6]
    weights = refs[6:10]
    own_qkv, own_out, own_one, own_two, own_table = refs[10:15]
    new_qkv, new_out, new_one, new_two, new_vectors, second_new = refs[15:21]
    qkv_row, qkv_col, out_row, out_col, one_row, one_col, two_row, two_col = refs[21:]
    lane = lax.broadcasted_iota(jnp.int32, (1, LANES), 1)

    def at(index):
        return sums_ref[0:1, index : index + 1]

    lengths = (width, width, width, width, width, long)
    means = [at(6 + m) / lengths[m] for m in range(6)]
    squares = [means[m] * at(m) for m in range(6)]
    squares = [squares[0] + squares[1] + squares[2], *squares[3:]]
    entries = (3 * width * width, width * width, width * long, width * long)
    step_size = []
    for m in range(4):
        damping = 1.0 / jnp.maximum(1.0, jnp.sqrt(squares[m] / entries[m] + 1e-06) / CLIP_LEVEL)
        step_size.append(LEARN_RATE * jnp.sqrt(at(12 + m) / entries[m] + 1e-06) * damping)
    spread = [(m, place, *span) for m, spans in enumerate(layout.matrices()) for place, span in enumerate(spans)]
    for m, place, start, size in spread:
        grad = total_ref[:, pl.ds(start, size)]
        col = col_ref[:, pl.ds(start, size)]
        step = step_size[max(0, m - 2)] * grad * lax.rsqrt(row_ref[:, m : m + 1] * col / means[m])
        if m < 3:
            part = slice(place * LANES, (place + 1) * LANES)
            own_qkv[m, :, part] = grad
            new_qkv[m, :, part] = weights[0][m, :, part] - step
            qkv_col[m : m + 1, part] = col
        elif m == 4:
            own_one[...] = grad
            new_one[...] = weights[2][...] - step
            one_col[...] = col
        else:
            own, new, weight = (own_out, new_out, weights[1]) if m == 3 else (own_two, new_two, weights[3])
            own[...] = grad.T
            new[...] = weight[...] - step.T
            (out_row if m == 3 else two_row)[...] = col
    row_flat = row_ref[...].T
    qkv_row[...] = row_flat[0:3]
    out_col[...] = row_flat[3:4]
    one_row[...] = row_flat[4:5]
    two_col[...] = row_flat[5:6]

    wide = (lane >= 7) & (lane < VEC - 1)
    counts = jnp.where(wide, float(long), float(width))

    def grouped(values):
        inside = jnp.sum(jnp.where(wide, values, 0.0), axis=1, keepdims=True)
        return jnp.where(wide, inside, values)

    table_grad = total_ref[:, pl.ds(layout.start["vec"], LANES)]
    update = table_grad * lax.rsqrt(second_ref[...])
    norm = jnp.sqrt(grouped(sums_ref[1:2, :]) / counts + 1e-06)
    size = jnp.sqrt(grouped(sums_ref[2:3, :]) / counts + 1e-06)
    fresh = vector_ref[...] - LEARN_RATE * size / jnp.maximum(1.0, norm / CLIP_LEVEL) * update
    own_table[...] = table_grad.T[:VEC]
    new_vectors[...] = fresh.T[:VEC]
    second_new[...] = second_ref[...].T[:VEC]


def update_weights(layout, width, long, columns, hidden, rows, values, vectors, weights):
    full = jnp.float32
    shapes = [
        (3, rows, columns),
        (columns, rows),
        (rows, hidden),
        (hidden, rows),
        (VEC, rows),
        (3, rows, columns),
        (columns, rows),
        (rows, hidden),
        (hidden, rows),
        (VEC, rows),
        (VEC, rows),
        (3, rows),
        (3, columns),
        (1, columns),
        (1, rows),
        (1, rows),
        (1, hidden),
        (1, hidden),
        (1, rows),
    ]
    return pl.pallas_call(
        functools.partial(update_kernel, layout, width, long),
        name="update_weights",
        out_shape=[jax.ShapeDtypeStruct(shape, full) for shape in shapes],
        compiler_params=pltpu.CompilerParams(vmem_limit_bytes=48 << 20),
    )(*values, vectors, *weights)


def paired(array, axis):
    moved = jnp.moveaxis(array, axis, -2)
    lead = moved.shape[:-2]
    blocks = moved.reshape(*lead, 3, moved.shape[-1] // LANES, LANES)
    return jnp.swapaxes(blocks, -3, -2).reshape(*lead, 3 * moved.shape[-1])


def on_device(
    inputs,
    cotangent,
    token_mask,
    w_qkv,
    w_out,
    w_fc1,
    w_fc2,
    vectors,
    qkv_row,
    qkv_col,
    out_row,
    out_col,
    fc1_row,
    fc1_col,
    fc2_row,
    fc2_col,
    vec_second,
):
    tensor_count = lax.axis_size("tensor")
    dims = grid_of(lax.axis_size("fsdp"))
    tensor_rank = lax.axis_index("tensor")
    rows_here, width = inputs.shape
    own_rows, columns = w_qkv.shape[1:]
    hidden = w_fc1.shape[1]
    low = jnp.bfloat16

    keep = lax.dynamic_slice_in_dim(token_mask, tensor_rank, 1, 0)
    keep_rows = keep.reshape(rows_here, 1).astype(jnp.float32)
    bias = jnp.where(keep > 0, 0.0, -1e30).astype(jnp.float32)

    pack = jnp.concatenate(
        [
            paired(w_qkv, 0),
            jnp.pad(vectors.T, ((0, 0), (0, LANES - VEC))),
            w_out.T,
            w_fc1,
            w_fc2.T,
        ],
        axis=1,
    ).astype(low)
    (
        weight_qkv,
        _,
        weight_out,
        *_,
        block_out,
        grad_middle,
        back_one,
        projected,
        mixed_rows,
        low_one,
        grad_one,
        grad_two,
        table,
        vec_sums,
        pre_sums,
    ) = forward(dims, tensor_count, pack, inputs, cotangent, keep_rows, bias, columns, hidden)
    layout = Layout(columns, hidden, ("two", "one", "out", "qkv", "vec"))
    col_state = {"qkv": paired(qkv_col, 0), "out": out_row, "one": fc1_col, "two": fc2_row}
    state_col = jnp.concatenate([col_state[name] for name in layout.order[:4]])[None]
    state_row = jnp.concatenate([qkv_row, out_col[None], fc1_row[None], fc2_col[None]], axis=0)
    state_row = jnp.pad(state_row.T, ((0, 0), (0, LANES - 6)))
    second = jnp.pad(vec_second.T, ((0, 0), (0, LANES - VEC)), constant_values=1.0)
    vectors_turned = jnp.pad(vectors.T, ((0, 0), (0, LANES - VEC)))
    weights = (w_qkv, w_out, w_fc1, w_fc2)
    input_grad, *values = backward(
        dims,
        tensor_count,
        layout,
        (grad_two, grad_one, weight_qkv, weight_out, projected, inputs, grad_middle),
        (mixed_rows, low_one, back_one, bias.reshape(rows_here, 1), table, vec_sums, pre_sums),
        weights,
        (state_col, state_row, second, vectors_turned),
    )
    outs = update_weights(
        layout, width, FF, columns, hidden, own_rows, values, vectors_turned, weights
    )
    outs = [out.reshape(-1) if out.shape[0] == 1 else out for out in outs]
    return (block_out, input_grad, *outs[:10], *outs[11:], outs[10])


def solution(mesh):
    in_specs = (
        P(("fsdp", "tensor"), None),
        P(("fsdp", "tensor"), None),
        P("fsdp", None),
        P(None, "fsdp", "tensor"),
        P("tensor", "fsdp"),
        P("fsdp", "tensor"),
        P("tensor", "fsdp"),
        P(None, "fsdp"),
        P(None, "fsdp"),
        P(None, "tensor"),
        P("tensor"),
        P("fsdp"),
        P("fsdp"),
        P("tensor"),
        P("tensor"),
        P("fsdp"),
        P(None, "fsdp"),
    )
    out_specs = (
        P(("fsdp", "tensor"), None),
        P(("fsdp", "tensor"), None),
        P(None, "fsdp", "tensor"),
        P("tensor", "fsdp"),
        P("fsdp", "tensor"),
        P("tensor", "fsdp"),
        P(None, "fsdp"),
        P(None, "fsdp", "tensor"),
        P("tensor", "fsdp"),
        P("fsdp", "tensor"),
        P("tensor", "fsdp"),
        P(None, "fsdp"),
        P(None, "fsdp"),
        P(None, "tensor"),
        P("tensor"),
        P("fsdp"),
        P("fsdp"),
        P("tensor"),
        P("tensor"),
        P("fsdp"),
        P(None, "fsdp"),
    )
    return jax.shard_map(
        on_device, mesh=mesh, in_specs=in_specs, out_specs=out_specs, check_vma=False
    )
```

```python
import functools

import jax
import jax.numpy as jnp
from jax import lax
from jax.experimental import pallas as pl
from jax.experimental.pallas import tpu as pltpu
from jax.sharding import PartitionSpec as P

HEAD_DIM = 64
FF = 4096
STEP = 20
VEC = 12
LANES = 128

EPS_NORM = 1e-05
EPS_ONE = 1e-30
CLIP_LEVEL = 1.0
LEARN_RATE = 0.5
MESH = pl.DeviceIdType.MESH
LOG2E = 1.4426950408889634
CONTRACT_LAST = (((1,), (1,)), ((), ()))


def grid_of(count):
    return {16: (4, 2, 2), 32: (2, 4, 4)}.get(count, (count, 1, 1))


class Place:
    def __init__(self, dims, tensor):
        self.dims = dims
        self.tensor = tensor
        fsdp = lax.axis_index("fsdp")
        _, ny, nx = dims
        self.at = (fsdp // (ny * nx), (fsdp // nx) % ny, fsdp % nx)
        self.rank = lax.axis_index("tensor")

    def moved(self, axis, step):
        place = list(self.at) + [self.rank]
        size = (*self.dims, self.tensor)[axis]
        place[axis] = lax.rem(place[axis] + step + size, size)
        return tuple(place)

    def device(self, place):
        z, y, x, rank = place
        return {"fsdp": (z * self.dims[1] + y) * self.dims[2] + x, "tensor": rank}

    def size(self, axis):
        return (*self.dims, self.tensor)[axis]

    def peers(self, *axes):
        places = [()]
        for axis in axes:
            places = [(*steps, step) for steps in places for step in range(self.size(axis))]
        found = []
        for steps in places[1:]:
            place = list(self.at) + [self.rank]
            for axis, step in zip(axes, steps):
                place[axis] = lax.rem(place[axis] + step, self.size(axis))
            found.append(self.device(tuple(place)))
        return found

    def barrier(self, groups):
        sem = pltpu.get_barrier_semaphore()
        count = 0
        for axes in groups:
            for device in self.peers(*axes):
                pl.semaphore_signal(sem, inc=1, device_id=device, device_id_type=MESH)
                count += 1
        if count:
            pl.semaphore_wait(sem, count)


def norm_rows(values):
    average = jnp.mean(values, axis=1, keepdims=True)
    center = values - average
    inverse = lax.rsqrt(jnp.mean(center * center, axis=1, keepdims=True) + EPS_NORM)
    return center * inverse, inverse


def dot(left, right, dims=(((1,), (0,)), ((), ()))):
    return lax.dot_general(left, right, dims, preferred_element_type=jnp.float32)


def turn(source, target):
    for start in range(0, source.shape[1], LANES):
        target[pl.ds(start, LANES), :] = source[:, pl.ds(start, LANES)].T


def attend_pair(heads, bias):
    mixed = []
    for head in range(2):
        query, key, value = (
            heads[:, kind * LANES + head * HEAD_DIM : kind * LANES + (head + 1) * HEAD_DIM] for kind in range(3)
        )
        scores = dot(query, key, CONTRACT_LAST) * (HEAD_DIM ** (-0.5) * LOG2E) + bias
        raised = jnp.exp2(scores - jnp.max(scores, axis=1, keepdims=True))
        summed = jnp.sum(raised, axis=1, keepdims=True)
        attention = (raised * (1.0 / summed)).astype(jnp.bfloat16)
        mixed.append(dot(attention, value).astype(jnp.bfloat16))
    return jnp.concatenate(mixed, axis=1)


class Steps:
    def __init__(self):
        self.steps = {}

    def add(self, name, run, time, rank, after=(), waits=(), starts=()):
        self.steps[name] = (run, time, rank, tuple(after), tuple(waits), tuple(starts))

    def arrange(self):
        now, free, arrival, done, order = 0.0, {}, {}, set(), []
        left = list(self.steps)
        while left:
            best, soonest = None, None
            for name in left:
                _, time, rank, after, waits, _ = self.steps[name]
                if any(other not in done for other in after) or any(wait not in arrival for wait in waits):
                    continue
                ready = max([arrival[wait] for wait in waits], default=0.0)
                if ready <= now:
                    if best is None or rank < self.steps[best][2]:
                        best = name
                elif soonest is None or ready < soonest:
                    soonest = ready
            if best is None:
                now = soonest
                continue
            _, time, _, _, _, starts = self.steps[best]
            now += time
            for transfer, link, length in starts:
                begin = max(now, free.get(link, 0.0))
                free[link] = begin + length
                arrival[transfer] = begin + length + LATENCY
            done.add(best)
            left.remove(best)
            order.append(best)
        return order, now

    def run(self):
        for name in self.arrange()[0]:
            self.steps[name][0]()


class Gather:
    def __init__(self, here, pack_ref, outs, parts, local_sem, send_sem, recv_sem):
        self.here = here
        self.pack = pack_ref
        self.outs = outs
        self.rows = pack_ref.shape[0]
        self.parts = parts
        self.sems = (local_sem, send_sem, recv_sem)
        self.own = (*here.at, here.rank)
        self.sent = []

    def region(self, item, part, place, free):
        out, _, chunk, _ = self.parts[item]
        index = tuple(slice(None) if a in free else place[a] for a in range(3))
        lead = () if chunk is None else (place[3], chunk)
        return self.outs[out].at[(*lead, *index, part)]

    def shard(self, item):
        _, offset, _, size = self.parts[item]
        return self.pack.at[:, pl.ds(offset, size)]

    def phases(self, item):
        return 3 if self.parts[item][2] is None else 4

    def moves(self, phase):
        whole, half = pl.ds(0, self.rows), self.rows // 2
        first, second = pl.ds(0, half), pl.ds(half, half)
        return (
            ((0, (), whole),),
            ((1, (0,), first), (2, (0,), second)),
            ((2, (0, 1), first), (1, (0, 2), second)),
            ((3, (0, 1, 2), whole),),
        )[phase]

    def copies(self, item, phase, landing):
        here = self.here
        found = []
        for axis, free, part in self.moves(phase):
            for step in range(1, here.size(axis)):
                own = self.region(item, part, self.own, free)
                if landing:
                    src = dst = self.region(item, part, here.moved(axis, -step), free)
                else:
                    src, dst = (self.shard(item) if phase == 0 else own), own
                at = len(found)
                found.append(
                    pltpu.make_async_remote_copy(
                        src_ref=src,
                        dst_ref=dst,
                        send_sem=self.sems[1].at[item, phase, at],
                        recv_sem=self.sems[2].at[item, phase, at],
                        device_id=here.device(here.moved(axis, step)),
                        device_id_type=MESH,
                    )
                )
        return found

    def keep(self, item):
        whole = pl.ds(0, self.rows)
        return pltpu.make_async_copy(
            self.shard(item), self.region(item, whole, self.own, ()), self.sems[0].at[item]
        )

    def advance(self, item, phase):
        if phase:
            for copy in self.copies(item, phase - 1, True):
                copy.wait_recv()
        if phase == 0:
            self.keep(item).start()
        if phase == 1:
            self.keep(item).wait()
        if phase < self.phases(item):
            for copy in self.copies(item, phase, False):
                copy.start()
                self.sent.append(copy)

    def finish(self):
        for copy in self.sent:
            copy.wait_send()


BLOCK = 512
DEPTH = 3
LATENCY = 1.5
UNIT = 16.0
CORE_UNIT = 40.0
PUMP = 0.4


def forward_kernel(dims, tensor, parts, tasks, *refs):
    input_ref, top_ref, mask_ref, vector_ref = refs[:4]
    own_weights = refs[4:8]
    outs, land = refs[8:13], refs[13:15]
    weight_qkv, weight_vec, weight_out, weight_one, weight_two = outs
    (
        block_out,
        grad_middle,
        back_one,
        projected,
        mixed,
        low_one,
        grad_one,
        grad_two,
        table,
        vec_sums,
        pre_sums,
        bias_column,
    ) = refs[15:27]
    (
        pack,
        keep_ref,
        square,
        vec_buf,
        qkv_buf,
        head_stage,
        out_buf,
        one_buf,
        two_buf,
        low_two,
        low_two_turned,
        back_two,
        back_two_turned,
        grad_low_two,
        hidden_bias,
        head_bias,
        one_stage,
        two_stage,
        one_keep,
        two_keep,
        other,
        active,
        grad_pre,
        load_sem,
        store_sem,
        keep_sem,
        head_sem,
        land_sem,
        local_sem,
        send_sem,
        recv_sem,
    ) = refs[27:]
    here = Place(dims, tensor)
    gather = Gather(here, pack, outs, parts, local_sem, send_sem, recv_sem)
    rows, width = input_ref.shape
    own_rows = pack.shape[0]
    per_rank = weight_qkv.shape[1]
    low = jnp.bfloat16
    step_rows = LANES

    def fill_pack():
        base = 0
        for pair in range(per_rank):
            for kind in range(3):
                part = own_weights[0][kind, :, pl.ds(pair * LANES, LANES)]
                pack[:, pl.ds(base, LANES)] = part.astype(low)
                base += LANES
        square[...] = jnp.zeros_like(square)
        square[pl.ds(0, VEC), :] = vector_ref[...]
        pack[:, pl.ds(base, LANES)] = square[...].T.astype(low)
        base += LANES
        for ref in own_weights[1:]:
            pack[:, pl.ds(base, ref.shape[1])] = ref[...].astype(low)
            base += ref.shape[1]

    def mask_row():
        return mask_ref[pl.ds(here.rank, 1), :].astype(jnp.float32)

    def mask_bias(keep):
        return jnp.where(keep > 0.0, 0.0, -1e30)

    def first_masks():
        turned = jnp.broadcast_to(mask_row(), (LANES, rows)).T
        keep_ref[...] = turned[:, 0:1]
        bias_column[...] = mask_bias(turned[:, 0:1])

    def row_steps(body, carry):
        return lax.fori_loop(
            0, rows // step_rows, lambda at, c: body(pl.ds(pl.multiple_of(at * step_rows, step_rows), step_rows), c), carry
        )

    def load(source, buffer, sem):
        return pltpu.make_async_copy(source, buffer, sem)

    def first_norm():
        first_masks()
        copy = load(weight_vec, vec_buf, load_sem.at[7])
        copy.start()
        copy.wait()
        whole = vec_buf[...].reshape(width, LANES).astype(jnp.float32).T
        table[...] = whole[:16]
        for at in range(VEC - 8):
            hidden_bias[:, pl.ds(at * width, width)] = whole[7 + at : 8 + at]
        for pair in range(width // LANES):
            for kind, row in ((0, 2), (2, 3)):
                head_bias[:, pl.ds((pair * 3 + kind) * LANES, LANES)] = whole[
                    row : row + 1, pair * LANES : (pair + 1) * LANES
                ]
            head_bias[:, pl.ds((pair * 3 + 1) * LANES, LANES)] = jnp.zeros((1, LANES), jnp.float32)

        def body(part, carry):
            normed, _ = norm_rows(input_ref[part, :])
            low_one[part, :] = (normed * table[0:1, :] + table[1:2, :]).astype(low)
            back_two[part, :] = (top_ref[part, :].astype(jnp.float32) * keep_ref[part, :]).astype(low)
            return carry

        row_steps(body, 0)
        turn(back_two, back_two_turned)

    def head_store(pair, slot):
        column = pl.ds(pl.multiple_of(pair * 3 * LANES, LANES), 3 * LANES)
        return pltpu.make_async_copy(head_stage.at[slot], projected.at[:, column], head_sem.at[slot])

    def pair_of(at):
        turn_at, place = divmod(at, tensor)
        return lax.rem(here.rank + place, tensor) * per_rank + turn_at

    def head_load(at):
        turn_at, place = divmod(at, tensor)
        source = weight_qkv.at[lax.rem(here.rank + place, tensor), turn_at]
        return load(source, qkv_buf.at[at % 2], load_sem.at[at % 2])

    def heads(at):
        head_load(at).wait()
        pair = pair_of(at)
        slot = at % 2
        column = pl.ds(pl.multiple_of(pair * 3 * LANES, LANES), 3 * LANES)
        weight = qkv_buf[slot].reshape(width, 3 * LANES)
        value = (dot(low_one[...], weight) + head_bias[:, column]).astype(low)
        if at > 1:
            head_store(pair, slot).wait()
        head_stage[slot] = value
        head_store(pair, slot).start()
        mixed[:, pl.ds(pl.multiple_of(pair * LANES, LANES), LANES)] = attend_pair(value, mask_bias(mask_row()))

    def out_load():
        return [
            load(weight_out.at[rank, 0], out_buf.at[rank], load_sem.at[2]) for rank in range(tensor)
        ]

    def second_norm():
        for copy in out_load():
            copy.wait()
        columns = width // tensor
        for rank in range(tensor):
            weight = out_buf[rank].reshape(width, columns)
            term = dot(mixed[:, pl.ds(rank * columns, columns)], weight, CONTRACT_LAST)
            if rank == 0:
                grad_middle[...] = term
            else:
                grad_middle[...] += term

        def body(part, carry):
            middle = input_ref[part, :] + (grad_middle[part, :] + table[4:5, :]) * keep_ref[part, :]
            grad_middle[part, :] = middle
            normed, _ = norm_rows(middle)
            low_two[part, :] = (normed * table[5:6, :] + table[6:7, :]).astype(low)
            return carry

        row_steps(body, 0)
        turn(low_two, low_two_turned)

    stages = (one_stage, two_stage)
    keeps = (one_keep, two_keep)

    def hand_over(at):
        chunk, place = divmod(at, tensor)
        target = (*here.at, lax.rem(here.rank + place + 1, tensor))
        return [
            pltpu.make_async_remote_copy(
                src_ref=stages[which].at[at % 2],
                dst_ref=land[which].at[place, chunk],
                send_sem=store_sem.at[which, at % 2],
                recv_sem=land_sem.at[which, place, chunk],
                device_id=here.device(target),
                device_id_type=MESH,
            )
            for which in range(2)
        ]

    def keep_store(chunk):
        return [
            pltpu.make_async_copy(
                keeps[which].at[chunk % 2],
                out.at[chunk],
                keep_sem.at[which, chunk % 2],
            )
            for which, out in enumerate((grad_one, grad_two))
        ]

    def hidden_column(at):
        chunk, place = divmod(at, tensor)
        base = (lax.rem(here.rank + place + 1, tensor) * weight_one.shape[1] + chunk) * BLOCK
        return pl.ds(pl.multiple_of(base, LANES), BLOCK)

    def hidden_load(at):
        chunk, place = divmod(at, tensor)
        rank = lax.rem(here.rank + place + 1, tensor)
        return [
            load(source.at[rank, chunk], buffer.at[at % 2], load_sem.at[3 + 2 * which + at % 2])
            for which, (source, buffer) in enumerate(((weight_one, one_buf), (weight_two, two_buf)))
        ]

    staged = {}

    def hidden(at):
        chunk, place = divmod(at, tensor)
        column = hidden_column(at)
        for copy in hidden_load(at):
            copy.wait()
        half = rows // 2
        bias = hidden_bias[:, column]

        def body(turn_at, total):
            part = pl.ds(pl.multiple_of(turn_at * half, half), half)
            one = one_buf[at % 2].reshape(width, BLOCK)
            two = two_buf[at % 2].reshape(width, BLOCK)
            preact = dot(low_two[part, :], one) + bias
            gate = jax.nn.sigmoid(1.702 * preact)
            value = (preact * gate).astype(low)
            active[part, :] = value
            derivative = gate + 1.702 * preact * gate * (1.0 - gate)
            grad = (dot(back_two[part, :], two) * derivative).astype(low)
            grad_pre[part, :] = grad
            if at == 0:
                block_out[part, :] = dot(value, two, CONTRACT_LAST)
                grad_low_two[part, :] = dot(grad, one, CONTRACT_LAST)
            else:
                block_out[part, :] += dot(value, two, CONTRACT_LAST)
                grad_low_two[part, :] += dot(grad, one, CONTRACT_LAST)
            return total + jnp.sum(grad.astype(jnp.float32), axis=0, keepdims=True)

        pre_sums[:, column] = lax.fori_loop(0, 2, body, jnp.zeros((1, BLOCK), jnp.float32))
        mine = place == tensor - 1
        if mine:
            targets = [ref.at[chunk % 2] for ref in keeps]
            if chunk > 1:
                for copy in keep_store(chunk):
                    copy.wait()
        else:
            targets = [ref.at[at % 2] for ref in stages]
            for copy in staged.pop(at % 2, ()):
                copy.wait_send()
        for target, left, right in (
            (targets[0], low_two_turned, grad_pre),
            (targets[1], back_two_turned, active),
        ):
            target[...] = dot(left[...], right[...]).astype(low).reshape(*target.shape)
        if not mine:
            staged[at % 2] = hand_over(at)
            for copy in staged[at % 2]:
                copy.start()

    def combine(chunk):
        for place in range(tensor - 1):
            for which, copy in enumerate(hand_over(chunk * tensor + place)):
                copy.wait_recv()
                fetch = load(land[which].at[place, chunk], other, load_sem.at[7])
                fetch.start()
                fetch.wait()
                keeps[which][chunk % 2] = keeps[which][chunk % 2] + other[...]
        for copy in keep_store(chunk):
            copy.start()

    def last_norm():
        def body(part, sums):
            middle = grad_middle[part, :]
            keep = keep_ref[part, :]
            top = top_ref[part, :].astype(jnp.float32)
            block_out[part, :] = middle + (block_out[part, :] + table[VEC - 1 : VEC, :]) * keep
            normed, inverse = norm_rows(middle)
            grad_low = grad_low_two[part, :]
            scaled = grad_low * table[5:6, :]
            first = jnp.mean(scaled, axis=1, keepdims=True)
            second = jnp.mean(scaled * normed, axis=1, keepdims=True)
            grad = top + inverse * (scaled - first - normed * second)
            grad_middle[part, :] = grad
            masked = grad * keep
            back_one[part, :] = masked.astype(low)
            terms = (masked, grad_low * normed, grad_low, top * keep)
            return tuple(old + jnp.sum(term, axis=0, keepdims=True) for old, term in zip(sums, terms))

        zero = jnp.zeros((1, width), jnp.float32)
        for at, value in enumerate(row_steps(body, (zero,) * 4)):
            vec_sums[at : at + 1, :] = value

    fill_pack()
    here.barrier(((0,), (1,), (2,), (3,)))
    steps = Steps()
    whole = sum(part[3] for part in parts)
    nz, ny, nx = dims

    def lengths(item, phase):
        share = parts[item][3] / whole
        return (
            (share * UNIT * nz, "z"),
            (share * UNIT * nz / 2, "xy"),
            (share * UNIT * nz, "xy"),
            (share * CORE_UNIT, "core"),
        )[phase]

    for item, part in enumerate(parts):
        phases = gather.phases(item)
        for phase in range(phases + 1):
            after = [("copy", item, phase - 1)] if phase else []
            if phase == 0 and item >= DEPTH:
                after = [("copy", item - DEPTH, 1)]
            length, link = lengths(item, min(phase, 3))
            steps.add(
                ("copy", item, phase),
                functools.partial(gather.advance, item, phase),
                PUMP,
                0.5 if phase == 0 else 0.0,
                after,
                [(item, phase - 1)] if phase else [],
                [((item, phase), link, length)] if phase < phases else [],
            )

    def landed(items):
        return [("copy", item, gather.phases(item)) for item in items]

    def start(copies):
        for copy in copies:
            copy.start()

    previous = None
    head_count, block_count = per_rank * tensor, FF // BLOCK
    for name, at, items in tasks:
        after = landed(items) + ([previous] if previous else [])
        begin, run, time = {
            "norm": (None, first_norm, 5.0),
            "heads": (lambda at=at: head_load(at).start(), lambda at=at: heads(at), 3.0),
            "out": (lambda: start(out_load()), second_norm, 5.0),
            "hidden": (lambda at=at: start(hidden_load(at)), lambda at=at: hidden(at), 5.5),
        }[name]
        if begin is not None:
            first = landed(items)
            if at > 1:
                first.append((name, at - 2))
            steps.add(("load", name, at), begin, 0.1, 0.2, first)
            after.append(("load", name, at))
        mine = name == "hidden" and at % tensor == tensor - 1
        chunk = at // tensor
        if mine and chunk > 1:
            after.append(("combine", chunk - 2))
        starts = []
        if name == "hidden" and not mine:
            starts = [(("hand", at), "core", CORE_UNIT / len(parts))]
        steps.add((name, at), run, time, 1.0, after, (), starts)
        if mine:
            waits = [("hand", chunk * tensor + place) for place in range(tensor - 1)]
            steps.add(
                ("combine", chunk), functools.partial(combine, chunk), 2.0, 0.8, [(name, at)], waits
            )
        previous = (name, at)
    steps.add(("last", 0), last_norm, 4.0, 0.9, [previous])
    steps.run()
    for slot in range(min(2, head_count)):
        head_store(0, slot).wait()
    for chunk in range(min(2, block_count // tensor)):
        for copy in keep_store(chunk):
            copy.wait()
    for copies in staged.values():
        for copy in copies:
            copy.wait_send()
    gather.finish()


def forward(dims, tensor, inputs, cotangent, token_mask, vectors, weights):
    own_rows, columns = weights[0].shape[1:]
    hidden = weights[2].shape[1]
    rows, width = inputs.shape
    low, full = jnp.bfloat16, jnp.float32
    widths = (3 * columns, LANES, columns, hidden, hidden)
    offsets = [sum(widths[:at]) for at in range(5)]
    per_rank = columns // LANES
    parts = [(1, offsets[1], None, LANES)]
    tasks = [("norm", 0, (0,))]
    for at in range(per_rank):
        size = 3 * LANES
        parts.append((0, offsets[0] + at * size, at, size))
        tasks += [("heads", at * tensor + place, (len(parts) - 1,)) for place in range(tensor)]
    tasks.append(("out", 0, (len(parts),)))
    parts.append((2, offsets[2], 0, columns))
    for block in range(hidden // BLOCK):
        needed = (len(parts), len(parts) + 1)
        parts += [(which, offsets[which] + block * BLOCK, block, BLOCK) for which in (3, 4)]
        tasks += [("hidden", block * tensor + place, needed) for place in range(tensor)]
    count = len(parts)
    peers = max(1, dims[0] - 1, dims[1] + dims[2] - 2, tensor - 1)
    anywhere = pl.BlockSpec(memory_space=pl.ANY)
    inside = pl.BlockSpec(memory_space=pltpu.VMEM)
    block = (*dims, own_rows, BLOCK)
    chunks = hidden // BLOCK

    def shape(kind, *size):
        return jax.ShapeDtypeStruct(size, kind)

    return pl.pallas_call(
        functools.partial(forward_kernel, dims, tensor, tuple(parts), tuple(tasks)),
        name="forward",
        out_shape=[
            shape(low, tensor, per_rank, *dims, own_rows, 3 * LANES),
            shape(low, *dims, own_rows, LANES),
            shape(low, tensor, 1, *dims, own_rows, columns),
            *[shape(low, tensor, chunks, *block)] * 2,
            *[shape(low, max(1, tensor - 1), chunks, *block)] * 2,
            shape(full, rows, width),
            shape(full, rows, width),
            shape(low, rows, width),
            shape(low, rows, 3 * width),
            shape(low, rows, width),
            shape(low, rows, width),
            *[shape(low, chunks, *block)] * 2,
            shape(full, 16, width),
            shape(full, 8, width),
            shape(full, 1, hidden * tensor),
            shape(full, rows, 1),
        ],
        in_specs=[inside] * 8,
        out_specs=[anywhere] * 7 + [inside] * 3 + [anywhere] + [inside] * 2 + [anywhere] * 2 + [inside] * 4,
        scratch_shapes=[
            pltpu.VMEM((own_rows, sum(widths)), low),
            pltpu.VMEM((rows, 1), full),
            pltpu.VMEM((LANES, own_rows), full),
            pltpu.VMEM((*dims, own_rows, LANES), low),
            pltpu.VMEM((2, *dims, own_rows, 3 * LANES), low),
            pltpu.VMEM((2, rows, 3 * LANES), low),
            pltpu.VMEM((tensor, *dims, own_rows, columns), low),
            pltpu.VMEM((2, *block), low),
            pltpu.VMEM((2, *block), low),
            pltpu.VMEM((rows, width), low),
            pltpu.VMEM((width, rows), low),
            pltpu.VMEM((rows, width), low),
            pltpu.VMEM((width, rows), low),
            pltpu.VMEM((rows, width), full),
            pltpu.VMEM((1, hidden * tensor), full),
            pltpu.VMEM((1, 3 * width), full),
            pltpu.VMEM((2, *block), low),
            pltpu.VMEM((2, *block), low),
            pltpu.VMEM((2, *block), low),
            pltpu.VMEM((2, *block), low),
            pltpu.VMEM(block, low),
            pltpu.VMEM((rows, BLOCK), low),
            pltpu.VMEM((rows, BLOCK), low),
            pltpu.SemaphoreType.DMA((8,)),
            pltpu.SemaphoreType.DMA((2, 2)),
            pltpu.SemaphoreType.DMA((2, 2)),
            pltpu.SemaphoreType.DMA((2,)),
            pltpu.SemaphoreType.DMA((2, max(1, tensor - 1), chunks)),
            pltpu.SemaphoreType.DMA((count,)),
            pltpu.SemaphoreType.DMA((count, 4, peers)),
            pltpu.SemaphoreType.DMA((count, 4, peers)),
        ],
        compiler_params=pltpu.CompilerParams(
            collective_id=0, has_side_effects=True, vmem_limit_bytes=62 << 20
        ),
    )(inputs, cotangent, token_mask, vectors, *weights)


class Layout:
    def __init__(self, columns, hidden, order):
        sizes = {"qkv": 3 * columns, "out": columns, "one": hidden, "two": hidden, "vec": LANES}
        self.order = order
        self.sizes = sizes
        self.start = {}
        at = 0
        for name in order:
            self.start[name] = at
            at += sizes[name]
        self.total = at
        self.columns = columns

    def span(self, name):
        return (self.start[name], self.sizes[name])

    def matrices(self):
        base = self.start["qkv"]
        pairs = range(self.columns // LANES)
        spans = [[(base + (pair * 3 + at) * LANES, LANES) for pair in pairs] for at in range(3)]
        return spans + [[self.span(name)] for name in ("out", "one", "two")]


def pick(values, lane):
    row = jnp.zeros((1, LANES), jnp.float32)
    for at, value in enumerate(values):
        row = jnp.where(lane == at, value, row)
    return row


def total_of(values):
    return jnp.sum(jnp.sum(values, axis=1, keepdims=True), axis=0, keepdims=True)


def attend_pair_back(heads, bias, grads):
    parts = ([], [], [])
    for head in range(2):
        query, key, value = (
            heads[:, kind * LANES + head * HEAD_DIM : kind * LANES + (head + 1) * HEAD_DIM] for kind in range(3)
        )
        grad = grads[:, head * HEAD_DIM : (head + 1) * HEAD_DIM]
        scores = dot(key, query, CONTRACT_LAST) * (HEAD_DIM ** (-0.5) * LOG2E) + bias
        raised = jnp.exp2(scores - jnp.max(scores, axis=0, keepdims=True))
        attention = raised * (1.0 / jnp.sum(raised, axis=0, keepdims=True))
        grad_value = dot(attention.astype(jnp.bfloat16), grad)
        grad_attention = dot(value, grad, CONTRACT_LAST)
        weighted = jnp.sum(attention * grad_attention, axis=0, keepdims=True)
        grad_scores = (attention * (grad_attention - weighted) * HEAD_DIM ** (-0.5)).astype(jnp.bfloat16)
        grad_key = dot(grad_scores, query)
        grad_query = dot(key.T, grad_scores).T
        for kind, part in enumerate((grad_query, grad_key, grad_value)):
            parts[kind].append(part.astype(jnp.bfloat16))
    return jnp.concatenate([piece for kind in parts for piece in kind], axis=1)


def backward_kernel(dims, tensor, items, layout, *refs):
    (
        sum_two,
        sum_one,
        weight_qkv,
        weight_out,
        projected,
        input_ref,
        middle_ref,
        mixed,
        low_one,
        back_one,
        bias_ref,
        table,
        vec_sums,
        pre_sums,
    ) = refs[:14]
    weights = refs[14:18]
    row_states, col_states = refs[18:22], refs[22:26]
    second_ref, vector_ref = refs[26:28]
    input_grad, total_ref, col_new_ref, row_new_ref, second_new_ref, sums_ref = refs[28:34]
    (
        own,
        from_core,
        one_x,
        one_y,
        two_y,
        two_x,
        from_z,
        col_sum,
        col_in,
        row_sum,
        row_in,
        small,
        small_in,
        square,
        turned,
        low_turned,
        back_turned,
        grad_mixed,
        out_buf,
        qkv_buf,
        head_buf,
        row_buf,
        out_stage,
        qkv_stage,
        vec_stage,
        head_sums,
        table_grad_ref,
        load_sem,
        stage_sem,
        core_sem,
        local_sem,
        send_sem,
        recv_sem,
        sum_send,
        sum_recv,
    ) = refs[34:]
    here = Place(dims, tensor)
    nz, ny, nx = dims
    low = jnp.bfloat16
    own_rows = own.shape[3]
    half_rows = own_rows // 2
    rows, width = input_grad.shape
    own_place = (*here.at, here.rank)
    count = len(items)
    core_start = layout.start["out"]

    def columns(item):
        _, start, size, _ = items[item]
        return pl.ds(start, size)

    def core_columns(item):
        _, start, size, _ = items[item]
        return pl.ds(start - core_start, size)

    def moves(phase):
        first, second = pl.ds(0, half_rows), pl.ds(half_rows, half_rows)
        return (
            (),
            ((2, (2,), first, one_x, 0), (1, (1,), second, one_y, nx - 1)),
            ((1, (1, 2), first, two_y, 0), (2, (1, 2), second, two_x, ny - 1)),
            ((0, (0, 1, 2), pl.ds(0, own_rows), from_z, 0),),
        )[phase]

    def copies(item, phase):
        found = []
        for axis, fixed, part, landing, _ in moves(phase):
            for step in range(1, here.size(axis)):
                target = here.moved(axis, step)
                index = tuple(target[a] if a in fixed else slice(None) for a in range(3))
                free = (slice(None),) * (3 - len(fixed))
                at = len(found)
                found.append(
                    pltpu.make_async_remote_copy(
                        src_ref=own.at[(*index, part, columns(item))],
                        dst_ref=landing.at[(step - 1, *free, slice(None), columns(item))],
                        send_sem=send_sem.at[item, phase, at],
                        recv_sem=recv_sem.at[item, phase, at],
                        device_id=here.device(target),
                        device_id_type=MESH,
                    )
                )
        return found

    def add_core(item):
        def body(at, carry):
            z, y, x = at // (ny * nx), at // nx % ny, at % nx
            value = own[z, y, x, :, columns(item)]
            for step in range(tensor - 1):
                value = value + from_core[step, z, y, x, :, core_columns(item)]
            own[z, y, x, :, columns(item)] = value
            return carry

        if tensor > 1:
            lax.fori_loop(0, nz * ny * nx, body, 0)

    def add_in(item, phase):
        column = columns(item)
        for axis, fixed, part, landing, _ in moves(phase):
            steps = here.size(axis) - 1
            if phase == 3:
                value = own[(*here.at, part, column)].astype(jnp.float32)
                for step in range(steps):
                    value = value + landing[step, :, column].astype(jnp.float32)
                total_ref[:, column] = value
                continue
            if steps == 0:
                continue
            free = [a for a in range(3) if a not in fixed]
            sizes = [dims[a] for a in free]
            loops = 1
            for size in sizes:
                loops *= size

            def body(at, carry):
                place = list(here.at)
                inner = []
                rest = at
                for axis_at, size in reversed(list(zip(free, sizes))):
                    place[axis_at] = rest % size
                    inner.insert(0, rest % size)
                    rest = rest // size
                where = (*place, part, column)
                value = own[where]
                for step in range(steps):
                    value = value + landing[(step, *inner, slice(None), column)]
                own[where] = value
                return carry

            lax.fori_loop(0, loops, body, 0)

    sent = []

    def exchange(kind, phase, axes, buffer, landing):
        moved = []
        for at, device in enumerate(here.peers(*axes)):
            copy = pltpu.make_async_remote_copy(
                src_ref=buffer.at[phase],
                dst_ref=landing.at[phase, at],
                send_sem=sum_send.at[kind, phase, at],
                recv_sem=sum_recv.at[kind, phase, at],
                device_id=device,
                device_id_type=MESH,
            )
            copy.start()
            moved.append(copy)
        sent.extend(moved)

        def finish():
            value = buffer[phase]
            for at, copy in enumerate(moved):
                copy.wait_recv()
                value = value + landing[phase, at]
            buffer[phase + 1] = value

        return finish

    def hand_over(item, step, source, sem):
        return pltpu.make_async_remote_copy(
            src_ref=source,
            dst_ref=from_core.at[step - 1, :, :, :, :, core_columns(item)],
            send_sem=sem,
            recv_sem=core_sem.at[item, step - 1],
            device_id=here.device(here.moved(3, step)),
            device_id_type=MESH,
        )

    arriving = {}

    def keep_own(item, value):
        own[:, :, :, :, columns(item)] = value.reshape(nz, ny, nx, own_rows, value.shape[1])

    out_items = [at for at, item in enumerate(items) if item[0] == "out"]
    qkv_items = [at for at, item in enumerate(items) if item[0] == "qkv"]
    vec_item = count - 1
    per_rank = len(qkv_items)
    steps_in_all = per_rank * tensor

    def rank_at(step):
        return lax.rem(here.rank + step, tensor)

    def pair_loads(at):
        turn_at, place = divmod(at, tensor)
        pair = rank_at(place + 1) * per_rank + turn_at
        column = pl.ds(pl.multiple_of(pair * 3 * LANES, LANES), 3 * LANES)
        near = at % 2
        return pair, column, [
            pltpu.make_async_copy(
                weight_qkv.at[rank_at(place + 1), turn_at], qkv_buf.at[near], load_sem.at[0, near]
            ),
            pltpu.make_async_copy(projected.at[:, column], head_buf.at[near], load_sem.at[1, near]),
        ]

    def out_task():
        fetch = [
            pltpu.make_async_copy(weight_out.at[rank, 0], out_buf.at[rank], load_sem.at[2, 0])
            for rank in range(tensor)
        ]
        for copy in fetch:
            copy.start()
        turn(back_one, back_turned)
        for copy in pair_loads(0)[2]:
            copy.start()
        size = out_stage.shape[5]
        item = out_items[0]
        for step in range(1, tensor + 1):
            column = pl.ds(pl.multiple_of(rank_at(step) * size, LANES), size)
            value = dot(back_turned[...], mixed[:, column]).astype(low)
            if step < tensor:
                out_stage[step - 1] = value.reshape(nz, ny, nx, own_rows, size)
                copy = hand_over(item, step, out_stage.at[step - 1], stage_sem.at[item, step - 1])
                copy.start()
                sent.append(copy)
                arriving.setdefault(item, []).append(copy)
            else:
                keep_own(item, value)
        for copy in fetch:
            copy.wait()
        for rank in range(tensor):
            weight = out_buf[rank].reshape(width, size)
            grad_mixed[:, pl.ds(rank * size, size)] = dot(back_one[...], weight).astype(low)
        turn(low_one, low_turned)

    def state_task():
        def fill(refs, other):
            square[...] = jnp.full_like(square, other)
            base = 0
            for ref in refs:
                square[pl.ds(base, ref.shape[0]), :] = ref[...]
                base += ref.shape[0]
            return square[...].T

        turned[0] = fill(row_states, 1.0)
        turned[1] = fill((second_ref,), 1.0)
        turned[2] = fill((vector_ref,), 0.0)

    staged = {}

    def pair_task(at):
        turn_at, place = divmod(at, tensor)
        pair, column, loads = pair_loads(at)
        for copy in loads:
            copy.wait()
        if at + 1 < steps_in_all:
            for copy in pair_loads(at + 1)[2]:
                copy.start()
        near = at % 2
        grads = grad_mixed[:, pl.ds(pl.multiple_of(pair * LANES, LANES), LANES)]
        value = attend_pair_back(head_buf[near], bias_ref[...], grads)
        head_sums[:, column] = jnp.sum(value.astype(jnp.float32), axis=0, keepdims=True)
        weight = qkv_buf[near].reshape(width, 3 * LANES)
        term = dot(value, weight, CONTRACT_LAST)
        if at == 0:
            input_grad[...] = term
        else:
            input_grad[...] += term
        item = qkv_items[turn_at]
        grad = dot(low_turned[...], value).astype(low)
        if place + 1 < tensor:
            if near in staged:
                staged[near].wait_send()
            qkv_stage[near] = grad.reshape(nz, ny, nx, own_rows, 3 * LANES)
            copy = hand_over(item, place + 1, qkv_stage.at[near], stage_sem.at[item, place])
            copy.start()
            staged[near] = copy
            arriving.setdefault(item, []).append(copy)
        else:
            keep_own(item, grad)

    def last_task():
        step_rows = LANES

        def fetch(at):
            near = lax.rem(at, 2)
            part = pl.ds(pl.multiple_of(at * step_rows, step_rows), step_rows)
            return [
                pltpu.make_async_copy(source.at[part, :], row_buf.at[which, near], load_sem.at[which, near])
                for which, source in enumerate((input_ref, middle_ref))
            ]

        for copy in fetch(0):
            copy.start()

        def body(at, sums):
            for copy in fetch(at):
                copy.wait()

            @pl.when(at + 1 < rows // step_rows)
            def _():
                for copy in fetch(at + 1):
                    copy.start()

            near = lax.rem(at, 2)
            part = pl.ds(pl.multiple_of(at * step_rows, step_rows), step_rows)
            normed, inverse = norm_rows(row_buf[0, near])
            grad_low = input_grad[part, :]
            scaled = grad_low * table[0:1, :]
            first = jnp.mean(scaled, axis=1, keepdims=True)
            second = jnp.mean(scaled * normed, axis=1, keepdims=True)
            input_grad[part, :] = row_buf[1, near] + inverse * (scaled - first - normed * second)
            terms = (grad_low * normed, grad_low)
            return tuple(old + jnp.sum(term, axis=0, keepdims=True) for old, term in zip(sums, terms))

        zero = jnp.zeros((1, width), jnp.float32)
        found = lax.fori_loop(0, rows // step_rows, body, (zero, zero))
        table_grad_ref[...] = jnp.zeros_like(table_grad_ref)
        for at in range(2):
            table_grad_ref[at : at + 1, :] = found[at]
        for pair in range(width // LANES):
            for kind, row in ((0, 2), (2, 3)):
                table_grad_ref[row : row + 1, pl.ds(pair * LANES, LANES)] = head_sums[
                    :, pl.ds((pair * 3 + kind) * LANES, LANES)
                ]
        for at, row in enumerate((4, 5, 6, VEC - 1)):
            table_grad_ref[row : row + 1, :] = vec_sums[at : at + 1, :]
        for at in range(VEC - 8):
            table_grad_ref[7 + at : 8 + at, :] = pre_sums[:, pl.ds(at * width, width)]
        value = table_grad_ref[...].T.astype(low)
        vec_stage[...] = value.reshape(nz, ny, nx, own_rows, LANES)
        for step in range(1, tensor):
            copy = hand_over(vec_item, step, vec_stage, stage_sem.at[vec_item, step - 1])
            copy.start()
            sent.append(copy)
            arriving.setdefault(vec_item, []).append(copy)
        keep_own(vec_item, value)

    here.barrier(((0, 3), (1, 2)))
    local = {}
    for item, (name, _, _, source) in enumerate(items):
        if name in ("one", "two"):
            array = sum_one if name == "one" else sum_two
            copy = pltpu.make_async_copy(
                array.at[source], own.at[:, :, :, :, columns(item)], local_sem.at[item]
            )
            copy.start()
            local[item] = copy

    def advance(item, phase):
        if phase > 1:
            for copy in copies(item, phase - 1):
                copy.wait_recv()
            add_in(item, phase - 1)
        elif item in local:
            local[item].wait()
        else:
            for copy in arriving.get(item, ()):
                copy.wait_recv()
            add_core(item)
        if phase < 4:
            for copy in copies(item, phase):
                copy.start()
                sent.append(copy)

    steps = Steps()
    owner = {item: ("out", 0) for item in out_items}
    owner |= {item: ("pair", tensor * (at + 1) - 1) for at, item in enumerate(qkv_items)}
    owner[vec_item] = ("last", 0)
    for item, (name, _, size, _) in enumerate(items):
        share = size / layout.total
        length = {1: share * UNIT * nz, 2: share * UNIT * nz / 2, 3: share * UNIT * nz}
        early = item not in owner
        for phase in range(1, 5):
            after = [("copy", item, phase - 1)] if phase > 1 else []
            waits = [(item, phase - 1)] if phase > 1 else []
            if phase == 1 and early and item >= DEPTH:
                after = [("copy", item - DEPTH, 2)]
            if phase == 1 and not early:
                after, waits = [owner[item]], [("core", owner[item])]
            steps.add(
                ("copy", item, phase),
                functools.partial(advance, item, phase),
                PUMP * (1.5 if phase == 2 else 1.0),
                (0.5 if phase == 1 and early else 0.0),
                after,
                waits,
                [((item, phase), "z" if phase == 3 else "xy", length[phase])] if phase < 4 else [],
            )
    steps.add(("state", 0), state_task, 1.0, 2.0)
    steps.add(("out", 0), out_task, 8.0, 1.0, (), (), [(("core", ("out", 0)), "core", CORE_UNIT / 12)])
    for at in range(steps_in_all):
        after = [("pair", at - 1) if at else ("out", 0)]
        starts = [(("core", ("pair", at)), "core", CORE_UNIT / 24)]
        steps.add(("pair", at), functools.partial(pair_task, at), 6.0, 1.0, after, (), starts)
    steps.add(
        ("last", 0), last_task, 4.0, 1.0, [("pair", steps_in_all - 1)], (), [(("core", ("last", 0)), "core", 1.0)]
    )
    steps.run()
    sent.extend(staged.values())

    decay_rate = 1.0 - STEP ** (-0.8)
    keep_old = 1.0 - decay_rate
    long = layout.sizes["one"] * tensor
    matrices = layout.matrices()
    lane = lax.broadcasted_iota(jnp.int32, (1, LANES), 1)
    row_parts = []
    for spans in matrices:
        row_part = 0.0
        for start, size in spans:
            value = total_ref[:, pl.ds(start, size)]
            square = value * value
            col_sum[0, :, pl.ds(start, size)] = jnp.sum(square, axis=0, keepdims=True)
            row_part = row_part + jnp.sum(square, axis=1, keepdims=True)
        row_parts.append(row_part)
    row_sum[0] = pick(row_parts, lane)
    finish_row = exchange(0, 0, (3,), row_sum, row_in)
    finish_col = exchange(1, 0, (0,), col_sum, col_in)
    vec_start = layout.start["vec"]
    table_grad = total_ref[:, pl.ds(vec_start, LANES)]
    second_new = decay_rate * turned[1] + keep_old * (table_grad * table_grad + EPS_ONE)
    second_new_ref[...] = second_new
    vector_update = table_grad * lax.rsqrt(second_new)
    vector_sums = jnp.sum(vector_update * vector_update, axis=0, keepdims=True) / tensor
    vector_weight = jnp.sum(turned[2] * turned[2], axis=0, keepdims=True) / tensor
    weight_sums = [total_of(jnp.sum(weights[0][...] * weights[0][...], axis=0))]
    weight_sums += [total_of(ref[...] * ref[...]) for ref in weights[1:]]
    finish_row()
    row_counts = pick([jnp.full((1, 1), 1.0 / size, jnp.float32) for size in (width, width, width, width, long, long)], lane)
    row_new = decay_rate * turned[0] + keep_old * (row_sum[1] * row_counts + EPS_ONE)
    row_new_ref[...] = row_new
    finish_col()
    exchange(1, 1, (1, 2), col_sum, col_in)()
    for at, spans in enumerate(matrices):
        for place, (start, size) in enumerate(spans):
            if at < 3:
                old = col_states[0][at : at + 1, pl.ds(place * LANES, LANES)]
            else:
                old = col_states[at - 2][...]
            fresh = keep_old * (col_sum[2, :, pl.ds(start, size)] / width + EPS_ONE)
            col_new_ref[:, pl.ds(start, size)] = decay_rate * old + fresh
    ratios = []
    means = []
    for at, spans in enumerate(matrices):
        row_at = row_new[:, at : at + 1]
        ratio = 0.0
        for start, size in spans:
            value = total_ref[:, pl.ds(start, size)]
            col_at = col_new_ref[:, pl.ds(start, size)]
            ratio = ratio + total_of(value * value / (row_at * col_at))
        ratios.append(ratio)
        if at in (3, 5):
            means.append(jnp.sum(col_at, axis=1, keepdims=True) / (nz * ny * nx))
        else:
            means.append(jnp.sum(row_at, axis=0, keepdims=True) / tensor)
    small[0] = jnp.concatenate(
        [pick(ratios + means + weight_sums, lane), vector_sums, vector_weight, jnp.zeros((5, LANES), jnp.float32)], axis=0
    )
    exchange(2, 0, (0, 3), small, small_in)()
    exchange(2, 1, (1, 2), small, small_in)()
    sums_ref[...] = small[2]
    for copy in sent:
        copy.wait_send()


def backward(dims, tensor, layout, large, near, weights, states):
    rows, width = near[0].shape
    own_rows = width // (dims[0] * dims[1] * dims[2])
    half_rows = own_rows // 2
    columns = layout.columns
    items = []
    for block in range(layout.sizes["one"] // BLOCK):
        for name in ("two", "one"):
            items.append((name, layout.start[name] + block * BLOCK, BLOCK, block))
    items.append(("out", layout.start["out"], columns, 0))
    for start in range(0, 3 * columns, 3 * LANES):
        items.append(("qkv", layout.start["qkv"] + start, 3 * LANES, start))
    items.append(("vec", layout.start["vec"], LANES, 0))
    nz, ny, nx = dims
    peers = max(1, nz - 1, ny + nx - 2)
    group = max(1, nz * tensor - 1, ny * nx - 1)
    others = max(1, tensor - 1)
    offset = layout.total
    from_here = offset - layout.start["out"]
    low, full = jnp.bfloat16, jnp.float32
    anywhere = pl.BlockSpec(memory_space=pl.ANY)
    inside = pl.BlockSpec(memory_space=pltpu.VMEM)

    def hold(*shape):
        return pltpu.VMEM(tuple(max(1, size) for size in shape), low)

    sums = offset - LANES
    count = len(items)
    return pl.pallas_call(
        functools.partial(backward_kernel, dims, tensor, tuple(items), layout),
        name="backward",
        out_shape=[
            jax.ShapeDtypeStruct((rows, width), full),
            jax.ShapeDtypeStruct((own_rows, offset), full),
            jax.ShapeDtypeStruct((1, sums), full),
            jax.ShapeDtypeStruct((own_rows, LANES), full),
            jax.ShapeDtypeStruct((own_rows, LANES), full),
            jax.ShapeDtypeStruct((8, LANES), full),
        ],
        in_specs=[anywhere] * len(large) + [inside] * (len(near) + len(weights) + len(states)),
        out_specs=[inside] * 6,
        scratch_shapes=[
            hold(nz, ny, nx, own_rows, offset),
            hold(others, nz, ny, nx, own_rows, from_here),
            hold(nx - 1, nz, ny, half_rows, offset),
            hold(ny - 1, nz, nx, half_rows, offset),
            hold(ny - 1, nz, half_rows, offset),
            hold(nx - 1, nz, half_rows, offset),
            hold(nz - 1, own_rows, offset),
            pltpu.VMEM((3, 1, sums), full),
            pltpu.VMEM((2, max(1, nz - 1, ny * nx - 1), 1, sums), full),
            pltpu.VMEM((2, own_rows, LANES), full),
            pltpu.VMEM((1, others, own_rows, LANES), full),
            pltpu.VMEM((3, 8, LANES), full),
            pltpu.VMEM((2, group, 8, LANES), full),
            pltpu.VMEM((LANES, own_rows), full),
            pltpu.VMEM((3, own_rows, LANES), full),
            hold(width, rows),
            hold(width, rows),
            hold(rows, width),
            hold(tensor, *dims, own_rows, columns),
            hold(2, *dims, own_rows, 3 * LANES),
            hold(2, rows, 3 * LANES),
            pltpu.VMEM((2, 2, LANES, width), full),
            hold(others, *dims, own_rows, columns),
            hold(2, *dims, own_rows, 3 * LANES),
            hold(*dims, own_rows, LANES),
            pltpu.VMEM((1, 3 * width), full),
            pltpu.VMEM((LANES, width), full),
            pltpu.SemaphoreType.DMA((3, 2)),
            pltpu.SemaphoreType.DMA((count, others)),
            pltpu.SemaphoreType.DMA((count, others)),
            pltpu.SemaphoreType.DMA((count,)),
            pltpu.SemaphoreType.DMA((count, 4, peers)),
            pltpu.SemaphoreType.DMA((count, 4, peers)),
            pltpu.SemaphoreType.DMA((3, 2, group)),
            pltpu.SemaphoreType.DMA((3, 2, group)),
        ],
        compiler_params=pltpu.CompilerParams(
            collective_id=1, has_side_effects=True, vmem_limit_bytes=63 << 20
        ),
    )(*large, *near, *weights, *states)


def update_kernel(layout, width, long, *refs):
    block_in, grad_in = refs[:2]
    far = refs[2:12]
    block_out, input_grad = refs[12:14]
    own_qkv, own_out, own_one, own_two, own_table = refs[14:19]
    new_qkv, new_out, new_one, new_two, new_vectors, second_new = refs[19:25]
    qkv_row, qkv_col, out_row, out_col, one_row, one_col, two_row, two_col = refs[25:33]
    near, sem = refs[33:43], refs[43]
    long_copies = [
        pltpu.make_async_copy(source, target, sem.at[at])
        for at, (source, target) in enumerate(((block_in, block_out), (grad_in, input_grad)))
    ]
    loads = [
        pltpu.make_async_copy(source, target, sem.at[2 + at]) for at, (source, target) in enumerate(zip(far, near))
    ]
    for copy in [*loads, *long_copies]:
        copy.start()
    for copy in loads:
        copy.wait()
    total_ref, col_ref, row_ref, second_ref, sums_ref, vector_ref = near[:6]
    weights = near[6:]
    lane = lax.broadcasted_iota(jnp.int32, (1, LANES), 1)

    def at(index):
        return sums_ref[0:1, index : index + 1]

    lengths = (width, width, width, width, width, long)
    means = [at(6 + m) / lengths[m] for m in range(6)]
    squares = [means[m] * at(m) for m in range(6)]
    squares = [squares[0] + squares[1] + squares[2], *squares[3:]]
    entries = (3 * width * width, width * width, width * long, width * long)
    step_size = []
    for m in range(4):
        damping = 1.0 / jnp.maximum(1.0, jnp.sqrt(squares[m] / entries[m] + 1e-06) / CLIP_LEVEL)
        step_size.append(LEARN_RATE * jnp.sqrt(at(12 + m) / entries[m] + 1e-06) * damping)
    spread = [(m, place, *span) for m, spans in enumerate(layout.matrices()) for place, span in enumerate(spans)]
    for m, place, start, size in spread:
        grad = total_ref[:, pl.ds(start, size)]
        col = col_ref[:, pl.ds(start, size)]
        step = step_size[max(0, m - 2)] * grad * lax.rsqrt(row_ref[:, m : m + 1] * col / means[m])
        if m < 3:
            part = slice(place * LANES, (place + 1) * LANES)
            own_qkv[m, :, part] = grad
            new_qkv[m, :, part] = weights[0][m, :, part] - step
            qkv_col[m : m + 1, part] = col
        else:
            own, new, state = (
                (own_out, new_out, out_row),
                (own_one, new_one, one_col),
                (own_two, new_two, two_row),
            )[m - 3]
            own[...] = grad
            new[...] = weights[m - 2][...] - step
            state[...] = col
    row_flat = row_ref[...].T
    qkv_row[...] = row_flat[0:3]
    out_col[...] = row_flat[3:4]
    one_row[...] = row_flat[4:5]
    two_col[...] = row_flat[5:6]

    wide = (lane >= 7) & (lane < VEC - 1)
    counts = jnp.where(wide, float(long), float(width))

    def grouped(values):
        inside = jnp.sum(jnp.where(wide, values, 0.0), axis=1, keepdims=True)
        return jnp.where(wide, inside, values)

    table_grad = total_ref[:, pl.ds(layout.start["vec"], LANES)]
    update = table_grad * lax.rsqrt(second_ref[...])
    norm = jnp.sqrt(grouped(sums_ref[1:2, :]) / counts + 1e-06)
    size = jnp.sqrt(grouped(sums_ref[2:3, :]) / counts + 1e-06)
    change = LEARN_RATE * size / jnp.maximum(1.0, norm / CLIP_LEVEL) * update
    own_table[...] = table_grad.T[:VEC]
    new_vectors[...] = vector_ref[...] - change.T[:VEC]
    second_new[...] = second_ref[...].T[:VEC]
    for copy in long_copies:
        copy.wait()


def update_weights(layout, width, long, columns, hidden, rows, results, values, vectors, weights):
    full = jnp.float32
    shapes = [
        *(result.shape for result in results),
        (3, rows, columns),
        (rows, columns),
        (rows, hidden),
        (rows, hidden),
        (VEC, rows),
        (3, rows, columns),
        (rows, columns),
        (rows, hidden),
        (rows, hidden),
        (VEC, rows),
        (VEC, rows),
        (3, rows),
        (3, columns),
        (1, columns),
        (1, rows),
        (1, rows),
        (1, hidden),
        (1, hidden),
        (1, rows),
    ]
    far = (*values, vectors, *weights)
    anywhere = pl.BlockSpec(memory_space=pl.ANY)
    inside = pl.BlockSpec(memory_space=pltpu.VMEM)
    return pl.pallas_call(
        functools.partial(update_kernel, layout, width, long),
        name="update_weights",
        out_shape=[jax.ShapeDtypeStruct(shape, full) for shape in shapes],
        in_specs=[anywhere] * (2 + len(far)),
        out_specs=[anywhere] * 2 + [inside] * (len(shapes) - 2),
        scratch_shapes=[
            *(pltpu.VMEM(array.shape, full) for array in far),
            pltpu.SemaphoreType.DMA((2 + len(far),)),
        ],
        compiler_params=pltpu.CompilerParams(vmem_limit_bytes=48 << 20),
    )(*results, *far)


def on_device(
    inputs,
    cotangent,
    token_mask,
    w_qkv,
    w_out,
    w_fc1,
    w_fc2,
    vectors,
    qkv_row,
    qkv_col,
    out_row,
    out_col,
    fc1_row,
    fc1_col,
    fc2_row,
    fc2_col,
    vec_second,
):
    tensor_count = lax.axis_size("tensor")
    dims = grid_of(lax.axis_size("fsdp"))
    width = inputs.shape[1]
    own_rows, columns = w_qkv.shape[1:]
    hidden = w_fc1.shape[1]
    weights = (w_qkv, w_out.T, w_fc1, w_fc2.T)
    (
        weight_qkv,
        _,
        weight_out,
        *_,
        block_out,
        grad_middle,
        back_one,
        projected,
        mixed_rows,
        low_one,
        grad_one,
        grad_two,
        table,
        vec_sums,
        pre_sums,
        bias_column,
    ) = forward(dims, tensor_count, inputs, cotangent, token_mask, vectors, weights)
    layout = Layout(columns, hidden, ("two", "one", "out", "qkv", "vec"))
    row_states = (qkv_row, out_col[None], fc1_row[None], fc2_col[None])
    col_states = (qkv_col, out_row[None], fc1_col[None], fc2_row[None])
    input_grad, *values = backward(
        dims,
        tensor_count,
        layout,
        (grad_two, grad_one, weight_qkv, weight_out, projected, inputs, grad_middle),
        (mixed_rows, low_one, back_one, bias_column, table, vec_sums, pre_sums),
        weights,
        (*row_states, *col_states, vec_second, vectors),
    )
    outs = update_weights(
        layout, width, FF, columns, hidden, own_rows, (block_out, input_grad), values, vectors, weights
    )
    outs = [out.reshape(-1) if out.shape[0] == 1 else out for out in outs]
    for at in (3, 5, 8, 10):
        outs[at] = outs[at].T
    return (*outs[:12], *outs[13:], outs[12])


def solution(mesh):
    in_specs = (
        P(("fsdp", "tensor"), None),
        P(("fsdp", "tensor"), None),
        P("fsdp", None),
        P(None, "fsdp", "tensor"),
        P("tensor", "fsdp"),
        P("fsdp", "tensor"),
        P("tensor", "fsdp"),
        P(None, "fsdp"),
        P(None, "fsdp"),
        P(None, "tensor"),
        P("tensor"),
        P("fsdp"),
        P("fsdp"),
        P("tensor"),
        P("tensor"),
        P("fsdp"),
        P(None, "fsdp"),
    )
    out_specs = (
        P(("fsdp", "tensor"), None),
        P(("fsdp", "tensor"), None),
        P(None, "fsdp", "tensor"),
        P("tensor", "fsdp"),
        P("fsdp", "tensor"),
        P("tensor", "fsdp"),
        P(None, "fsdp"),
        P(None, "fsdp", "tensor"),
        P("tensor", "fsdp"),
        P("fsdp", "tensor"),
        P("tensor", "fsdp"),
        P(None, "fsdp"),
        P(None, "fsdp"),
        P(None, "tensor"),
        P("tensor"),
        P("fsdp"),
        P("fsdp"),
        P("tensor"),
        P("tensor"),
        P("fsdp"),
        P(None, "fsdp"),
    )
    return jax.shard_map(
        on_device, mesh=mesh, in_specs=in_specs, out_specs=out_specs, check_vma=False
    )
```

```python
import functools

import jax
import jax.numpy as jnp
from jax import lax
from jax.experimental import pallas as pl
from jax.experimental.pallas import tpu as pltpu
from jax.sharding import PartitionSpec as P

HEAD_DIM = 64
FF = 4096
STEP = 20
VEC = 12
LANES = 128

EPS_NORM = 1e-05
EPS_ONE = 1e-30
CLIP_LEVEL = 1.0
LEARN_RATE = 0.5
MESH = pl.DeviceIdType.MESH
LOG2E = 1.4426950408889634
CONTRACT_LAST = (((1,), (1,)), ((), ()))


def grid_of(count):
    return {16: (4, 2, 2), 32: (2, 4, 4)}.get(count, (count, 1, 1))


class Place:
    def __init__(self, dims, tensor):
        self.dims = dims
        self.tensor = tensor
        fsdp = lax.axis_index("fsdp")
        _, ny, nx = dims
        self.at = (fsdp // (ny * nx), (fsdp // nx) % ny, fsdp % nx)
        self.rank = lax.axis_index("tensor")

    def moved(self, axis, step):
        place = list(self.at) + [self.rank]
        size = (*self.dims, self.tensor)[axis]
        place[axis] = lax.rem(place[axis] + step + size, size)
        return tuple(place)

    def device(self, place):
        z, y, x, rank = place
        return {"fsdp": (z * self.dims[1] + y) * self.dims[2] + x, "tensor": rank}

    def size(self, axis):
        return (*self.dims, self.tensor)[axis]

    def peers(self, *axes):
        places = [()]
        for axis in axes:
            places = [(*steps, step) for steps in places for step in range(self.size(axis))]
        found = []
        for steps in places[1:]:
            place = list(self.at) + [self.rank]
            for axis, step in zip(axes, steps):
                place[axis] = lax.rem(place[axis] + step, self.size(axis))
            found.append(self.device(tuple(place)))
        return found

    def barrier(self, groups):
        sem = pltpu.get_barrier_semaphore()
        count = 0
        for axes in groups:
            for device in self.peers(*axes):
                pl.semaphore_signal(sem, inc=1, device_id=device, device_id_type=MESH)
                count += 1
        if count:
            pl.semaphore_wait(sem, count)


def norm_rows(values):
    average = jnp.mean(values, axis=1, keepdims=True)
    center = values - average
    inverse = lax.rsqrt(jnp.mean(center * center, axis=1, keepdims=True) + EPS_NORM)
    return center * inverse, inverse


def dot(left, right, dims=(((1,), (0,)), ((), ()))):
    return lax.dot_general(left, right, dims, preferred_element_type=jnp.float32)


def turn(source, target):
    for start in range(0, source.shape[1], LANES):
        target[pl.ds(start, LANES), :] = source[:, pl.ds(start, LANES)].T


def attend_pair(heads, bias):
    mixed = []
    for head in range(2):
        query, key, value = (
            heads[:, kind * LANES + head * HEAD_DIM : kind * LANES + (head + 1) * HEAD_DIM] for kind in range(3)
        )
        scores = dot(query, key, CONTRACT_LAST) * (HEAD_DIM ** (-0.5) * LOG2E) + bias
        raised = jnp.exp2(scores - jnp.max(scores, axis=1, keepdims=True))
        summed = jnp.sum(raised, axis=1, keepdims=True)
        attention = (raised * (1.0 / summed)).astype(jnp.bfloat16)
        mixed.append(dot(attention, value).astype(jnp.bfloat16))
    return jnp.concatenate(mixed, axis=1)


class Steps:
    def __init__(self):
        self.steps = {}

    def add(self, name, run, time, rank, after=(), waits=(), starts=()):
        self.steps[name] = (run, time, rank, tuple(after), tuple(waits), tuple(starts))

    def arrange(self):
        now, free, arrival, done, order = 0.0, {}, {}, set(), []
        left = list(self.steps)
        while left:
            best, soonest = None, None
            for name in left:
                _, time, rank, after, waits, _ = self.steps[name]
                if any(other not in done for other in after) or any(wait not in arrival for wait in waits):
                    continue
                ready = max([arrival[wait] for wait in waits], default=0.0)
                if ready <= now:
                    if best is None or rank < self.steps[best][2]:
                        best = name
                elif soonest is None or ready < soonest:
                    soonest = ready
            if best is None:
                now = soonest
                continue
            _, time, _, _, _, starts = self.steps[best]
            now += time
            for transfer, link, length in starts:
                begin = max(now, free.get(link, 0.0))
                free[link] = begin + length
                arrival[transfer] = begin + length + LATENCY
            done.add(best)
            left.remove(best)
            order.append(best)
        return order, now

    def run(self):
        for name in self.arrange()[0]:
            self.steps[name][0]()


class Gather:
    def __init__(self, here, pack_ref, outs, parts, local_sem, send_sem, recv_sem):
        self.here = here
        self.pack = pack_ref
        self.outs = outs
        self.rows = pack_ref.shape[0]
        self.parts = parts
        self.sems = (local_sem, send_sem, recv_sem)
        self.own = (*here.at, here.rank)
        self.sent = []

    def region(self, item, part, place, free):
        out, _, chunk, _ = self.parts[item]
        index = tuple(slice(None) if a in free else place[a] for a in range(3))
        lead = () if chunk is None else (place[3], chunk)
        return self.outs[out].at[(*lead, *index, part)]

    def shard(self, item):
        _, offset, _, size = self.parts[item]
        return self.pack.at[:, pl.ds(offset, size)]

    def phases(self, item):
        return 3 if self.parts[item][2] is None else 4

    def moves(self, phase):
        whole, half = pl.ds(0, self.rows), self.rows // 2
        first, second = pl.ds(0, half), pl.ds(half, half)
        return (
            ((0, (), whole),),
            ((1, (0,), first), (2, (0,), second)),
            ((2, (0, 1), first), (1, (0, 2), second)),
            ((3, (0, 1, 2), whole),),
        )[phase]

    def copies(self, item, phase, landing):
        here = self.here
        found = []
        for axis, free, part in self.moves(phase):
            for step in range(1, here.size(axis)):
                own = self.region(item, part, self.own, free)
                if landing:
                    src = dst = self.region(item, part, here.moved(axis, -step), free)
                else:
                    src, dst = (self.shard(item) if phase == 0 else own), own
                at = len(found)
                found.append(
                    pltpu.make_async_remote_copy(
                        src_ref=src,
                        dst_ref=dst,
                        send_sem=self.sems[1].at[item, phase, at],
                        recv_sem=self.sems[2].at[item, phase, at],
                        device_id=here.device(here.moved(axis, step)),
                        device_id_type=MESH,
                    )
                )
        return found

    def keep(self, item):
        whole = pl.ds(0, self.rows)
        return pltpu.make_async_copy(
            self.shard(item), self.region(item, whole, self.own, ()), self.sems[0].at[item]
        )

    def advance(self, item, phase):
        if phase:
            for copy in self.copies(item, phase - 1, True):
                copy.wait_recv()
        if phase == 0:
            self.keep(item).start()
        if phase == 1:
            self.keep(item).wait()
        if phase < self.phases(item):
            for copy in self.copies(item, phase, False):
                copy.start()
                self.sent.append(copy)

    def finish(self):
        for copy in self.sent:
            copy.wait_send()


BLOCK = 512
DEPTH = 4
LATENCY = 1.5
UNIT = 20.0
CORE_UNIT = 40.0
PUMP = 0.4


def forward_kernel(dims, tensor, parts, tasks, *refs):
    input_ref, top_ref, mask_ref, vector_ref = refs[:4]
    own_weights = refs[4:8]
    outs, land = refs[8:13], refs[13:15]
    weight_qkv, weight_vec, weight_out, weight_one, weight_two = outs
    (
        block_out,
        grad_middle,
        back_one,
        projected,
        mixed,
        low_one,
        grad_one,
        grad_two,
        table,
        vec_sums,
        pre_sums,
        bias_column,
    ) = refs[15:27]
    (
        pack,
        keep_ref,
        square,
        vec_buf,
        qkv_buf,
        head_stage,
        out_buf,
        one_buf,
        two_buf,
        low_two,
        low_two_turned,
        back_two,
        back_two_turned,
        grad_low_two,
        hidden_bias,
        head_bias,
        one_stage,
        two_stage,
        one_keep,
        two_keep,
        other,
        active,
        grad_pre,
        load_sem,
        store_sem,
        keep_sem,
        head_sem,
        land_sem,
        local_sem,
        send_sem,
        recv_sem,
    ) = refs[27:]
    here = Place(dims, tensor)
    gather = Gather(here, pack, outs, parts, local_sem, send_sem, recv_sem)
    rows, width = input_ref.shape
    own_rows = pack.shape[0]
    per_rank = weight_qkv.shape[1]
    low = jnp.bfloat16
    step_rows = LANES

    def fill_pack():
        base = 0
        for pair in range(per_rank):
            for kind in range(3):
                part = own_weights[0][kind, :, pl.ds(pair * LANES, LANES)]
                pack[:, pl.ds(base, LANES)] = part.astype(low)
                base += LANES
        square[...] = jnp.zeros_like(square)
        square[pl.ds(0, VEC), :] = vector_ref[...]
        pack[:, pl.ds(base, LANES)] = square[...].T.astype(low)
        base += LANES
        for ref in own_weights[1:]:
            pack[:, pl.ds(base, ref.shape[1])] = ref[...].astype(low)
            base += ref.shape[1]

    def mask_row():
        return mask_ref[pl.ds(here.rank, 1), :].astype(jnp.float32)

    def mask_bias(keep):
        return jnp.where(keep > 0.0, 0.0, -1e30)

    def first_masks():
        turned = jnp.broadcast_to(mask_row(), (LANES, rows)).T
        keep_ref[...] = turned[:, 0:1]
        bias_column[...] = mask_bias(turned[:, 0:1])

    def row_steps(body, carry):
        return lax.fori_loop(
            0, rows // step_rows, lambda at, c: body(pl.ds(pl.multiple_of(at * step_rows, step_rows), step_rows), c), carry
        )

    def load(source, buffer, sem):
        return pltpu.make_async_copy(source, buffer, sem)

    def first_norm():
        first_masks()
        copy = load(weight_vec, vec_buf, load_sem.at[7])
        copy.start()
        copy.wait()
        whole = vec_buf[...].reshape(width, LANES).astype(jnp.float32).T
        table[...] = whole[:16]
        for at in range(VEC - 8):
            hidden_bias[:, pl.ds(at * width, width)] = whole[7 + at : 8 + at]
        for pair in range(width // LANES):
            for kind, row in ((0, 2), (2, 3)):
                head_bias[:, pl.ds((pair * 3 + kind) * LANES, LANES)] = whole[
                    row : row + 1, pair * LANES : (pair + 1) * LANES
                ]
            head_bias[:, pl.ds((pair * 3 + 1) * LANES, LANES)] = jnp.zeros((1, LANES), jnp.float32)

        def body(part, carry):
            normed, _ = norm_rows(input_ref[part, :])
            low_one[part, :] = (normed * table[0:1, :] + table[1:2, :]).astype(low)
            back_two[part, :] = (top_ref[part, :].astype(jnp.float32) * keep_ref[part, :]).astype(low)
            return carry

        row_steps(body, 0)
        turn(back_two, back_two_turned)

    def head_store(pair, slot):
        column = pl.ds(pl.multiple_of(pair * 3 * LANES, LANES), 3 * LANES)
        return pltpu.make_async_copy(head_stage.at[slot], projected.at[:, column], head_sem.at[slot])

    def pair_of(at):
        turn_at, place = divmod(at, tensor)
        return lax.rem(here.rank + place, tensor) * per_rank + turn_at

    def head_load(at):
        turn_at, place = divmod(at, tensor)
        source = weight_qkv.at[lax.rem(here.rank + place, tensor), turn_at]
        return load(source, qkv_buf.at[at % 2], load_sem.at[at % 2])

    def heads(at):
        head_load(at).wait()
        pair = pair_of(at)
        slot = at % 2
        column = pl.ds(pl.multiple_of(pair * 3 * LANES, LANES), 3 * LANES)
        weight = qkv_buf[slot].reshape(width, 3 * LANES)
        value = (dot(low_one[...], weight) + head_bias[:, column]).astype(low)
        if at > 1:
            head_store(pair, slot).wait()
        head_stage[slot] = value
        head_store(pair, slot).start()
        mixed[:, pl.ds(pl.multiple_of(pair * LANES, LANES), LANES)] = attend_pair(value, mask_bias(mask_row()))

    def out_load():
        return [
            load(weight_out.at[rank, 0], out_buf.at[rank], load_sem.at[2]) for rank in range(tensor)
        ]

    def second_norm():
        for copy in out_load():
            copy.wait()
        columns = width // tensor
        for rank in range(tensor):
            weight = out_buf[rank].reshape(width, columns)
            term = dot(mixed[:, pl.ds(rank * columns, columns)], weight, CONTRACT_LAST)
            if rank == 0:
                grad_middle[...] = term
            else:
                grad_middle[...] += term

        def body(part, carry):
            middle = input_ref[part, :] + (grad_middle[part, :] + table[4:5, :]) * keep_ref[part, :]
            grad_middle[part, :] = middle
            normed, _ = norm_rows(middle)
            low_two[part, :] = (normed * table[5:6, :] + table[6:7, :]).astype(low)
            return carry

        row_steps(body, 0)
        turn(low_two, low_two_turned)

    stages = (one_stage, two_stage)
    keeps = (one_keep, two_keep)

    def hand_over(at):
        chunk, place = divmod(at, tensor)
        target = (*here.at, lax.rem(here.rank + place + 1, tensor))
        return [
            pltpu.make_async_remote_copy(
                src_ref=stages[which].at[at % 2],
                dst_ref=land[which].at[place, chunk],
                send_sem=store_sem.at[which, at % 2],
                recv_sem=land_sem.at[which, place, chunk],
                device_id=here.device(target),
                device_id_type=MESH,
            )
            for which in range(2)
        ]

    def keep_store(chunk):
        return [
            pltpu.make_async_copy(
                keeps[which].at[chunk % 2],
                out.at[chunk],
                keep_sem.at[which, chunk % 2],
            )
            for which, out in enumerate((grad_one, grad_two))
        ]

    def hidden_column(at):
        chunk, place = divmod(at, tensor)
        base = (lax.rem(here.rank + place + 1, tensor) * weight_one.shape[1] + chunk) * BLOCK
        return pl.ds(pl.multiple_of(base, LANES), BLOCK)

    def hidden_load(at):
        chunk, place = divmod(at, tensor)
        rank = lax.rem(here.rank + place + 1, tensor)
        return [
            load(source.at[rank, chunk], buffer.at[at % 2], load_sem.at[3 + 2 * which + at % 2])
            for which, (source, buffer) in enumerate(((weight_one, one_buf), (weight_two, two_buf)))
        ]

    staged = {}

    def hidden(at):
        chunk, place = divmod(at, tensor)
        column = hidden_column(at)
        for copy in hidden_load(at):
            copy.wait()
        half = rows // 2
        bias = hidden_bias[:, column]

        def body(turn_at, total):
            part = pl.ds(pl.multiple_of(turn_at * half, half), half)
            one = one_buf[at % 2].reshape(width, BLOCK)
            two = two_buf[at % 2].reshape(width, BLOCK)
            preact = dot(low_two[part, :], one) + bias
            gate = jax.nn.sigmoid(1.702 * preact)
            value = (preact * gate).astype(low)
            active[part, :] = value
            derivative = gate + 1.702 * preact * gate * (1.0 - gate)
            grad = (dot(back_two[part, :], two) * derivative).astype(low)
            grad_pre[part, :] = grad
            if at == 0:
                block_out[part, :] = dot(value, two, CONTRACT_LAST)
                grad_low_two[part, :] = dot(grad, one, CONTRACT_LAST)
            else:
                block_out[part, :] += dot(value, two, CONTRACT_LAST)
                grad_low_two[part, :] += dot(grad, one, CONTRACT_LAST)
            return total + jnp.sum(grad.astype(jnp.float32), axis=0, keepdims=True)

        pre_sums[:, column] = lax.fori_loop(0, 2, body, jnp.zeros((1, BLOCK), jnp.float32))
        mine = place == tensor - 1
        if mine:
            targets = [ref.at[chunk % 2] for ref in keeps]
            if chunk > 1:
                for copy in keep_store(chunk):
                    copy.wait()
        else:
            targets = [ref.at[at % 2] for ref in stages]
            for copy in staged.pop(at % 2, ()):
                copy.wait_send()
        for target, left, right in (
            (targets[0], low_two_turned, grad_pre),
            (targets[1], back_two_turned, active),
        ):
            target[...] = dot(left[...], right[...]).astype(low).reshape(*target.shape)
        if not mine:
            staged[at % 2] = hand_over(at)
            for copy in staged[at % 2]:
                copy.start()

    def combine(chunk):
        for place in range(tensor - 1):
            for which, copy in enumerate(hand_over(chunk * tensor + place)):
                copy.wait_recv()
                fetch = load(land[which].at[place, chunk], other, load_sem.at[7])
                fetch.start()
                fetch.wait()
                keeps[which][chunk % 2] = keeps[which][chunk % 2] + other[...]
        for copy in keep_store(chunk):
            copy.start()

    def last_norm():
        def body(part, sums):
            middle = grad_middle[part, :]
            keep = keep_ref[part, :]
            top = top_ref[part, :].astype(jnp.float32)
            block_out[part, :] = middle + (block_out[part, :] + table[VEC - 1 : VEC, :]) * keep
            normed, inverse = norm_rows(middle)
            grad_low = grad_low_two[part, :]
            scaled = grad_low * table[5:6, :]
            first = jnp.mean(scaled, axis=1, keepdims=True)
            second = jnp.mean(scaled * normed, axis=1, keepdims=True)
            grad = top + inverse * (scaled - first - normed * second)
            grad_middle[part, :] = grad
            masked = grad * keep
            back_one[part, :] = masked.astype(low)
            terms = (masked, grad_low * normed, grad_low, top * keep)
            return tuple(old + jnp.sum(term, axis=0, keepdims=True) for old, term in zip(sums, terms))

        zero = jnp.zeros((1, width), jnp.float32)
        for at, value in enumerate(row_steps(body, (zero,) * 4)):
            vec_sums[at : at + 1, :] = value

    fill_pack()
    here.barrier(((0,), (1,), (2,), (3,)))
    steps = Steps()
    whole = sum(part[3] for part in parts)
    nz, ny, nx = dims

    def lengths(item, phase):
        share = parts[item][3] / whole
        return (
            (share * UNIT * nz, "z"),
            (share * UNIT * nz / 2, "xy"),
            (share * UNIT * nz, "xy"),
            (share * CORE_UNIT, "core"),
        )[phase]

    for item, part in enumerate(parts):
        phases = gather.phases(item)
        for phase in range(phases + 1):
            after = [("copy", item, phase - 1)] if phase else []
            if phase == 0 and item >= DEPTH:
                after = [("copy", item - DEPTH, 1)]
            length, link = lengths(item, min(phase, 3))
            steps.add(
                ("copy", item, phase),
                functools.partial(gather.advance, item, phase),
                PUMP,
                0.5 if phase == 0 else 0.0,
                after,
                [(item, phase - 1)] if phase else [],
                [((item, phase), link, length)] if phase < phases else [],
            )

    def landed(items):
        return [("copy", item, gather.phases(item)) for item in items]

    def start(copies):
        for copy in copies:
            copy.start()

    previous = None
    head_count, block_count = per_rank * tensor, FF // BLOCK
    for name, at, items in tasks:
        after = landed(items) + ([previous] if previous else [])
        begin, run, time = {
            "norm": (None, first_norm, 5.0),
            "heads": (lambda at=at: head_load(at).start(), lambda at=at: heads(at), 3.0),
            "out": (lambda: start(out_load()), second_norm, 5.0),
            "hidden": (lambda at=at: start(hidden_load(at)), lambda at=at: hidden(at), 5.5),
        }[name]
        if begin is not None:
            first = landed(items)
            if at > 1:
                first.append((name, at - 2))
            steps.add(("load", name, at), begin, 0.1, 0.2, first)
            after.append(("load", name, at))
        mine = name == "hidden" and at % tensor == tensor - 1
        chunk = at // tensor
        if mine and chunk > 1:
            after.append(("combine", chunk - 2))
        starts = []
        if name == "hidden" and not mine:
            starts = [(("hand", at), "core", CORE_UNIT / len(parts))]
        steps.add((name, at), run, time, 1.0, after, (), starts)
        if mine:
            waits = [("hand", chunk * tensor + place) for place in range(tensor - 1)]
            steps.add(
                ("combine", chunk), functools.partial(combine, chunk), 2.0, 0.8, [(name, at)], waits
            )
        previous = (name, at)
    steps.add(("last", 0), last_norm, 4.0, 0.9, [previous])
    steps.run()
    for slot in range(min(2, head_count)):
        head_store(0, slot).wait()
    for chunk in range(min(2, block_count // tensor)):
        for copy in keep_store(chunk):
            copy.wait()
    for copies in staged.values():
        for copy in copies:
            copy.wait_send()
    gather.finish()


def forward(dims, tensor, inputs, cotangent, token_mask, vectors, weights):
    own_rows, columns = weights[0].shape[1:]
    hidden = weights[2].shape[1]
    rows, width = inputs.shape
    low, full = jnp.bfloat16, jnp.float32
    widths = (3 * columns, LANES, columns, hidden, hidden)
    offsets = [sum(widths[:at]) for at in range(5)]
    per_rank = columns // LANES
    parts = [(1, offsets[1], None, LANES)]
    tasks = [("norm", 0, (0,))]
    for at in range(per_rank):
        size = 3 * LANES
        parts.append((0, offsets[0] + at * size, at, size))
        tasks += [("heads", at * tensor + place, (len(parts) - 1,)) for place in range(tensor)]
    tasks.append(("out", 0, (len(parts),)))
    parts.append((2, offsets[2], 0, columns))
    for block in range(hidden // BLOCK):
        needed = (len(parts), len(parts) + 1)
        parts += [(which, offsets[which] + block * BLOCK, block, BLOCK) for which in (3, 4)]
        tasks += [("hidden", block * tensor + place, needed) for place in range(tensor)]
    count = len(parts)
    peers = max(1, dims[0] - 1, dims[1] + dims[2] - 2, tensor - 1)
    anywhere = pl.BlockSpec(memory_space=pl.ANY)
    inside = pl.BlockSpec(memory_space=pltpu.VMEM)
    block = (*dims, own_rows, BLOCK)
    chunks = hidden // BLOCK

    def shape(kind, *size):
        return jax.ShapeDtypeStruct(size, kind)

    return pl.pallas_call(
        functools.partial(forward_kernel, dims, tensor, tuple(parts), tuple(tasks)),
        name="forward",
        out_shape=[
            shape(low, tensor, per_rank, *dims, own_rows, 3 * LANES),
            shape(low, *dims, own_rows, LANES),
            shape(low, tensor, 1, *dims, own_rows, columns),
            *[shape(low, tensor, chunks, *block)] * 2,
            *[shape(low, max(1, tensor - 1), chunks, *block)] * 2,
            shape(full, rows, width),
            shape(full, rows, width),
            shape(low, rows, width),
            shape(low, rows, 3 * width),
            shape(low, rows, width),
            shape(low, rows, width),
            *[shape(low, chunks, *block)] * 2,
            shape(full, 16, width),
            shape(full, 8, width),
            shape(full, 1, hidden * tensor),
            shape(full, rows, 1),
        ],
        in_specs=[inside] * 8,
        out_specs=[anywhere] * 7 + [inside] * 3 + [anywhere] + [inside] * 2 + [anywhere] * 2 + [inside] * 4,
        scratch_shapes=[
            pltpu.VMEM((own_rows, sum(widths)), low),
            pltpu.VMEM((rows, 1), full),
            pltpu.VMEM((LANES, own_rows), full),
            pltpu.VMEM((*dims, own_rows, LANES), low),
            pltpu.VMEM((2, *dims, own_rows, 3 * LANES), low),
            pltpu.VMEM((2, rows, 3 * LANES), low),
            pltpu.VMEM((tensor, *dims, own_rows, columns), low),
            pltpu.VMEM((2, *block), low),
            pltpu.VMEM((2, *block), low),
            pltpu.VMEM((rows, width), low),
            pltpu.VMEM((width, rows), low),
            pltpu.VMEM((rows, width), low),
            pltpu.VMEM((width, rows), low),
            pltpu.VMEM((rows, width), full),
            pltpu.VMEM((1, hidden * tensor), full),
            pltpu.VMEM((1, 3 * width), full),
            pltpu.VMEM((2, *block), low),
            pltpu.VMEM((2, *block), low),
            pltpu.VMEM((2, *block), low),
            pltpu.VMEM((2, *block), low),
            pltpu.VMEM(block, low),
            pltpu.VMEM((rows, BLOCK), low),
            pltpu.VMEM((rows, BLOCK), low),
            pltpu.SemaphoreType.DMA((8,)),
            pltpu.SemaphoreType.DMA((2, 2)),
            pltpu.SemaphoreType.DMA((2, 2)),
            pltpu.SemaphoreType.DMA((2,)),
            pltpu.SemaphoreType.DMA((2, max(1, tensor - 1), chunks)),
            pltpu.SemaphoreType.DMA((count,)),
            pltpu.SemaphoreType.DMA((count, 4, peers)),
            pltpu.SemaphoreType.DMA((count, 4, peers)),
        ],
        compiler_params=pltpu.CompilerParams(
            collective_id=0, has_side_effects=True, vmem_limit_bytes=62 << 20
        ),
    )(inputs, cotangent, token_mask, vectors, *weights)


class Layout:
    def __init__(self, columns, hidden, order):
        sizes = {"qkv": 3 * columns, "out": columns, "one": hidden, "two": hidden, "vec": LANES}
        self.order = order
        self.sizes = sizes
        self.start = {}
        at = 0
        for name in order:
            self.start[name] = at
            at += sizes[name]
        self.total = at
        self.columns = columns

    def span(self, name):
        return (self.start[name], self.sizes[name])

    def matrices(self):
        base = self.start["qkv"]
        pairs = range(self.columns // LANES)
        spans = [[(base + (pair * 3 + at) * LANES, LANES) for pair in pairs] for at in range(3)]
        return spans + [[self.span(name)] for name in ("out", "one", "two")]


def pick(values, lane):
    row = jnp.zeros((1, LANES), jnp.float32)
    for at, value in enumerate(values):
        row = jnp.where(lane == at, value, row)
    return row


def total_of(values):
    return jnp.sum(jnp.sum(values, axis=1, keepdims=True), axis=0, keepdims=True)


def attend_pair_back(heads, bias, grads):
    parts = ([], [], [])
    for head in range(2):
        query, key, value = (
            heads[:, kind * LANES + head * HEAD_DIM : kind * LANES + (head + 1) * HEAD_DIM] for kind in range(3)
        )
        grad = grads[:, head * HEAD_DIM : (head + 1) * HEAD_DIM]
        scores = dot(key, query, CONTRACT_LAST) * (HEAD_DIM ** (-0.5) * LOG2E) + bias
        raised = jnp.exp2(scores - jnp.max(scores, axis=0, keepdims=True))
        attention = raised * (1.0 / jnp.sum(raised, axis=0, keepdims=True))
        grad_value = dot(attention.astype(jnp.bfloat16), grad)
        grad_attention = dot(value, grad, CONTRACT_LAST)
        weighted = jnp.sum(attention * grad_attention, axis=0, keepdims=True)
        grad_scores = (attention * (grad_attention - weighted) * HEAD_DIM ** (-0.5)).astype(jnp.bfloat16)
        grad_key = dot(grad_scores, query)
        grad_query = dot(key.T, grad_scores).T
        for kind, part in enumerate((grad_query, grad_key, grad_value)):
            parts[kind].append(part.astype(jnp.bfloat16))
    return jnp.concatenate([piece for kind in parts for piece in kind], axis=1)


def backward_kernel(dims, tensor, items, layout, *refs):
    (
        sum_two,
        sum_one,
        weight_qkv,
        weight_out,
        projected,
        input_ref,
        middle_ref,
        mixed,
        low_one,
        back_one,
        bias_ref,
        table,
        vec_sums,
        pre_sums,
    ) = refs[:14]
    weights = refs[14:18]
    row_states, col_states = refs[18:22], refs[22:26]
    second_ref, vector_ref = refs[26:28]
    input_grad, total_ref, col_new_ref, row_new_ref, second_new_ref, sums_ref = refs[28:34]
    (
        own,
        from_core,
        one_x,
        one_y,
        two_y,
        two_x,
        from_z,
        col_sum,
        col_in,
        row_sum,
        row_in,
        small,
        small_in,
        square,
        turned,
        low_turned,
        back_turned,
        grad_mixed,
        out_buf,
        qkv_buf,
        head_buf,
        row_buf,
        out_stage,
        qkv_stage,
        vec_stage,
        head_sums,
        table_grad_ref,
        load_sem,
        stage_sem,
        core_sem,
        local_sem,
        send_sem,
        recv_sem,
        sum_send,
        sum_recv,
    ) = refs[34:]
    here = Place(dims, tensor)
    nz, ny, nx = dims
    low = jnp.bfloat16
    own_rows = own.shape[3]
    half_rows = own_rows // 2
    rows, width = input_grad.shape
    own_place = (*here.at, here.rank)
    count = len(items)
    core_start = layout.start["out"]

    def columns(item):
        _, start, size, _ = items[item]
        return pl.ds(start, size)

    def core_columns(item):
        _, start, size, _ = items[item]
        return pl.ds(start - core_start, size)

    def moves(phase):
        first, second = pl.ds(0, half_rows), pl.ds(half_rows, half_rows)
        return (
            (),
            ((2, (2,), first, one_x, 0), (1, (1,), second, one_y, nx - 1)),
            ((1, (1, 2), first, two_y, 0), (2, (1, 2), second, two_x, ny - 1)),
            ((0, (0, 1, 2), pl.ds(0, own_rows), from_z, 0),),
        )[phase]

    def copies(item, phase):
        found = []
        for axis, fixed, part, landing, _ in moves(phase):
            for step in range(1, here.size(axis)):
                target = here.moved(axis, step)
                index = tuple(target[a] if a in fixed else slice(None) for a in range(3))
                free = (slice(None),) * (3 - len(fixed))
                at = len(found)
                found.append(
                    pltpu.make_async_remote_copy(
                        src_ref=own.at[(*index, part, columns(item))],
                        dst_ref=landing.at[(step - 1, *free, slice(None), columns(item))],
                        send_sem=send_sem.at[item, phase, at],
                        recv_sem=recv_sem.at[item, phase, at],
                        device_id=here.device(target),
                        device_id_type=MESH,
                    )
                )
        return found

    def add_core(item):
        def body(at, carry):
            z, y, x = at // (ny * nx), at // nx % ny, at % nx
            value = own[z, y, x, :, columns(item)]
            for step in range(tensor - 1):
                value = value + from_core[step, z, y, x, :, core_columns(item)]
            own[z, y, x, :, columns(item)] = value
            return carry

        if tensor > 1:
            lax.fori_loop(0, nz * ny * nx, body, 0)

    def add_in(item, phase):
        column = columns(item)
        for axis, fixed, part, landing, _ in moves(phase):
            steps = here.size(axis) - 1
            if phase == 3:
                value = own[(*here.at, part, column)].astype(jnp.float32)
                for step in range(steps):
                    value = value + landing[step, :, column].astype(jnp.float32)
                total_ref[:, column] = value
                continue
            if steps == 0:
                continue
            free = [a for a in range(3) if a not in fixed]
            sizes = [dims[a] for a in free]
            loops = 1
            for size in sizes:
                loops *= size

            def body(at, carry):
                place = list(here.at)
                inner = []
                rest = at
                for axis_at, size in reversed(list(zip(free, sizes))):
                    place[axis_at] = rest % size
                    inner.insert(0, rest % size)
                    rest = rest // size
                where = (*place, part, column)
                value = own[where]
                for step in range(steps):
                    value = value + landing[(step, *inner, slice(None), column)]
                own[where] = value
                return carry

            lax.fori_loop(0, loops, body, 0)

    sent = []

    def exchange(kind, phase, axes, buffer, landing):
        moved = []
        for at, device in enumerate(here.peers(*axes)):
            copy = pltpu.make_async_remote_copy(
                src_ref=buffer.at[phase],
                dst_ref=landing.at[phase, at],
                send_sem=sum_send.at[kind, phase, at],
                recv_sem=sum_recv.at[kind, phase, at],
                device_id=device,
                device_id_type=MESH,
            )
            copy.start()
            moved.append(copy)
        sent.extend(moved)

        def finish():
            value = buffer[phase]
            for at, copy in enumerate(moved):
                copy.wait_recv()
                value = value + landing[phase, at]
            buffer[phase + 1] = value

        return finish

    def hand_over(item, step, source, sem):
        return pltpu.make_async_remote_copy(
            src_ref=source,
            dst_ref=from_core.at[step - 1, :, :, :, :, core_columns(item)],
            send_sem=sem,
            recv_sem=core_sem.at[item, step - 1],
            device_id=here.device(here.moved(3, step)),
            device_id_type=MESH,
        )

    arriving = {}

    def keep_own(item, value):
        own[:, :, :, :, columns(item)] = value.reshape(nz, ny, nx, own_rows, value.shape[1])

    out_items = [at for at, item in enumerate(items) if item[0] == "out"]
    qkv_items = [at for at, item in enumerate(items) if item[0] == "qkv"]
    vec_item = count - 1
    per_rank = len(qkv_items)
    steps_in_all = per_rank * tensor

    def rank_at(step):
        return lax.rem(here.rank + step, tensor)

    def pair_loads(at):
        turn_at, place = divmod(at, tensor)
        pair = rank_at(place + 1) * per_rank + turn_at
        column = pl.ds(pl.multiple_of(pair * 3 * LANES, LANES), 3 * LANES)
        near = at % 2
        return pair, column, [
            pltpu.make_async_copy(
                weight_qkv.at[rank_at(place + 1), turn_at], qkv_buf.at[near], load_sem.at[0, near]
            ),
            pltpu.make_async_copy(projected.at[:, column], head_buf.at[near], load_sem.at[1, near]),
        ]

    def out_task():
        fetch = [
            pltpu.make_async_copy(weight_out.at[rank, 0], out_buf.at[rank], load_sem.at[2, 0])
            for rank in range(tensor)
        ]
        for copy in fetch:
            copy.start()
        turn(back_one, back_turned)
        for copy in pair_loads(0)[2]:
            copy.start()
        size = out_stage.shape[5]
        item = out_items[0]
        for step in range(1, tensor + 1):
            column = pl.ds(pl.multiple_of(rank_at(step) * size, LANES), size)
            value = dot(back_turned[...], mixed[:, column]).astype(low)
            if step < tensor:
                out_stage[step - 1] = value.reshape(nz, ny, nx, own_rows, size)
                copy = hand_over(item, step, out_stage.at[step - 1], stage_sem.at[item, step - 1])
                copy.start()
                sent.append(copy)
                arriving.setdefault(item, []).append(copy)
            else:
                keep_own(item, value)
        for copy in fetch:
            copy.wait()
        for rank in range(tensor):
            weight = out_buf[rank].reshape(width, size)
            grad_mixed[:, pl.ds(rank * size, size)] = dot(back_one[...], weight).astype(low)
        turn(low_one, low_turned)

    def state_task():
        def fill(refs, other):
            square[...] = jnp.full_like(square, other)
            base = 0
            for ref in refs:
                square[pl.ds(base, ref.shape[0]), :] = ref[...]
                base += ref.shape[0]
            return square[...].T

        turned[0] = fill(row_states, 1.0)
        turned[1] = fill((second_ref,), 1.0)
        turned[2] = fill((vector_ref,), 0.0)

    staged = {}

    def pair_task(at):
        turn_at, place = divmod(at, tensor)
        pair, column, loads = pair_loads(at)
        for copy in loads:
            copy.wait()
        if at + 1 < steps_in_all:
            for copy in pair_loads(at + 1)[2]:
                copy.start()
        near = at % 2
        grads = grad_mixed[:, pl.ds(pl.multiple_of(pair * LANES, LANES), LANES)]
        value = attend_pair_back(head_buf[near], bias_ref[...], grads)
        head_sums[:, column] = jnp.sum(value.astype(jnp.float32), axis=0, keepdims=True)
        weight = qkv_buf[near].reshape(width, 3 * LANES)
        term = dot(value, weight, CONTRACT_LAST)
        if at == 0:
            input_grad[...] = term
        else:
            input_grad[...] += term
        item = qkv_items[turn_at]
        grad = dot(low_turned[...], value).astype(low)
        if place + 1 < tensor:
            if near in staged:
                staged[near].wait_send()
            qkv_stage[near] = grad.reshape(nz, ny, nx, own_rows, 3 * LANES)
            copy = hand_over(item, place + 1, qkv_stage.at[near], stage_sem.at[item, place])
            copy.start()
            staged[near] = copy
            arriving.setdefault(item, []).append(copy)
        else:
            keep_own(item, grad)

    def last_task():
        step_rows = LANES

        def fetch(at):
            near = lax.rem(at, 2)
            part = pl.ds(pl.multiple_of(at * step_rows, step_rows), step_rows)
            return [
                pltpu.make_async_copy(source.at[part, :], row_buf.at[which, near], load_sem.at[which, near])
                for which, source in enumerate((input_ref, middle_ref))
            ]

        for copy in fetch(0):
            copy.start()

        def body(at, sums):
            for copy in fetch(at):
                copy.wait()

            @pl.when(at + 1 < rows // step_rows)
            def _():
                for copy in fetch(at + 1):
                    copy.start()

            near = lax.rem(at, 2)
            part = pl.ds(pl.multiple_of(at * step_rows, step_rows), step_rows)
            normed, inverse = norm_rows(row_buf[0, near])
            grad_low = input_grad[part, :]
            scaled = grad_low * table[0:1, :]
            first = jnp.mean(scaled, axis=1, keepdims=True)
            second = jnp.mean(scaled * normed, axis=1, keepdims=True)
            input_grad[part, :] = row_buf[1, near] + inverse * (scaled - first - normed * second)
            terms = (grad_low * normed, grad_low)
            return tuple(old + jnp.sum(term, axis=0, keepdims=True) for old, term in zip(sums, terms))

        zero = jnp.zeros((1, width), jnp.float32)
        found = lax.fori_loop(0, rows // step_rows, body, (zero, zero))
        table_grad_ref[...] = jnp.zeros_like(table_grad_ref)
        for at in range(2):
            table_grad_ref[at : at + 1, :] = found[at]
        for pair in range(width // LANES):
            for kind, row in ((0, 2), (2, 3)):
                table_grad_ref[row : row + 1, pl.ds(pair * LANES, LANES)] = head_sums[
                    :, pl.ds((pair * 3 + kind) * LANES, LANES)
                ]
        for at, row in enumerate((4, 5, 6, VEC - 1)):
            table_grad_ref[row : row + 1, :] = vec_sums[at : at + 1, :]
        for at in range(VEC - 8):
            table_grad_ref[7 + at : 8 + at, :] = pre_sums[:, pl.ds(at * width, width)]
        value = table_grad_ref[...].T.astype(low)
        vec_stage[...] = value.reshape(nz, ny, nx, own_rows, LANES)
        for step in range(1, tensor):
            copy = hand_over(vec_item, step, vec_stage, stage_sem.at[vec_item, step - 1])
            copy.start()
            sent.append(copy)
            arriving.setdefault(vec_item, []).append(copy)
        keep_own(vec_item, value)

    here.barrier(((0, 3), (1, 2)))
    local = {}
    for item, (name, _, _, source) in enumerate(items):
        if name in ("one", "two"):
            array = sum_one if name == "one" else sum_two
            copy = pltpu.make_async_copy(
                array.at[source], own.at[:, :, :, :, columns(item)], local_sem.at[item]
            )
            copy.start()
            local[item] = copy

    def advance(item, phase):
        if phase > 1:
            for copy in copies(item, phase - 1):
                copy.wait_recv()
            add_in(item, phase - 1)
        elif item in local:
            local[item].wait()
        else:
            for copy in arriving.get(item, ()):
                copy.wait_recv()
            add_core(item)
        if phase < 4:
            for copy in copies(item, phase):
                copy.start()
                sent.append(copy)

    steps = Steps()
    owner = {item: ("out", 0) for item in out_items}
    owner |= {item: ("pair", tensor * (at + 1) - 1) for at, item in enumerate(qkv_items)}
    owner[vec_item] = ("last", 0)
    for item, (name, _, size, _) in enumerate(items):
        share = size / layout.total
        length = {1: share * UNIT * nz, 2: share * UNIT * nz / 2, 3: share * UNIT * nz}
        early = item not in owner
        for phase in range(1, 5):
            after = [("copy", item, phase - 1)] if phase > 1 else []
            waits = [(item, phase - 1)] if phase > 1 else []
            if phase == 1 and early and item >= DEPTH:
                after = [("copy", item - DEPTH, 2)]
            if phase == 1 and not early:
                after, waits = [owner[item]], [("core", owner[item])]
            steps.add(
                ("copy", item, phase),
                functools.partial(advance, item, phase),
                PUMP * (1.5 if phase == 2 else 1.0),
                (0.5 if phase == 1 and early else 0.0),
                after,
                waits,
                [((item, phase), "z" if phase == 3 else "xy", length[phase])] if phase < 4 else [],
            )
    steps.add(("state", 0), state_task, 1.0, 2.0)
    steps.add(("out", 0), out_task, 8.0, 1.0, (), (), [(("core", ("out", 0)), "core", CORE_UNIT / 12)])
    for at in range(steps_in_all):
        after = [("pair", at - 1) if at else ("out", 0)]
        starts = [(("core", ("pair", at)), "core", CORE_UNIT / 24)]
        steps.add(("pair", at), functools.partial(pair_task, at), 6.0, 1.0, after, (), starts)
    steps.add(
        ("last", 0), last_task, 4.0, 1.0, [("pair", steps_in_all - 1)], (), [(("core", ("last", 0)), "core", 1.0)]
    )
    steps.run()
    sent.extend(staged.values())

    decay_rate = 1.0 - STEP ** (-0.8)
    keep_old = 1.0 - decay_rate
    long = layout.sizes["one"] * tensor
    matrices = layout.matrices()
    lane = lax.broadcasted_iota(jnp.int32, (1, LANES), 1)
    row_parts = []
    for spans in matrices:
        row_part = 0.0
        for start, size in spans:
            value = total_ref[:, pl.ds(start, size)]
            square = value * value
            col_sum[0, :, pl.ds(start, size)] = jnp.sum(square, axis=0, keepdims=True)
            row_part = row_part + jnp.sum(square, axis=1, keepdims=True)
        row_parts.append(row_part)
    row_sum[0] = pick(row_parts, lane)
    finish_row = exchange(0, 0, (3,), row_sum, row_in)
    finish_col = exchange(1, 0, (0,), col_sum, col_in)
    vec_start = layout.start["vec"]
    table_grad = total_ref[:, pl.ds(vec_start, LANES)]
    second_new = decay_rate * turned[1] + keep_old * (table_grad * table_grad + EPS_ONE)
    second_new_ref[...] = second_new
    vector_update = table_grad * lax.rsqrt(second_new)
    vector_sums = jnp.sum(vector_update * vector_update, axis=0, keepdims=True) / tensor
    vector_weight = jnp.sum(turned[2] * turned[2], axis=0, keepdims=True) / tensor
    weight_sums = [total_of(jnp.sum(weights[0][...] * weights[0][...], axis=0))]
    weight_sums += [total_of(ref[...] * ref[...]) for ref in weights[1:]]
    finish_row()
    row_counts = pick([jnp.full((1, 1), 1.0 / size, jnp.float32) for size in (width, width, width, width, long, long)], lane)
    row_new = decay_rate * turned[0] + keep_old * (row_sum[1] * row_counts + EPS_ONE)
    row_new_ref[...] = row_new
    finish_col()
    exchange(1, 1, (1, 2), col_sum, col_in)()
    for at, spans in enumerate(matrices):
        for place, (start, size) in enumerate(spans):
            if at < 3:
                old = col_states[0][at : at + 1, pl.ds(place * LANES, LANES)]
            else:
                old = col_states[at - 2][...]
            fresh = keep_old * (col_sum[2, :, pl.ds(start, size)] / width + EPS_ONE)
            col_new_ref[:, pl.ds(start, size)] = decay_rate * old + fresh
    ratios = []
    means = []
    for at, spans in enumerate(matrices):
        row_at = row_new[:, at : at + 1]
        ratio = 0.0
        for start, size in spans:
            value = total_ref[:, pl.ds(start, size)]
            col_at = col_new_ref[:, pl.ds(start, size)]
            ratio = ratio + total_of(value * value / (row_at * col_at))
        ratios.append(ratio)
        if at in (3, 5):
            means.append(jnp.sum(col_at, axis=1, keepdims=True) / (nz * ny * nx))
        else:
            means.append(jnp.sum(row_at, axis=0, keepdims=True) / tensor)
    small[0] = jnp.concatenate(
        [pick(ratios + means + weight_sums, lane), vector_sums, vector_weight, jnp.zeros((5, LANES), jnp.float32)], axis=0
    )
    exchange(2, 0, (0, 3), small, small_in)()
    exchange(2, 1, (1, 2), small, small_in)()
    sums_ref[...] = small[2]
    for copy in sent:
        copy.wait_send()


def backward(dims, tensor, layout, large, near, weights, states):
    rows, width = near[0].shape
    own_rows = width // (dims[0] * dims[1] * dims[2])
    half_rows = own_rows // 2
    columns = layout.columns
    items = []
    for block in range(layout.sizes["one"] // BLOCK):
        for name in ("two", "one"):
            items.append((name, layout.start[name] + block * BLOCK, BLOCK, block))
    items.append(("out", layout.start["out"], columns, 0))
    for start in range(0, 3 * columns, 3 * LANES):
        items.append(("qkv", layout.start["qkv"] + start, 3 * LANES, start))
    items.append(("vec", layout.start["vec"], LANES, 0))
    nz, ny, nx = dims
    peers = max(1, nz - 1, ny + nx - 2)
    group = max(1, nz * tensor - 1, ny * nx - 1)
    others = max(1, tensor - 1)
    offset = layout.total
    from_here = offset - layout.start["out"]
    low, full = jnp.bfloat16, jnp.float32
    anywhere = pl.BlockSpec(memory_space=pl.ANY)
    inside = pl.BlockSpec(memory_space=pltpu.VMEM)

    def hold(*shape):
        return pltpu.VMEM(tuple(max(1, size) for size in shape), low)

    sums = offset - LANES
    count = len(items)
    return pl.pallas_call(
        functools.partial(backward_kernel, dims, tensor, tuple(items), layout),
        name="backward",
        out_shape=[
            jax.ShapeDtypeStruct((rows, width), full),
            jax.ShapeDtypeStruct((own_rows, offset), full),
            jax.ShapeDtypeStruct((1, sums), full),
            jax.ShapeDtypeStruct((own_rows, LANES), full),
            jax.ShapeDtypeStruct((own_rows, LANES), full),
            jax.ShapeDtypeStruct((8, LANES), full),
        ],
        in_specs=[anywhere] * len(large) + [inside] * (len(near) + len(weights) + len(states)),
        out_specs=[inside] * 6,
        scratch_shapes=[
            hold(nz, ny, nx, own_rows, offset),
            hold(others, nz, ny, nx, own_rows, from_here),
            hold(nx - 1, nz, ny, half_rows, offset),
            hold(ny - 1, nz, nx, half_rows, offset),
            hold(ny - 1, nz, half_rows, offset),
            hold(nx - 1, nz, half_rows, offset),
            hold(nz - 1, own_rows, offset),
            pltpu.VMEM((3, 1, sums), full),
            pltpu.VMEM((2, max(1, nz - 1, ny * nx - 1), 1, sums), full),
            pltpu.VMEM((2, own_rows, LANES), full),
            pltpu.VMEM((1, others, own_rows, LANES), full),
            pltpu.VMEM((3, 8, LANES), full),
            pltpu.VMEM((2, group, 8, LANES), full),
            pltpu.VMEM((LANES, own_rows), full),
            pltpu.VMEM((3, own_rows, LANES), full),
            hold(width, rows),
            hold(width, rows),
            hold(rows, width),
            hold(tensor, *dims, own_rows, columns),
            hold(2, *dims, own_rows, 3 * LANES),
            hold(2, rows, 3 * LANES),
            pltpu.VMEM((2, 2, LANES, width), full),
            hold(others, *dims, own_rows, columns),
            hold(2, *dims, own_rows, 3 * LANES),
            hold(*dims, own_rows, LANES),
            pltpu.VMEM((1, 3 * width), full),
            pltpu.VMEM((LANES, width), full),
            pltpu.SemaphoreType.DMA((3, 2)),
            pltpu.SemaphoreType.DMA((count, others)),
            pltpu.SemaphoreType.DMA((count, others)),
            pltpu.SemaphoreType.DMA((count,)),
            pltpu.SemaphoreType.DMA((count, 4, peers)),
            pltpu.SemaphoreType.DMA((count, 4, peers)),
            pltpu.SemaphoreType.DMA((3, 2, group)),
            pltpu.SemaphoreType.DMA((3, 2, group)),
        ],
        compiler_params=pltpu.CompilerParams(
            collective_id=1, has_side_effects=True, vmem_limit_bytes=63 << 20
        ),
    )(*large, *near, *weights, *states)


def update_kernel(layout, width, long, *refs):
    block_in, grad_in = refs[:2]
    far = refs[2:12]
    block_out, input_grad = refs[12:14]
    own_qkv, own_out, own_one, own_two, own_table = refs[14:19]
    new_qkv, new_out, new_one, new_two, new_vectors, second_new = refs[19:25]
    qkv_row, qkv_col, out_row, out_col, one_row, one_col, two_row, two_col = refs[25:33]
    near, passing, sem = refs[33:43], refs[43:45], refs[45]
    loads = [
        pltpu.make_async_copy(source, target, sem.at[at])
        for at, (source, target) in enumerate(zip((*far, block_in, grad_in), (*near, *passing)))
    ]
    long_copies = [
        pltpu.make_async_copy(source, target, sem.at[12 + at])
        for at, (source, target) in enumerate(zip(passing, (block_out, input_grad)))
    ]
    for copy in loads:
        copy.start()
    for copy in loads:
        copy.wait()
    for copy in long_copies:
        copy.start()
    total_ref, col_ref, row_ref, second_ref, sums_ref, vector_ref = near[:6]
    weights = near[6:]
    lane = lax.broadcasted_iota(jnp.int32, (1, LANES), 1)

    def at(index):
        return sums_ref[0:1, index : index + 1]

    lengths = (width, width, width, width, width, long)
    means = [at(6 + m) / lengths[m] for m in range(6)]
    squares = [means[m] * at(m) for m in range(6)]
    squares = [squares[0] + squares[1] + squares[2], *squares[3:]]
    entries = (3 * width * width, width * width, width * long, width * long)
    step_size = []
    for m in range(4):
        damping = 1.0 / jnp.maximum(1.0, jnp.sqrt(squares[m] / entries[m] + 1e-06) / CLIP_LEVEL)
        step_size.append(LEARN_RATE * jnp.sqrt(at(12 + m) / entries[m] + 1e-06) * damping)
    spread = [(m, place, *span) for m, spans in enumerate(layout.matrices()) for place, span in enumerate(spans)]
    for m, place, start, size in spread:
        grad = total_ref[:, pl.ds(start, size)]
        col = col_ref[:, pl.ds(start, size)]
        step = step_size[max(0, m - 2)] * grad * lax.rsqrt(row_ref[:, m : m + 1] * col / means[m])
        if m < 3:
            part = slice(place * LANES, (place + 1) * LANES)
            own_qkv[m, :, part] = grad
            new_qkv[m, :, part] = weights[0][m, :, part] - step
            qkv_col[m : m + 1, part] = col
        else:
            own, new, state = (
                (own_out, new_out, out_row),
                (own_one, new_one, one_col),
                (own_two, new_two, two_row),
            )[m - 3]
            own[...] = grad
            new[...] = weights[m - 2][...] - step
            state[...] = col
    row_flat = row_ref[...].T
    qkv_row[...] = row_flat[0:3]
    out_col[...] = row_flat[3:4]
    one_row[...] = row_flat[4:5]
    two_col[...] = row_flat[5:6]

    wide = (lane >= 7) & (lane < VEC - 1)
    counts = jnp.where(wide, float(long), float(width))

    def grouped(values):
        inside = jnp.sum(jnp.where(wide, values, 0.0), axis=1, keepdims=True)
        return jnp.where(wide, inside, values)

    table_grad = total_ref[:, pl.ds(layout.start["vec"], LANES)]
    update = table_grad * lax.rsqrt(second_ref[...])
    norm = jnp.sqrt(grouped(sums_ref[1:2, :]) / counts + 1e-06)
    size = jnp.sqrt(grouped(sums_ref[2:3, :]) / counts + 1e-06)
    change = LEARN_RATE * size / jnp.maximum(1.0, norm / CLIP_LEVEL) * update
    own_table[...] = table_grad.T[:VEC]
    new_vectors[...] = vector_ref[...] - change.T[:VEC]
    second_new[...] = second_ref[...].T[:VEC]
    for copy in long_copies:
        copy.wait()


def update_weights(layout, width, long, columns, hidden, rows, results, values, vectors, weights):
    full = jnp.float32
    shapes = [
        *(result.shape for result in results),
        (3, rows, columns),
        (rows, columns),
        (rows, hidden),
        (rows, hidden),
        (VEC, rows),
        (3, rows, columns),
        (rows, columns),
        (rows, hidden),
        (rows, hidden),
        (VEC, rows),
        (VEC, rows),
        (3, rows),
        (3, columns),
        (1, columns),
        (1, rows),
        (1, rows),
        (1, hidden),
        (1, hidden),
        (1, rows),
    ]
    far = (*values, vectors, *weights)
    anywhere = pl.BlockSpec(memory_space=pl.ANY)
    inside = pl.BlockSpec(memory_space=pltpu.VMEM)
    return pl.pallas_call(
        functools.partial(update_kernel, layout, width, long),
        name="update_weights",
        out_shape=[jax.ShapeDtypeStruct(shape, full) for shape in shapes],
        in_specs=[anywhere] * (2 + len(far)),
        out_specs=[anywhere] * 2 + [inside] * (len(shapes) - 2),
        scratch_shapes=[
            *(pltpu.VMEM(array.shape, full) for array in (*far, *results)),
            pltpu.SemaphoreType.DMA((4 + len(far),)),
        ],
        compiler_params=pltpu.CompilerParams(vmem_limit_bytes=63 << 20),
    )(*results, *far)


def on_device(
    inputs,
    cotangent,
    token_mask,
    w_qkv,
    w_out,
    w_fc1,
    w_fc2,
    vectors,
    qkv_row,
    qkv_col,
    out_row,
    out_col,
    fc1_row,
    fc1_col,
    fc2_row,
    fc2_col,
    vec_second,
):
    tensor_count = lax.axis_size("tensor")
    dims = grid_of(lax.axis_size("fsdp"))
    width = inputs.shape[1]
    own_rows, columns = w_qkv.shape[1:]
    hidden = w_fc1.shape[1]
    weights = (w_qkv, w_out.T, w_fc1, w_fc2.T)
    (
        weight_qkv,
        _,
        weight_out,
        *_,
        block_out,
        grad_middle,
        back_one,
        projected,
        mixed_rows,
        low_one,
        grad_one,
        grad_two,
        table,
        vec_sums,
        pre_sums,
        bias_column,
    ) = forward(dims, tensor_count, inputs, cotangent, token_mask, vectors, weights)
    layout = Layout(columns, hidden, ("two", "one", "out", "qkv", "vec"))
    row_states = (qkv_row, out_col[None], fc1_row[None], fc2_col[None])
    col_states = (qkv_col, out_row[None], fc1_col[None], fc2_row[None])
    input_grad, *values = backward(
        dims,
        tensor_count,
        layout,
        (grad_two, grad_one, weight_qkv, weight_out, projected, inputs, grad_middle),
        (mixed_rows, low_one, back_one, bias_column, table, vec_sums, pre_sums),
        weights,
        (*row_states, *col_states, vec_second, vectors),
    )
    outs = update_weights(
        layout, width, FF, columns, hidden, own_rows, (block_out, input_grad), values, vectors, weights
    )
    outs = [out.reshape(-1) if out.shape[0] == 1 else out for out in outs]
    for at in (3, 5, 8, 10):
        outs[at] = outs[at].T
    return (*outs[:12], *outs[13:], outs[12])


def solution(mesh):
    in_specs = (
        P(("fsdp", "tensor"), None),
        P(("fsdp", "tensor"), None),
        P("fsdp", None),
        P(None, "fsdp", "tensor"),
        P("tensor", "fsdp"),
        P("fsdp", "tensor"),
        P("tensor", "fsdp"),
        P(None, "fsdp"),
        P(None, "fsdp"),
        P(None, "tensor"),
        P("tensor"),
        P("fsdp"),
        P("fsdp"),
        P("tensor"),
        P("tensor"),
        P("fsdp"),
        P(None, "fsdp"),
    )
    out_specs = (
        P(("fsdp", "tensor"), None),
        P(("fsdp", "tensor"), None),
        P(None, "fsdp", "tensor"),
        P("tensor", "fsdp"),
        P("fsdp", "tensor"),
        P("tensor", "fsdp"),
        P(None, "fsdp"),
        P(None, "fsdp", "tensor"),
        P("tensor", "fsdp"),
        P("fsdp", "tensor"),
        P("tensor", "fsdp"),
        P(None, "fsdp"),
        P(None, "fsdp"),
        P(None, "tensor"),
        P("tensor"),
        P("fsdp"),
        P("fsdp"),
        P("tensor"),
        P("tensor"),
        P("fsdp"),
        P(None, "fsdp"),
    )
    return jax.shard_map(
        on_device, mesh=mesh, in_specs=in_specs, out_specs=out_specs, check_vma=False
    )
```

```python
import functools

import jax
import jax.numpy as jnp
from jax import lax
from jax.experimental import pallas as pl
from jax.experimental.pallas import tpu as pltpu
from jax.sharding import PartitionSpec as P

HEAD_DIM = 64
FF = 4096
STEP = 20
VEC = 12
LANES = 128

EPS_NORM = 1e-05
EPS_ONE = 1e-30
CLIP_LEVEL = 1.0
LEARN_RATE = 0.5
MESH = pl.DeviceIdType.MESH
LOG2E = 1.4426950408889634
CONTRACT_LAST = (((1,), (1,)), ((), ()))


def grid_of(count):
    return {16: (4, 2, 2), 32: (2, 4, 4)}.get(count, (count, 1, 1))


class Place:
    def __init__(self, dims, tensor):
        self.dims = dims
        self.tensor = tensor
        fsdp = lax.axis_index("fsdp")
        _, ny, nx = dims
        self.at = (fsdp // (ny * nx), (fsdp // nx) % ny, fsdp % nx)
        self.rank = lax.axis_index("tensor")

    def moved(self, axis, step):
        place = list(self.at) + [self.rank]
        size = (*self.dims, self.tensor)[axis]
        place[axis] = lax.rem(place[axis] + step + size, size)
        return tuple(place)

    def device(self, place):
        z, y, x, rank = place
        return {"fsdp": (z * self.dims[1] + y) * self.dims[2] + x, "tensor": rank}

    def size(self, axis):
        return (*self.dims, self.tensor)[axis]

    def peers(self, *axes):
        places = [()]
        for axis in axes:
            places = [(*steps, step) for steps in places for step in range(self.size(axis))]
        found = []
        for steps in places[1:]:
            place = list(self.at) + [self.rank]
            for axis, step in zip(axes, steps):
                place[axis] = lax.rem(place[axis] + step, self.size(axis))
            found.append(self.device(tuple(place)))
        return found

    def barrier(self, groups):
        sem = pltpu.get_barrier_semaphore()
        count = 0
        for axes in groups:
            for device in self.peers(*axes):
                pl.semaphore_signal(sem, inc=1, device_id=device, device_id_type=MESH)
                count += 1
        if count:
            pl.semaphore_wait(sem, count)


def norm_rows(values):
    average = jnp.mean(values, axis=1, keepdims=True)
    center = values - average
    inverse = lax.rsqrt(jnp.mean(center * center, axis=1, keepdims=True) + EPS_NORM)
    return center * inverse, inverse


def dot(left, right, dims=(((1,), (0,)), ((), ()))):
    return lax.dot_general(left, right, dims, preferred_element_type=jnp.float32)


def turn(source, target):
    for start in range(0, source.shape[1], LANES):
        target[pl.ds(start, LANES), :] = source[:, pl.ds(start, LANES)].T


def attend_pair(heads, bias):
    mixed = []
    for head in range(2):
        query, key, value = (
            heads[:, kind * LANES + head * HEAD_DIM : kind * LANES + (head + 1) * HEAD_DIM] for kind in range(3)
        )
        scores = dot(query, key, CONTRACT_LAST) * (HEAD_DIM ** (-0.5) * LOG2E) + bias
        raised = jnp.exp2(scores - jnp.max(scores, axis=1, keepdims=True))
        summed = jnp.sum(raised, axis=1, keepdims=True)
        attention = (raised * (1.0 / summed)).astype(jnp.bfloat16)
        mixed.append(dot(attention, value).astype(jnp.bfloat16))
    return jnp.concatenate(mixed, axis=1)


class Steps:
    def __init__(self):
        self.steps = {}

    def add(self, name, run, time, rank, after=(), waits=(), starts=()):
        self.steps[name] = (run, time, rank, tuple(after), tuple(waits), tuple(starts))

    def arrange(self):
        now, free, arrival, done, order = 0.0, {}, {}, set(), []
        left = list(self.steps)
        while left:
            best, soonest = None, None
            for name in left:
                _, time, rank, after, waits, _ = self.steps[name]
                if any(other not in done for other in after) or any(wait not in arrival for wait in waits):
                    continue
                ready = max([arrival[wait] for wait in waits], default=0.0)
                if ready <= now:
                    if best is None or rank < self.steps[best][2]:
                        best = name
                elif soonest is None or ready < soonest:
                    soonest = ready
            if best is None:
                now = soonest
                continue
            _, time, _, _, _, starts = self.steps[best]
            now += time
            for transfer, link, length in starts:
                begin = max(now, free.get(link, 0.0))
                free[link] = begin + length
                arrival[transfer] = begin + length + LATENCY
            done.add(best)
            left.remove(best)
            order.append(best)
        return order, now

    def run(self):
        for name in self.arrange()[0]:
            self.steps[name][0]()


class Gather:
    def __init__(self, here, pack_ref, outs, parts, local_sem, send_sem, recv_sem):
        self.here = here
        self.pack = pack_ref
        self.outs = outs
        self.rows = pack_ref.shape[0]
        self.parts = parts
        self.late = [item for item, part in enumerate(parts) if part[0] == LATE_ARRAY]
        self.sems = (local_sem, send_sem, recv_sem)
        self.own = (*here.at, here.rank)
        self.sent = []

    def region(self, item, part, place, free):
        out, _, chunk, _ = self.parts[item]
        index = tuple(slice(None) if a in free else place[a] for a in range(3))
        lead = () if chunk is None else (place[3], chunk)
        return self.outs[out].at[(*lead, *index, part)]

    def shard(self, item, part):
        _, offset, _, size = self.parts[item]
        return self.pack.at[part, pl.ds(offset, size)]

    def phases(self, item):
        return 3 if self.parts[item][2] is None else 4

    def moves(self, item, phase):
        whole, half = pl.ds(0, self.rows), self.rows // 2
        first, second = pl.ds(0, half), pl.ds(half, half)
        if item in self.late:
            return (
                ((2, (), first), (1, (), second)),
                ((1, (2,), first), (2, (1,), second)),
                ((0, (1, 2), whole),),
                ((3, (0, 1, 2), whole),),
            )[phase]
        return (
            ((0, (), whole),),
            ((1, (0,), first), (2, (0,), second)),
            ((2, (0, 1), first), (1, (0, 2), second)),
            ((3, (0, 1, 2), whole),),
        )[phase]

    def copies(self, item, phase, landing):
        here = self.here
        found = []
        for axis, free, part in self.moves(item, phase):
            for step in range(1, here.size(axis)):
                own = self.region(item, part, self.own, free)
                if landing:
                    src = dst = self.region(item, part, here.moved(axis, -step), free)
                else:
                    src, dst = (self.shard(item, part) if phase == 0 else own), own
                at = len(found)
                found.append(
                    pltpu.make_async_remote_copy(
                        src_ref=src,
                        dst_ref=dst,
                        send_sem=self.sems[1].at[item, phase, at],
                        recv_sem=self.sems[2].at[item, phase, at],
                        device_id=here.device(here.moved(axis, step)),
                        device_id_type=MESH,
                    )
                )
        return found

    def keep(self, item):
        whole = pl.ds(0, self.rows)
        return pltpu.make_async_copy(
            self.shard(item, whole), self.region(item, whole, self.own, ()), self.sems[0].at[item]
        )

    def advance(self, item, phase):
        if phase:
            for copy in self.copies(item, phase - 1, True):
                copy.wait_recv()
        if phase == 0:
            self.keep(item).start()
        if phase == 1:
            self.keep(item).wait()
        if phase < self.phases(item):
            for copy in self.copies(item, phase, False):
                copy.start()
                self.sent.append(copy)

    def finish(self):
        for copy in self.sent:
            copy.wait_send()


BLOCK = 512
DEPTH = 4
LATENCY = 1.5
UNIT = 20.0
CORE_UNIT = 40.0
LATE_ARRAY = 2
LATE_NAME = "out"
PUMP = 0.4


def forward_kernel(dims, tensor, parts, tasks, *refs):
    input_ref, top_ref, mask_ref, vector_ref = refs[:4]
    own_weights = refs[4:8]
    outs, land = refs[8:13], refs[13:15]
    weight_qkv, weight_vec, weight_out, weight_one, weight_two = outs
    far = refs[15:20]
    projected, grad_one, grad_two, table, vec_sums, pre_sums, bias_column = refs[20:27]
    (
        block_out,
        grad_middle,
        back_one,
        mixed,
        low_one,
        pack,
        keep_ref,
        square,
        vec_buf,
        qkv_buf,
        head_stage,
        out_buf,
        one_buf,
        two_buf,
        low_two,
        low_two_turned,
        back_two,
        back_two_turned,
        grad_low_two,
        hidden_bias,
        head_bias,
        one_stage,
        two_stage,
        one_keep,
        two_keep,
        other,
        active,
        grad_pre,
        load_sem,
        store_sem,
        keep_sem,
        head_sem,
        land_sem,
        far_sem,
        local_sem,
        send_sem,
        recv_sem,
    ) = refs[27:]
    near = (block_out, grad_middle, back_one, mixed, low_one)

    def far_store(at):
        return pltpu.make_async_copy(near[at], far[at], far_sem.at[at])

    here = Place(dims, tensor)
    gather = Gather(here, pack, outs, parts, local_sem, send_sem, recv_sem)
    rows, width = input_ref.shape
    own_rows = pack.shape[0]
    per_rank = weight_qkv.shape[1]
    low = jnp.bfloat16
    step_rows = LANES

    def fill_pack():
        base = 0
        for pair in range(per_rank):
            for kind in range(3):
                part = own_weights[0][kind, :, pl.ds(pair * LANES, LANES)]
                pack[:, pl.ds(base, LANES)] = part.astype(low)
                base += LANES
        square[...] = jnp.zeros_like(square)
        square[pl.ds(0, VEC), :] = vector_ref[...]
        pack[:, pl.ds(base, LANES)] = square[...].T.astype(low)
        base += LANES
        for ref in own_weights[1:]:
            pack[:, pl.ds(base, ref.shape[1])] = ref[...].astype(low)
            base += ref.shape[1]

    def mask_row():
        return mask_ref[pl.ds(here.rank, 1), :].astype(jnp.float32)

    def mask_bias(keep):
        return jnp.where(keep > 0.0, 0.0, -1e30)

    def first_masks():
        turned = jnp.broadcast_to(mask_row(), (LANES, rows)).T
        keep_ref[...] = turned[:, 0:1]
        bias_column[...] = mask_bias(turned[:, 0:1])

    def row_steps(body, carry):
        return lax.fori_loop(
            0, rows // step_rows, lambda at, c: body(pl.ds(pl.multiple_of(at * step_rows, step_rows), step_rows), c), carry
        )

    def load(source, buffer, sem):
        return pltpu.make_async_copy(source, buffer, sem)

    def first_norm():
        first_masks()
        copy = load(weight_vec, vec_buf, load_sem.at[7])
        copy.start()
        copy.wait()
        whole = vec_buf[...].reshape(width, LANES).astype(jnp.float32).T
        table[...] = whole[:16]
        for at in range(VEC - 8):
            hidden_bias[:, pl.ds(at * width, width)] = whole[7 + at : 8 + at]
        for pair in range(width // LANES):
            for kind, row in ((0, 2), (2, 3)):
                head_bias[:, pl.ds((pair * 3 + kind) * LANES, LANES)] = whole[
                    row : row + 1, pair * LANES : (pair + 1) * LANES
                ]
            head_bias[:, pl.ds((pair * 3 + 1) * LANES, LANES)] = jnp.zeros((1, LANES), jnp.float32)

        def body(part, carry):
            normed, _ = norm_rows(input_ref[part, :])
            low_one[part, :] = (normed * table[0:1, :] + table[1:2, :]).astype(low)
            back_two[part, :] = (top_ref[part, :].astype(jnp.float32) * keep_ref[part, :]).astype(low)
            return carry

        row_steps(body, 0)
        far_store(4).start()
        turn(back_two, back_two_turned)

    def head_store(pair, slot):
        column = pl.ds(pl.multiple_of(pair * 3 * LANES, LANES), 3 * LANES)
        return pltpu.make_async_copy(head_stage.at[slot], projected.at[:, column], head_sem.at[slot])

    def pair_of(at):
        turn_at, place = divmod(at, tensor)
        return lax.rem(here.rank + place, tensor) * per_rank + turn_at

    def head_load(at):
        turn_at, place = divmod(at, tensor)
        source = weight_qkv.at[lax.rem(here.rank + place, tensor), turn_at]
        return load(source, qkv_buf.at[at % 2], load_sem.at[at % 2])

    def heads(at):
        head_load(at).wait()
        pair = pair_of(at)
        slot = at % 2
        column = pl.ds(pl.multiple_of(pair * 3 * LANES, LANES), 3 * LANES)
        weight = qkv_buf[slot].reshape(width, 3 * LANES)
        value = (dot(low_one[...], weight) + head_bias[:, column]).astype(low)
        if at > 1:
            head_store(pair, slot).wait()
        head_stage[slot] = value
        head_store(pair, slot).start()
        mixed[:, pl.ds(pl.multiple_of(pair * LANES, LANES), LANES)] = attend_pair(value, mask_bias(mask_row()))

    def out_load():
        return [
            load(weight_out.at[rank, 0], out_buf.at[rank], load_sem.at[2]) for rank in range(tensor)
        ]

    def second_norm():
        far_store(3).start()
        for copy in out_load():
            copy.wait()
        columns = width // tensor
        for rank in range(tensor):
            weight = out_buf[rank].reshape(width, columns)
            term = dot(mixed[:, pl.ds(rank * columns, columns)], weight, CONTRACT_LAST)
            if rank == 0:
                grad_middle[...] = term
            else:
                grad_middle[...] += term

        def body(part, carry):
            middle = input_ref[part, :] + (grad_middle[part, :] + table[4:5, :]) * keep_ref[part, :]
            grad_middle[part, :] = middle
            normed, _ = norm_rows(middle)
            low_two[part, :] = (normed * table[5:6, :] + table[6:7, :]).astype(low)
            return carry

        row_steps(body, 0)
        turn(low_two, low_two_turned)

    stages = (one_stage, two_stage)
    keeps = (one_keep, two_keep)

    def hand_over(at):
        chunk, place = divmod(at, tensor)
        target = (*here.at, lax.rem(here.rank + place + 1, tensor))
        return [
            pltpu.make_async_remote_copy(
                src_ref=stages[which].at[at % 2],
                dst_ref=land[which].at[place, chunk],
                send_sem=store_sem.at[which, at % 2],
                recv_sem=land_sem.at[which, place, chunk],
                device_id=here.device(target),
                device_id_type=MESH,
            )
            for which in range(2)
        ]

    def keep_store(chunk):
        return [
            pltpu.make_async_copy(
                keeps[which].at[chunk % 2],
                out.at[chunk],
                keep_sem.at[which, chunk % 2],
            )
            for which, out in enumerate((grad_one, grad_two))
        ]

    def hidden_column(at):
        chunk, place = divmod(at, tensor)
        base = (lax.rem(here.rank + place + 1, tensor) * weight_one.shape[1] + chunk) * BLOCK
        return pl.ds(pl.multiple_of(base, LANES), BLOCK)

    def hidden_load(at):
        chunk, place = divmod(at, tensor)
        rank = lax.rem(here.rank + place + 1, tensor)
        return [
            load(source.at[rank, chunk], buffer.at[at % 2], load_sem.at[3 + 2 * which + at % 2])
            for which, (source, buffer) in enumerate(((weight_one, one_buf), (weight_two, two_buf)))
        ]

    staged = {}

    def hidden(at):
        chunk, place = divmod(at, tensor)
        column = hidden_column(at)
        for copy in hidden_load(at):
            copy.wait()
        half = rows // 2
        bias = hidden_bias[:, column]

        def body(turn_at, total):
            part = pl.ds(pl.multiple_of(turn_at * half, half), half)
            one = one_buf[at % 2].reshape(width, BLOCK)
            two = two_buf[at % 2].reshape(width, BLOCK)
            preact = dot(low_two[part, :], one) + bias
            gate = jax.nn.sigmoid(1.702 * preact)
            value = (preact * gate).astype(low)
            active[part, :] = value
            derivative = gate + 1.702 * preact * gate * (1.0 - gate)
            grad = (dot(back_two[part, :], two) * derivative).astype(low)
            grad_pre[part, :] = grad
            if at == 0:
                block_out[part, :] = dot(value, two, CONTRACT_LAST)
                grad_low_two[part, :] = dot(grad, one, CONTRACT_LAST)
            else:
                block_out[part, :] += dot(value, two, CONTRACT_LAST)
                grad_low_two[part, :] += dot(grad, one, CONTRACT_LAST)
            return total + jnp.sum(grad.astype(jnp.float32), axis=0, keepdims=True)

        pre_sums[:, column] = lax.fori_loop(0, 2, body, jnp.zeros((1, BLOCK), jnp.float32))
        mine = place == tensor - 1
        if mine:
            targets = [ref.at[chunk % 2] for ref in keeps]
            if chunk > 1:
                for copy in keep_store(chunk):
                    copy.wait()
        else:
            targets = [ref.at[at % 2] for ref in stages]
            for copy in staged.pop(at % 2, ()):
                copy.wait_send()
        for target, left, right in (
            (targets[0], low_two_turned, grad_pre),
            (targets[1], back_two_turned, active),
        ):
            target[...] = dot(left[...], right[...]).astype(low).reshape(*target.shape)
        if not mine:
            staged[at % 2] = hand_over(at)
            for copy in staged[at % 2]:
                copy.start()

    def combine(chunk):
        for place in range(tensor - 1):
            for which, copy in enumerate(hand_over(chunk * tensor + place)):
                copy.wait_recv()
                fetch = load(land[which].at[place, chunk], other, load_sem.at[7])
                fetch.start()
                fetch.wait()
                keeps[which][chunk % 2] = keeps[which][chunk % 2] + other[...]
        for copy in keep_store(chunk):
            copy.start()

    def last_norm():
        def body(part, sums):
            middle = grad_middle[part, :]
            keep = keep_ref[part, :]
            top = top_ref[part, :].astype(jnp.float32)
            block_out[part, :] = middle + (block_out[part, :] + table[VEC - 1 : VEC, :]) * keep
            normed, inverse = norm_rows(middle)
            grad_low = grad_low_two[part, :]
            scaled = grad_low * table[5:6, :]
            first = jnp.mean(scaled, axis=1, keepdims=True)
            second = jnp.mean(scaled * normed, axis=1, keepdims=True)
            grad = top + inverse * (scaled - first - normed * second)
            grad_middle[part, :] = grad
            masked = grad * keep
            back_one[part, :] = masked.astype(low)
            terms = (masked, grad_low * normed, grad_low, top * keep)
            return tuple(old + jnp.sum(term, axis=0, keepdims=True) for old, term in zip(sums, terms))

        zero = jnp.zeros((1, width), jnp.float32)
        for at, value in enumerate(row_steps(body, (zero,) * 4)):
            vec_sums[at : at + 1, :] = value
        for at in range(3):
            far_store(at).start()

    fill_pack()
    here.barrier(((0,), (1,), (2,), (3,)))
    steps = Steps()
    whole = sum(part[3] for part in parts)
    nz, ny, nx = dims

    def lengths(item, phase):
        share = parts[item][3] / whole
        if item in gather.late:
            return (
                (share * UNIT / 2, "xy"),
                (share * UNIT, "xy"),
                (share * UNIT * nz * ny * nx, "z"),
                (share * CORE_UNIT, "core"),
            )[phase]
        return (
            (share * UNIT * nz, "z"),
            (share * UNIT * nz / 2, "xy"),
            (share * UNIT * nz, "xy"),
            (share * CORE_UNIT, "core"),
        )[phase]

    for item, part in enumerate(parts):
        phases = gather.phases(item)
        for phase in range(phases + 1):
            after = [("copy", item, phase - 1)] if phase else []
            if phase == 0 and item >= DEPTH and item not in gather.late:
                after = [("copy", item - DEPTH, 1)]
            length, link = lengths(item, min(phase, 3))
            steps.add(
                ("copy", item, phase),
                functools.partial(gather.advance, item, phase),
                PUMP,
                0.5 if phase == 0 else 0.0,
                after,
                [(item, phase - 1)] if phase else [],
                [((item, phase), link, length)] if phase < phases else [],
            )

    def landed(items):
        return [("copy", item, gather.phases(item)) for item in items]

    def start(copies):
        for copy in copies:
            copy.start()

    previous = None
    head_count, block_count = per_rank * tensor, FF // BLOCK
    for name, at, items in tasks:
        after = landed(items) + ([previous] if previous else [])
        begin, run, time = {
            "norm": (None, first_norm, 5.0),
            "heads": (lambda at=at: head_load(at).start(), lambda at=at: heads(at), 3.0),
            "out": (lambda: start(out_load()), second_norm, 5.0),
            "hidden": (lambda at=at: start(hidden_load(at)), lambda at=at: hidden(at), 5.5),
        }[name]
        if begin is not None:
            first = landed(items)
            if at > 1:
                first.append((name, at - 2))
            steps.add(("load", name, at), begin, 0.1, 0.2, first)
            after.append(("load", name, at))
        mine = name == "hidden" and at % tensor == tensor - 1
        chunk = at // tensor
        if mine and chunk > 1:
            after.append(("combine", chunk - 2))
        starts = []
        if name == "hidden" and not mine:
            starts = [(("hand", at), "core", CORE_UNIT / len(parts))]
        steps.add((name, at), run, time, 1.0, after, (), starts)
        if mine:
            waits = [("hand", chunk * tensor + place) for place in range(tensor - 1)]
            steps.add(
                ("combine", chunk), functools.partial(combine, chunk), 2.0, 0.8, [(name, at)], waits
            )
        previous = (name, at)
    steps.add(("last", 0), last_norm, 4.0, 0.9, [previous])
    steps.run()
    for at in range(5):
        far_store(at).wait()
    for slot in range(min(2, head_count)):
        head_store(0, slot).wait()
    for chunk in range(min(2, block_count // tensor)):
        for copy in keep_store(chunk):
            copy.wait()
    for copies in staged.values():
        for copy in copies:
            copy.wait_send()
    gather.finish()


def forward(dims, tensor, inputs, cotangent, token_mask, vectors, weights):
    own_rows, columns = weights[0].shape[1:]
    hidden = weights[2].shape[1]
    rows, width = inputs.shape
    low, full = jnp.bfloat16, jnp.float32
    widths = (3 * columns, LANES, columns, hidden, hidden)
    offsets = [sum(widths[:at]) for at in range(5)]
    per_rank = columns // LANES
    parts = [(1, offsets[1], None, LANES)]
    tasks = [("norm", 0, (0,))]
    for at in range(per_rank):
        size = 3 * LANES
        parts.append((0, offsets[0] + at * size, at, size))
        tasks += [("heads", at * tensor + place, (len(parts) - 1,)) for place in range(tensor)]
    tasks.append(("out", 0, (len(parts),)))
    parts.append((2, offsets[2], 0, columns))
    for block in range(hidden // BLOCK):
        needed = (len(parts), len(parts) + 1)
        parts += [(which, offsets[which] + block * BLOCK, block, BLOCK) for which in (3, 4)]
        tasks += [("hidden", block * tensor + place, needed) for place in range(tensor)]
    count = len(parts)
    peers = max(1, dims[0] - 1, dims[1] + dims[2] - 2, tensor - 1)
    anywhere = pl.BlockSpec(memory_space=pl.ANY)
    inside = pl.BlockSpec(memory_space=pltpu.VMEM)
    block = (*dims, own_rows, BLOCK)
    chunks = hidden // BLOCK

    def shape(kind, *size):
        return jax.ShapeDtypeStruct(size, kind)

    return pl.pallas_call(
        functools.partial(forward_kernel, dims, tensor, tuple(parts), tuple(tasks)),
        name="forward",
        out_shape=[
            shape(low, tensor, per_rank, *dims, own_rows, 3 * LANES),
            shape(low, *dims, own_rows, LANES),
            shape(low, tensor, 1, *dims, own_rows, columns),
            *[shape(low, tensor, chunks, *block)] * 2,
            *[shape(low, max(1, tensor - 1), chunks, *block)] * 2,
            shape(full, rows, width),
            shape(full, rows, width),
            *[shape(low, rows, width)] * 3,
            shape(low, rows, 3 * width),
            *[shape(low, chunks, *block)] * 2,
            shape(full, 16, width),
            shape(full, 8, width),
            shape(full, 1, hidden * tensor),
            shape(full, rows, 1),
        ],
        in_specs=[inside] * 8,
        out_specs=[anywhere] * 15 + [inside] * 4,
        scratch_shapes=[
            pltpu.VMEM((rows, width), full),
            pltpu.VMEM((rows, width), full),
            *[pltpu.VMEM((rows, width), low)] * 3,
            pltpu.VMEM((own_rows, sum(widths)), low),
            pltpu.VMEM((rows, 1), full),
            pltpu.VMEM((LANES, own_rows), full),
            pltpu.VMEM((*dims, own_rows, LANES), low),
            pltpu.VMEM((2, *dims, own_rows, 3 * LANES), low),
            pltpu.VMEM((2, rows, 3 * LANES), low),
            pltpu.VMEM((tensor, *dims, own_rows, columns), low),
            pltpu.VMEM((2, *block), low),
            pltpu.VMEM((2, *block), low),
            pltpu.VMEM((rows, width), low),
            pltpu.VMEM((width, rows), low),
            pltpu.VMEM((rows, width), low),
            pltpu.VMEM((width, rows), low),
            pltpu.VMEM((rows, width), full),
            pltpu.VMEM((1, hidden * tensor), full),
            pltpu.VMEM((1, 3 * width), full),
            pltpu.VMEM((2, *block), low),
            pltpu.VMEM((2, *block), low),
            pltpu.VMEM((2, *block), low),
            pltpu.VMEM((2, *block), low),
            pltpu.VMEM(block, low),
            pltpu.VMEM((rows, BLOCK), low),
            pltpu.VMEM((rows, BLOCK), low),
            pltpu.SemaphoreType.DMA((8,)),
            pltpu.SemaphoreType.DMA((2, 2)),
            pltpu.SemaphoreType.DMA((2, 2)),
            pltpu.SemaphoreType.DMA((2,)),
            pltpu.SemaphoreType.DMA((2, max(1, tensor - 1), chunks)),
            pltpu.SemaphoreType.DMA((5,)),
            pltpu.SemaphoreType.DMA((count,)),
            pltpu.SemaphoreType.DMA((count, 4, peers)),
            pltpu.SemaphoreType.DMA((count, 4, peers)),
        ],
        compiler_params=pltpu.CompilerParams(
            collective_id=0, has_side_effects=True, vmem_limit_bytes=62 << 20
        ),
    )(inputs, cotangent, token_mask, vectors, *weights)


class Layout:
    def __init__(self, columns, hidden, order):
        sizes = {"qkv": 3 * columns, "out": columns, "one": hidden, "two": hidden, "vec": LANES}
        self.order = order
        self.sizes = sizes
        self.start = {}
        at = 0
        for name in order:
            self.start[name] = at
            at += sizes[name]
        self.total = at
        self.columns = columns

    def span(self, name):
        return (self.start[name], self.sizes[name])

    def matrices(self):
        base = self.start["qkv"]
        pairs = range(self.columns // LANES)
        spans = [[(base + (pair * 3 + at) * LANES, LANES) for pair in pairs] for at in range(3)]
        return spans + [[self.span(name)] for name in ("out", "one", "two")]


def pick(values, lane):
    row = jnp.zeros((1, LANES), jnp.float32)
    for at, value in enumerate(values):
        row = jnp.where(lane == at, value, row)
    return row


def total_of(values):
    return jnp.sum(jnp.sum(values, axis=1, keepdims=True), axis=0, keepdims=True)


def attend_pair_back(heads, bias, grads):
    parts = ([], [], [])
    for head in range(2):
        query, key, value = (
            heads[:, kind * LANES + head * HEAD_DIM : kind * LANES + (head + 1) * HEAD_DIM] for kind in range(3)
        )
        grad = grads[:, head * HEAD_DIM : (head + 1) * HEAD_DIM]
        scores = dot(key, query, CONTRACT_LAST) * (HEAD_DIM ** (-0.5) * LOG2E) + bias
        raised = jnp.exp2(scores - jnp.max(scores, axis=0, keepdims=True))
        attention = raised * (1.0 / jnp.sum(raised, axis=0, keepdims=True))
        grad_value = dot(attention.astype(jnp.bfloat16), grad)
        grad_attention = dot(value, grad, CONTRACT_LAST)
        weighted = jnp.sum(attention * grad_attention, axis=0, keepdims=True)
        grad_scores = (attention * (grad_attention - weighted) * HEAD_DIM ** (-0.5)).astype(jnp.bfloat16)
        grad_key = dot(grad_scores, query)
        grad_query = dot(key.T, grad_scores).T
        for kind, part in enumerate((grad_query, grad_key, grad_value)):
            parts[kind].append(part.astype(jnp.bfloat16))
    return jnp.concatenate([piece for kind in parts for piece in kind], axis=1)


def backward_kernel(dims, tensor, items, layout, *refs):
    (
        sum_two,
        sum_one,
        weight_qkv,
        weight_out,
        projected,
        input_ref,
        middle_ref,
        *far,
        bias_ref,
        table,
        vec_sums,
        pre_sums,
    ) = refs[:14]
    far = (*far, *refs[14:18])
    row_states, col_states = refs[18:22], refs[22:26]
    second_ref, vector_ref = refs[26:28]
    input_grad, total_ref, col_new_ref, row_new_ref, second_new_ref, sums_ref = refs[28:34]
    (
        own,
        from_core,
        one_x,
        one_y,
        two_y,
        two_x,
        from_z,
        late_z,
        late_one_y,
        late_one_x,
        late_two_x,
        late_two_y,
        col_sum,
        col_in,
        row_sum,
        row_in,
        small,
        small_in,
        square,
        turned,
        mixed,
        low_one,
        back_one,
        *weights,
        low_turned,
        back_turned,
        grad_mixed,
        out_buf,
        qkv_buf,
        head_buf,
        row_buf,
        out_stage,
        qkv_stage,
        vec_stage,
        head_sums,
        table_grad_ref,
        load_sem,
        stage_sem,
        core_sem,
        local_sem,
        send_sem,
        recv_sem,
        sum_send,
        sum_recv,
        far_sem,
    ) = refs[34:]
    near = (mixed, low_one, back_one, *weights)

    def far_load(at):
        return pltpu.make_async_copy(far[at], near[at], far_sem.at[at])

    here = Place(dims, tensor)
    nz, ny, nx = dims
    low = jnp.bfloat16
    own_rows = own.shape[3]
    half_rows = own_rows // 2
    rows, width = input_grad.shape
    own_place = (*here.at, here.rank)
    count = len(items)
    core_start = layout.start["out"]

    def columns(item):
        _, start, size, _ = items[item]
        return pl.ds(start, size)

    def core_columns(item):
        _, start, size, _ = items[item]
        return pl.ds(start - core_start, size)

    def moves(item, phase):
        first, second, whole = pl.ds(0, half_rows), pl.ds(half_rows, half_rows), pl.ds(0, own_rows)
        name, start, size, _ = items[item]
        column = columns(item)
        if name == LATE_NAME:
            column = pl.ds(start - layout.start[LATE_NAME], size)
            return (
                (),
                ((0, (0,), whole, late_z, column),),
                ((1, (0, 1), first, late_one_y, column), (2, (0, 2), second, late_one_x, column)),
                ((2, (0, 1, 2), first, late_two_x, column), (1, (0, 1, 2), second, late_two_y, column)),
            )[phase]
        return (
            (),
            ((2, (2,), first, one_x, column), (1, (1,), second, one_y, column)),
            ((1, (1, 2), first, two_y, column), (2, (1, 2), second, two_x, column)),
            ((0, (0, 1, 2), whole, from_z, column),),
        )[phase]

    def copies(item, phase):
        found = []
        for axis, fixed, part, landing, column in moves(item, phase):
            for step in range(1, here.size(axis)):
                target = here.moved(axis, step)
                index = tuple(target[a] if a in fixed else slice(None) for a in range(3))
                free = (slice(None),) * (3 - len(fixed))
                at = len(found)
                found.append(
                    pltpu.make_async_remote_copy(
                        src_ref=own.at[(*index, part, columns(item))],
                        dst_ref=landing.at[(step - 1, *free, slice(None), column)],
                        send_sem=send_sem.at[item, phase, at],
                        recv_sem=recv_sem.at[item, phase, at],
                        device_id=here.device(target),
                        device_id_type=MESH,
                    )
                )
        return found

    def add_core(item):
        def body(at, carry):
            z, y, x = at // (ny * nx), at // nx % ny, at % nx
            value = own[z, y, x, :, columns(item)]
            for step in range(tensor - 1):
                value = value + from_core[step, z, y, x, :, core_columns(item)]
            own[z, y, x, :, columns(item)] = value
            return carry

        if tensor > 1:
            lax.fori_loop(0, nz * ny * nx, body, 0)

    def add_in(item, phase):
        wide = columns(item)
        for axis, fixed, part, landing, column in moves(item, phase):
            steps = here.size(axis) - 1
            if phase == 3:
                value = own[(*here.at, part, wide)].astype(jnp.float32)
                for step in range(steps):
                    value = value + landing[step, :, column].astype(jnp.float32)
                total_ref[part, wide] = value
                continue
            if steps == 0:
                continue
            free = [a for a in range(3) if a not in fixed]
            sizes = [dims[a] for a in free]
            loops = 1
            for size in sizes:
                loops *= size

            def body(at, carry):
                place = list(here.at)
                inner = []
                rest = at
                for axis_at, size in reversed(list(zip(free, sizes))):
                    place[axis_at] = rest % size
                    inner.insert(0, rest % size)
                    rest = rest // size
                where = (*place, part, wide)
                value = own[where]
                for step in range(steps):
                    value = value + landing[(step, *inner, slice(None), column)]
                own[where] = value
                return carry

            lax.fori_loop(0, loops, body, 0)

    sent = []

    def exchange(kind, phase, axes, buffer, landing):
        moved = []
        for at, device in enumerate(here.peers(*axes)):
            copy = pltpu.make_async_remote_copy(
                src_ref=buffer.at[phase],
                dst_ref=landing.at[phase, at],
                send_sem=sum_send.at[kind, phase, at],
                recv_sem=sum_recv.at[kind, phase, at],
                device_id=device,
                device_id_type=MESH,
            )
            copy.start()
            moved.append(copy)
        sent.extend(moved)

        def finish():
            value = buffer[phase]
            for at, copy in enumerate(moved):
                copy.wait_recv()
                value = value + landing[phase, at]
            buffer[phase + 1] = value

        return finish

    def hand_over(item, step, source, sem):
        return pltpu.make_async_remote_copy(
            src_ref=source,
            dst_ref=from_core.at[step - 1, :, :, :, :, core_columns(item)],
            send_sem=sem,
            recv_sem=core_sem.at[item, step - 1],
            device_id=here.device(here.moved(3, step)),
            device_id_type=MESH,
        )

    arriving = {}

    def keep_own(item, value):
        own[:, :, :, :, columns(item)] = value.reshape(nz, ny, nx, own_rows, value.shape[1])

    out_items = [at for at, item in enumerate(items) if item[0] == "out"]
    qkv_items = [at for at, item in enumerate(items) if item[0] == "qkv"]
    vec_item = count - 1
    per_rank = len(qkv_items)
    steps_in_all = per_rank * tensor

    def rank_at(step):
        return lax.rem(here.rank + step, tensor)

    def pair_loads(at):
        turn_at, place = divmod(at, tensor)
        pair = rank_at(place + 1) * per_rank + turn_at
        column = pl.ds(pl.multiple_of(pair * 3 * LANES, LANES), 3 * LANES)
        near = at % 2
        return pair, column, [
            pltpu.make_async_copy(
                weight_qkv.at[rank_at(place + 1), turn_at], qkv_buf.at[near], load_sem.at[0, near]
            ),
            pltpu.make_async_copy(projected.at[:, column], head_buf.at[near], load_sem.at[1, near]),
        ]

    def out_task():
        fetch = [
            pltpu.make_async_copy(weight_out.at[rank, 0], out_buf.at[rank], load_sem.at[2, 0])
            for rank in range(tensor)
        ]
        for copy in fetch:
            copy.start()
        far_load(2).wait()
        turn(back_one, back_turned)
        far_load(0).wait()
        for copy in pair_loads(0)[2]:
            copy.start()
        size = out_stage.shape[5]
        item = out_items[0]
        for step in range(1, tensor + 1):
            column = pl.ds(pl.multiple_of(rank_at(step) * size, LANES), size)
            value = dot(back_turned[...], mixed[:, column]).astype(low)
            if step < tensor:
                out_stage[step - 1] = value.reshape(nz, ny, nx, own_rows, size)
                copy = hand_over(item, step, out_stage.at[step - 1], stage_sem.at[item, step - 1])
                copy.start()
                sent.append(copy)
                arriving.setdefault(item, []).append(copy)
            else:
                keep_own(item, value)
        for copy in fetch:
            copy.wait()
        for rank in range(tensor):
            weight = out_buf[rank].reshape(width, size)
            grad_mixed[:, pl.ds(rank * size, size)] = dot(back_one[...], weight).astype(low)
        far_load(1).wait()
        turn(low_one, low_turned)

    def state_task():
        def fill(refs, other):
            square[...] = jnp.full_like(square, other)
            base = 0
            for ref in refs:
                square[pl.ds(base, ref.shape[0]), :] = ref[...]
                base += ref.shape[0]
            return square[...].T

        for at in range(3, 7):
            far_load(at).wait()
        turned[0] = fill(row_states, 1.0)
        turned[1] = fill((second_ref,), 1.0)
        turned[2] = fill((vector_ref,), 0.0)

    staged = {}

    def pair_task(at):
        turn_at, place = divmod(at, tensor)
        pair, column, loads = pair_loads(at)
        for copy in loads:
            copy.wait()
        if at + 1 < steps_in_all:
            for copy in pair_loads(at + 1)[2]:
                copy.start()
        near = at % 2
        grads = grad_mixed[:, pl.ds(pl.multiple_of(pair * LANES, LANES), LANES)]
        value = attend_pair_back(head_buf[near], bias_ref[...], grads)
        head_sums[:, column] = jnp.sum(value.astype(jnp.float32), axis=0, keepdims=True)
        weight = qkv_buf[near].reshape(width, 3 * LANES)
        term = dot(value, weight, CONTRACT_LAST)
        if at == 0:
            input_grad[...] = term
        else:
            input_grad[...] += term
        item = qkv_items[turn_at]
        grad = dot(low_turned[...], value).astype(low)
        if place + 1 < tensor:
            if near in staged:
                staged[near].wait_send()
            qkv_stage[near] = grad.reshape(nz, ny, nx, own_rows, 3 * LANES)
            copy = hand_over(item, place + 1, qkv_stage.at[near], stage_sem.at[item, place])
            copy.start()
            staged[near] = copy
            arriving.setdefault(item, []).append(copy)
        else:
            keep_own(item, grad)

    def last_task():
        step_rows = LANES

        def fetch(at):
            near = lax.rem(at, 2)
            part = pl.ds(pl.multiple_of(at * step_rows, step_rows), step_rows)
            return [
                pltpu.make_async_copy(source.at[part, :], row_buf.at[which, near], load_sem.at[which, near])
                for which, source in enumerate((input_ref, middle_ref))
            ]

        for copy in fetch(0):
            copy.start()

        def body(at, sums):
            for copy in fetch(at):
                copy.wait()

            @pl.when(at + 1 < rows // step_rows)
            def _():
                for copy in fetch(at + 1):
                    copy.start()

            near = lax.rem(at, 2)
            part = pl.ds(pl.multiple_of(at * step_rows, step_rows), step_rows)
            normed, inverse = norm_rows(row_buf[0, near])
            grad_low = input_grad[part, :]
            scaled = grad_low * table[0:1, :]
            first = jnp.mean(scaled, axis=1, keepdims=True)
            second = jnp.mean(scaled * normed, axis=1, keepdims=True)
            input_grad[part, :] = row_buf[1, near] + inverse * (scaled - first - normed * second)
            terms = (grad_low * normed, grad_low)
            return tuple(old + jnp.sum(term, axis=0, keepdims=True) for old, term in zip(sums, terms))

        zero = jnp.zeros((1, width), jnp.float32)
        found = lax.fori_loop(0, rows // step_rows, body, (zero, zero))
        table_grad_ref[...] = jnp.zeros_like(table_grad_ref)
        for at in range(2):
            table_grad_ref[at : at + 1, :] = found[at]
        for pair in range(width // LANES):
            for kind, row in ((0, 2), (2, 3)):
                table_grad_ref[row : row + 1, pl.ds(pair * LANES, LANES)] = head_sums[
                    :, pl.ds((pair * 3 + kind) * LANES, LANES)
                ]
        for at, row in enumerate((4, 5, 6, VEC - 1)):
            table_grad_ref[row : row + 1, :] = vec_sums[at : at + 1, :]
        for at in range(VEC - 8):
            table_grad_ref[7 + at : 8 + at, :] = pre_sums[:, pl.ds(at * width, width)]
        value = table_grad_ref[...].T.astype(low)
        vec_stage[...] = value.reshape(nz, ny, nx, own_rows, LANES)
        for step in range(1, tensor):
            copy = hand_over(vec_item, step, vec_stage, stage_sem.at[vec_item, step - 1])
            copy.start()
            sent.append(copy)
            arriving.setdefault(vec_item, []).append(copy)
        keep_own(vec_item, value)

    for at in (2, 0, 1, 3, 4, 5, 6):
        far_load(at).start()
    here.barrier(((0, 3), (1, 2)))
    local = {}
    for item, (name, _, _, source) in enumerate(items):
        if name in ("one", "two"):
            array = sum_one if name == "one" else sum_two
            copy = pltpu.make_async_copy(
                array.at[source], own.at[:, :, :, :, columns(item)], local_sem.at[item]
            )
            copy.start()
            local[item] = copy

    def advance(item, phase):
        if phase > 1:
            for copy in copies(item, phase - 1):
                copy.wait_recv()
            add_in(item, phase - 1)
        elif item in local:
            local[item].wait()
        else:
            for copy in arriving.get(item, ()):
                copy.wait_recv()
            add_core(item)
        if phase < 4:
            for copy in copies(item, phase):
                copy.start()
                sent.append(copy)

    steps = Steps()
    owner = {item: ("out", 0) for item in out_items}
    owner |= {item: ("pair", tensor * (at + 1) - 1) for at, item in enumerate(qkv_items)}
    owner[vec_item] = ("last", 0)
    for item, (name, _, size, _) in enumerate(items):
        share = size / layout.total
        length = {1: share * UNIT * nz, 2: share * UNIT * nz / 2, 3: share * UNIT * nz}
        links = {1: "xy", 2: "xy", 3: "z"}
        if name == LATE_NAME:
            length = {1: share * UNIT * nz * ny * nx, 2: share * UNIT, 3: share * UNIT / 2}
            links = {1: "z", 2: "xy", 3: "xy"}
        early = item not in owner
        for phase in range(1, 5):
            after = [("copy", item, phase - 1)] if phase > 1 else []
            waits = [(item, phase - 1)] if phase > 1 else []
            if phase == 1 and early and item >= DEPTH:
                after = [("copy", item - DEPTH, 2)]
            if phase == 1 and not early:
                after, waits = [owner[item]], [("core", owner[item])]
            steps.add(
                ("copy", item, phase),
                functools.partial(advance, item, phase),
                PUMP * (1.5 if phase == 2 else 1.0),
                (0.5 if phase == 1 and early else 0.0),
                after,
                waits,
                [((item, phase), links[phase], length[phase])] if phase < 4 else [],
            )
    steps.add(("state", 0), state_task, 1.0, 2.0)
    steps.add(("out", 0), out_task, 8.0, 1.0, (), (), [(("core", ("out", 0)), "core", CORE_UNIT / 12)])
    for at in range(steps_in_all):
        after = [("pair", at - 1) if at else ("out", 0)]
        starts = [(("core", ("pair", at)), "core", CORE_UNIT / 24)]
        steps.add(("pair", at), functools.partial(pair_task, at), 6.0, 1.0, after, (), starts)
    steps.add(
        ("last", 0), last_task, 4.0, 1.0, [("pair", steps_in_all - 1)], (), [(("core", ("last", 0)), "core", 1.0)]
    )
    steps.run()
    sent.extend(staged.values())

    decay_rate = 1.0 - STEP ** (-0.8)
    keep_old = 1.0 - decay_rate
    long = layout.sizes["one"] * tensor
    matrices = layout.matrices()
    lane = lax.broadcasted_iota(jnp.int32, (1, LANES), 1)
    row_parts = []
    for spans in matrices:
        row_part = 0.0
        for start, size in spans:
            value = total_ref[:, pl.ds(start, size)]
            square = value * value
            col_sum[0, :, pl.ds(start, size)] = jnp.sum(square, axis=0, keepdims=True)
            row_part = row_part + jnp.sum(square, axis=1, keepdims=True)
        row_parts.append(row_part)
    row_sum[0] = pick(row_parts, lane)
    finish_row = exchange(0, 0, (3,), row_sum, row_in)
    finish_col = exchange(1, 0, (0,), col_sum, col_in)
    vec_start = layout.start["vec"]
    table_grad = total_ref[:, pl.ds(vec_start, LANES)]
    second_new = decay_rate * turned[1] + keep_old * (table_grad * table_grad + EPS_ONE)
    second_new_ref[...] = second_new
    vector_update = table_grad * lax.rsqrt(second_new)
    vector_sums = jnp.sum(vector_update * vector_update, axis=0, keepdims=True) / tensor
    vector_weight = jnp.sum(turned[2] * turned[2], axis=0, keepdims=True) / tensor
    weight_sums = [total_of(jnp.sum(weights[0][...] * weights[0][...], axis=0))]
    weight_sums += [total_of(ref[...] * ref[...]) for ref in weights[1:]]
    finish_row()
    row_counts = pick([jnp.full((1, 1), 1.0 / size, jnp.float32) for size in (width, width, width, width, long, long)], lane)
    row_new = decay_rate * turned[0] + keep_old * (row_sum[1] * row_counts + EPS_ONE)
    row_new_ref[...] = row_new
    finish_col()
    exchange(1, 1, (1, 2), col_sum, col_in)()
    for at, spans in enumerate(matrices):
        for place, (start, size) in enumerate(spans):
            if at < 3:
                old = col_states[0][at : at + 1, pl.ds(place * LANES, LANES)]
            else:
                old = col_states[at - 2][...]
            fresh = keep_old * (col_sum[2, :, pl.ds(start, size)] / width + EPS_ONE)
            col_new_ref[:, pl.ds(start, size)] = decay_rate * old + fresh
    ratios = []
    means = []
    for at, spans in enumerate(matrices):
        row_at = row_new[:, at : at + 1]
        ratio = 0.0
        for start, size in spans:
            value = total_ref[:, pl.ds(start, size)]
            col_at = col_new_ref[:, pl.ds(start, size)]
            ratio = ratio + total_of(value * value / (row_at * col_at))
        ratios.append(ratio)
        if at in (3, 5):
            means.append(jnp.sum(col_at, axis=1, keepdims=True) / (nz * ny * nx))
        else:
            means.append(jnp.sum(row_at, axis=0, keepdims=True) / tensor)
    small[0] = jnp.concatenate(
        [pick(ratios + means + weight_sums, lane), vector_sums, vector_weight, jnp.zeros((5, LANES), jnp.float32)], axis=0
    )
    exchange(2, 0, (0, 3), small, small_in)()
    exchange(2, 1, (1, 2), small, small_in)()
    sums_ref[...] = small[2]
    for copy in sent:
        copy.wait_send()


def backward(dims, tensor, layout, large, near, weights, states):
    rows, width = large[-1].shape
    own_rows = width // (dims[0] * dims[1] * dims[2])
    half_rows = own_rows // 2
    columns = layout.columns
    items = []
    for block in range(layout.sizes["one"] // BLOCK):
        for name in ("two", "one"):
            items.append((name, layout.start[name] + block * BLOCK, BLOCK, block))
    items.append(("out", layout.start["out"], columns, 0))
    for start in range(0, 3 * columns, 3 * LANES):
        items.append(("qkv", layout.start["qkv"] + start, 3 * LANES, start))
    items.append(("vec", layout.start["vec"], LANES, 0))
    nz, ny, nx = dims
    peers = max(1, nz - 1, ny + nx - 2)
    group = max(1, nz * tensor - 1, ny * nx - 1)
    others = max(1, tensor - 1)
    offset = layout.total
    from_here = offset - layout.start["out"]
    low, full = jnp.bfloat16, jnp.float32
    anywhere = pl.BlockSpec(memory_space=pl.ANY)
    inside = pl.BlockSpec(memory_space=pltpu.VMEM)

    def hold(*shape):
        return pltpu.VMEM(tuple(max(1, size) for size in shape), low)

    sums = offset - LANES
    count = len(items)
    return pl.pallas_call(
        functools.partial(backward_kernel, dims, tensor, tuple(items), layout),
        name="backward",
        out_shape=[
            jax.ShapeDtypeStruct((rows, width), full),
            jax.ShapeDtypeStruct((own_rows, offset), full),
            jax.ShapeDtypeStruct((1, sums), full),
            jax.ShapeDtypeStruct((own_rows, LANES), full),
            jax.ShapeDtypeStruct((own_rows, LANES), full),
            jax.ShapeDtypeStruct((8, LANES), full),
        ],
        in_specs=[anywhere] * len(large) + [inside] * len(near) + [anywhere] * 4 + [inside] * len(states),
        out_specs=[inside] * 6,
        scratch_shapes=[
            hold(nz, ny, nx, own_rows, offset),
            hold(others, nz, ny, nx, own_rows, from_here),
            hold(nx - 1, nz, ny, half_rows, offset),
            hold(ny - 1, nz, nx, half_rows, offset),
            hold(ny - 1, nz, half_rows, offset),
            hold(nx - 1, nz, half_rows, offset),
            hold(nz - 1, own_rows, offset),
            hold(nz - 1, ny, nx, own_rows, columns),
            hold(ny - 1, nx, half_rows, columns),
            hold(nx - 1, ny, half_rows, columns),
            hold(nx - 1, half_rows, columns),
            hold(ny - 1, half_rows, columns),
            pltpu.VMEM((3, 1, sums), full),
            pltpu.VMEM((2, max(1, nz - 1, ny * nx - 1), 1, sums), full),
            pltpu.VMEM((2, own_rows, LANES), full),
            pltpu.VMEM((1, others, own_rows, LANES), full),
            pltpu.VMEM((3, 8, LANES), full),
            pltpu.VMEM((2, group, 8, LANES), full),
            pltpu.VMEM((LANES, own_rows), full),
            pltpu.VMEM((3, own_rows, LANES), full),
            *[hold(rows, width)] * 3,
            *(pltpu.VMEM(weight.shape, full) for weight in weights),
            hold(width, rows),
            hold(width, rows),
            hold(rows, width),
            hold(tensor, *dims, own_rows, columns),
            hold(2, *dims, own_rows, 3 * LANES),
            hold(2, rows, 3 * LANES),
            pltpu.VMEM((2, 2, LANES, width), full),
            hold(others, *dims, own_rows, columns),
            hold(2, *dims, own_rows, 3 * LANES),
            hold(*dims, own_rows, LANES),
            pltpu.VMEM((1, 3 * width), full),
            pltpu.VMEM((LANES, width), full),
            pltpu.SemaphoreType.DMA((3, 2)),
            pltpu.SemaphoreType.DMA((count, others)),
            pltpu.SemaphoreType.DMA((count, others)),
            pltpu.SemaphoreType.DMA((count,)),
            pltpu.SemaphoreType.DMA((count, 4, peers)),
            pltpu.SemaphoreType.DMA((count, 4, peers)),
            pltpu.SemaphoreType.DMA((3, 2, group)),
            pltpu.SemaphoreType.DMA((3, 2, group)),
            pltpu.SemaphoreType.DMA((7,)),
        ],
        compiler_params=pltpu.CompilerParams(
            collective_id=1, has_side_effects=True, vmem_limit_bytes=63 << 20
        ),
    )(*large, *near, *weights, *states)


def update_kernel(layout, width, long, *refs):
    block_in, grad_in = refs[:2]
    far = refs[2:12]
    block_out, input_grad = refs[12:14]
    own_qkv, own_out, own_one, own_two, own_table = refs[14:19]
    new_qkv, new_out, new_one, new_two, new_vectors, second_new = refs[19:25]
    qkv_row, qkv_col, out_row, out_col, one_row, one_col, two_row, two_col = refs[25:33]
    near, passing, sem = refs[33:43], refs[43:45], refs[45]
    loads = [
        pltpu.make_async_copy(source, target, sem.at[at])
        for at, (source, target) in enumerate(zip((*far, block_in, grad_in), (*near, *passing)))
    ]
    long_copies = [
        pltpu.make_async_copy(source, target, sem.at[12 + at])
        for at, (source, target) in enumerate(zip(passing, (block_out, input_grad)))
    ]
    for copy in loads:
        copy.start()
    for copy in loads:
        copy.wait()
    for copy in long_copies:
        copy.start()
    total_ref, col_ref, row_ref, second_ref, sums_ref, vector_ref = near[:6]
    weights = near[6:]
    lane = lax.broadcasted_iota(jnp.int32, (1, LANES), 1)

    def at(index):
        return sums_ref[0:1, index : index + 1]

    lengths = (width, width, width, width, width, long)
    means = [at(6 + m) / lengths[m] for m in range(6)]
    squares = [means[m] * at(m) for m in range(6)]
    squares = [squares[0] + squares[1] + squares[2], *squares[3:]]
    entries = (3 * width * width, width * width, width * long, width * long)
    step_size = []
    for m in range(4):
        damping = 1.0 / jnp.maximum(1.0, jnp.sqrt(squares[m] / entries[m] + 1e-06) / CLIP_LEVEL)
        step_size.append(LEARN_RATE * jnp.sqrt(at(12 + m) / entries[m] + 1e-06) * damping)
    spread = [(m, place, *span) for m, spans in enumerate(layout.matrices()) for place, span in enumerate(spans)]
    for m, place, start, size in spread:
        grad = total_ref[:, pl.ds(start, size)]
        col = col_ref[:, pl.ds(start, size)]
        step = step_size[max(0, m - 2)] * grad * lax.rsqrt(row_ref[:, m : m + 1] * col / means[m])
        if m < 3:
            part = slice(place * LANES, (place + 1) * LANES)
            own_qkv[m, :, part] = grad
            new_qkv[m, :, part] = weights[0][m, :, part] - step
            qkv_col[m : m + 1, part] = col
        else:
            own, new, state = (
                (own_out, new_out, out_row),
                (own_one, new_one, one_col),
                (own_two, new_two, two_row),
            )[m - 3]
            own[...] = grad
            new[...] = weights[m - 2][...] - step
            state[...] = col
    row_flat = row_ref[...].T
    qkv_row[...] = row_flat[0:3]
    out_col[...] = row_flat[3:4]
    one_row[...] = row_flat[4:5]
    two_col[...] = row_flat[5:6]

    wide = (lane >= 7) & (lane < VEC - 1)
    counts = jnp.where(wide, float(long), float(width))

    def grouped(values):
        inside = jnp.sum(jnp.where(wide, values, 0.0), axis=1, keepdims=True)
        return jnp.where(wide, inside, values)

    table_grad = total_ref[:, pl.ds(layout.start["vec"], LANES)]
    update = table_grad * lax.rsqrt(second_ref[...])
    norm = jnp.sqrt(grouped(sums_ref[1:2, :]) / counts + 1e-06)
    size = jnp.sqrt(grouped(sums_ref[2:3, :]) / counts + 1e-06)
    change = LEARN_RATE * size / jnp.maximum(1.0, norm / CLIP_LEVEL) * update
    own_table[...] = table_grad.T[:VEC]
    new_vectors[...] = vector_ref[...] - change.T[:VEC]
    second_new[...] = second_ref[...].T[:VEC]
    for copy in long_copies:
        copy.wait()


def update_weights(layout, width, long, columns, hidden, rows, results, values, vectors, weights):
    full = jnp.float32
    shapes = [
        *(result.shape for result in results),
        (3, rows, columns),
        (rows, columns),
        (rows, hidden),
        (rows, hidden),
        (VEC, rows),
        (3, rows, columns),
        (rows, columns),
        (rows, hidden),
        (rows, hidden),
        (VEC, rows),
        (VEC, rows),
        (3, rows),
        (3, columns),
        (1, columns),
        (1, rows),
        (1, rows),
        (1, hidden),
        (1, hidden),
        (1, rows),
    ]
    far = (*values, vectors, *weights)
    anywhere = pl.BlockSpec(memory_space=pl.ANY)
    inside = pl.BlockSpec(memory_space=pltpu.VMEM)
    return pl.pallas_call(
        functools.partial(update_kernel, layout, width, long),
        name="update_weights",
        out_shape=[jax.ShapeDtypeStruct(shape, full) for shape in shapes],
        in_specs=[anywhere] * (2 + len(far)),
        out_specs=[anywhere] * 2 + [inside] * (len(shapes) - 2),
        scratch_shapes=[
            *(pltpu.VMEM(array.shape, full) for array in (*far, *results)),
            pltpu.SemaphoreType.DMA((4 + len(far),)),
        ],
        compiler_params=pltpu.CompilerParams(vmem_limit_bytes=63 << 20),
    )(*results, *far)


def on_device(
    inputs,
    cotangent,
    token_mask,
    w_qkv,
    w_out,
    w_fc1,
    w_fc2,
    vectors,
    qkv_row,
    qkv_col,
    out_row,
    out_col,
    fc1_row,
    fc1_col,
    fc2_row,
    fc2_col,
    vec_second,
):
    tensor_count = lax.axis_size("tensor")
    dims = grid_of(lax.axis_size("fsdp"))
    width = inputs.shape[1]
    own_rows, columns = w_qkv.shape[1:]
    hidden = w_fc1.shape[1]
    weights = (w_qkv, w_out.T, w_fc1, w_fc2.T)
    (
        weight_qkv,
        _,
        weight_out,
        *_,
        block_out,
        grad_middle,
        back_one,
        mixed_rows,
        low_one,
        projected,
        grad_one,
        grad_two,
        table,
        vec_sums,
        pre_sums,
        bias_column,
    ) = forward(dims, tensor_count, inputs, cotangent, token_mask, vectors, weights)
    layout = Layout(columns, hidden, ("two", "one", "out", "qkv", "vec"))
    row_states = (qkv_row, out_col[None], fc1_row[None], fc2_col[None])
    col_states = (qkv_col, out_row[None], fc1_col[None], fc2_row[None])
    input_grad, *values = backward(
        dims,
        tensor_count,
        layout,
        (
            grad_two,
            grad_one,
            weight_qkv,
            weight_out,
            projected,
            inputs,
            grad_middle,
            mixed_rows,
            low_one,
            back_one,
        ),
        (bias_column, table, vec_sums, pre_sums),
        weights,
        (*row_states, *col_states, vec_second, vectors),
    )
    outs = update_weights(
        layout, width, FF, columns, hidden, own_rows, (block_out, input_grad), values, vectors, weights
    )
    outs = [out.reshape(-1) if out.shape[0] == 1 else out for out in outs]
    for at in (3, 5, 8, 10):
        outs[at] = outs[at].T
    return (*outs[:12], *outs[13:], outs[12])


def solution(mesh):
    in_specs = (
        P(("fsdp", "tensor"), None),
        P(("fsdp", "tensor"), None),
        P("fsdp", None),
        P(None, "fsdp", "tensor"),
        P("tensor", "fsdp"),
        P("fsdp", "tensor"),
        P("tensor", "fsdp"),
        P(None, "fsdp"),
        P(None, "fsdp"),
        P(None, "tensor"),
        P("tensor"),
        P("fsdp"),
        P("fsdp"),
        P("tensor"),
        P("tensor"),
        P("fsdp"),
        P(None, "fsdp"),
    )
    out_specs = (
        P(("fsdp", "tensor"), None),
        P(("fsdp", "tensor"), None),
        P(None, "fsdp", "tensor"),
        P("tensor", "fsdp"),
        P("fsdp", "tensor"),
        P("tensor", "fsdp"),
        P(None, "fsdp"),
        P(None, "fsdp", "tensor"),
        P("tensor", "fsdp"),
        P("fsdp", "tensor"),
        P("tensor", "fsdp"),
        P(None, "fsdp"),
        P(None, "fsdp"),
        P(None, "tensor"),
        P("tensor"),
        P("fsdp"),
        P("fsdp"),
        P("tensor"),
        P("tensor"),
        P("fsdp"),
        P(None, "fsdp"),
    )
    return jax.shard_map(
        on_device, mesh=mesh, in_specs=in_specs, out_specs=out_specs, check_vma=False
    )
```

```python
import functools

import jax
import jax.numpy as jnp
from jax import lax
from jax.experimental import pallas as pl
from jax.experimental.pallas import tpu as pltpu
from jax.sharding import PartitionSpec as P

HEAD_DIM = 64
FF = 4096
STEP = 20
VEC = 12
LANES = 128

EPS_NORM = 1e-05
EPS_ONE = 1e-30
CLIP_LEVEL = 1.0
LEARN_RATE = 0.5
MESH = pl.DeviceIdType.MESH
LOG2E = 1.4426950408889634
CONTRACT_LAST = (((1,), (1,)), ((), ()))


def grid_of(count):
    return {16: (4, 2, 2), 32: (2, 4, 4)}.get(count, (count, 1, 1))


class Place:
    def __init__(self, dims, tensor):
        self.dims = dims
        self.tensor = tensor
        fsdp = lax.axis_index("fsdp")
        _, ny, nx = dims
        self.at = (fsdp // (ny * nx), (fsdp // nx) % ny, fsdp % nx)
        self.rank = lax.axis_index("tensor")

    def moved(self, axis, step):
        place = list(self.at) + [self.rank]
        size = (*self.dims, self.tensor)[axis]
        place[axis] = lax.rem(place[axis] + step + size, size)
        return tuple(place)

    def device(self, place):
        z, y, x, rank = place
        return {"fsdp": (z * self.dims[1] + y) * self.dims[2] + x, "tensor": rank}

    def size(self, axis):
        return (*self.dims, self.tensor)[axis]

    def line(self):
        z = self.at[0]
        pair = z // 2 * 2
        middle = (z == 1) | (z == 2)
        return pair, 2 - pair, z + 1 - 2 * (z % 2), middle

    def at_z(self, z):
        return self.device((z, self.at[1], self.at[2], self.rank))

    def peers(self, *axes):
        places = [()]
        for axis in axes:
            places = [(*steps, step) for steps in places for step in range(self.size(axis))]
        found = []
        for steps in places[1:]:
            place = list(self.at) + [self.rank]
            for axis, step in zip(axes, steps):
                place[axis] = lax.rem(place[axis] + step, self.size(axis))
            found.append(self.device(tuple(place)))
        return found

    def barrier(self, groups):
        sem = pltpu.get_barrier_semaphore()
        count = 0
        for axes in groups:
            for device in self.peers(*axes):
                pl.semaphore_signal(sem, inc=1, device_id=device, device_id_type=MESH)
                count += 1
        if count:
            pl.semaphore_wait(sem, count)


def norm_rows(values):
    average = jnp.mean(values, axis=1, keepdims=True)
    center = values - average
    inverse = lax.rsqrt(jnp.mean(center * center, axis=1, keepdims=True) + EPS_NORM)
    return center * inverse, inverse


def dot(left, right, dims=(((1,), (0,)), ((), ()))):
    return lax.dot_general(left, right, dims, preferred_element_type=jnp.float32)


def turn(source, target):
    for start in range(0, source.shape[1], LANES):
        target[pl.ds(start, LANES), :] = source[:, pl.ds(start, LANES)].T


def attend_pair(heads, bias):
    mixed = []
    for head in range(2):
        query, key, value = (
            heads[:, kind * LANES + head * HEAD_DIM : kind * LANES + (head + 1) * HEAD_DIM] for kind in range(3)
        )
        scores = dot(query, key, CONTRACT_LAST) * (HEAD_DIM ** (-0.5) * LOG2E) + bias
        raised = jnp.exp2(scores - jnp.max(scores, axis=1, keepdims=True))
        summed = jnp.sum(raised, axis=1, keepdims=True)
        attention = (raised * (1.0 / summed)).astype(jnp.bfloat16)
        mixed.append(dot(attention, value).astype(jnp.bfloat16))
    return jnp.concatenate(mixed, axis=1)


def guarded(condition, run):
    if condition is None:
        run()
    else:
        pl.when(condition)(run)


def along_z(count):
    return ("pair", "middle", "back") if count == 4 else ("all",)


class Steps:
    def __init__(self):
        self.steps = {}

    def add(self, name, run, time, rank, after=(), waits=(), starts=()):
        self.steps[name] = (run, time, rank, tuple(after), tuple(waits), tuple(starts))

    def arrange(self):
        now, free, arrival, done, order = 0.0, {}, {}, set(), []
        left = list(self.steps)
        while left:
            best, soonest = None, None
            for name in left:
                _, time, rank, after, waits, _ = self.steps[name]
                if any(other not in done for other in after) or any(wait not in arrival for wait in waits):
                    continue
                ready = max([arrival[wait] for wait in waits], default=0.0)
                if ready <= now:
                    if best is None or rank < self.steps[best][2]:
                        best = name
                elif soonest is None or ready < soonest:
                    soonest = ready
            if best is None:
                now = soonest
                continue
            _, time, _, _, _, starts = self.steps[best]
            now += time
            for transfer, link, length in starts:
                begin = max(now, free.get(link, 0.0))
                free[link] = begin + length
                arrival[transfer] = begin + length + LATENCY
            done.add(best)
            left.remove(best)
            order.append(best)
        return order, now

    def run(self):
        for name in self.arrange()[0]:
            self.steps[name][0]()


class Gather:
    def __init__(self, here, pack_ref, outs, parts, local_sem, send_sem, recv_sem):
        self.here = here
        self.pack = pack_ref
        self.outs = outs
        self.rows = pack_ref.shape[0]
        self.parts = parts
        self.late = [len(parts) - at for at in LATE_PARTS if at < len(parts)]
        self.sems = (local_sem, send_sem, recv_sem)
        self.own = (*here.at, here.rank)
        self.sent = []

    def region(self, item, part, place, free):
        out, _, chunk, _ = self.parts[item]
        index = tuple(slice(None) if a in free else place[a] for a in range(3))
        lead = () if chunk is None else (place[3], chunk)
        return self.outs[out].at[(*lead, *index, part)]

    def shard(self, item, part):
        _, offset, _, size = self.parts[item]
        return self.pack.at[part, pl.ds(offset, size)]

    def phases(self, item):
        lengthwise = along_z(self.here.dims[0]) if self.parts[item][0] in (3, 4) else ("all",)
        across = ("first", "second")
        order = (*across, *lengthwise) if item in self.late else (*lengthwise, *across)
        return order if self.parts[item][2] is None else (*order, "core")

    def moves(self, item, phase):
        here, own = self.here, self.own
        kind = self.phases(item)[phase]
        late = item in self.late
        whole, half = pl.ds(0, self.rows), self.rows // 2
        first, second = pl.ds(0, half), pl.ds(half, half)
        found = []
        if kind in ("pair", "middle", "back"):
            free = (1, 2) if late else ()
            pair, far, near, middle = here.line()

            def blocks(z):
                return self.region(item, whole, (z, *own[1:]), free)

            if kind == "pair":
                sent = self.shard(item, whole) if phase == 0 else blocks(own[0])
                found.append((here.at_z(near), sent, blocks(own[0]), blocks(near), None, None))
            elif kind == "middle":
                pairs = blocks(pl.ds(pair, 2))
                found.append((here.at_z(3 - own[0]), pairs, pairs, blocks(pl.ds(far, 2)), middle, middle))
            else:
                pairs = blocks(pl.ds(far, 2))
                outside = jnp.logical_not(middle)
                found.append((here.at_z(near), pairs, pairs, pairs, middle, outside))
            return found
        before = () if late else (0,)
        steps = {
            "all": ((0, (1, 2) if late else (), whole),),
            "first": ((2, before, first), (1, before, second))
            if late
            else ((1, before, first), (2, before, second)),
            "second": ((1, (*before, 2), first), (2, (*before, 1), second))
            if late
            else ((2, (*before, 1), first), (1, (*before, 2), second)),
            "core": ((3, (0, 1, 2), whole),),
        }[kind]
        for axis, free, part in steps:
            for step in range(1, here.size(axis)):
                place = self.region(item, part, own, free)
                sent = self.shard(item, part) if phase == 0 else place
                landed = self.region(item, part, here.moved(axis, -step), free)
                found.append((here.device(here.moved(axis, step)), sent, place, landed, None, None))
        return found

    def copies(self, item, phase, landing):
        found = []
        for at, (device, sent, place, landed, sends, receives) in enumerate(self.moves(item, phase)):
            copy = pltpu.make_async_remote_copy(
                src_ref=landed if landing else sent,
                dst_ref=landed if landing else place,
                send_sem=self.sems[1].at[item, phase, at],
                recv_sem=self.sems[2].at[item, phase, at],
                device_id=device,
                device_id_type=MESH,
            )
            found.append((receives if landing else sends, copy))
        return found

    def keep(self, item):
        whole = pl.ds(0, self.rows)
        return pltpu.make_async_copy(
            self.shard(item, whole), self.region(item, whole, self.own, ()), self.sems[0].at[item]
        )

    def advance(self, item, phase):
        if phase:
            for condition, copy in self.copies(item, phase - 1, True):
                guarded(condition, copy.wait_recv)
        if phase == 0:
            self.keep(item).start()
        if phase == 1:
            self.keep(item).wait()
        if phase < len(self.phases(item)):
            for condition, copy in self.copies(item, phase, False):
                guarded(condition, copy.start)
                self.sent.append((condition, copy))

    def finish(self):
        for condition, copy in self.sent:
            guarded(condition, copy.wait_send)


BLOCK = 512
DEPTH = 3
LATENCY = 1.5
UNIT = 20.0
CORE_UNIT = 40.0
LATE_PARTS = (6,)
LATE_ITEMS = (0, 1)
PUMP = 0.4


def forward_kernel(dims, tensor, parts, tasks, *refs):
    input_ref, top_ref, mask_ref, vector_ref = refs[:4]
    own_weights = refs[4:8]
    outs, land = refs[8:13], refs[13:15]
    weight_qkv, weight_vec, weight_out, weight_one, weight_two = outs
    far = refs[15:20]
    projected, grad_one, grad_two, table, vec_sums, pre_sums, bias_column = refs[20:27]
    (
        block_out,
        grad_middle,
        back_one,
        mixed,
        low_one,
        pack,
        keep_ref,
        square,
        vec_buf,
        qkv_buf,
        head_stage,
        out_buf,
        one_buf,
        two_buf,
        low_two,
        low_two_turned,
        back_two,
        back_two_turned,
        grad_low_two,
        hidden_bias,
        head_bias,
        one_stage,
        two_stage,
        one_keep,
        two_keep,
        other,
        active,
        grad_pre,
        load_sem,
        store_sem,
        keep_sem,
        head_sem,
        land_sem,
        far_sem,
        local_sem,
        send_sem,
        recv_sem,
    ) = refs[27:]
    near = (block_out, grad_middle, back_one, mixed, low_one)

    def far_store(at):
        return pltpu.make_async_copy(near[at], far[at], far_sem.at[at])

    here = Place(dims, tensor)
    gather = Gather(here, pack, outs, parts, local_sem, send_sem, recv_sem)
    rows, width = input_ref.shape
    own_rows = pack.shape[0]
    per_rank = weight_qkv.shape[1]
    low = jnp.bfloat16
    step_rows = LANES

    def fill_pack():
        base = 0
        for pair in range(per_rank):
            for kind in range(3):
                part = own_weights[0][kind, :, pl.ds(pair * LANES, LANES)]
                pack[:, pl.ds(base, LANES)] = part.astype(low)
                base += LANES
        square[...] = jnp.zeros_like(square)
        square[pl.ds(0, VEC), :] = vector_ref[...]
        pack[:, pl.ds(base, LANES)] = square[...].T.astype(low)
        base += LANES
        for ref in own_weights[1:]:
            pack[:, pl.ds(base, ref.shape[1])] = ref[...].astype(low)
            base += ref.shape[1]

    def mask_row():
        return mask_ref[pl.ds(here.rank, 1), :].astype(jnp.float32)

    def mask_bias(keep):
        return jnp.where(keep > 0.0, 0.0, -1e30)

    def first_masks():
        turned = jnp.broadcast_to(mask_row(), (LANES, rows)).T
        keep_ref[...] = turned[:, 0:1]
        bias_column[...] = mask_bias(turned[:, 0:1])

    def row_steps(body, carry):
        return lax.fori_loop(
            0, rows // step_rows, lambda at, c: body(pl.ds(pl.multiple_of(at * step_rows, step_rows), step_rows), c), carry
        )

    def load(source, buffer, sem):
        return pltpu.make_async_copy(source, buffer, sem)

    def first_norm():
        first_masks()
        copy = load(weight_vec, vec_buf, load_sem.at[7])
        copy.start()
        copy.wait()
        whole = vec_buf[...].reshape(width, LANES).astype(jnp.float32).T
        table[...] = whole[:16]
        for at in range(VEC - 8):
            hidden_bias[:, pl.ds(at * width, width)] = whole[7 + at : 8 + at]
        for pair in range(width // LANES):
            for kind, row in ((0, 2), (2, 3)):
                head_bias[:, pl.ds((pair * 3 + kind) * LANES, LANES)] = whole[
                    row : row + 1, pair * LANES : (pair + 1) * LANES
                ]
            head_bias[:, pl.ds((pair * 3 + 1) * LANES, LANES)] = jnp.zeros((1, LANES), jnp.float32)

        def body(part, carry):
            normed, _ = norm_rows(input_ref[part, :])
            low_one[part, :] = (normed * table[0:1, :] + table[1:2, :]).astype(low)
            back_two[part, :] = (top_ref[part, :].astype(jnp.float32) * keep_ref[part, :]).astype(low)
            return carry

        row_steps(body, 0)
        far_store(4).start()
        turn(back_two, back_two_turned)

    def head_store(pair, slot):
        column = pl.ds(pl.multiple_of(pair * 3 * LANES, LANES), 3 * LANES)
        return pltpu.make_async_copy(head_stage.at[slot], projected.at[:, column], head_sem.at[slot])

    def pair_of(at):
        turn_at, place = divmod(at, tensor)
        return lax.rem(here.rank + place, tensor) * per_rank + turn_at

    def head_load(at):
        turn_at, place = divmod(at, tensor)
        source = weight_qkv.at[lax.rem(here.rank + place, tensor), turn_at]
        return load(source, qkv_buf.at[at % 2], load_sem.at[at % 2])

    def heads(at):
        head_load(at).wait()
        pair = pair_of(at)
        slot = at % 2
        column = pl.ds(pl.multiple_of(pair * 3 * LANES, LANES), 3 * LANES)
        weight = qkv_buf[slot].reshape(width, 3 * LANES)
        value = (dot(low_one[...], weight) + head_bias[:, column]).astype(low)
        if at > 1:
            head_store(pair, slot).wait()
        head_stage[slot] = value
        head_store(pair, slot).start()
        mixed[:, pl.ds(pl.multiple_of(pair * LANES, LANES), LANES)] = attend_pair(value, mask_bias(mask_row()))

    def out_load():
        return [
            load(weight_out.at[rank, 0], out_buf.at[rank], load_sem.at[2]) for rank in range(tensor)
        ]

    def second_norm():
        far_store(3).start()
        for copy in out_load():
            copy.wait()
        columns = width // tensor
        for rank in range(tensor):
            weight = out_buf[rank].reshape(width, columns)
            term = dot(mixed[:, pl.ds(rank * columns, columns)], weight, CONTRACT_LAST)
            if rank == 0:
                grad_middle[...] = term
            else:
                grad_middle[...] += term

        def body(part, carry):
            middle = input_ref[part, :] + (grad_middle[part, :] + table[4:5, :]) * keep_ref[part, :]
            grad_middle[part, :] = middle
            normed, _ = norm_rows(middle)
            low_two[part, :] = (normed * table[5:6, :] + table[6:7, :]).astype(low)
            return carry

        row_steps(body, 0)
        turn(low_two, low_two_turned)

    stages = (one_stage, two_stage)
    keeps = (one_keep, two_keep)

    def hand_over(at):
        chunk, place = divmod(at, tensor)
        target = (*here.at, lax.rem(here.rank + place + 1, tensor))
        return [
            pltpu.make_async_remote_copy(
                src_ref=stages[which].at[at % 2],
                dst_ref=land[which].at[place, chunk],
                send_sem=store_sem.at[which, at % 2],
                recv_sem=land_sem.at[which, place, chunk],
                device_id=here.device(target),
                device_id_type=MESH,
            )
            for which in range(2)
        ]

    def keep_store(chunk):
        return [
            pltpu.make_async_copy(
                keeps[which].at[chunk % 2],
                out.at[chunk],
                keep_sem.at[which, chunk % 2],
            )
            for which, out in enumerate((grad_one, grad_two))
        ]

    def hidden_column(at):
        chunk, place = divmod(at, tensor)
        base = (lax.rem(here.rank + place + 1, tensor) * weight_one.shape[1] + chunk) * BLOCK
        return pl.ds(pl.multiple_of(base, LANES), BLOCK)

    def hidden_load(at):
        chunk, place = divmod(at, tensor)
        rank = lax.rem(here.rank + place + 1, tensor)
        return [
            load(source.at[rank, chunk], buffer.at[at % 2], load_sem.at[3 + 2 * which + at % 2])
            for which, (source, buffer) in enumerate(((weight_one, one_buf), (weight_two, two_buf)))
        ]

    staged = {}

    def hidden(at):
        chunk, place = divmod(at, tensor)
        column = hidden_column(at)
        for copy in hidden_load(at):
            copy.wait()
        half = rows // 2
        bias = hidden_bias[:, column]

        def body(turn_at, total):
            part = pl.ds(pl.multiple_of(turn_at * half, half), half)
            one = one_buf[at % 2].reshape(width, BLOCK)
            two = two_buf[at % 2].reshape(width, BLOCK)
            preact = dot(low_two[part, :], one) + bias
            gate = jax.nn.sigmoid(1.702 * preact)
            value = (preact * gate).astype(low)
            active[part, :] = value
            derivative = gate + 1.702 * preact * gate * (1.0 - gate)
            grad = (dot(back_two[part, :], two) * derivative).astype(low)
            grad_pre[part, :] = grad
            if at == 0:
                block_out[part, :] = dot(value, two, CONTRACT_LAST)
                grad_low_two[part, :] = dot(grad, one, CONTRACT_LAST)
            else:
                block_out[part, :] += dot(value, two, CONTRACT_LAST)
                grad_low_two[part, :] += dot(grad, one, CONTRACT_LAST)
            return total + jnp.sum(grad.astype(jnp.float32), axis=0, keepdims=True)

        pre_sums[:, column] = lax.fori_loop(0, 2, body, jnp.zeros((1, BLOCK), jnp.float32))
        mine = place == tensor - 1
        if mine:
            targets = [ref.at[chunk % 2] for ref in keeps]
            if chunk > 1:
                for copy in keep_store(chunk):
                    copy.wait()
        else:
            targets = [ref.at[at % 2] for ref in stages]
            for copy in staged.pop(at % 2, ()):
                copy.wait_send()
        for target, left, right in (
            (targets[0], low_two_turned, grad_pre),
            (targets[1], back_two_turned, active),
        ):
            target[...] = dot(left[...], right[...]).astype(low).reshape(*target.shape)
        if not mine:
            staged[at % 2] = hand_over(at)
            for copy in staged[at % 2]:
                copy.start()

    def combine(chunk):
        for place in range(tensor - 1):
            for which, copy in enumerate(hand_over(chunk * tensor + place)):
                copy.wait_recv()
                fetch = load(land[which].at[place, chunk], other, load_sem.at[7])
                fetch.start()
                fetch.wait()
                keeps[which][chunk % 2] = keeps[which][chunk % 2] + other[...]
        for copy in keep_store(chunk):
            copy.start()

    def last_norm():
        def body(part, sums):
            middle = grad_middle[part, :]
            keep = keep_ref[part, :]
            top = top_ref[part, :].astype(jnp.float32)
            block_out[part, :] = middle + (block_out[part, :] + table[VEC - 1 : VEC, :]) * keep
            normed, inverse = norm_rows(middle)
            grad_low = grad_low_two[part, :]
            scaled = grad_low * table[5:6, :]
            first = jnp.mean(scaled, axis=1, keepdims=True)
            second = jnp.mean(scaled * normed, axis=1, keepdims=True)
            grad = top + inverse * (scaled - first - normed * second)
            grad_middle[part, :] = grad
            masked = grad * keep
            back_one[part, :] = masked.astype(low)
            terms = (masked, grad_low * normed, grad_low, top * keep)
            return tuple(old + jnp.sum(term, axis=0, keepdims=True) for old, term in zip(sums, terms))

        zero = jnp.zeros((1, width), jnp.float32)
        for at, value in enumerate(row_steps(body, (zero,) * 4)):
            vec_sums[at : at + 1, :] = value
        for at in range(3):
            far_store(at).start()

    fill_pack()
    here.barrier(((0,), (1,), (2,), (3,)))
    steps = Steps()
    whole = sum(part[3] for part in parts)
    nz, ny, nx = dims

    def lengths(item, phase):
        share = parts[item][3] / whole * UNIT
        across = ny * nx if item in gather.late else 1
        along = 1 if item in gather.late else nz
        return {
            "pair": (share * across, "end"),
            "middle": (share * across * 2, "middle"),
            "back": (share * across * 2, "end"),
            "all": (share * across * nz, "end"),
            "first": (share * along / 2, "xy"),
            "second": (share * along, "xy"),
            "core": (share * CORE_UNIT / UNIT, "core"),
        }[gather.phases(item)[phase]]

    for item, part in enumerate(parts):
        phases = len(gather.phases(item))
        for phase in range(phases + 1):
            after = [("copy", item, phase - 1)] if phase else []
            if phase == 0 and item >= DEPTH and item not in gather.late:
                after = [("copy", item - DEPTH, 1)]
            if item in gather.late:
                if phase == 0:
                    after = [("copy", DEPTH, 1)]
                if phase == 2:
                    after += [("copy", other, 1) for other in range(min(len(parts), item + 3)) if other not in gather.late]
            length, link = lengths(item, min(phase, phases - 1))
            steps.add(
                ("copy", item, phase),
                functools.partial(gather.advance, item, phase),
                PUMP,
                0.5 if phase == 0 else 0.0,
                after,
                [(item, phase - 1)] if phase else [],
                [((item, phase), link, length)] if phase < phases else [],
            )

    def landed(items):
        return [("copy", item, len(gather.phases(item))) for item in items]

    def start(copies):
        for copy in copies:
            copy.start()

    previous = None
    head_count, block_count = per_rank * tensor, FF // BLOCK
    for name, at, items in tasks:
        after = landed(items) + ([previous] if previous else [])
        begin, run, time = {
            "norm": (None, first_norm, 5.0),
            "heads": (lambda at=at: head_load(at).start(), lambda at=at: heads(at), 3.0),
            "out": (lambda: start(out_load()), second_norm, 5.0),
            "hidden": (lambda at=at: start(hidden_load(at)), lambda at=at: hidden(at), 5.5),
        }[name]
        if begin is not None:
            first = landed(items)
            if at > 1:
                first.append((name, at - 2))
            steps.add(("load", name, at), begin, 0.1, 0.2, first)
            after.append(("load", name, at))
        mine = name == "hidden" and at % tensor == tensor - 1
        chunk = at // tensor
        if mine and chunk > 1:
            after.append(("combine", chunk - 2))
        starts = []
        if name == "hidden" and not mine:
            starts = [(("hand", at), "core", CORE_UNIT / len(parts))]
        steps.add((name, at), run, time, 1.0, after, (), starts)
        if mine:
            waits = [("hand", chunk * tensor + place) for place in range(tensor - 1)]
            steps.add(
                ("combine", chunk), functools.partial(combine, chunk), 2.0, 0.8, [(name, at)], waits
            )
        previous = (name, at)
    steps.add(("last", 0), last_norm, 4.0, 0.9, [previous])
    steps.run()
    for at in range(5):
        far_store(at).wait()
    for slot in range(min(2, head_count)):
        head_store(0, slot).wait()
    for chunk in range(min(2, block_count // tensor)):
        for copy in keep_store(chunk):
            copy.wait()
    for copies in staged.values():
        for copy in copies:
            copy.wait_send()
    gather.finish()


def forward(dims, tensor, inputs, cotangent, token_mask, vectors, weights):
    own_rows, columns = weights[0].shape[1:]
    hidden = weights[2].shape[1]
    rows, width = inputs.shape
    low, full = jnp.bfloat16, jnp.float32
    widths = (3 * columns, LANES, columns, hidden, hidden)
    offsets = [sum(widths[:at]) for at in range(5)]
    per_rank = columns // LANES
    parts = [(1, offsets[1], None, LANES)]
    tasks = [("norm", 0, (0,))]
    for at in range(per_rank):
        size = 3 * LANES
        parts.append((0, offsets[0] + at * size, at, size))
        tasks += [("heads", at * tensor + place, (len(parts) - 1,)) for place in range(tensor)]
    tasks.append(("out", 0, (len(parts),)))
    parts.append((2, offsets[2], 0, columns))
    for block in range(hidden // BLOCK):
        needed = (len(parts), len(parts) + 1)
        parts += [(which, offsets[which] + block * BLOCK, block, BLOCK) for which in (3, 4)]
        tasks += [("hidden", block * tensor + place, needed) for place in range(tensor)]
    count = len(parts)
    peers = max(1, dims[0] - 1, dims[1] + dims[2] - 2, tensor - 1)
    anywhere = pl.BlockSpec(memory_space=pl.ANY)
    inside = pl.BlockSpec(memory_space=pltpu.VMEM)
    block = (*dims, own_rows, BLOCK)
    chunks = hidden // BLOCK

    def shape(kind, *size):
        return jax.ShapeDtypeStruct(size, kind)

    return pl.pallas_call(
        functools.partial(forward_kernel, dims, tensor, tuple(parts), tuple(tasks)),
        name="forward",
        out_shape=[
            shape(low, tensor, per_rank, *dims, own_rows, 3 * LANES),
            shape(low, *dims, own_rows, LANES),
            shape(low, tensor, 1, *dims, own_rows, columns),
            *[shape(low, tensor, chunks, *block)] * 2,
            *[shape(low, max(1, tensor - 1), chunks, *block)] * 2,
            shape(full, rows, width),
            shape(full, rows, width),
            *[shape(low, rows, width)] * 3,
            shape(low, rows, 3 * width),
            *[shape(low, chunks, *block)] * 2,
            shape(full, 16, width),
            shape(full, 8, width),
            shape(full, 1, hidden * tensor),
            shape(full, rows, 1),
        ],
        in_specs=[inside] * 8,
        out_specs=[anywhere] * 15 + [inside] * 4,
        scratch_shapes=[
            pltpu.VMEM((rows, width), full),
            pltpu.VMEM((rows, width), full),
            *[pltpu.VMEM((rows, width), low)] * 3,
            pltpu.VMEM((own_rows, sum(widths)), low),
            pltpu.VMEM((rows, 1), full),
            pltpu.VMEM((LANES, own_rows), full),
            pltpu.VMEM((*dims, own_rows, LANES), low),
            pltpu.VMEM((2, *dims, own_rows, 3 * LANES), low),
            pltpu.VMEM((2, rows, 3 * LANES), low),
            pltpu.VMEM((tensor, *dims, own_rows, columns), low),
            pltpu.VMEM((2, *block), low),
            pltpu.VMEM((2, *block), low),
            pltpu.VMEM((rows, width), low),
            pltpu.VMEM((width, rows), low),
            pltpu.VMEM((rows, width), low),
            pltpu.VMEM((width, rows), low),
            pltpu.VMEM((rows, width), full),
            pltpu.VMEM((1, hidden * tensor), full),
            pltpu.VMEM((1, 3 * width), full),
            pltpu.VMEM((2, *block), low),
            pltpu.VMEM((2, *block), low),
            pltpu.VMEM((2, *block), low),
            pltpu.VMEM((2, *block), low),
            pltpu.VMEM(block, low),
            pltpu.VMEM((rows, BLOCK), low),
            pltpu.VMEM((rows, BLOCK), low),
            pltpu.SemaphoreType.DMA((8,)),
            pltpu.SemaphoreType.DMA((2, 2)),
            pltpu.SemaphoreType.DMA((2, 2)),
            pltpu.SemaphoreType.DMA((2,)),
            pltpu.SemaphoreType.DMA((2, max(1, tensor - 1), chunks)),
            pltpu.SemaphoreType.DMA((5,)),
            pltpu.SemaphoreType.DMA((count,)),
            pltpu.SemaphoreType.DMA((count, 6, peers)),
            pltpu.SemaphoreType.DMA((count, 6, peers)),
        ],
        compiler_params=pltpu.CompilerParams(
            collective_id=0, has_side_effects=True, vmem_limit_bytes=62 << 20
        ),
    )(inputs, cotangent, token_mask, vectors, *weights)


class Layout:
    def __init__(self, columns, hidden, order):
        sizes = {"qkv": 3 * columns, "out": columns, "one": hidden, "two": hidden, "vec": LANES}
        self.order = order
        self.sizes = sizes
        self.start = {}
        at = 0
        for name in order:
            self.start[name] = at
            at += sizes[name]
        self.total = at
        self.columns = columns

    def span(self, name):
        return (self.start[name], self.sizes[name])

    def matrices(self):
        base = self.start["qkv"]
        pairs = range(self.columns // LANES)
        spans = [[(base + (pair * 3 + at) * LANES, LANES) for pair in pairs] for at in range(3)]
        return spans + [[self.span(name)] for name in ("out", "one", "two")]


def pick(values, lane):
    row = jnp.zeros((1, LANES), jnp.float32)
    for at, value in enumerate(values):
        row = jnp.where(lane == at, value, row)
    return row


def total_of(values):
    return jnp.sum(jnp.sum(values, axis=1, keepdims=True), axis=0, keepdims=True)


def attend_pair_back(heads, bias, grads):
    parts = ([], [], [])
    for head in range(2):
        query, key, value = (
            heads[:, kind * LANES + head * HEAD_DIM : kind * LANES + (head + 1) * HEAD_DIM] for kind in range(3)
        )
        grad = grads[:, head * HEAD_DIM : (head + 1) * HEAD_DIM]
        scores = dot(key, query, CONTRACT_LAST) * (HEAD_DIM ** (-0.5) * LOG2E) + bias
        raised = jnp.exp2(scores - jnp.max(scores, axis=0, keepdims=True))
        attention = raised * (1.0 / jnp.sum(raised, axis=0, keepdims=True))
        grad_value = dot(attention.astype(jnp.bfloat16), grad)
        grad_attention = dot(value, grad, CONTRACT_LAST)
        weighted = jnp.sum(attention * grad_attention, axis=0, keepdims=True)
        grad_scores = (attention * (grad_attention - weighted) * HEAD_DIM ** (-0.5)).astype(jnp.bfloat16)
        grad_key = dot(grad_scores, query)
        grad_query = dot(key.T, grad_scores).T
        for kind, part in enumerate((grad_query, grad_key, grad_value)):
            parts[kind].append(part.astype(jnp.bfloat16))
    return jnp.concatenate([piece for kind in parts for piece in kind], axis=1)


def backward_kernel(dims, tensor, items, layout, *refs):
    (
        sum_two,
        sum_one,
        weight_qkv,
        weight_out,
        projected,
        input_ref,
        middle_ref,
        *far,
        bias_ref,
        table,
        vec_sums,
        pre_sums,
    ) = refs[:14]
    far = (*far, *refs[14:18])
    row_states, col_states = refs[18:22], refs[22:26]
    second_ref, vector_ref = refs[26:28]
    input_grad, total_ref, col_new_ref, row_new_ref, second_new_ref, sums_ref = refs[28:34]
    (
        own,
        from_core,
        one_x,
        one_y,
        two_y,
        two_x,
        from_z,
        late_z,
        late_one_y,
        late_one_x,
        late_two_x,
        late_two_y,
        col_sum,
        col_in,
        row_sum,
        row_in,
        small,
        small_in,
        square,
        turned,
        mixed,
        back_one,
        *weights,
        low_turned,
        back_turned,
        grad_mixed,
        out_buf,
        qkv_buf,
        head_buf,
        row_buf,
        out_stage,
        qkv_stage,
        vec_stage,
        head_sums,
        table_grad_ref,
        load_sem,
        stage_sem,
        core_sem,
        local_sem,
        send_sem,
        recv_sem,
        sum_send,
        sum_recv,
        far_sem,
    ) = refs[34:]
    low_one = mixed
    near = (mixed, low_one, back_one, *weights)

    def far_load(at):
        return pltpu.make_async_copy(far[at], near[at], far_sem.at[at])

    here = Place(dims, tensor)
    nz, ny, nx = dims
    low = jnp.bfloat16
    own_rows = own.shape[3]
    half_rows = own_rows // 2
    rows, width = input_grad.shape
    own_place = (*here.at, here.rank)
    count = len(items)
    core_start = layout.start["out"]

    def columns(item):
        _, start, size, _ = items[item]
        return pl.ds(start, size)

    def core_columns(item):
        _, start, size, _ = items[item]
        return pl.ds(start - core_start, size)

    def phases(item):
        lengthwise = along_z(nz)[::-1]
        across = ("first", "second")
        return (*lengthwise, *across) if item in late else (*across, *lengthwise)

    def moves(item, phase):
        first, second, whole = pl.ds(0, half_rows), pl.ds(half_rows, half_rows), pl.ds(0, own_rows)
        kind = phases(item)[phase]
        name, start, size, _ = items[item]
        column = columns(item)
        found = []
        if kind in ("pair", "middle", "back"):
            pair, far, near, middle = here.line()
            outside = jnp.logical_not(middle)
            rest = (slice(None), slice(None)) if item in late else here.at[1:]
            buffer = late_z if item in late else from_z
            landing_column = pl.ds(late.index(item) * BLOCK, size) if item in late else column
            free = (slice(None), slice(None)) if item in late else ()
            z = here.at[0]
            device, sent_z, add_z, slots, sends, receives = {
                "back": (near, pl.ds(far, 2), pl.ds(far, 2), pl.ds(0, 2), outside, middle),
                "middle": (3 - z, pl.ds(far, 2), pl.ds(pair, 2), pl.ds(2, 2), middle, middle),
                "pair": (near, near, z, 4, None, None),
            }[kind]
            found.append(
                (
                    here.at_z(device),
                    own.at[(sent_z, *rest, whole, column)],
                    buffer.at[(slots, *free, slice(None), landing_column)],
                    (add_z, *rest),
                    whole,
                    sends,
                    receives,
                )
            )
            return found
        if item in late:
            column = pl.ds(late.index(item) * BLOCK, size)
            steps = {
                "all": ((0, (0,), whole, late_z),),
                "first": ((1, (0, 1), first, late_one_y), (2, (0, 2), second, late_one_x)),
                "second": ((2, (0, 1, 2), first, late_two_x), (1, (0, 1, 2), second, late_two_y)),
            }[kind]
        else:
            steps = {
                "first": ((2, (2,), first, one_x), (1, (1,), second, one_y)),
                "second": ((1, (1, 2), first, two_y), (2, (1, 2), second, two_x)),
                "all": ((0, (0, 1, 2), whole, from_z),),
            }[kind]
        for axis, fixed, part, landing in steps:
            for step in range(1, here.size(axis)):
                target = here.moved(axis, step)
                index = tuple(target[a] if a in fixed else slice(None) for a in range(3))
                added = tuple(here.at[a] if a in fixed else slice(None) for a in range(3))
                free = (slice(None),) * (3 - len(fixed))
                found.append(
                    (
                        here.device(target),
                        own.at[(*index, part, columns(item))],
                        landing.at[(step - 1, *free, slice(None), column)],
                        added,
                        part,
                        None,
                        None,
                    )
                )
        return found

    def copies(item, phase):
        found = []
        for at, (device, source, landing, added, part, sends, receives) in enumerate(moves(item, phase)):
            copy = pltpu.make_async_remote_copy(
                src_ref=source,
                dst_ref=landing,
                send_sem=send_sem.at[item, phase, at],
                recv_sem=recv_sem.at[item, phase, at],
                device_id=device,
                device_id_type=MESH,
            )
            found.append((sends, receives, copy, added, part, landing))
        return found

    def add_core(item):
        def body(at, carry):
            z, y, x = at // (ny * nx), at // nx % ny, at % nx
            value = own[z, y, x, :, columns(item)]
            for step in range(tensor - 1):
                value = value + from_core[step, z, y, x, :, core_columns(item)]
            own[z, y, x, :, columns(item)] = value
            return carry

        if tensor > 1:
            lax.fori_loop(0, nz * ny * nx, body, 0)

    def add_in(item, landing, added, part):
        sizes, starts = [], []
        for axis, at in enumerate(added):
            if isinstance(at, slice):
                sizes.append(dims[axis])
                starts.append(0)
            elif hasattr(at, "start"):
                sizes.append(at.size)
                starts.append(at.start)
            else:
                sizes.append(None)
                starts.append(at)
        loops = 1
        for size in sizes:
            loops *= size or 1

        def body(at, carry):
            place, inner, rest = [], [], at
            for size, start in reversed(list(zip(sizes, starts))):
                if size is None:
                    place.insert(0, start)
                else:
                    place.insert(0, start + rest % size)
                    inner.insert(0, rest % size)
                    rest = rest // size
            where = (*place, part, columns(item))
            own[where] = own[where] + landing[tuple(inner)]
            return carry

        if loops == 1:
            body(0, 0)
        else:
            lax.fori_loop(0, loops, body, 0)

    def put_total(item, arrived):
        wide = columns(item)
        parts_of = {}
        for landing, part in arrived:
            parts_of.setdefault((part.start, part.size), []).append(landing)
        for (start, size), landings in parts_of.items():
            part = pl.ds(start, size)
            value = own[(*here.at, part, wide)].astype(jnp.float32)
            for landing in landings:
                value = value + landing[...].astype(jnp.float32)
            total_ref[part, wide] = value

    sent = []
    guarded_sent = []
    late = [at for at in LATE_ITEMS if items[at][0] in ("one", "two")]

    def exchange(kind, phase, axes, buffer, landing):
        moved = []
        for at, device in enumerate(here.peers(*axes)):
            copy = pltpu.make_async_remote_copy(
                src_ref=buffer.at[phase],
                dst_ref=landing.at[phase, at],
                send_sem=sum_send.at[kind, phase, at],
                recv_sem=sum_recv.at[kind, phase, at],
                device_id=device,
                device_id_type=MESH,
            )
            copy.start()
            moved.append(copy)
        sent.extend(moved)

        def finish():
            value = buffer[phase]
            for at, copy in enumerate(moved):
                copy.wait_recv()
                value = value + landing[phase, at]
            buffer[phase + 1] = value

        return finish

    def hand_over(item, step, source, sem):
        return pltpu.make_async_remote_copy(
            src_ref=source,
            dst_ref=from_core.at[step - 1, :, :, :, :, core_columns(item)],
            send_sem=sem,
            recv_sem=core_sem.at[item, step - 1],
            device_id=here.device(here.moved(3, step)),
            device_id_type=MESH,
        )

    arriving = {}

    def keep_own(item, value):
        own[:, :, :, :, columns(item)] = value.reshape(nz, ny, nx, own_rows, value.shape[1])

    out_items = [at for at, item in enumerate(items) if item[0] == "out"]
    qkv_items = [at for at, item in enumerate(items) if item[0] == "qkv"]
    vec_item = count - 1
    per_rank = len(qkv_items)
    steps_in_all = per_rank * tensor

    def rank_at(step):
        return lax.rem(here.rank + step, tensor)

    def pair_loads(at):
        turn_at, place = divmod(at, tensor)
        pair = rank_at(place + 1) * per_rank + turn_at
        column = pl.ds(pl.multiple_of(pair * 3 * LANES, LANES), 3 * LANES)
        near = at % 2
        return pair, column, [
            pltpu.make_async_copy(
                weight_qkv.at[rank_at(place + 1), turn_at], qkv_buf.at[near], load_sem.at[0, near]
            ),
            pltpu.make_async_copy(projected.at[:, column], head_buf.at[near], load_sem.at[1, near]),
        ]

    def out_task():
        fetch = [
            pltpu.make_async_copy(weight_out.at[rank, 0], out_buf.at[rank], load_sem.at[2, 0])
            for rank in range(tensor)
        ]
        for copy in fetch:
            copy.start()
        far_load(2).wait()
        turn(back_one, back_turned)
        far_load(0).wait()
        for copy in pair_loads(0)[2]:
            copy.start()
        size = out_stage.shape[5]
        item = out_items[0]
        for step in range(1, tensor + 1):
            column = pl.ds(pl.multiple_of(rank_at(step) * size, LANES), size)
            value = dot(back_turned[...], mixed[:, column]).astype(low)
            if step < tensor:
                out_stage[step - 1] = value.reshape(nz, ny, nx, own_rows, size)
                copy = hand_over(item, step, out_stage.at[step - 1], stage_sem.at[item, step - 1])
                copy.start()
                sent.append(copy)
                arriving.setdefault(item, []).append(copy)
            else:
                keep_own(item, value)
        far_load(1).start()
        for copy in fetch:
            copy.wait()
        for rank in range(tensor):
            weight = out_buf[rank].reshape(width, size)
            grad_mixed[:, pl.ds(rank * size, size)] = dot(back_one[...], weight).astype(low)
        far_load(1).wait()
        turn(low_one, low_turned)

    def state_task():
        def fill(refs, other):
            square[...] = jnp.full_like(square, other)
            base = 0
            for ref in refs:
                square[pl.ds(base, ref.shape[0]), :] = ref[...]
                base += ref.shape[0]
            return square[...].T

        for at in range(3, 7):
            far_load(at).wait()
        turned[0] = fill(row_states, 1.0)
        turned[1] = fill((second_ref,), 1.0)
        turned[2] = fill((vector_ref,), 0.0)

    staged = {}

    def pair_task(at):
        turn_at, place = divmod(at, tensor)
        pair, column, loads = pair_loads(at)
        for copy in loads:
            copy.wait()
        if at + 1 < steps_in_all:
            for copy in pair_loads(at + 1)[2]:
                copy.start()
        near = at % 2
        grads = grad_mixed[:, pl.ds(pl.multiple_of(pair * LANES, LANES), LANES)]
        value = attend_pair_back(head_buf[near], bias_ref[...], grads)
        head_sums[:, column] = jnp.sum(value.astype(jnp.float32), axis=0, keepdims=True)
        weight = qkv_buf[near].reshape(width, 3 * LANES)
        term = dot(value, weight, CONTRACT_LAST)
        if at == 0:
            input_grad[...] = term
        else:
            input_grad[...] += term
        item = qkv_items[turn_at]
        grad = dot(low_turned[...], value).astype(low)
        if place + 1 < tensor:
            if 0 in staged:
                staged[0].wait_send()
            qkv_stage[...] = grad.reshape(nz, ny, nx, own_rows, 3 * LANES)
            copy = hand_over(item, place + 1, qkv_stage, stage_sem.at[item, place])
            copy.start()
            staged[0] = copy
            arriving.setdefault(item, []).append(copy)
        else:
            keep_own(item, grad)

    def last_task():
        step_rows = row_buf.shape[2]

        def fetch(at):
            near = lax.rem(at, 2)
            part = pl.ds(pl.multiple_of(at * step_rows, step_rows), step_rows)
            return [
                pltpu.make_async_copy(source.at[part, :], row_buf.at[which, near], load_sem.at[which, near])
                for which, source in enumerate((input_ref, middle_ref))
            ]

        for copy in fetch(0):
            copy.start()

        def body(at, sums):
            for copy in fetch(at):
                copy.wait()

            @pl.when(at + 1 < rows // step_rows)
            def _():
                for copy in fetch(at + 1):
                    copy.start()

            near = lax.rem(at, 2)
            part = pl.ds(pl.multiple_of(at * step_rows, step_rows), step_rows)
            normed, inverse = norm_rows(row_buf[0, near])
            grad_low = input_grad[part, :]
            scaled = grad_low * table[0:1, :]
            first = jnp.mean(scaled, axis=1, keepdims=True)
            second = jnp.mean(scaled * normed, axis=1, keepdims=True)
            input_grad[part, :] = row_buf[1, near] + inverse * (scaled - first - normed * second)
            terms = (grad_low * normed, grad_low)
            return tuple(old + jnp.sum(term, axis=0, keepdims=True) for old, term in zip(sums, terms))

        zero = jnp.zeros((1, width), jnp.float32)
        found = lax.fori_loop(0, rows // step_rows, body, (zero, zero))
        table_grad_ref[...] = jnp.zeros_like(table_grad_ref)
        for at in range(2):
            table_grad_ref[at : at + 1, :] = found[at]
        for pair in range(width // LANES):
            for kind, row in ((0, 2), (2, 3)):
                table_grad_ref[row : row + 1, pl.ds(pair * LANES, LANES)] = head_sums[
                    :, pl.ds((pair * 3 + kind) * LANES, LANES)
                ]
        for at, row in enumerate((4, 5, 6, VEC - 1)):
            table_grad_ref[row : row + 1, :] = vec_sums[at : at + 1, :]
        for at in range(VEC - 8):
            table_grad_ref[7 + at : 8 + at, :] = pre_sums[:, pl.ds(at * width, width)]
        value = table_grad_ref[...].T.astype(low)
        vec_stage[...] = value.reshape(nz, ny, nx, own_rows, LANES)
        for step in range(1, tensor):
            copy = hand_over(vec_item, step, vec_stage, stage_sem.at[vec_item, step - 1])
            copy.start()
            sent.append(copy)
            arriving.setdefault(vec_item, []).append(copy)
        keep_own(vec_item, value)

    for at in (2, 0, 3, 4, 5, 6):
        far_load(at).start()
    here.barrier(((0, 3), (1, 2)))
    local = {}
    for item, (name, _, _, source) in enumerate(items):
        if name in ("one", "two"):
            array = sum_one if name == "one" else sum_two
            copy = pltpu.make_async_copy(
                array.at[source], own.at[:, :, :, :, columns(item)], local_sem.at[item]
            )
            copy.start()
            local[item] = copy

    def advance(item, phase):
        last = len(phases(item))
        if phase > 0:
            arrived = []
            for _, receives, copy, added, part, landing in copies(item, phase - 1):

                def take(copy=copy, landing=landing, added=added, part=part):
                    copy.wait_recv()
                    if phase < last:
                        add_in(item, landing, added, part)

                guarded(receives, take)
                arrived.append((landing, part))
            if phase == last:
                put_total(item, arrived)
        elif item in local:
            local[item].wait()
        else:
            for copy in arriving.get(item, ()):
                copy.wait_recv()
            add_core(item)
        if phase < last:
            for sends, _, copy, *_ in copies(item, phase):
                guarded(sends, copy.start)
                guarded_sent.append((sends, copy))

    steps = Steps()
    owner = {item: ("out", 0) for item in out_items}
    owner |= {item: ("pair", tensor * (at + 1) - 1) for at, item in enumerate(qkv_items)}
    owner[vec_item] = ("last", 0)
    for item, (name, _, size, _) in enumerate(items):
        share = size / layout.total * UNIT
        across = ny * nx if item in late else 1
        along = 1 if item in late else nz
        lengths = {
            "pair": (share * across, "end"),
            "middle": (share * across * 2, "middle"),
            "back": (share * across * 2, "end"),
            "all": (share * across * nz, "end"),
            "first": (share * along, "xy"),
            "second": (share * along / 2, "xy"),
        }
        if item in late:
            lengths |= {"first": (share, "xy"), "second": (share / 2, "xy")}
        early = item not in owner
        kinds = phases(item)
        for phase in range(len(kinds) + 1):
            after = [("copy", item, phase - 1)] if phase else []
            waits = [(item, phase - 1)] if phase else []
            if phase == 0 and early and item >= DEPTH + len(late):
                after = [("copy", item - DEPTH, 1)]
            if phase == 0 and not early:
                after, waits = [owner[item]], [("core", owner[item])]
            starts = []
            if phase < len(kinds):
                length, link = lengths[kinds[phase]]
                starts = [((item, phase), link, length)]
            steps.add(
                ("copy", item, phase),
                functools.partial(advance, item, phase),
                PUMP * (1.5 if phase == 1 else 1.0),
                (0.5 if phase == 0 and early else 0.0),
                after,
                waits,
                starts,
            )
    steps.add(("state", 0), state_task, 1.0, 2.0)
    steps.add(("out", 0), out_task, 8.0, 1.0, (), (), [(("core", ("out", 0)), "core", CORE_UNIT / 12)])
    for at in range(steps_in_all):
        after = [("pair", at - 1) if at else ("out", 0)]
        starts = [(("core", ("pair", at)), "core", CORE_UNIT / 24)]
        steps.add(("pair", at), functools.partial(pair_task, at), 6.0, 1.0, after, (), starts)
    steps.add(
        ("last", 0), last_task, 4.0, 1.0, [("pair", steps_in_all - 1)], (), [(("core", ("last", 0)), "core", 1.0)]
    )
    steps.run()
    sent.extend(staged.values())

    decay_rate = 1.0 - STEP ** (-0.8)
    keep_old = 1.0 - decay_rate
    long = layout.sizes["one"] * tensor
    matrices = layout.matrices()
    lane = lax.broadcasted_iota(jnp.int32, (1, LANES), 1)
    row_parts = []
    for spans in matrices:
        row_part = 0.0
        for start, size in spans:
            value = total_ref[:, pl.ds(start, size)]
            square = value * value
            col_sum[0, :, pl.ds(start, size)] = jnp.sum(square, axis=0, keepdims=True)
            row_part = row_part + jnp.sum(square, axis=1, keepdims=True)
        row_parts.append(row_part)
    row_sum[0] = pick(row_parts, lane)
    finish_row = exchange(0, 0, (3,), row_sum, row_in)
    finish_col = exchange(1, 0, (0,), col_sum, col_in)
    vec_start = layout.start["vec"]
    table_grad = total_ref[:, pl.ds(vec_start, LANES)]
    second_new = decay_rate * turned[1] + keep_old * (table_grad * table_grad + EPS_ONE)
    second_new_ref[...] = second_new
    vector_update = table_grad * lax.rsqrt(second_new)
    vector_sums = jnp.sum(vector_update * vector_update, axis=0, keepdims=True) / tensor
    vector_weight = jnp.sum(turned[2] * turned[2], axis=0, keepdims=True) / tensor
    weight_sums = [total_of(jnp.sum(weights[0][...] * weights[0][...], axis=0))]
    weight_sums += [total_of(ref[...] * ref[...]) for ref in weights[1:]]
    finish_row()
    row_counts = pick([jnp.full((1, 1), 1.0 / size, jnp.float32) for size in (width, width, width, width, long, long)], lane)
    row_new = decay_rate * turned[0] + keep_old * (row_sum[1] * row_counts + EPS_ONE)
    row_new_ref[...] = row_new
    finish_col()
    exchange(1, 1, (1, 2), col_sum, col_in)()
    for at, spans in enumerate(matrices):
        for place, (start, size) in enumerate(spans):
            if at < 3:
                old = col_states[0][at : at + 1, pl.ds(place * LANES, LANES)]
            else:
                old = col_states[at - 2][...]
            fresh = keep_old * (col_sum[2, :, pl.ds(start, size)] / width + EPS_ONE)
            col_new_ref[:, pl.ds(start, size)] = decay_rate * old + fresh
    ratios = []
    means = []
    for at, spans in enumerate(matrices):
        row_at = row_new[:, at : at + 1]
        ratio = 0.0
        for start, size in spans:
            value = total_ref[:, pl.ds(start, size)]
            col_at = col_new_ref[:, pl.ds(start, size)]
            ratio = ratio + total_of(value * value / (row_at * col_at))
        ratios.append(ratio)
        if at in (3, 5):
            means.append(jnp.sum(col_at, axis=1, keepdims=True) / (nz * ny * nx))
        else:
            means.append(jnp.sum(row_at, axis=0, keepdims=True) / tensor)
    small[0] = jnp.concatenate(
        [pick(ratios + means + weight_sums, lane), vector_sums, vector_weight, jnp.zeros((5, LANES), jnp.float32)], axis=0
    )
    exchange(2, 0, (0, 3), small, small_in)()
    exchange(2, 1, (1, 2), small, small_in)()
    sums_ref[...] = small[2]
    for copy in sent:
        copy.wait_send()
    for condition, copy in guarded_sent:
        guarded(condition, copy.wait_send)


def backward(dims, tensor, layout, large, near, weights, states):
    rows, width = large[-1].shape
    own_rows = width // (dims[0] * dims[1] * dims[2])
    half_rows = own_rows // 2
    columns = layout.columns
    items = []
    for block in range(layout.sizes["one"] // BLOCK):
        for name in ("two", "one"):
            items.append((name, layout.start[name] + block * BLOCK, BLOCK, block))
    items.append(("out", layout.start["out"], columns, 0))
    for start in range(0, 3 * columns, 3 * LANES):
        items.append(("qkv", layout.start["qkv"] + start, 3 * LANES, start))
    items.append(("vec", layout.start["vec"], LANES, 0))
    nz, ny, nx = dims
    peers = max(1, nz - 1, ny + nx - 2)
    group = max(1, nz * tensor - 1, ny * nx - 1)
    others = max(1, tensor - 1)
    offset = layout.total
    from_here = offset - layout.start["out"]
    late_width = BLOCK * max(1, len(LATE_ITEMS))
    low, full = jnp.bfloat16, jnp.float32
    anywhere = pl.BlockSpec(memory_space=pl.ANY)
    inside = pl.BlockSpec(memory_space=pltpu.VMEM)

    def hold(*shape):
        return pltpu.VMEM(tuple(max(1, size) for size in shape), low)

    sums = offset - LANES
    count = len(items)
    return pl.pallas_call(
        functools.partial(backward_kernel, dims, tensor, tuple(items), layout),
        name="backward",
        out_shape=[
            jax.ShapeDtypeStruct((rows, width), full),
            jax.ShapeDtypeStruct((own_rows, offset), full),
            jax.ShapeDtypeStruct((1, sums), full),
            jax.ShapeDtypeStruct((own_rows, LANES), full),
            jax.ShapeDtypeStruct((own_rows, LANES), full),
            jax.ShapeDtypeStruct((8, LANES), full),
        ],
        in_specs=[anywhere] * len(large) + [inside] * len(near) + [anywhere] * 4 + [inside] * len(states),
        out_specs=[inside] * 6,
        scratch_shapes=[
            hold(nz, ny, nx, own_rows, offset),
            hold(others, nz, ny, nx, own_rows, from_here),
            hold(nx - 1, nz, ny, half_rows, offset),
            hold(ny - 1, nz, nx, half_rows, offset),
            hold(ny - 1, nz, half_rows, offset),
            hold(nx - 1, nz, half_rows, offset),
            hold(5 if nz == 4 else nz - 1, own_rows, offset),
            hold(5 if nz == 4 else nz - 1, ny, nx, own_rows, late_width),
            hold(ny - 1, nx, half_rows, late_width),
            hold(nx - 1, ny, half_rows, late_width),
            hold(nx - 1, half_rows, late_width),
            hold(ny - 1, half_rows, late_width),
            pltpu.VMEM((3, 1, sums), full),
            pltpu.VMEM((2, max(1, nz - 1, ny * nx - 1), 1, sums), full),
            pltpu.VMEM((2, own_rows, LANES), full),
            pltpu.VMEM((1, others, own_rows, LANES), full),
            pltpu.VMEM((3, 8, LANES), full),
            pltpu.VMEM((2, group, 8, LANES), full),
            pltpu.VMEM((LANES, own_rows), full),
            pltpu.VMEM((3, own_rows, LANES), full),
            *[hold(rows, width)] * 2,
            *(pltpu.VMEM(weight.shape, full) for weight in weights),
            hold(width, rows),
            hold(width, rows),
            hold(rows, width),
            hold(tensor, *dims, own_rows, columns),
            hold(2, *dims, own_rows, 3 * LANES),
            hold(2, rows, 3 * LANES),
            pltpu.VMEM((2, 2, LANES // 2, width), full),
            hold(others, *dims, own_rows, columns),
            hold(*dims, own_rows, 3 * LANES),
            hold(*dims, own_rows, LANES),
            pltpu.VMEM((1, 3 * width), full),
            pltpu.VMEM((LANES, width), full),
            pltpu.SemaphoreType.DMA((3, 2)),
            pltpu.SemaphoreType.DMA((count, others)),
            pltpu.SemaphoreType.DMA((count, others)),
            pltpu.SemaphoreType.DMA((count,)),
            pltpu.SemaphoreType.DMA((count, 5, peers)),
            pltpu.SemaphoreType.DMA((count, 5, peers)),
            pltpu.SemaphoreType.DMA((3, 2, group)),
            pltpu.SemaphoreType.DMA((3, 2, group)),
            pltpu.SemaphoreType.DMA((7,)),
        ],
        compiler_params=pltpu.CompilerParams(
            collective_id=1, has_side_effects=True, vmem_limit_bytes=63 << 20
        ),
    )(*large, *near, *weights, *states)


def update_kernel(layout, width, long, *refs):
    block_in, grad_in = refs[:2]
    far = refs[2:12]
    block_out, input_grad = refs[12:14]
    own_qkv, own_out, own_one, own_two, own_table = refs[14:19]
    new_qkv, new_out, new_one, new_two, new_vectors, second_new = refs[19:25]
    qkv_row, qkv_col, out_row, out_col, one_row, one_col, two_row, two_col = refs[25:33]
    near, passing, sem = refs[33:43], refs[43:45], refs[45]
    loads = [
        pltpu.make_async_copy(source, target, sem.at[at])
        for at, (source, target) in enumerate(zip((*far, block_in, grad_in), (*near, *passing)))
    ]
    long_copies = [
        pltpu.make_async_copy(source, target, sem.at[12 + at])
        for at, (source, target) in enumerate(zip(passing, (block_out, input_grad)))
    ]
    for copy in loads:
        copy.start()
    for copy in loads:
        copy.wait()
    for copy in long_copies:
        copy.start()
    total_ref, col_ref, row_ref, second_ref, sums_ref, vector_ref = near[:6]
    weights = near[6:]
    lane = lax.broadcasted_iota(jnp.int32, (1, LANES), 1)

    def at(index):
        return sums_ref[0:1, index : index + 1]

    lengths = (width, width, width, width, width, long)
    means = [at(6 + m) / lengths[m] for m in range(6)]
    squares = [means[m] * at(m) for m in range(6)]
    squares = [squares[0] + squares[1] + squares[2], *squares[3:]]
    entries = (3 * width * width, width * width, width * long, width * long)
    step_size = []
    for m in range(4):
        damping = 1.0 / jnp.maximum(1.0, jnp.sqrt(squares[m] / entries[m] + 1e-06) / CLIP_LEVEL)
        step_size.append(LEARN_RATE * jnp.sqrt(at(12 + m) / entries[m] + 1e-06) * damping)
    spread = [(m, place, *span) for m, spans in enumerate(layout.matrices()) for place, span in enumerate(spans)]
    for m, place, start, size in spread:
        grad = total_ref[:, pl.ds(start, size)]
        col = col_ref[:, pl.ds(start, size)]
        step = step_size[max(0, m - 2)] * grad * lax.rsqrt(row_ref[:, m : m + 1] * col / means[m])
        if m < 3:
            part = slice(place * LANES, (place + 1) * LANES)
            own_qkv[m, :, part] = grad
            new_qkv[m, :, part] = weights[0][m, :, part] - step
            qkv_col[m : m + 1, part] = col
        else:
            own, new, state = (
                (own_out, new_out, out_row),
                (own_one, new_one, one_col),
                (own_two, new_two, two_row),
            )[m - 3]
            own[...] = grad
            new[...] = weights[m - 2][...] - step
            state[...] = col
    row_flat = row_ref[...].T
    qkv_row[...] = row_flat[0:3]
    out_col[...] = row_flat[3:4]
    one_row[...] = row_flat[4:5]
    two_col[...] = row_flat[5:6]

    wide = (lane >= 7) & (lane < VEC - 1)
    counts = jnp.where(wide, float(long), float(width))

    def grouped(values):
        inside = jnp.sum(jnp.where(wide, values, 0.0), axis=1, keepdims=True)
        return jnp.where(wide, inside, values)

    table_grad = total_ref[:, pl.ds(layout.start["vec"], LANES)]
    update = table_grad * lax.rsqrt(second_ref[...])
    norm = jnp.sqrt(grouped(sums_ref[1:2, :]) / counts + 1e-06)
    size = jnp.sqrt(grouped(sums_ref[2:3, :]) / counts + 1e-06)
    change = LEARN_RATE * size / jnp.maximum(1.0, norm / CLIP_LEVEL) * update
    own_table[...] = table_grad.T[:VEC]
    new_vectors[...] = vector_ref[...] - change.T[:VEC]
    second_new[...] = second_ref[...].T[:VEC]
    for copy in long_copies:
        copy.wait()


def update_weights(layout, width, long, columns, hidden, rows, results, values, vectors, weights):
    full = jnp.float32
    shapes = [
        *(result.shape for result in results),
        (3, rows, columns),
        (rows, columns),
        (rows, hidden),
        (rows, hidden),
        (VEC, rows),
        (3, rows, columns),
        (rows, columns),
        (rows, hidden),
        (rows, hidden),
        (VEC, rows),
        (VEC, rows),
        (3, rows),
        (3, columns),
        (1, columns),
        (1, rows),
        (1, rows),
        (1, hidden),
        (1, hidden),
        (1, rows),
    ]
    far = (*values, vectors, *weights)
    anywhere = pl.BlockSpec(memory_space=pl.ANY)
    inside = pl.BlockSpec(memory_space=pltpu.VMEM)
    return pl.pallas_call(
        functools.partial(update_kernel, layout, width, long),
        name="update_weights",
        out_shape=[jax.ShapeDtypeStruct(shape, full) for shape in shapes],
        in_specs=[anywhere] * (2 + len(far)),
        out_specs=[anywhere] * 2 + [inside] * (len(shapes) - 2),
        scratch_shapes=[
            *(pltpu.VMEM(array.shape, full) for array in (*far, *results)),
            pltpu.SemaphoreType.DMA((4 + len(far),)),
        ],
        compiler_params=pltpu.CompilerParams(vmem_limit_bytes=63 << 20),
    )(*results, *far)


def on_device(
    inputs,
    cotangent,
    token_mask,
    w_qkv,
    w_out,
    w_fc1,
    w_fc2,
    vectors,
    qkv_row,
    qkv_col,
    out_row,
    out_col,
    fc1_row,
    fc1_col,
    fc2_row,
    fc2_col,
    vec_second,
):
    tensor_count = lax.axis_size("tensor")
    dims = grid_of(lax.axis_size("fsdp"))
    width = inputs.shape[1]
    own_rows, columns = w_qkv.shape[1:]
    hidden = w_fc1.shape[1]
    weights = (w_qkv, w_out.T, w_fc1, w_fc2.T)
    (
        weight_qkv,
        _,
        weight_out,
        *_,
        block_out,
        grad_middle,
        back_one,
        mixed_rows,
        low_one,
        projected,
        grad_one,
        grad_two,
        table,
        vec_sums,
        pre_sums,
        bias_column,
    ) = forward(dims, tensor_count, inputs, cotangent, token_mask, vectors, weights)
    layout = Layout(columns, hidden, ("two", "one", "out", "qkv", "vec"))
    row_states = (qkv_row, out_col[None], fc1_row[None], fc2_col[None])
    col_states = (qkv_col, out_row[None], fc1_col[None], fc2_row[None])
    input_grad, *values = backward(
        dims,
        tensor_count,
        layout,
        (
            grad_two,
            grad_one,
            weight_qkv,
            weight_out,
            projected,
            inputs,
            grad_middle,
            mixed_rows,
            low_one,
            back_one,
        ),
        (bias_column, table, vec_sums, pre_sums),
        weights,
        (*row_states, *col_states, vec_second, vectors),
    )
    outs = update_weights(
        layout, width, FF, columns, hidden, own_rows, (block_out, input_grad), values, vectors, weights
    )
    outs = [out.reshape(-1) if out.shape[0] == 1 else out for out in outs]
    for at in (3, 5, 8, 10):
        outs[at] = outs[at].T
    return (*outs[:12], *outs[13:], outs[12])


def solution(mesh):
    in_specs = (
        P(("fsdp", "tensor"), None),
        P(("fsdp", "tensor"), None),
        P("fsdp", None),
        P(None, "fsdp", "tensor"),
        P("tensor", "fsdp"),
        P("fsdp", "tensor"),
        P("tensor", "fsdp"),
        P(None, "fsdp"),
        P(None, "fsdp"),
        P(None, "tensor"),
        P("tensor"),
        P("fsdp"),
        P("fsdp"),
        P("tensor"),
        P("tensor"),
        P("fsdp"),
        P(None, "fsdp"),
    )
    out_specs = (
        P(("fsdp", "tensor"), None),
        P(("fsdp", "tensor"), None),
        P(None, "fsdp", "tensor"),
        P("tensor", "fsdp"),
        P("fsdp", "tensor"),
        P("tensor", "fsdp"),
        P(None, "fsdp"),
        P(None, "fsdp", "tensor"),
        P("tensor", "fsdp"),
        P("fsdp", "tensor"),
        P("tensor", "fsdp"),
        P(None, "fsdp"),
        P(None, "fsdp"),
        P(None, "tensor"),
        P("tensor"),
        P("fsdp"),
        P("fsdp"),
        P("tensor"),
        P("tensor"),
        P("fsdp"),
        P(None, "fsdp"),
    )
    return jax.shard_map(
        on_device, mesh=mesh, in_specs=in_specs, out_specs=out_specs, check_vma=False
    )
```

```python
import functools

import jax
import jax.numpy as jnp
from jax import lax
from jax.experimental import pallas as pl
from jax.experimental.pallas import tpu as pltpu
from jax.sharding import PartitionSpec as P

HEAD_DIM = 64
FF = 4096
STEP = 20
VEC = 12
LANES = 128

EPS_NORM = 1e-05
EPS_ONE = 1e-30
CLIP_LEVEL = 1.0
LEARN_RATE = 0.5
MESH = pl.DeviceIdType.MESH
LOG2E = 1.4426950408889634
CONTRACT_LAST = (((1,), (1,)), ((), ()))


def grid_of(count):
    return {16: (4, 2, 2), 32: (2, 4, 4)}.get(count, (count, 1, 1))


class Place:
    def __init__(self, dims, tensor):
        self.dims = dims
        self.tensor = tensor
        fsdp = lax.axis_index("fsdp")
        _, ny, nx = dims
        self.at = (fsdp // (ny * nx), (fsdp // nx) % ny, fsdp % nx)
        self.rank = lax.axis_index("tensor")

    def moved(self, axis, step):
        place = list(self.at) + [self.rank]
        size = (*self.dims, self.tensor)[axis]
        place[axis] = lax.rem(place[axis] + step + size, size)
        return tuple(place)

    def device(self, place):
        z, y, x, rank = place
        return {"fsdp": (z * self.dims[1] + y) * self.dims[2] + x, "tensor": rank}

    def size(self, axis):
        return (*self.dims, self.tensor)[axis]

    def line(self):
        z = self.at[0]
        pair = z // 2 * 2
        middle = (z == 1) | (z == 2)
        return pair, 2 - pair, z + 1 - 2 * (z % 2), middle

    def at_z(self, z):
        return self.device((z, self.at[1], self.at[2], self.rank))

    def peers(self, *axes):
        places = [()]
        for axis in axes:
            places = [(*steps, step) for steps in places for step in range(self.size(axis))]
        found = []
        for steps in places[1:]:
            place = list(self.at) + [self.rank]
            for axis, step in zip(axes, steps):
                place[axis] = lax.rem(place[axis] + step, self.size(axis))
            found.append(self.device(tuple(place)))
        return found

    def barrier(self, groups):
        sem = pltpu.get_barrier_semaphore()
        count = 0
        for axes in groups:
            for device in self.peers(*axes):
                pl.semaphore_signal(sem, inc=1, device_id=device, device_id_type=MESH)
                count += 1
        if count:
            pl.semaphore_wait(sem, count)


def norm_rows(values):
    average = jnp.mean(values, axis=1, keepdims=True)
    center = values - average
    inverse = lax.rsqrt(jnp.mean(center * center, axis=1, keepdims=True) + EPS_NORM)
    return center * inverse, inverse


def dot(left, right, dims=(((1,), (0,)), ((), ()))):
    return lax.dot_general(left, right, dims, preferred_element_type=jnp.float32)


def turn(source, target):
    for start in range(0, source.shape[1], LANES):
        target[pl.ds(start, LANES), :] = source[:, pl.ds(start, LANES)].T


def head_lanes(head):
    lane = lax.broadcasted_iota(jnp.int32, (1, LANES), 1)
    return lane // HEAD_DIM == head


def attend_pair(heads_ref, bias):
    def body(head, mixed):
        query, key, value = (heads_ref[:, kind * LANES : (kind + 1) * LANES] for kind in range(3))
        lanes = head_lanes(head)
        key = jnp.where(lanes, key, jnp.zeros_like(key))
        value = jnp.where(lanes, value, jnp.zeros_like(value))
        scores = dot(query, key, CONTRACT_LAST) * (HEAD_DIM ** (-0.5) * LOG2E) + bias
        raised = jnp.exp2(scores - jnp.max(scores, axis=1, keepdims=True))
        summed = jnp.sum(raised, axis=1, keepdims=True)
        attention = (raised * (1.0 / summed)).astype(jnp.bfloat16)
        return mixed + dot(attention, value)

    zero = jnp.zeros((heads_ref.shape[0], LANES), jnp.float32)
    return lax.fori_loop(0, 2, body, zero).astype(jnp.bfloat16)


def guarded(condition, run):
    if condition is None:
        run()
    else:
        pl.when(condition)(run)


def along_z(count):
    return ("pair", "middle", "back") if count == 4 else ("all",)


class Steps:
    def __init__(self):
        self.steps = {}

    def add(self, name, run, time, rank, after=(), waits=(), starts=()):
        self.steps[name] = (run, time, rank, tuple(after), tuple(waits), tuple(starts))

    def arrange(self):
        now, free, arrival, done, order = 0.0, {}, {}, set(), []
        left = list(self.steps)
        while left:
            best, soonest = None, None
            for name in left:
                _, time, rank, after, waits, _ = self.steps[name]
                if any(other not in done for other in after) or any(wait not in arrival for wait in waits):
                    continue
                ready = max([arrival[wait] for wait in waits], default=0.0)
                if ready <= now:
                    if best is None or rank < self.steps[best][2]:
                        best = name
                elif soonest is None or ready < soonest:
                    soonest = ready
            if best is None:
                now = soonest
                continue
            _, time, _, _, _, starts = self.steps[best]
            now += time
            for transfer, link, length in starts:
                begin = max(now, free.get(link, 0.0))
                free[link] = begin + length
                arrival[transfer] = begin + length + LATENCY
            done.add(best)
            left.remove(best)
            order.append(best)
        return order, now

    def run(self):
        for name in self.arrange()[0]:
            self.steps[name][0]()


class Gather:
    def __init__(self, here, pack_ref, outs, parts, local_sem, send_sem, recv_sem):
        self.here = here
        self.pack = pack_ref
        self.outs = outs
        self.rows = pack_ref.shape[0]
        self.parts = parts
        self.late = [len(parts) - at for at in LATE_PARTS if at < len(parts)]
        self.sems = (local_sem, send_sem, recv_sem)
        self.own = (*here.at, here.rank)
        self.sent = []

    def region(self, item, part, place, free):
        out, _, chunk, _ = self.parts[item]
        index = tuple(slice(None) if a in free else place[a] for a in range(3))
        lead = () if chunk is None else (place[3], chunk)
        return self.outs[out].at[(*lead, *index, part)]

    def shard(self, item, part):
        _, offset, _, size = self.parts[item]
        return self.pack.at[part, pl.ds(offset, size)]

    def phases(self, item):
        lengthwise = along_z(self.here.dims[0]) if self.parts[item][0] in (3, 4) else ("all",)
        across = ("first", "second")
        order = (*across, *lengthwise) if item in self.late else (*lengthwise, *across)
        return order if self.parts[item][2] is None else (*order, "core")

    def moves(self, item, phase):
        here, own = self.here, self.own
        kind = self.phases(item)[phase]
        late = item in self.late
        whole, half = pl.ds(0, self.rows), self.rows // 2
        first, second = pl.ds(0, half), pl.ds(half, half)
        found = []
        if kind in ("pair", "middle", "back"):
            free = (1, 2) if late else ()
            pair, far, near, middle = here.line()

            def blocks(z):
                return self.region(item, whole, (z, *own[1:]), free)

            if kind == "pair":
                sent = self.shard(item, whole) if phase == 0 else blocks(own[0])
                found.append((here.at_z(near), sent, blocks(own[0]), blocks(near), None, None))
            elif kind == "middle":
                pairs = blocks(pl.ds(pair, 2))
                found.append((here.at_z(3 - own[0]), pairs, pairs, blocks(pl.ds(far, 2)), middle, middle))
            else:
                pairs = blocks(pl.ds(far, 2))
                outside = jnp.logical_not(middle)
                found.append((here.at_z(near), pairs, pairs, pairs, middle, outside))
            return found
        before = () if late else (0,)
        steps = {
            "all": ((0, (1, 2) if late else (), whole),),
            "first": ((2, before, first), (1, before, second))
            if late
            else ((1, before, first), (2, before, second)),
            "second": ((1, (*before, 2), first), (2, (*before, 1), second))
            if late
            else ((2, (*before, 1), first), (1, (*before, 2), second)),
            "core": ((3, (0, 1, 2), whole),),
        }[kind]
        for axis, free, part in steps:
            for step in range(1, here.size(axis)):
                place = self.region(item, part, own, free)
                sent = self.shard(item, part) if phase == 0 else place
                landed = self.region(item, part, here.moved(axis, -step), free)
                found.append((here.device(here.moved(axis, step)), sent, place, landed, None, None))
        return found

    def copies(self, item, phase, landing):
        found = []
        for at, (device, sent, place, landed, sends, receives) in enumerate(self.moves(item, phase)):
            copy = pltpu.make_async_remote_copy(
                src_ref=landed if landing else sent,
                dst_ref=landed if landing else place,
                send_sem=self.sems[1].at[item, phase, at],
                recv_sem=self.sems[2].at[item, phase, at],
                device_id=device,
                device_id_type=MESH,
            )
            found.append((receives if landing else sends, copy))
        return found

    def keep(self, item):
        whole = pl.ds(0, self.rows)
        return pltpu.make_async_copy(
            self.shard(item, whole), self.region(item, whole, self.own, ()), self.sems[0].at[item]
        )

    def advance(self, item, phase):
        if phase:
            for condition, copy in self.copies(item, phase - 1, True):
                guarded(condition, copy.wait_recv)
        if phase == 0:
            self.keep(item).start()
        if phase == 1:
            self.keep(item).wait()
        if phase < len(self.phases(item)):
            for condition, copy in self.copies(item, phase, False):
                guarded(condition, copy.start)
                self.sent.append((condition, copy))

    def finish(self):
        for condition, copy in self.sent:
            guarded(condition, copy.wait_send)


BLOCK = 512
DEPTH = 3
LATENCY = 1.5
UNIT = 20.0
CORE_UNIT = 40.0
LATE_PARTS = (6,)
LATE_ITEMS = (0, 1)
PUMP = 0.4


def forward_kernel(dims, tensor, parts, tasks, *refs):
    input_ref, top_ref, mask_ref, vector_ref = refs[:4]
    own_weights = refs[4:8]
    outs, land = refs[8:13], refs[13:15]
    weight_qkv, weight_vec, weight_out, weight_one, weight_two = outs
    far = refs[15:20]
    projected, grad_one, grad_two, table, vec_sums, pre_sums, bias_column = refs[20:27]
    (
        block_out,
        grad_middle,
        back_one,
        mixed,
        low_one,
        low_turned,
        pack,
        keep_ref,
        square,
        vec_buf,
        qkv_buf,
        head_stage,
        out_buf,
        one_buf,
        two_buf,
        low_two,
        low_two_turned,
        back_two,
        back_two_turned,
        grad_low_two,
        hidden_bias,
        head_bias,
        one_stage,
        two_stage,
        one_keep,
        two_keep,
        other,
        active,
        grad_pre,
        load_sem,
        store_sem,
        keep_sem,
        head_sem,
        land_sem,
        far_sem,
        local_sem,
        send_sem,
        recv_sem,
    ) = refs[27:]
    near = (block_out, grad_middle, back_one, mixed, low_turned)

    def far_store(at):
        return pltpu.make_async_copy(near[at], far[at], far_sem.at[at])

    here = Place(dims, tensor)
    gather = Gather(here, pack, outs, parts, local_sem, send_sem, recv_sem)
    rows, width = input_ref.shape
    own_rows = pack.shape[0]
    per_rank = weight_qkv.shape[1]
    low = jnp.bfloat16
    step_rows = LANES

    def fill_pack():
        base = 0
        for pair in range(per_rank):
            for kind in range(3):
                part = own_weights[0][kind, :, pl.ds(pair * LANES, LANES)]
                pack[:, pl.ds(base, LANES)] = part.astype(low)
                base += LANES
        square[...] = jnp.zeros_like(square)
        square[pl.ds(0, VEC), :] = vector_ref[...]
        pack[:, pl.ds(base, LANES)] = square[...].T.astype(low)
        base += LANES
        for ref in own_weights[1:]:
            pack[:, pl.ds(base, ref.shape[1])] = ref[...].astype(low)
            base += ref.shape[1]

    def mask_row():
        return mask_ref[pl.ds(here.rank, 1), :].astype(jnp.float32)

    def mask_bias(keep):
        return jnp.where(keep > 0.0, 0.0, -1e30)

    def first_masks():
        turned = jnp.broadcast_to(mask_row(), (LANES, rows)).T
        keep_ref[...] = turned[:, 0:1]
        bias_column[...] = mask_bias(turned[:, 0:1])

    def row_steps(body, carry):
        return lax.fori_loop(
            0, rows // step_rows, lambda at, c: body(pl.ds(pl.multiple_of(at * step_rows, step_rows), step_rows), c), carry
        )

    def load(source, buffer, sem):
        return pltpu.make_async_copy(source, buffer, sem)

    def first_norm():
        first_masks()
        copy = load(weight_vec, vec_buf, load_sem.at[7])
        copy.start()
        copy.wait()
        whole = vec_buf[...].reshape(width, LANES).astype(jnp.float32).T
        table[...] = whole[:16]
        for at in range(VEC - 8):
            hidden_bias[:, pl.ds(at * width, width)] = whole[7 + at : 8 + at]
        for pair in range(width // LANES):
            for kind, row in ((0, 2), (2, 3)):
                head_bias[:, pl.ds((pair * 3 + kind) * LANES, LANES)] = whole[
                    row : row + 1, pair * LANES : (pair + 1) * LANES
                ]
            head_bias[:, pl.ds((pair * 3 + 1) * LANES, LANES)] = jnp.zeros((1, LANES), jnp.float32)

        def body(part, carry):
            normed, _ = norm_rows(input_ref[part, :])
            low_one[part, :] = (normed * table[0:1, :] + table[1:2, :]).astype(low)
            back_two[part, :] = (top_ref[part, :].astype(jnp.float32) * keep_ref[part, :]).astype(low)
            return carry

        row_steps(body, 0)
        turn(back_two, back_two_turned)

    def head_store(pair, slot):
        column = pl.ds(pl.multiple_of(pair * 3 * LANES, LANES), 3 * LANES)
        return pltpu.make_async_copy(head_stage.at[slot], projected.at[:, column], head_sem.at[slot])

    def turn_first():
        turn(low_one, low_turned)
        far_store(4).start()

    def pair_of(at):
        turn_at, place = divmod(at, tensor)
        return lax.rem(here.rank + place, tensor) * per_rank + turn_at

    def head_load(at):
        turn_at, place = divmod(at, tensor)
        source = weight_qkv.at[lax.rem(here.rank + place, tensor), turn_at]
        return load(source, qkv_buf.at[at % 2], load_sem.at[at % 2])

    def heads(at):
        head_load(at).wait()
        pair = pair_of(at)
        slot = at % 2
        column = pl.ds(pl.multiple_of(pair * 3 * LANES, LANES), 3 * LANES)
        weight = qkv_buf[slot].reshape(width, 3 * LANES)
        value = (dot(low_one[...], weight) + head_bias[:, column]).astype(low)
        if at > 1:
            head_store(pair, slot).wait()
        head_stage[slot] = value
        head_store(pair, slot).start()
        mixed[:, pl.ds(pl.multiple_of(pair * LANES, LANES), LANES)] = attend_pair(head_stage.at[slot], mask_bias(mask_row()))

    def out_load():
        return [
            load(weight_out.at[rank, 0], out_buf.at[rank], load_sem.at[2]) for rank in range(tensor)
        ]

    def second_norm():
        far_store(3).start()
        for copy in out_load():
            copy.wait()
        columns = width // tensor
        for rank in range(tensor):
            weight = out_buf[rank].reshape(width, columns)
            term = dot(mixed[:, pl.ds(rank * columns, columns)], weight, CONTRACT_LAST)
            if rank == 0:
                grad_middle[...] = term
            else:
                grad_middle[...] += term

        def body(part, carry):
            middle = input_ref[part, :] + (grad_middle[part, :] + table[4:5, :]) * keep_ref[part, :]
            grad_middle[part, :] = middle
            normed, _ = norm_rows(middle)
            low_two[part, :] = (normed * table[5:6, :] + table[6:7, :]).astype(low)
            return carry

        row_steps(body, 0)
        turn(low_two, low_two_turned)

    stages = (one_stage, two_stage)
    keeps = (one_keep, two_keep)

    def hand_over(at):
        chunk, place = divmod(at, tensor)
        target = (*here.at, lax.rem(here.rank + place + 1, tensor))
        return [
            pltpu.make_async_remote_copy(
                src_ref=stages[which].at[at % 2],
                dst_ref=land[which].at[place, chunk],
                send_sem=store_sem.at[which, at % 2],
                recv_sem=land_sem.at[which, place, chunk],
                device_id=here.device(target),
                device_id_type=MESH,
            )
            for which in range(2)
        ]

    def keep_store(chunk):
        return [
            pltpu.make_async_copy(
                keeps[which].at[chunk % 2],
                out.at[chunk],
                keep_sem.at[which, chunk % 2],
            )
            for which, out in enumerate((grad_one, grad_two))
        ]

    def hidden_column(at):
        chunk, place = divmod(at, tensor)
        base = (lax.rem(here.rank + place + 1, tensor) * weight_one.shape[1] + chunk) * BLOCK
        return pl.ds(pl.multiple_of(base, LANES), BLOCK)

    def hidden_load(at):
        chunk, place = divmod(at, tensor)
        rank = lax.rem(here.rank + place + 1, tensor)
        return [
            load(source.at[rank, chunk], buffer.at[at % 2], load_sem.at[3 + 2 * which + at % 2])
            for which, (source, buffer) in enumerate(((weight_one, one_buf), (weight_two, two_buf)))
        ]

    staged = {}

    def hidden(at):
        chunk, place = divmod(at, tensor)
        column = hidden_column(at)
        for copy in hidden_load(at):
            copy.wait()
        half = rows // 2
        bias = hidden_bias[:, column]

        def body(turn_at, total):
            part = pl.ds(pl.multiple_of(turn_at * half, half), half)
            one = one_buf[at % 2].reshape(width, BLOCK)
            two = two_buf[at % 2].reshape(width, BLOCK)
            preact = dot(low_two[part, :], one) + bias
            gate = jax.nn.sigmoid(1.702 * preact)
            value = (preact * gate).astype(low)
            active[part, :] = value
            derivative = gate + 1.702 * preact * gate * (1.0 - gate)
            grad = (dot(back_two[part, :], two) * derivative).astype(low)
            grad_pre[part, :] = grad
            if at == 0:
                block_out[part, :] = dot(value, two, CONTRACT_LAST)
                grad_low_two[part, :] = dot(grad, one, CONTRACT_LAST)
            else:
                block_out[part, :] += dot(value, two, CONTRACT_LAST)
                grad_low_two[part, :] += dot(grad, one, CONTRACT_LAST)
            return total + jnp.sum(grad.astype(jnp.float32), axis=0, keepdims=True)

        pre_sums[:, column] = lax.fori_loop(0, 2, body, jnp.zeros((1, BLOCK), jnp.float32))
        mine = place == tensor - 1
        if mine:
            targets = [ref.at[chunk % 2] for ref in keeps]
            if chunk > 1:
                for copy in keep_store(chunk):
                    copy.wait()
        else:
            targets = [ref.at[at % 2] for ref in stages]
            for copy in staged.pop(at % 2, ()):
                copy.wait_send()
        for target, left, right in (
            (targets[0], low_two_turned, grad_pre),
            (targets[1], back_two_turned, active),
        ):

            def gradient(at_z, carry, target=target, left=left, right=right):
                size = width // dims[0]
                part = pl.ds(pl.multiple_of(at_z * size, size), size)
                value = dot(left[part, :], right[...]).astype(low)
                target[at_z] = value.reshape(*target.shape[1:])
                return carry

            lax.fori_loop(0, dims[0], gradient, 0)
        if not mine:
            staged[at % 2] = hand_over(at)
            for copy in staged[at % 2]:
                copy.start()

    def combine(chunk):
        for place in range(tensor - 1):
            for which, copy in enumerate(hand_over(chunk * tensor + place)):
                copy.wait_recv()
                fetch = load(land[which].at[place, chunk], other, load_sem.at[7])
                fetch.start()
                fetch.wait()
                keeps[which][chunk % 2] = keeps[which][chunk % 2] + other[...]
        for copy in keep_store(chunk):
            copy.start()

    def last_norm():
        def body(part, sums):
            middle = grad_middle[part, :]
            keep = keep_ref[part, :]
            top = top_ref[part, :].astype(jnp.float32)
            block_out[part, :] = middle + (block_out[part, :] + table[VEC - 1 : VEC, :]) * keep
            normed, inverse = norm_rows(middle)
            grad_low = grad_low_two[part, :]
            scaled = grad_low * table[5:6, :]
            first = jnp.mean(scaled, axis=1, keepdims=True)
            second = jnp.mean(scaled * normed, axis=1, keepdims=True)
            grad = top + inverse * (scaled - first - normed * second)
            grad_middle[part, :] = grad
            masked = grad * keep
            back_one[part, :] = masked.astype(low)
            terms = (masked, grad_low * normed, grad_low, top * keep)
            return tuple(old + jnp.sum(term, axis=0, keepdims=True) for old, term in zip(sums, terms))

        zero = jnp.zeros((1, width), jnp.float32)
        for at, value in enumerate(row_steps(body, (zero,) * 4)):
            vec_sums[at : at + 1, :] = value
        for at in range(3):
            far_store(at).start()

    fill_pack()
    here.barrier(((0,), (1,), (2,), (3,)))
    steps = Steps()
    whole = sum(part[3] for part in parts)
    nz, ny, nx = dims

    def lengths(item, phase):
        share = parts[item][3] / whole * UNIT
        across = ny * nx if item in gather.late else 1
        along = 1 if item in gather.late else nz
        return {
            "pair": (share * across, "end"),
            "middle": (share * across * 2, "middle"),
            "back": (share * across * 2, "end"),
            "all": (share * across * nz, "end"),
            "first": (share * along / 2, "xy"),
            "second": (share * along, "xy"),
            "core": (share * CORE_UNIT / UNIT, "core"),
        }[gather.phases(item)[phase]]

    for item, part in enumerate(parts):
        phases = len(gather.phases(item))
        for phase in range(phases + 1):
            after = [("copy", item, phase - 1)] if phase else []
            if phase == 0 and item >= DEPTH and item not in gather.late:
                after = [("copy", item - DEPTH, 1)]
            if item in gather.late:
                if phase == 0:
                    after = [("copy", DEPTH, 1)]
                if phase == 2:
                    after += [("copy", other, 1) for other in range(min(len(parts), item + 3)) if other not in gather.late]
            length, link = lengths(item, min(phase, phases - 1))
            steps.add(
                ("copy", item, phase),
                functools.partial(gather.advance, item, phase),
                PUMP,
                0.5 if phase == 0 else 0.0,
                after,
                [(item, phase - 1)] if phase else [],
                [((item, phase), link, length)] if phase < phases else [],
            )

    def landed(items):
        return [("copy", item, len(gather.phases(item))) for item in items]

    def start(copies):
        for copy in copies:
            copy.start()

    previous = None
    head_count, block_count = per_rank * tensor, FF // BLOCK
    for name, at, items in tasks:
        after = landed(items) + ([previous] if previous else [])
        begin, run, time = {
            "norm": (None, first_norm, 4.0),
            "turn": (None, turn_first, 1.5),
            "heads": (lambda at=at: head_load(at).start(), lambda at=at: heads(at), 3.0),
            "out": (lambda: start(out_load()), second_norm, 5.0),
            "hidden": (lambda at=at: start(hidden_load(at)), lambda at=at: hidden(at), 5.5),
        }[name]
        if begin is not None:
            first = landed(items)
            if at > 1:
                first.append((name, at - 2))
            steps.add(("load", name, at), begin, 0.1, 0.2, first)
            after.append(("load", name, at))
        mine = name == "hidden" and at % tensor == tensor - 1
        chunk = at // tensor
        if mine and chunk > 1:
            after.append(("combine", chunk - 2))
        starts = []
        if name == "hidden" and not mine:
            starts = [(("hand", at), "core", CORE_UNIT / len(parts))]
        steps.add((name, at), run, time, 1.0, after, (), starts)
        if mine:
            waits = [("hand", chunk * tensor + place) for place in range(tensor - 1)]
            steps.add(
                ("combine", chunk), functools.partial(combine, chunk), 2.0, 0.8, [(name, at)], waits
            )
        previous = (name, at)
    steps.add(("last", 0), last_norm, 4.0, 0.9, [previous])
    steps.run()
    for at in range(5):
        far_store(at).wait()
    for slot in range(min(2, head_count)):
        head_store(0, slot).wait()
    for chunk in range(min(2, block_count // tensor)):
        for copy in keep_store(chunk):
            copy.wait()
    for copies in staged.values():
        for copy in copies:
            copy.wait_send()
    gather.finish()


def forward(dims, tensor, inputs, cotangent, token_mask, vectors, weights):
    own_rows, columns = weights[0].shape[1:]
    hidden = weights[2].shape[1]
    rows, width = inputs.shape
    low, full = jnp.bfloat16, jnp.float32
    widths = (3 * columns, LANES, columns, hidden, hidden)
    offsets = [sum(widths[:at]) for at in range(5)]
    per_rank = columns // LANES
    parts = [(1, offsets[1], None, LANES)]
    tasks = [("norm", 0, (0,)), ("turn", 0, (0,))]
    for at in range(per_rank):
        size = 3 * LANES
        parts.append((0, offsets[0] + at * size, at, size))
        tasks += [("heads", at * tensor + place, (len(parts) - 1,)) for place in range(tensor)]
    tasks.append(("out", 0, (len(parts),)))
    parts.append((2, offsets[2], 0, columns))
    for block in range(hidden // BLOCK):
        needed = (len(parts), len(parts) + 1)
        parts += [(which, offsets[which] + block * BLOCK, block, BLOCK) for which in (3, 4)]
        tasks += [("hidden", block * tensor + place, needed) for place in range(tensor)]
    count = len(parts)
    peers = max(1, dims[0] - 1, dims[1] + dims[2] - 2, tensor - 1)
    anywhere = pl.BlockSpec(memory_space=pl.ANY)
    inside = pl.BlockSpec(memory_space=pltpu.VMEM)
    block = (*dims, own_rows, BLOCK)
    chunks = hidden // BLOCK

    def shape(kind, *size):
        return jax.ShapeDtypeStruct(size, kind)

    return pl.pallas_call(
        functools.partial(forward_kernel, dims, tensor, tuple(parts), tuple(tasks)),
        name="forward",
        out_shape=[
            shape(low, tensor, per_rank, *dims, own_rows, 3 * LANES),
            shape(low, *dims, own_rows, LANES),
            shape(low, tensor, 1, *dims, own_rows, columns),
            *[shape(low, tensor, chunks, *block)] * 2,
            *[shape(low, max(1, tensor - 1), chunks, *block)] * 2,
            shape(full, rows, width),
            shape(full, rows, width),
            *[shape(low, rows, width)] * 2,
            shape(low, width, rows),
            shape(low, rows, 3 * width),
            *[shape(low, chunks, *block)] * 2,
            shape(full, 16, width),
            shape(full, 8, width),
            shape(full, 1, hidden * tensor),
            shape(full, rows, 1),
        ],
        in_specs=[inside] * 8,
        out_specs=[anywhere] * 15 + [inside] * 4,
        scratch_shapes=[
            pltpu.VMEM((rows, width), full),
            pltpu.VMEM((rows, width), full),
            *[pltpu.VMEM((rows, width), low)] * 3,
            pltpu.VMEM((width, rows), low),
            pltpu.VMEM((own_rows, sum(widths)), low),
            pltpu.VMEM((rows, 1), full),
            pltpu.VMEM((LANES, own_rows), full),
            pltpu.VMEM((*dims, own_rows, LANES), low),
            pltpu.VMEM((2, *dims, own_rows, 3 * LANES), low),
            pltpu.VMEM((2, rows, 3 * LANES), low),
            pltpu.VMEM((tensor, *dims, own_rows, columns), low),
            pltpu.VMEM((2, *block), low),
            pltpu.VMEM((2, *block), low),
            pltpu.VMEM((rows, width), low),
            pltpu.VMEM((width, rows), low),
            pltpu.VMEM((rows, width), low),
            pltpu.VMEM((width, rows), low),
            pltpu.VMEM((rows, width), full),
            pltpu.VMEM((1, hidden * tensor), full),
            pltpu.VMEM((1, 3 * width), full),
            pltpu.VMEM((2, *block), low),
            pltpu.VMEM((2, *block), low),
            pltpu.VMEM((2, *block), low),
            pltpu.VMEM((2, *block), low),
            pltpu.VMEM(block, low),
            pltpu.VMEM((rows, BLOCK), low),
            pltpu.VMEM((rows, BLOCK), low),
            pltpu.SemaphoreType.DMA((8,)),
            pltpu.SemaphoreType.DMA((2, 2)),
            pltpu.SemaphoreType.DMA((2, 2)),
            pltpu.SemaphoreType.DMA((2,)),
            pltpu.SemaphoreType.DMA((2, max(1, tensor - 1), chunks)),
            pltpu.SemaphoreType.DMA((5,)),
            pltpu.SemaphoreType.DMA((count,)),
            pltpu.SemaphoreType.DMA((count, 6, peers)),
            pltpu.SemaphoreType.DMA((count, 6, peers)),
        ],
        compiler_params=pltpu.CompilerParams(
            collective_id=0, has_side_effects=True, vmem_limit_bytes=62 << 20
        ),
    )(inputs, cotangent, token_mask, vectors, *weights)


class Layout:
    def __init__(self, columns, hidden, order):
        sizes = {"qkv": 3 * columns, "out": columns, "one": hidden, "two": hidden, "vec": LANES}
        self.order = order
        self.sizes = sizes
        self.start = {}
        at = 0
        for name in order:
            self.start[name] = at
            at += sizes[name]
        self.total = at
        self.columns = columns

    def span(self, name):
        return (self.start[name], self.sizes[name])

    def matrices(self):
        base = self.start["qkv"]
        pairs = range(self.columns // LANES)
        spans = [[(base + (pair * 3 + at) * LANES, LANES) for pair in pairs] for at in range(3)]
        return spans + [[self.span(name)] for name in ("out", "one", "two")]


def pick(values, lane):
    row = jnp.zeros((1, LANES), jnp.float32)
    for at, value in enumerate(values):
        row = jnp.where(lane == at, value, row)
    return row


def total_of(values):
    return jnp.sum(jnp.sum(values, axis=1, keepdims=True), axis=0, keepdims=True)


def attend_pair_back(heads_ref, bias_ref, grads, totals):
    def body(head, carry):
        query, key, value = (heads_ref[:, kind * LANES : (kind + 1) * LANES] for kind in range(3))
        grad = grads[...]
        lanes = head_lanes(head)
        key = jnp.where(lanes, key, jnp.zeros_like(key))
        value = jnp.where(lanes, value, jnp.zeros_like(value))
        scores = dot(key, query, CONTRACT_LAST) * (HEAD_DIM ** (-0.5) * LOG2E) + bias_ref[...]
        raised = jnp.exp2(scores - jnp.max(scores, axis=0, keepdims=True))
        attention = raised * (1.0 / jnp.sum(raised, axis=0, keepdims=True))
        grad_value = dot(attention.astype(jnp.bfloat16), grad)
        grad_attention = dot(value, grad, CONTRACT_LAST)
        weighted = jnp.sum(attention * grad_attention, axis=0, keepdims=True)
        grad_scores = (attention * (grad_attention - weighted) * HEAD_DIM ** (-0.5)).astype(jnp.bfloat16)
        totals[1] = jnp.where(lanes, dot(grad_scores, query), totals[1])
        totals[2] = jnp.where(lanes, grad_value, totals[2])
        totals[0] = jnp.where(lanes, dot(key.T, grad_scores).T, totals[0])
        return carry

    totals[...] = jnp.zeros_like(totals)
    lax.fori_loop(0, 2, body, 0)
    return jnp.concatenate([totals[kind].astype(jnp.bfloat16) for kind in range(3)], axis=1)


def backward_kernel(dims, tensor, items, layout, *refs):
    (
        sum_two,
        sum_one,
        weight_qkv,
        weight_out,
        projected,
        input_ref,
        middle_ref,
        *far,
        bias_ref,
        table,
        vec_sums,
        pre_sums,
    ) = refs[:14]
    far = (*far, *refs[14:18])
    row_states, col_states = refs[18:22], refs[22:26]
    second_ref, vector_ref = refs[26:28]
    input_grad_out, total_ref, col_new_ref, row_new_ref, second_new_ref, sums_ref = refs[28:34]
    (
        input_grad,
        own,
        from_core,
        one_x,
        one_y,
        two_y,
        two_x,
        from_z,
        late_z,
        late_one_y,
        late_one_x,
        late_two_x,
        late_two_y,
        col_sum,
        col_in,
        row_sum,
        row_in,
        small,
        small_in,
        square,
        turned,
        mixed,
        back_one,
        *weights,
        low_turned,
        back_turned,
        grad_mixed,
        out_buf,
        qkv_buf,
        head_buf,
        row_buf,
        out_stage,
        qkv_stage,
        vec_stage,
        head_sums,
        head_totals,
        table_grad_ref,
        load_sem,
        stage_sem,
        core_sem,
        local_sem,
        send_sem,
        recv_sem,
        sum_send,
        sum_recv,
        far_sem,
    ) = refs[34:]
    near = (mixed, low_turned, back_one, *weights)

    def far_load(at):
        return pltpu.make_async_copy(far[at], near[at], far_sem.at[at])

    here = Place(dims, tensor)
    nz, ny, nx = dims
    low = jnp.bfloat16
    own_rows = own.shape[3]
    half_rows = own_rows // 2
    rows, width = input_grad.shape
    own_place = (*here.at, here.rank)
    count = len(items)
    core_start = layout.start["out"]

    def columns(item):
        _, start, size, _ = items[item]
        return pl.ds(start, size)

    def core_columns(item):
        _, start, size, _ = items[item]
        return pl.ds(start - core_start, size)

    def phases(item):
        lengthwise = along_z(nz)[::-1]
        across = ("first", "second")
        return (*lengthwise, *across) if item in late else (*across, *lengthwise)

    def moves(item, phase):
        first, second, whole = pl.ds(0, half_rows), pl.ds(half_rows, half_rows), pl.ds(0, own_rows)
        kind = phases(item)[phase]
        name, start, size, _ = items[item]
        column = columns(item)
        found = []
        if kind in ("pair", "middle", "back"):
            pair, far, near, middle = here.line()
            outside = jnp.logical_not(middle)
            rest = (slice(None), slice(None)) if item in late else here.at[1:]
            buffer = late_z if item in late else from_z
            landing_column = pl.ds(late.index(item) * BLOCK, size) if item in late else column
            free = (slice(None), slice(None)) if item in late else ()
            z = here.at[0]
            device, sent_z, add_z, slots, sends, receives = {
                "back": (near, pl.ds(far, 2), pl.ds(far, 2), pl.ds(0, 2), outside, middle),
                "middle": (3 - z, pl.ds(far, 2), pl.ds(pair, 2), pl.ds(2, 2), middle, middle),
                "pair": (near, near, z, 4, None, None),
            }[kind]
            found.append(
                (
                    here.at_z(device),
                    own.at[(sent_z, *rest, whole, column)],
                    buffer.at[(slots, *free, slice(None), landing_column)],
                    (add_z, *rest),
                    whole,
                    sends,
                    receives,
                )
            )
            return found
        if item in late:
            column = pl.ds(late.index(item) * BLOCK, size)
            steps = {
                "all": ((0, (0,), whole, late_z),),
                "first": ((1, (0, 1), first, late_one_y), (2, (0, 2), second, late_one_x)),
                "second": ((2, (0, 1, 2), first, late_two_x), (1, (0, 1, 2), second, late_two_y)),
            }[kind]
        else:
            steps = {
                "first": ((2, (2,), first, one_x), (1, (1,), second, one_y)),
                "second": ((1, (1, 2), first, two_y), (2, (1, 2), second, two_x)),
                "all": ((0, (0, 1, 2), whole, from_z),),
            }[kind]
        for axis, fixed, part, landing in steps:
            for step in range(1, here.size(axis)):
                target = here.moved(axis, step)
                index = tuple(target[a] if a in fixed else slice(None) for a in range(3))
                added = tuple(here.at[a] if a in fixed else slice(None) for a in range(3))
                free = (slice(None),) * (3 - len(fixed))
                found.append(
                    (
                        here.device(target),
                        own.at[(*index, part, columns(item))],
                        landing.at[(step - 1, *free, slice(None), column)],
                        added,
                        part,
                        None,
                        None,
                    )
                )
        return found

    def copies(item, phase):
        found = []
        for at, (device, source, landing, added, part, sends, receives) in enumerate(moves(item, phase)):
            copy = pltpu.make_async_remote_copy(
                src_ref=source,
                dst_ref=landing,
                send_sem=send_sem.at[item, phase, at],
                recv_sem=recv_sem.at[item, phase, at],
                device_id=device,
                device_id_type=MESH,
            )
            found.append((sends, receives, copy, added, part, landing))
        return found

    def add_core(item):
        def body(at, carry):
            z, y, x = at // (ny * nx), at // nx % ny, at % nx
            value = own[z, y, x, :, columns(item)]
            for step in range(tensor - 1):
                value = value + from_core[step, z, y, x, :, core_columns(item)]
            own[z, y, x, :, columns(item)] = value
            return carry

        if tensor > 1:
            lax.fori_loop(0, nz * ny * nx, body, 0)

    def add_in(item, landing, added, part):
        sizes, starts = [], []
        for axis, at in enumerate(added):
            if isinstance(at, slice):
                sizes.append(dims[axis])
                starts.append(0)
            elif hasattr(at, "start"):
                sizes.append(at.size)
                starts.append(at.start)
            else:
                sizes.append(None)
                starts.append(at)
        loops = 1
        for size in sizes:
            loops *= size or 1

        def body(at, carry):
            place, inner, rest = [], [], at
            for size, start in reversed(list(zip(sizes, starts))):
                if size is None:
                    place.insert(0, start)
                else:
                    place.insert(0, start + rest % size)
                    inner.insert(0, rest % size)
                    rest = rest // size
            where = (*place, part, columns(item))
            own[where] = own[where] + landing[tuple(inner)]
            return carry

        if loops == 1:
            body(0, 0)
        else:
            lax.fori_loop(0, loops, body, 0)

    def put_total(item, arrived):
        wide = columns(item)
        parts_of = {}
        for landing, part in arrived:
            parts_of.setdefault((part.start, part.size), []).append(landing)
        for (start, size), landings in parts_of.items():
            part = pl.ds(start, size)
            value = own[(*here.at, part, wide)].astype(jnp.float32)
            for landing in landings:
                value = value + landing[...].astype(jnp.float32)
            total_ref[part, wide] = value
        if items[item][0] == "vec":
            return
        for at, spans in enumerate(layout.matrices()):
            for start, size in spans:
                low_end, high_end = max(start, wide.start), min(start + size, wide.start + wide.size)
                if low_end < high_end:
                    square = total_ref[:, pl.ds(low_end, high_end - low_end)]
                    square = square * square
                    col_sum[0, :, pl.ds(low_end, high_end - low_end)] = jnp.sum(square, axis=0, keepdims=True)
                    found = jnp.sum(square, axis=1, keepdims=True)
                    row_sum[0] = row_sum[0] + jnp.where(lane == at, found, 0.0)

    sent = []
    lane = lax.broadcasted_iota(jnp.int32, (1, LANES), 1)
    row_sum[0] = jnp.zeros_like(row_sum[0])
    guarded_sent = []
    late = [at for at in LATE_ITEMS if items[at][0] in ("one", "two")]

    def exchange(kind, phase, axes, buffer, landing):
        moved = []
        for at, device in enumerate(here.peers(*axes)):
            copy = pltpu.make_async_remote_copy(
                src_ref=buffer.at[phase],
                dst_ref=landing.at[phase, at],
                send_sem=sum_send.at[kind, phase, at],
                recv_sem=sum_recv.at[kind, phase, at],
                device_id=device,
                device_id_type=MESH,
            )
            copy.start()
            moved.append(copy)
        sent.extend(moved)

        def finish():
            value = buffer[phase]
            for at, copy in enumerate(moved):
                copy.wait_recv()
                value = value + landing[phase, at]
            buffer[phase + 1] = value

        return finish

    def hand_over(item, step, source, sem):
        return pltpu.make_async_remote_copy(
            src_ref=source,
            dst_ref=from_core.at[step - 1, :, :, :, :, core_columns(item)],
            send_sem=sem,
            recv_sem=core_sem.at[item, step - 1],
            device_id=here.device(here.moved(3, step)),
            device_id_type=MESH,
        )

    arriving = {}

    def keep_own(item, value):
        own[:, :, :, :, columns(item)] = value.reshape(nz, ny, nx, own_rows, value.shape[1])

    out_items = [at for at, item in enumerate(items) if item[0] == "out"]
    qkv_items = [at for at, item in enumerate(items) if item[0] == "qkv"]
    vec_item = count - 1
    per_rank = len(qkv_items)
    steps_in_all = per_rank * tensor

    def rank_at(step):
        return lax.rem(here.rank + step, tensor)

    def pair_loads(at):
        turn_at, place = divmod(at, tensor)
        pair = rank_at(place + 1) * per_rank + turn_at
        column = pl.ds(pl.multiple_of(pair * 3 * LANES, LANES), 3 * LANES)
        near = at % 2
        return pair, column, [
            pltpu.make_async_copy(
                weight_qkv.at[rank_at(place + 1), turn_at], qkv_buf.at[near], load_sem.at[0, near]
            ),
            pltpu.make_async_copy(projected.at[:, column], head_buf.at[near], load_sem.at[1, near]),
        ]

    def out_task():
        fetch = [
            pltpu.make_async_copy(weight_out.at[rank, 0], out_buf.at[rank], load_sem.at[2, 0])
            for rank in range(tensor)
        ]
        for copy in fetch:
            copy.start()
        far_load(2).wait()
        turn(back_one, back_turned)
        far_load(0).wait()
        for copy in pair_loads(0)[2]:
            copy.start()
        size = out_stage.shape[5]
        item = out_items[0]
        for step in range(1, tensor + 1):
            column = pl.ds(pl.multiple_of(rank_at(step) * size, LANES), size)
            value = dot(back_turned[...], mixed[:, column]).astype(low)
            if step < tensor:
                out_stage[step - 1] = value.reshape(nz, ny, nx, own_rows, size)
                copy = hand_over(item, step, out_stage.at[step - 1], stage_sem.at[item, step - 1])
                copy.start()
                sent.append(copy)
                arriving.setdefault(item, []).append(copy)
            else:
                keep_own(item, value)
        for copy in fetch:
            copy.wait()
        for rank in range(tensor):
            weight = out_buf[rank].reshape(width, size)
            grad_mixed[:, pl.ds(rank * size, size)] = dot(back_one[...], weight).astype(low)
        far_load(1).wait()

    def state_task():
        def fill(refs, other):
            square[...] = jnp.full_like(square, other)
            base = 0
            for ref in refs:
                square[pl.ds(base, ref.shape[0]), :] = ref[...]
                base += ref.shape[0]
            return square[...].T

        for at in range(3, 7):
            far_load(at).wait()
        turned[0] = fill(row_states, 1.0)
        turned[1] = fill((second_ref,), 1.0)
        turned[2] = fill((vector_ref,), 0.0)

    staged = {}

    def pair_task(at):
        turn_at, place = divmod(at, tensor)
        pair, column, loads = pair_loads(at)
        for copy in loads:
            copy.wait()
        if at + 1 < steps_in_all:
            for copy in pair_loads(at + 1)[2]:
                copy.start()
        near = at % 2
        grads = grad_mixed.at[:, pl.ds(pl.multiple_of(pair * LANES, LANES), LANES)]
        value = attend_pair_back(head_buf.at[near], bias_ref, grads, head_totals)
        head_sums[:, column] = jnp.sum(value.astype(jnp.float32), axis=0, keepdims=True)
        weight = qkv_buf[near].reshape(width, 3 * LANES)
        term = dot(value, weight, CONTRACT_LAST)
        if at == 0:
            input_grad[...] = term
        else:
            input_grad[...] += term
        item = qkv_items[turn_at]
        mine = place + 1 == tensor
        if not mine and 0 in staged:
            staged[0].wait_send()

        def gradient(at_z, carry):
            size = width // nz
            part = pl.ds(pl.multiple_of(at_z * size, size), size)
            grad = dot(low_turned[part, :], value).astype(low)
            grad = grad.reshape(ny, nx, own_rows, 3 * LANES)
            if mine:
                own[at_z, :, :, :, columns(item)] = grad
            else:
                qkv_stage[at_z] = grad
            return carry

        lax.fori_loop(0, nz, gradient, 0)
        if not mine:
            copy = hand_over(item, place + 1, qkv_stage, stage_sem.at[item, place])
            copy.start()
            staged[0] = copy
            arriving.setdefault(item, []).append(copy)

    def grad_store():
        return pltpu.make_async_copy(input_grad, input_grad_out, far_sem.at[7])

    def last_task():
        step_rows = row_buf.shape[2]

        def fetch(at):
            near = lax.rem(at, 2)
            part = pl.ds(pl.multiple_of(at * step_rows, step_rows), step_rows)
            return [
                pltpu.make_async_copy(source.at[part, :], row_buf.at[which, near], load_sem.at[which, near])
                for which, source in enumerate((input_ref, middle_ref))
            ]

        for copy in fetch(0):
            copy.start()

        def body(at, sums):
            for copy in fetch(at):
                copy.wait()

            @pl.when(at + 1 < rows // step_rows)
            def _():
                for copy in fetch(at + 1):
                    copy.start()

            near = lax.rem(at, 2)
            part = pl.ds(pl.multiple_of(at * step_rows, step_rows), step_rows)
            normed, inverse = norm_rows(row_buf[0, near])
            grad_low = input_grad[part, :]
            scaled = grad_low * table[0:1, :]
            first = jnp.mean(scaled, axis=1, keepdims=True)
            second = jnp.mean(scaled * normed, axis=1, keepdims=True)
            input_grad[part, :] = row_buf[1, near] + inverse * (scaled - first - normed * second)
            terms = (grad_low * normed, grad_low)
            return tuple(old + jnp.sum(term, axis=0, keepdims=True) for old, term in zip(sums, terms))

        zero = jnp.zeros((1, width), jnp.float32)
        found = lax.fori_loop(0, rows // step_rows, body, (zero, zero))
        grad_store().start()
        table_grad_ref[...] = jnp.zeros_like(table_grad_ref)
        for at in range(2):
            table_grad_ref[at : at + 1, :] = found[at]
        for pair in range(width // LANES):
            for kind, row in ((0, 2), (2, 3)):
                table_grad_ref[row : row + 1, pl.ds(pair * LANES, LANES)] = head_sums[
                    :, pl.ds((pair * 3 + kind) * LANES, LANES)
                ]
        for at, row in enumerate((4, 5, 6, VEC - 1)):
            table_grad_ref[row : row + 1, :] = vec_sums[at : at + 1, :]
        for at in range(VEC - 8):
            table_grad_ref[7 + at : 8 + at, :] = pre_sums[:, pl.ds(at * width, width)]
        value = table_grad_ref[...].T.astype(low)
        vec_stage[...] = value.reshape(nz, ny, nx, own_rows, LANES)
        for step in range(1, tensor):
            copy = hand_over(vec_item, step, vec_stage, stage_sem.at[vec_item, step - 1])
            copy.start()
            sent.append(copy)
            arriving.setdefault(vec_item, []).append(copy)
        keep_own(vec_item, value)

    for at in (2, 0, 1, 3, 4, 5, 6):
        far_load(at).start()
    here.barrier(((0, 3), (1, 2)))
    local = {}
    for item, (name, _, _, source) in enumerate(items):
        if name in ("one", "two"):
            array = sum_one if name == "one" else sum_two
            copy = pltpu.make_async_copy(
                array.at[source], own.at[:, :, :, :, columns(item)], local_sem.at[item]
            )
            copy.start()
            local[item] = copy

    def advance(item, phase):
        last = len(phases(item))
        if phase > 0:
            arrived = []
            for _, receives, copy, added, part, landing in copies(item, phase - 1):

                def take(copy=copy, landing=landing, added=added, part=part):
                    copy.wait_recv()
                    if phase < last:
                        add_in(item, landing, added, part)

                guarded(receives, take)
                arrived.append((landing, part))
            if phase == last:
                put_total(item, arrived)
        elif item in local:
            local[item].wait()
        else:
            for copy in arriving.get(item, ()):
                copy.wait_recv()
            add_core(item)
        if phase < last:
            for sends, _, copy, *_ in copies(item, phase):
                guarded(sends, copy.start)
                guarded_sent.append((sends, copy))

    steps = Steps()
    owner = {item: ("out", 0) for item in out_items}
    owner |= {item: ("pair", tensor * (at + 1) - 1) for at, item in enumerate(qkv_items)}
    owner[vec_item] = ("last", 0)
    for item, (name, _, size, _) in enumerate(items):
        share = size / layout.total * UNIT
        across = ny * nx if item in late else 1
        along = 1 if item in late else nz
        lengths = {
            "pair": (share * across, "end"),
            "middle": (share * across * 2, "middle"),
            "back": (share * across * 2, "end"),
            "all": (share * across * nz, "end"),
            "first": (share * along, "xy"),
            "second": (share * along / 2, "xy"),
        }
        if item in late:
            lengths |= {"first": (share, "xy"), "second": (share / 2, "xy")}
        early = item not in owner
        kinds = phases(item)
        for phase in range(len(kinds) + 1):
            after = [("copy", item, phase - 1)] if phase else []
            waits = [(item, phase - 1)] if phase else []
            if phase == 0 and early and item >= DEPTH + len(late):
                after = [("copy", item - DEPTH, 1)]
            if phase == 0 and not early:
                after, waits = [owner[item]], [("core", owner[item])]
            starts = []
            if phase < len(kinds):
                length, link = lengths[kinds[phase]]
                starts = [((item, phase), link, length)]
            steps.add(
                ("copy", item, phase),
                functools.partial(advance, item, phase),
                PUMP * (1.5 if phase == 1 else 1.0),
                (0.5 if phase == 0 and early else 0.0),
                after,
                waits,
                starts,
            )
    steps.add(("state", 0), state_task, 1.0, 2.0)
    steps.add(("out", 0), out_task, 8.0, 1.0, (), (), [(("core", ("out", 0)), "core", CORE_UNIT / 12)])
    for at in range(steps_in_all):
        after = [("pair", at - 1) if at else ("out", 0)]
        starts = [(("core", ("pair", at)), "core", CORE_UNIT / 24)]
        steps.add(("pair", at), functools.partial(pair_task, at), 6.0, 1.0, after, (), starts)
    steps.add(
        ("last", 0), last_task, 4.0, 1.0, [("pair", steps_in_all - 1)], (), [(("core", ("last", 0)), "core", 1.0)]
    )
    steps.run()
    sent.extend(staged.values())

    decay_rate = 1.0 - STEP ** (-0.8)
    keep_old = 1.0 - decay_rate
    long = layout.sizes["one"] * tensor
    matrices = layout.matrices()
    finish_row = exchange(0, 0, (3,), row_sum, row_in)
    finish_col = exchange(1, 0, (0,), col_sum, col_in)
    vec_start = layout.start["vec"]
    table_grad = total_ref[:, pl.ds(vec_start, LANES)]
    second_new = decay_rate * turned[1] + keep_old * (table_grad * table_grad + EPS_ONE)
    second_new_ref[...] = second_new
    vector_update = table_grad * lax.rsqrt(second_new)
    vector_sums = jnp.sum(vector_update * vector_update, axis=0, keepdims=True) / tensor
    vector_weight = jnp.sum(turned[2] * turned[2], axis=0, keepdims=True) / tensor
    weight_sums = [total_of(jnp.sum(weights[0][...] * weights[0][...], axis=0))]
    weight_sums += [total_of(ref[...] * ref[...]) for ref in weights[1:]]
    finish_row()
    row_counts = pick([jnp.full((1, 1), 1.0 / size, jnp.float32) for size in (width, width, width, width, long, long)], lane)
    row_new = decay_rate * turned[0] + keep_old * (row_sum[1] * row_counts + EPS_ONE)
    row_new_ref[...] = row_new
    finish_col()
    exchange(1, 1, (1, 2), col_sum, col_in)()
    for at, spans in enumerate(matrices):
        for place, (start, size) in enumerate(spans):
            if at < 3:
                old = col_states[0][at : at + 1, pl.ds(place * LANES, LANES)]
            else:
                old = col_states[at - 2][...]
            fresh = keep_old * (col_sum[2, :, pl.ds(start, size)] / width + EPS_ONE)
            col_new_ref[:, pl.ds(start, size)] = decay_rate * old + fresh
    ratios = []
    means = []
    for at, spans in enumerate(matrices):
        row_at = row_new[:, at : at + 1]
        ratio = 0.0
        for start, size in spans:
            value = total_ref[:, pl.ds(start, size)]
            col_at = col_new_ref[:, pl.ds(start, size)]
            ratio = ratio + total_of(value * value / (row_at * col_at))
        ratios.append(ratio)
        if at in (3, 5):
            means.append(jnp.sum(col_at, axis=1, keepdims=True) / (nz * ny * nx))
        else:
            means.append(jnp.sum(row_at, axis=0, keepdims=True) / tensor)
    small[0] = jnp.concatenate(
        [pick(ratios + means + weight_sums, lane), vector_sums, vector_weight, jnp.zeros((5, LANES), jnp.float32)], axis=0
    )
    exchange(2, 0, (0, 3), small, small_in)()
    exchange(2, 1, (1, 2), small, small_in)()
    sums_ref[...] = small[2]
    grad_store().wait()
    for copy in sent:
        copy.wait_send()
    for condition, copy in guarded_sent:
        guarded(condition, copy.wait_send)


def backward(dims, tensor, layout, large, near, weights, states):
    rows, width = large[-1].shape
    own_rows = width // (dims[0] * dims[1] * dims[2])
    half_rows = own_rows // 2
    columns = layout.columns
    items = []
    for block in range(layout.sizes["one"] // BLOCK):
        for name in ("two", "one"):
            items.append((name, layout.start[name] + block * BLOCK, BLOCK, block))
    items.append(("out", layout.start["out"], columns, 0))
    for start in range(0, 3 * columns, 3 * LANES):
        items.append(("qkv", layout.start["qkv"] + start, 3 * LANES, start))
    items.append(("vec", layout.start["vec"], LANES, 0))
    nz, ny, nx = dims
    peers = max(1, nz - 1, ny + nx - 2)
    group = max(1, nz * tensor - 1, ny * nx - 1)
    others = max(1, tensor - 1)
    offset = layout.total
    from_here = offset - layout.start["out"]
    late_width = BLOCK * max(1, len(LATE_ITEMS))
    low, full = jnp.bfloat16, jnp.float32
    anywhere = pl.BlockSpec(memory_space=pl.ANY)
    inside = pl.BlockSpec(memory_space=pltpu.VMEM)

    def hold(*shape):
        return pltpu.VMEM(tuple(max(1, size) for size in shape), low)

    sums = offset - LANES
    count = len(items)
    return pl.pallas_call(
        functools.partial(backward_kernel, dims, tensor, tuple(items), layout),
        name="backward",
        out_shape=[
            jax.ShapeDtypeStruct((rows, width), full),
            jax.ShapeDtypeStruct((own_rows, offset), full),
            jax.ShapeDtypeStruct((1, sums), full),
            jax.ShapeDtypeStruct((own_rows, LANES), full),
            jax.ShapeDtypeStruct((own_rows, LANES), full),
            jax.ShapeDtypeStruct((8, LANES), full),
        ],
        in_specs=[anywhere] * len(large) + [inside] * len(near) + [anywhere] * 4 + [inside] * len(states),
        out_specs=[anywhere] + [inside] * 5,
        scratch_shapes=[
            pltpu.VMEM((rows, width), full),
            hold(nz, ny, nx, own_rows, offset),
            hold(others, nz, ny, nx, own_rows, from_here),
            hold(nx - 1, nz, ny, half_rows, offset),
            hold(ny - 1, nz, nx, half_rows, offset),
            hold(ny - 1, nz, half_rows, offset),
            hold(nx - 1, nz, half_rows, offset),
            hold(5 if nz == 4 else nz - 1, own_rows, offset),
            hold(5 if nz == 4 else nz - 1, ny, nx, own_rows, late_width),
            hold(ny - 1, nx, half_rows, late_width),
            hold(nx - 1, ny, half_rows, late_width),
            hold(nx - 1, half_rows, late_width),
            hold(ny - 1, half_rows, late_width),
            pltpu.VMEM((3, 1, sums), full),
            pltpu.VMEM((2, max(1, nz - 1, ny * nx - 1), 1, sums), full),
            pltpu.VMEM((2, own_rows, LANES), full),
            pltpu.VMEM((1, others, own_rows, LANES), full),
            pltpu.VMEM((3, 8, LANES), full),
            pltpu.VMEM((2, group, 8, LANES), full),
            pltpu.VMEM((LANES, own_rows), full),
            pltpu.VMEM((3, own_rows, LANES), full),
            *[hold(rows, width)] * 2,
            *(pltpu.VMEM(weight.shape, full) for weight in weights),
            hold(width, rows),
            hold(width, rows),
            hold(rows, width),
            hold(tensor, *dims, own_rows, columns),
            hold(2, *dims, own_rows, 3 * LANES),
            hold(2, rows, 3 * LANES),
            pltpu.VMEM((2, 2, LANES // 2, width), full),
            hold(others, *dims, own_rows, columns),
            hold(*dims, own_rows, 3 * LANES),
            hold(*dims, own_rows, LANES),
            pltpu.VMEM((1, 3 * width), full),
            pltpu.VMEM((3, rows, LANES), full),
            pltpu.VMEM((LANES, width), full),
            pltpu.SemaphoreType.DMA((3, 2)),
            pltpu.SemaphoreType.DMA((count, others)),
            pltpu.SemaphoreType.DMA((count, others)),
            pltpu.SemaphoreType.DMA((count,)),
            pltpu.SemaphoreType.DMA((count, 5, peers)),
            pltpu.SemaphoreType.DMA((count, 5, peers)),
            pltpu.SemaphoreType.DMA((3, 2, group)),
            pltpu.SemaphoreType.DMA((3, 2, group)),
            pltpu.SemaphoreType.DMA((8,)),
        ],
        compiler_params=pltpu.CompilerParams(
            collective_id=1, has_side_effects=True, vmem_limit_bytes=63 << 20
        ),
    )(*large, *near, *weights, *states)


def update_kernel(layout, width, long, *refs):
    block_in, grad_in = refs[:2]
    far = refs[2:12]
    block_out, input_grad = refs[12:14]
    own_qkv, own_out, own_one, own_two, own_table = refs[14:19]
    new_qkv, new_out, new_one, new_two, new_vectors, second_new = refs[19:25]
    qkv_row, qkv_col, out_row, out_col, one_row, one_col, two_row, two_col = refs[25:33]
    near, passing, sem = refs[33:43], refs[43:45], refs[45]
    loads = [
        pltpu.make_async_copy(source, target, sem.at[at])
        for at, (source, target) in enumerate(zip((*far, block_in, grad_in), (*near, *passing)))
    ]
    long_copies = [
        pltpu.make_async_copy(source, target, sem.at[12 + at])
        for at, (source, target) in enumerate(zip(passing, (block_out, input_grad)))
    ]
    for copy in loads:
        copy.start()
    for copy in loads:
        copy.wait()
    for copy in long_copies:
        copy.start()
    total_ref, col_ref, row_ref, second_ref, sums_ref, vector_ref = near[:6]
    weights = near[6:]
    lane = lax.broadcasted_iota(jnp.int32, (1, LANES), 1)

    def at(index):
        return sums_ref[0:1, index : index + 1]

    lengths = (width, width, width, width, width, long)
    means = [at(6 + m) / lengths[m] for m in range(6)]
    squares = [means[m] * at(m) for m in range(6)]
    squares = [squares[0] + squares[1] + squares[2], *squares[3:]]
    entries = (3 * width * width, width * width, width * long, width * long)
    step_size = []
    for m in range(4):
        damping = 1.0 / jnp.maximum(1.0, jnp.sqrt(squares[m] / entries[m] + 1e-06) / CLIP_LEVEL)
        step_size.append(LEARN_RATE * jnp.sqrt(at(12 + m) / entries[m] + 1e-06) * damping)
    spread = [(m, place, *span) for m, spans in enumerate(layout.matrices()) for place, span in enumerate(spans)]
    for m, place, start, size in spread:
        grad = total_ref[:, pl.ds(start, size)]
        col = col_ref[:, pl.ds(start, size)]
        step = step_size[max(0, m - 2)] * grad * lax.rsqrt(row_ref[:, m : m + 1] * col / means[m])
        if m < 3:
            part = slice(place * LANES, (place + 1) * LANES)
            own_qkv[m, :, part] = grad
            new_qkv[m, :, part] = weights[0][m, :, part] - step
            qkv_col[m : m + 1, part] = col
        else:
            own, new, state = (
                (own_out, new_out, out_row),
                (own_one, new_one, one_col),
                (own_two, new_two, two_row),
            )[m - 3]
            own[...] = grad
            new[...] = weights[m - 2][...] - step
            state[...] = col
    row_flat = row_ref[...].T
    qkv_row[...] = row_flat[0:3]
    out_col[...] = row_flat[3:4]
    one_row[...] = row_flat[4:5]
    two_col[...] = row_flat[5:6]

    wide = (lane >= 7) & (lane < VEC - 1)
    counts = jnp.where(wide, float(long), float(width))

    def grouped(values):
        inside = jnp.sum(jnp.where(wide, values, 0.0), axis=1, keepdims=True)
        return jnp.where(wide, inside, values)

    table_grad = total_ref[:, pl.ds(layout.start["vec"], LANES)]
    update = table_grad * lax.rsqrt(second_ref[...])
    norm = jnp.sqrt(grouped(sums_ref[1:2, :]) / counts + 1e-06)
    size = jnp.sqrt(grouped(sums_ref[2:3, :]) / counts + 1e-06)
    change = LEARN_RATE * size / jnp.maximum(1.0, norm / CLIP_LEVEL) * update
    own_table[...] = table_grad.T[:VEC]
    new_vectors[...] = vector_ref[...] - change.T[:VEC]
    second_new[...] = second_ref[...].T[:VEC]
    for copy in long_copies:
        copy.wait()


def update_weights(layout, width, long, columns, hidden, rows, results, values, vectors, weights):
    full = jnp.float32
    shapes = [
        *(result.shape for result in results),
        (3, rows, columns),
        (rows, columns),
        (rows, hidden),
        (rows, hidden),
        (VEC, rows),
        (3, rows, columns),
        (rows, columns),
        (rows, hidden),
        (rows, hidden),
        (VEC, rows),
        (VEC, rows),
        (3, rows),
        (3, columns),
        (1, columns),
        (1, rows),
        (1, rows),
        (1, hidden),
        (1, hidden),
        (1, rows),
    ]
    far = (*values, vectors, *weights)
    anywhere = pl.BlockSpec(memory_space=pl.ANY)
    inside = pl.BlockSpec(memory_space=pltpu.VMEM)
    return pl.pallas_call(
        functools.partial(update_kernel, layout, width, long),
        name="update_weights",
        out_shape=[jax.ShapeDtypeStruct(shape, full) for shape in shapes],
        in_specs=[anywhere] * (2 + len(far)),
        out_specs=[anywhere] * 2 + [inside] * (len(shapes) - 2),
        scratch_shapes=[
            *(pltpu.VMEM(array.shape, full) for array in (*far, *results)),
            pltpu.SemaphoreType.DMA((4 + len(far),)),
        ],
        compiler_params=pltpu.CompilerParams(vmem_limit_bytes=63 << 20),
    )(*results, *far)


def on_device(
    inputs,
    cotangent,
    token_mask,
    w_qkv,
    w_out,
    w_fc1,
    w_fc2,
    vectors,
    qkv_row,
    qkv_col,
    out_row,
    out_col,
    fc1_row,
    fc1_col,
    fc2_row,
    fc2_col,
    vec_second,
):
    tensor_count = lax.axis_size("tensor")
    dims = grid_of(lax.axis_size("fsdp"))
    width = inputs.shape[1]
    own_rows, columns = w_qkv.shape[1:]
    hidden = w_fc1.shape[1]
    weights = (w_qkv, w_out.T, w_fc1, w_fc2.T)
    (
        weight_qkv,
        _,
        weight_out,
        *_,
        block_out,
        grad_middle,
        back_one,
        mixed_rows,
        low_turned,
        projected,
        grad_one,
        grad_two,
        table,
        vec_sums,
        pre_sums,
        bias_column,
    ) = forward(dims, tensor_count, inputs, cotangent, token_mask, vectors, weights)
    layout = Layout(columns, hidden, ("two", "one", "out", "qkv", "vec"))
    row_states = (qkv_row, out_col[None], fc1_row[None], fc2_col[None])
    col_states = (qkv_col, out_row[None], fc1_col[None], fc2_row[None])
    input_grad, *values = backward(
        dims,
        tensor_count,
        layout,
        (
            grad_two,
            grad_one,
            weight_qkv,
            weight_out,
            projected,
            inputs,
            grad_middle,
            mixed_rows,
            low_turned,
            back_one,
        ),
        (bias_column, table, vec_sums, pre_sums),
        weights,
        (*row_states, *col_states, vec_second, vectors),
    )
    outs = update_weights(
        layout, width, FF, columns, hidden, own_rows, (block_out, input_grad), values, vectors, weights
    )
    outs = [out.reshape(-1) if out.shape[0] == 1 else out for out in outs]
    for at in (3, 5, 8, 10):
        outs[at] = outs[at].T
    return (*outs[:12], *outs[13:], outs[12])


def solution(mesh):
    in_specs = (
        P(("fsdp", "tensor"), None),
        P(("fsdp", "tensor"), None),
        P("fsdp", None),
        P(None, "fsdp", "tensor"),
        P("tensor", "fsdp"),
        P("fsdp", "tensor"),
        P("tensor", "fsdp"),
        P(None, "fsdp"),
        P(None, "fsdp"),
        P(None, "tensor"),
        P("tensor"),
        P("fsdp"),
        P("fsdp"),
        P("tensor"),
        P("tensor"),
        P("fsdp"),
        P(None, "fsdp"),
    )
    out_specs = (
        P(("fsdp", "tensor"), None),
        P(("fsdp", "tensor"), None),
        P(None, "fsdp", "tensor"),
        P("tensor", "fsdp"),
        P("fsdp", "tensor"),
        P("tensor", "fsdp"),
        P(None, "fsdp"),
        P(None, "fsdp", "tensor"),
        P("tensor", "fsdp"),
        P("fsdp", "tensor"),
        P("tensor", "fsdp"),
        P(None, "fsdp"),
        P(None, "fsdp"),
        P(None, "tensor"),
        P("tensor"),
        P("fsdp"),
        P("fsdp"),
        P("tensor"),
        P("tensor"),
        P("fsdp"),
        P(None, "fsdp"),
    )
    return jax.shard_map(
        on_device, mesh=mesh, in_specs=in_specs, out_specs=out_specs, check_vma=False
    )
```

```python
import functools

import jax
import jax.numpy as jnp
from jax import lax
from jax.experimental import pallas as pl
from jax.experimental.pallas import tpu as pltpu
from jax.sharding import PartitionSpec as P

HEAD_DIM = 64
FF = 4096
STEP = 20
VEC = 12
LANES = 128

EPS_NORM = 1e-05
EPS_ONE = 1e-30
CLIP_LEVEL = 1.0
LEARN_RATE = 0.5
MESH = pl.DeviceIdType.MESH
LOG2E = 1.4426950408889634
CONTRACT_LAST = (((1,), (1,)), ((), ()))


def grid_of(count):
    return {16: (4, 2, 2), 32: (2, 4, 4)}.get(count, (count, 1, 1))


class Place:
    def __init__(self, dims, tensor):
        self.dims = dims
        self.tensor = tensor
        fsdp = lax.axis_index("fsdp")
        _, ny, nx = dims
        self.at = (fsdp // (ny * nx), (fsdp // nx) % ny, fsdp % nx)
        self.rank = lax.axis_index("tensor")

    def moved(self, axis, step):
        place = list(self.at) + [self.rank]
        size = (*self.dims, self.tensor)[axis]
        place[axis] = lax.rem(place[axis] + step + size, size)
        return tuple(place)

    def device(self, place):
        z, y, x, rank = place
        return {"fsdp": (z * self.dims[1] + y) * self.dims[2] + x, "tensor": rank}

    def size(self, axis):
        return (*self.dims, self.tensor)[axis]

    def line(self):
        z = self.at[0]
        pair = z // 2 * 2
        middle = (z == 1) | (z == 2)
        return pair, 2 - pair, z + 1 - 2 * (z % 2), middle

    def at_z(self, z):
        return self.device((z, self.at[1], self.at[2], self.rank))

    def peers(self, *axes):
        places = [()]
        for axis in axes:
            places = [(*steps, step) for steps in places for step in range(self.size(axis))]
        found = []
        for steps in places[1:]:
            place = list(self.at) + [self.rank]
            for axis, step in zip(axes, steps):
                place[axis] = lax.rem(place[axis] + step, self.size(axis))
            found.append(self.device(tuple(place)))
        return found

    def barrier(self, groups):
        sem = pltpu.get_barrier_semaphore()
        count = 0
        for axes in groups:
            for device in self.peers(*axes):
                pl.semaphore_signal(sem, inc=1, device_id=device, device_id_type=MESH)
                count += 1
        if count:
            pl.semaphore_wait(sem, count)


def norm_rows(values):
    average = jnp.mean(values, axis=1, keepdims=True)
    center = values - average
    inverse = lax.rsqrt(jnp.mean(center * center, axis=1, keepdims=True) + EPS_NORM)
    return center * inverse, inverse


def dot(left, right, dims=(((1,), (0,)), ((), ()))):
    return lax.dot_general(left, right, dims, preferred_element_type=jnp.float32)


def turn(source, target):
    for start in range(0, source.shape[1], LANES):
        target[pl.ds(start, LANES), :] = source[:, pl.ds(start, LANES)].T


def head_lanes(head):
    lane = lax.broadcasted_iota(jnp.int32, (1, LANES), 1)
    return lane // HEAD_DIM == head


def attend_pair(heads, bias):
    query, keys, values = (heads[:, kind * LANES : (kind + 1) * LANES] for kind in range(3))
    mixed = 0.0
    for head in range(2):
        lanes = head_lanes(head)
        key = jnp.where(lanes, keys, jnp.zeros_like(keys))
        value = jnp.where(lanes, values, jnp.zeros_like(values))
        scores = dot(query, key, CONTRACT_LAST) * (HEAD_DIM ** (-0.5) * LOG2E) + bias
        raised = jnp.exp2(scores - jnp.max(scores, axis=1, keepdims=True))
        summed = jnp.sum(raised, axis=1, keepdims=True)
        attention = (raised * (1.0 / summed)).astype(jnp.bfloat16)
        mixed = mixed + dot(attention, value)
    return mixed.astype(jnp.bfloat16)


def guarded(condition, run):
    if condition is None:
        run()
    else:
        pl.when(condition)(run)


def along_z(count):
    return ("pair", "middle", "back") if count == 4 else ("all",)


class Steps:
    def __init__(self):
        self.steps = {}

    def add(self, name, run, time, rank, after=(), waits=(), starts=()):
        self.steps[name] = (run, time, rank, tuple(after), tuple(waits), tuple(starts))

    def arrange(self):
        now, free, arrival, done, order = 0.0, {}, {}, set(), []
        left = list(self.steps)
        while left:
            best, soonest = None, None
            for name in left:
                _, time, rank, after, waits, _ = self.steps[name]
                if any(other not in done for other in after) or any(wait not in arrival for wait in waits):
                    continue
                ready = max([arrival[wait] for wait in waits], default=0.0)
                if ready <= now:
                    if best is None or rank < self.steps[best][2]:
                        best = name
                elif soonest is None or ready < soonest:
                    soonest = ready
            if best is None:
                now = soonest
                continue
            _, time, _, _, _, starts = self.steps[best]
            now += time
            for transfer, link, length in starts:
                begin = max(now, free.get(link, 0.0))
                free[link] = begin + length
                arrival[transfer] = begin + length + LATENCY
            done.add(best)
            left.remove(best)
            order.append(best)
        return order, now

    def run(self):
        for name in self.arrange()[0]:
            self.steps[name][0]()


class Gather:
    def __init__(self, here, pack_ref, outs, parts, local_sem, send_sem, recv_sem):
        self.here = here
        self.pack = pack_ref
        self.outs = outs
        self.rows = pack_ref.shape[0]
        self.parts = parts
        self.late = [len(parts) - at for at in LATE_PARTS if at < len(parts)]
        self.sems = (local_sem, send_sem, recv_sem)
        self.own = (*here.at, here.rank)
        self.sent = []

    def region(self, item, part, place, free):
        out, _, chunk, _ = self.parts[item]
        index = tuple(slice(None) if a in free else place[a] for a in range(3))
        lead = () if chunk is None else (place[3], chunk)
        return self.outs[out].at[(*lead, *index, part)]

    def shard(self, item, part):
        _, offset, _, size = self.parts[item]
        return self.pack.at[part, pl.ds(offset, size)]

    def phases(self, item):
        lengthwise = along_z(self.here.dims[0]) if self.parts[item][0] in (3, 4) else ("all",)
        across = ("first", "second")
        order = (*across, *lengthwise) if item in self.late else (*lengthwise, *across)
        return order if self.parts[item][2] is None else (*order, "core")

    def moves(self, item, phase):
        here, own = self.here, self.own
        kind = self.phases(item)[phase]
        late = item in self.late
        whole, half = pl.ds(0, self.rows), self.rows // 2
        first, second = pl.ds(0, half), pl.ds(half, half)
        found = []
        if kind in ("pair", "middle", "back"):
            free = (1, 2) if late else ()
            pair, far, near, middle = here.line()

            def blocks(z):
                return self.region(item, whole, (z, *own[1:]), free)

            if kind == "pair":
                sent = self.shard(item, whole) if phase == 0 else blocks(own[0])
                found.append((here.at_z(near), sent, blocks(own[0]), blocks(near), None, None))
            elif kind == "middle":
                pairs = blocks(pl.ds(pair, 2))
                found.append((here.at_z(3 - own[0]), pairs, pairs, blocks(pl.ds(far, 2)), middle, middle))
            else:
                pairs = blocks(pl.ds(far, 2))
                outside = jnp.logical_not(middle)
                found.append((here.at_z(near), pairs, pairs, pairs, middle, outside))
            return found
        before = () if late else (0,)
        steps = {
            "all": ((0, (1, 2) if late else (), whole),),
            "first": ((2, before, first), (1, before, second))
            if late
            else ((1, before, first), (2, before, second)),
            "second": ((1, (*before, 2), first), (2, (*before, 1), second))
            if late
            else ((2, (*before, 1), first), (1, (*before, 2), second)),
            "core": ((3, (0, 1, 2), whole),),
        }[kind]
        for axis, free, part in steps:
            for step in range(1, here.size(axis)):
                place = self.region(item, part, own, free)
                sent = self.shard(item, part) if phase == 0 else place
                landed = self.region(item, part, here.moved(axis, -step), free)
                found.append((here.device(here.moved(axis, step)), sent, place, landed, None, None))
        return found

    def copies(self, item, phase, landing):
        found = []
        for at, (device, sent, place, landed, sends, receives) in enumerate(self.moves(item, phase)):
            copy = pltpu.make_async_remote_copy(
                src_ref=landed if landing else sent,
                dst_ref=landed if landing else place,
                send_sem=self.sems[1].at[item, phase, at],
                recv_sem=self.sems[2].at[item, phase, at],
                device_id=device,
                device_id_type=MESH,
            )
            found.append((receives if landing else sends, copy))
        return found

    def keep(self, item):
        whole = pl.ds(0, self.rows)
        return pltpu.make_async_copy(
            self.shard(item, whole), self.region(item, whole, self.own, ()), self.sems[0].at[item]
        )

    def advance(self, item, phase):
        if phase:
            for condition, copy in self.copies(item, phase - 1, True):
                guarded(condition, copy.wait_recv)
        if phase == 0:
            self.keep(item).start()
        if phase == 1:
            self.keep(item).wait()
        if phase < len(self.phases(item)):
            for condition, copy in self.copies(item, phase, False):
                guarded(condition, copy.start)
                self.sent.append((condition, copy))

    def finish(self):
        for condition, copy in self.sent:
            guarded(condition, copy.wait_send)


BLOCK = 512
DEPTH = 3
LATENCY = 1.5
UNIT = 20.0
CORE_UNIT = 40.0
LATE_PARTS = (6,)
LATE_ITEMS = (0, 1)
PUMP = 0.4


def forward_kernel(dims, tensor, parts, tasks, *refs):
    input_ref, top_ref, mask_ref, vector_ref = refs[:4]
    own_weights = refs[4:8]
    outs, land = refs[8:13], refs[13:15]
    weight_qkv, weight_vec, weight_out, weight_one, weight_two = outs
    far = refs[15:20]
    projected, grad_one, grad_two, table, vec_sums, pre_sums, bias_column = refs[20:27]
    (
        block_out,
        grad_middle,
        back_one,
        mixed,
        low_one,
        low_turned,
        pack,
        keep_ref,
        square,
        vec_buf,
        qkv_buf,
        head_stage,
        out_buf,
        one_buf,
        two_buf,
        low_two,
        low_two_turned,
        back_two,
        back_two_turned,
        grad_low_two,
        hidden_bias,
        head_bias,
        one_stage,
        two_stage,
        one_keep,
        two_keep,
        other,
        active,
        grad_pre,
        load_sem,
        store_sem,
        keep_sem,
        head_sem,
        land_sem,
        far_sem,
        local_sem,
        send_sem,
        recv_sem,
    ) = refs[27:]
    near = (block_out, grad_middle, back_one, mixed, low_turned)

    def far_store(at):
        return pltpu.make_async_copy(near[at], far[at], far_sem.at[at])

    here = Place(dims, tensor)
    gather = Gather(here, pack, outs, parts, local_sem, send_sem, recv_sem)
    rows, width = input_ref.shape
    own_rows = pack.shape[0]
    per_rank = weight_qkv.shape[1]
    low = jnp.bfloat16
    step_rows = LANES

    def fill_pack():
        base = 0
        for pair in range(per_rank):
            for kind in range(3):
                part = own_weights[0][kind, :, pl.ds(pair * LANES, LANES)]
                pack[:, pl.ds(base, LANES)] = part.astype(low)
                base += LANES
        square[...] = jnp.zeros_like(square)
        square[pl.ds(0, VEC), :] = vector_ref[...]
        pack[:, pl.ds(base, LANES)] = square[...].T.astype(low)
        base += LANES
        for ref in own_weights[1:]:
            pack[:, pl.ds(base, ref.shape[1])] = ref[...].astype(low)
            base += ref.shape[1]

    def mask_row():
        return mask_ref[pl.ds(here.rank, 1), :].astype(jnp.float32)

    def mask_bias(keep):
        return jnp.where(keep > 0.0, 0.0, -1e30)

    def first_masks():
        turned = jnp.broadcast_to(mask_row(), (LANES, rows)).T
        keep_ref[...] = turned[:, 0:1]
        bias_column[...] = mask_bias(turned[:, 0:1])

    def row_steps(body, carry):
        return lax.fori_loop(
            0, rows // step_rows, lambda at, c: body(pl.ds(pl.multiple_of(at * step_rows, step_rows), step_rows), c), carry
        )

    def load(source, buffer, sem):
        return pltpu.make_async_copy(source, buffer, sem)

    def first_norm():
        first_masks()
        copy = load(weight_vec, vec_buf, load_sem.at[7])
        copy.start()
        copy.wait()
        whole = vec_buf[...].reshape(width, LANES).astype(jnp.float32).T
        table[...] = whole[:16]
        for at in range(VEC - 8):
            hidden_bias[:, pl.ds(at * width, width)] = whole[7 + at : 8 + at]
        for pair in range(width // LANES):
            for kind, row in ((0, 2), (2, 3)):
                head_bias[:, pl.ds((pair * 3 + kind) * LANES, LANES)] = whole[
                    row : row + 1, pair * LANES : (pair + 1) * LANES
                ]
            head_bias[:, pl.ds((pair * 3 + 1) * LANES, LANES)] = jnp.zeros((1, LANES), jnp.float32)

        def body(part, carry):
            normed, _ = norm_rows(input_ref[part, :])
            low_one[part, :] = (normed * table[0:1, :] + table[1:2, :]).astype(low)
            back_two[part, :] = (top_ref[part, :].astype(jnp.float32) * keep_ref[part, :]).astype(low)
            return carry

        row_steps(body, 0)
        turn(back_two, back_two_turned)

    def head_store(pair, slot):
        column = pl.ds(pl.multiple_of(pair * 3 * LANES, LANES), 3 * LANES)
        return pltpu.make_async_copy(head_stage.at[slot], projected.at[:, column], head_sem.at[slot])

    def turn_first():
        turn(low_one, low_turned)
        far_store(4).start()

    def pair_of(at):
        turn_at, place = divmod(at, tensor)
        return lax.rem(here.rank + place, tensor) * per_rank + turn_at

    def head_load(at):
        turn_at, place = divmod(at, tensor)
        source = weight_qkv.at[lax.rem(here.rank + place, tensor), turn_at]
        return load(source, qkv_buf.at[at % 2], load_sem.at[at % 2])

    def heads(at):
        head_load(at).wait()
        pair = pair_of(at)
        slot = at % 2
        column = pl.ds(pl.multiple_of(pair * 3 * LANES, LANES), 3 * LANES)
        weight = qkv_buf[slot].reshape(width, 3 * LANES)
        value = (dot(low_one[...], weight) + head_bias[:, column]).astype(low)
        if at > 1:
            head_store(pair, slot).wait()
        head_stage[slot] = value
        head_store(pair, slot).start()
        mixed[:, pl.ds(pl.multiple_of(pair * LANES, LANES), LANES)] = attend_pair(value, mask_bias(mask_row()))

    def out_load():
        return [
            load(weight_out.at[rank, 0], out_buf.at[rank], load_sem.at[2]) for rank in range(tensor)
        ]

    def second_norm():
        far_store(3).start()
        for copy in out_load():
            copy.wait()
        columns = width // tensor
        for rank in range(tensor):
            weight = out_buf[rank].reshape(width, columns)
            term = dot(mixed[:, pl.ds(rank * columns, columns)], weight, CONTRACT_LAST)
            if rank == 0:
                grad_middle[...] = term
            else:
                grad_middle[...] += term

        def body(part, carry):
            middle = input_ref[part, :] + (grad_middle[part, :] + table[4:5, :]) * keep_ref[part, :]
            grad_middle[part, :] = middle
            normed, _ = norm_rows(middle)
            low_two[part, :] = (normed * table[5:6, :] + table[6:7, :]).astype(low)
            return carry

        row_steps(body, 0)
        turn(low_two, low_two_turned)

    stages = (one_stage, two_stage)
    keeps = (one_keep, two_keep)

    def hand_over(at):
        chunk, place = divmod(at, tensor)
        target = (*here.at, lax.rem(here.rank + place + 1, tensor))
        return [
            pltpu.make_async_remote_copy(
                src_ref=stages[which].at[at % 2],
                dst_ref=land[which].at[place, chunk],
                send_sem=store_sem.at[which, at % 2],
                recv_sem=land_sem.at[which, place, chunk],
                device_id=here.device(target),
                device_id_type=MESH,
            )
            for which in range(2)
        ]

    def keep_store(chunk):
        return [
            pltpu.make_async_copy(
                keeps[which].at[chunk % 2],
                out.at[chunk],
                keep_sem.at[which, chunk % 2],
            )
            for which, out in enumerate((grad_one, grad_two))
        ]

    def hidden_column(at):
        chunk, place = divmod(at, tensor)
        base = (lax.rem(here.rank + place + 1, tensor) * weight_one.shape[1] + chunk) * BLOCK
        return pl.ds(pl.multiple_of(base, LANES), BLOCK)

    def hidden_load(at):
        chunk, place = divmod(at, tensor)
        rank = lax.rem(here.rank + place + 1, tensor)
        return [
            load(source.at[rank, chunk], buffer.at[at % 2], load_sem.at[3 + 2 * which + at % 2])
            for which, (source, buffer) in enumerate(((weight_one, one_buf), (weight_two, two_buf)))
        ]

    staged = {}

    def hidden(at):
        chunk, place = divmod(at, tensor)
        column = hidden_column(at)
        for copy in hidden_load(at):
            copy.wait()
        half = rows // 2
        bias = hidden_bias[:, column]

        def body(turn_at, total):
            part = pl.ds(pl.multiple_of(turn_at * half, half), half)
            one = one_buf[at % 2].reshape(width, BLOCK)
            two = two_buf[at % 2].reshape(width, BLOCK)
            preact = dot(low_two[part, :], one) + bias
            gate = jax.nn.sigmoid(1.702 * preact)
            value = (preact * gate).astype(low)
            active[part, :] = value
            derivative = gate + 1.702 * preact * gate * (1.0 - gate)
            grad = (dot(back_two[part, :], two) * derivative).astype(low)
            grad_pre[part, :] = grad
            if at == 0:
                block_out[part, :] = dot(value, two, CONTRACT_LAST)
                grad_low_two[part, :] = dot(grad, one, CONTRACT_LAST)
            else:
                block_out[part, :] += dot(value, two, CONTRACT_LAST)
                grad_low_two[part, :] += dot(grad, one, CONTRACT_LAST)
            return total + jnp.sum(grad.astype(jnp.float32), axis=0, keepdims=True)

        pre_sums[:, column] = lax.fori_loop(0, 2, body, jnp.zeros((1, BLOCK), jnp.float32))
        mine = place == tensor - 1
        if mine:
            targets = [ref.at[chunk % 2] for ref in keeps]
            if chunk > 1:
                for copy in keep_store(chunk):
                    copy.wait()
        else:
            targets = [ref.at[at % 2] for ref in stages]
            for copy in staged.pop(at % 2, ()):
                copy.wait_send()
        for target, left, right in (
            (targets[0], low_two_turned, grad_pre),
            (targets[1], back_two_turned, active),
        ):
            target[...] = dot(left[...], right[...]).astype(low).reshape(*target.shape)
        if not mine:
            staged[at % 2] = hand_over(at)
            for copy in staged[at % 2]:
                copy.start()

    def combine(chunk):
        for place in range(tensor - 1):
            for which, copy in enumerate(hand_over(chunk * tensor + place)):
                copy.wait_recv()
                fetch = load(land[which].at[place, chunk], other, load_sem.at[7])
                fetch.start()
                fetch.wait()
                keeps[which][chunk % 2] = keeps[which][chunk % 2] + other[...]
        for copy in keep_store(chunk):
            copy.start()

    def last_norm():
        def body(part, sums):
            middle = grad_middle[part, :]
            keep = keep_ref[part, :]
            top = top_ref[part, :].astype(jnp.float32)
            block_out[part, :] = middle + (block_out[part, :] + table[VEC - 1 : VEC, :]) * keep
            normed, inverse = norm_rows(middle)
            grad_low = grad_low_two[part, :]
            scaled = grad_low * table[5:6, :]
            first = jnp.mean(scaled, axis=1, keepdims=True)
            second = jnp.mean(scaled * normed, axis=1, keepdims=True)
            grad = top + inverse * (scaled - first - normed * second)
            grad_middle[part, :] = grad
            masked = grad * keep
            back_one[part, :] = masked.astype(low)
            terms = (masked, grad_low * normed, grad_low, top * keep)
            return tuple(old + jnp.sum(term, axis=0, keepdims=True) for old, term in zip(sums, terms))

        zero = jnp.zeros((1, width), jnp.float32)
        for at, value in enumerate(row_steps(body, (zero,) * 4)):
            vec_sums[at : at + 1, :] = value
        for at in range(3):
            far_store(at).start()

    fill_pack()
    here.barrier(((0,), (1,), (2,), (3,)))
    steps = Steps()
    whole = sum(part[3] for part in parts)
    nz, ny, nx = dims

    def lengths(item, phase):
        share = parts[item][3] / whole * UNIT
        across = ny * nx if item in gather.late else 1
        along = 1 if item in gather.late else nz
        return {
            "pair": (share * across, "end"),
            "middle": (share * across * 2, "middle"),
            "back": (share * across * 2, "end"),
            "all": (share * across * nz, "end"),
            "first": (share * along / 2, "xy"),
            "second": (share * along, "xy"),
            "core": (share * CORE_UNIT / UNIT, "core"),
        }[gather.phases(item)[phase]]

    for item, part in enumerate(parts):
        phases = len(gather.phases(item))
        for phase in range(phases + 1):
            after = [("copy", item, phase - 1)] if phase else []
            if phase == 0 and item >= DEPTH and item not in gather.late:
                after = [("copy", item - DEPTH, 1)]
            if item in gather.late:
                if phase == 0:
                    after = [("copy", DEPTH, 1)]
                if phase == 2:
                    after += [("copy", other, 1) for other in range(min(len(parts), item + 3)) if other not in gather.late]
            length, link = lengths(item, min(phase, phases - 1))
            steps.add(
                ("copy", item, phase),
                functools.partial(gather.advance, item, phase),
                PUMP,
                0.5 if phase == 0 else 0.0,
                after,
                [(item, phase - 1)] if phase else [],
                [((item, phase), link, length)] if phase < phases else [],
            )

    def landed(items):
        return [("copy", item, len(gather.phases(item))) for item in items]

    def start(copies):
        for copy in copies:
            copy.start()

    previous = None
    head_count, block_count = per_rank * tensor, FF // BLOCK
    for name, at, items in tasks:
        after = landed(items) + ([previous] if previous else [])
        begin, run, time = {
            "norm": (None, first_norm, 4.0),
            "turn": (None, turn_first, 1.5),
            "heads": (lambda at=at: head_load(at).start(), lambda at=at: heads(at), 3.0),
            "out": (lambda: start(out_load()), second_norm, 5.0),
            "hidden": (lambda at=at: start(hidden_load(at)), lambda at=at: hidden(at), 5.5),
        }[name]
        if begin is not None:
            first = landed(items)
            if at > 1:
                first.append((name, at - 2))
            steps.add(("load", name, at), begin, 0.1, 0.2, first)
            after.append(("load", name, at))
        mine = name == "hidden" and at % tensor == tensor - 1
        chunk = at // tensor
        if mine and chunk > 1:
            after.append(("combine", chunk - 2))
        starts = []
        if name == "hidden" and not mine:
            starts = [(("hand", at), "core", CORE_UNIT / len(parts))]
        steps.add((name, at), run, time, 1.0, after, (), starts)
        if mine:
            waits = [("hand", chunk * tensor + place) for place in range(tensor - 1)]
            steps.add(
                ("combine", chunk), functools.partial(combine, chunk), 2.0, 0.8, [(name, at)], waits
            )
        previous = (name, at)
    steps.add(("last", 0), last_norm, 4.0, 0.9, [previous])
    steps.run()
    for at in range(5):
        far_store(at).wait()
    for slot in range(min(2, head_count)):
        head_store(0, slot).wait()
    for chunk in range(min(2, block_count // tensor)):
        for copy in keep_store(chunk):
            copy.wait()
    for copies in staged.values():
        for copy in copies:
            copy.wait_send()
    gather.finish()


def forward(dims, tensor, inputs, cotangent, token_mask, vectors, weights):
    own_rows, columns = weights[0].shape[1:]
    hidden = weights[2].shape[1]
    rows, width = inputs.shape
    low, full = jnp.bfloat16, jnp.float32
    widths = (3 * columns, LANES, columns, hidden, hidden)
    offsets = [sum(widths[:at]) for at in range(5)]
    per_rank = columns // LANES
    parts = [(1, offsets[1], None, LANES)]
    tasks = [("norm", 0, (0,)), ("turn", 0, (0,))]
    for at in range(per_rank):
        size = 3 * LANES
        parts.append((0, offsets[0] + at * size, at, size))
        tasks += [("heads", at * tensor + place, (len(parts) - 1,)) for place in range(tensor)]
    tasks.append(("out", 0, (len(parts),)))
    parts.append((2, offsets[2], 0, columns))
    for block in range(hidden // BLOCK):
        needed = (len(parts), len(parts) + 1)
        parts += [(which, offsets[which] + block * BLOCK, block, BLOCK) for which in (3, 4)]
        tasks += [("hidden", block * tensor + place, needed) for place in range(tensor)]
    count = len(parts)
    peers = max(1, dims[0] - 1, dims[1] + dims[2] - 2, tensor - 1)
    anywhere = pl.BlockSpec(memory_space=pl.ANY)
    inside = pl.BlockSpec(memory_space=pltpu.VMEM)
    block = (*dims, own_rows, BLOCK)
    chunks = hidden // BLOCK

    def shape(kind, *size):
        return jax.ShapeDtypeStruct(size, kind)

    return pl.pallas_call(
        functools.partial(forward_kernel, dims, tensor, tuple(parts), tuple(tasks)),
        name="forward",
        out_shape=[
            shape(low, tensor, per_rank, *dims, own_rows, 3 * LANES),
            shape(low, *dims, own_rows, LANES),
            shape(low, tensor, 1, *dims, own_rows, columns),
            *[shape(low, tensor, chunks, *block)] * 2,
            *[shape(low, max(1, tensor - 1), chunks, *block)] * 2,
            shape(full, rows, width),
            shape(full, rows, width),
            *[shape(low, rows, width)] * 2,
            shape(low, width, rows),
            shape(low, rows, 3 * width),
            *[shape(low, chunks, *block)] * 2,
            shape(full, 16, width),
            shape(full, 8, width),
            shape(full, 1, hidden * tensor),
            shape(full, rows, 1),
        ],
        in_specs=[inside] * 8,
        out_specs=[anywhere] * 15 + [inside] * 4,
        scratch_shapes=[
            pltpu.VMEM((rows, width), full),
            pltpu.VMEM((rows, width), full),
            *[pltpu.VMEM((rows, width), low)] * 3,
            pltpu.VMEM((width, rows), low),
            pltpu.VMEM((own_rows, sum(widths)), low),
            pltpu.VMEM((rows, 1), full),
            pltpu.VMEM((LANES, own_rows), full),
            pltpu.VMEM((*dims, own_rows, LANES), low),
            pltpu.VMEM((2, *dims, own_rows, 3 * LANES), low),
            pltpu.VMEM((2, rows, 3 * LANES), low),
            pltpu.VMEM((tensor, *dims, own_rows, columns), low),
            pltpu.VMEM((2, *block), low),
            pltpu.VMEM((2, *block), low),
            pltpu.VMEM((rows, width), low),
            pltpu.VMEM((width, rows), low),
            pltpu.VMEM((rows, width), low),
            pltpu.VMEM((width, rows), low),
            pltpu.VMEM((rows, width), full),
            pltpu.VMEM((1, hidden * tensor), full),
            pltpu.VMEM((1, 3 * width), full),
            pltpu.VMEM((2, *block), low),
            pltpu.VMEM((2, *block), low),
            pltpu.VMEM((2, *block), low),
            pltpu.VMEM((2, *block), low),
            pltpu.VMEM(block, low),
            pltpu.VMEM((rows, BLOCK), low),
            pltpu.VMEM((rows, BLOCK), low),
            pltpu.SemaphoreType.DMA((8,)),
            pltpu.SemaphoreType.DMA((2, 2)),
            pltpu.SemaphoreType.DMA((2, 2)),
            pltpu.SemaphoreType.DMA((2,)),
            pltpu.SemaphoreType.DMA((2, max(1, tensor - 1), chunks)),
            pltpu.SemaphoreType.DMA((5,)),
            pltpu.SemaphoreType.DMA((count,)),
            pltpu.SemaphoreType.DMA((count, 6, peers)),
            pltpu.SemaphoreType.DMA((count, 6, peers)),
        ],
        compiler_params=pltpu.CompilerParams(
            collective_id=0, has_side_effects=True, vmem_limit_bytes=62 << 20
        ),
    )(inputs, cotangent, token_mask, vectors, *weights)


class Layout:
    def __init__(self, columns, hidden, order):
        sizes = {"qkv": 3 * columns, "out": columns, "one": hidden, "two": hidden, "vec": LANES}
        self.order = order
        self.sizes = sizes
        self.start = {}
        at = 0
        for name in order:
            self.start[name] = at
            at += sizes[name]
        self.total = at
        self.columns = columns

    def span(self, name):
        return (self.start[name], self.sizes[name])

    def matrices(self):
        base = self.start["qkv"]
        pairs = range(self.columns // LANES)
        spans = [[(base + (pair * 3 + at) * LANES, LANES) for pair in pairs] for at in range(3)]
        return spans + [[self.span(name)] for name in ("out", "one", "two")]


def pick(values, lane):
    row = jnp.zeros((1, LANES), jnp.float32)
    for at, value in enumerate(values):
        row = jnp.where(lane == at, value, row)
    return row


def total_of(values):
    return jnp.sum(jnp.sum(values, axis=1, keepdims=True), axis=0, keepdims=True)


def attend_pair_back(heads, bias, grad):
    query, keys, values = (heads[:, kind * LANES : (kind + 1) * LANES] for kind in range(3))
    found = []
    for head in range(2):
        lanes = head_lanes(head)
        key = jnp.where(lanes, keys, jnp.zeros_like(keys))
        value = jnp.where(lanes, values, jnp.zeros_like(values))
        scores = dot(key, query, CONTRACT_LAST) * (HEAD_DIM ** (-0.5) * LOG2E) + bias
        raised = jnp.exp2(scores - jnp.max(scores, axis=0, keepdims=True))
        attention = raised * (1.0 / jnp.sum(raised, axis=0, keepdims=True))
        grad_value = dot(attention.astype(jnp.bfloat16), grad).astype(jnp.bfloat16)
        grad_attention = dot(value, grad, CONTRACT_LAST)
        weighted = jnp.sum(attention * grad_attention, axis=0, keepdims=True)
        grad_scores = (attention * (grad_attention - weighted) * HEAD_DIM ** (-0.5)).astype(jnp.bfloat16)
        grad_key = dot(grad_scores, query).astype(jnp.bfloat16)
        grad_query = dot(key.T, grad_scores).T.astype(jnp.bfloat16)
        found.append((grad_query, grad_key, grad_value))
    first = head_lanes(0)
    return jnp.concatenate([jnp.where(first, left, right) for left, right in zip(*found)], axis=1)


def backward_kernel(dims, tensor, items, layout, *refs):
    (
        sum_two,
        sum_one,
        weight_qkv,
        weight_out,
        projected,
        input_ref,
        middle_ref,
        *far,
        bias_ref,
        table,
        vec_sums,
        pre_sums,
    ) = refs[:14]
    far = (*far, *refs[14:18])
    row_states, col_states = refs[18:22], refs[22:26]
    second_ref, vector_ref = refs[26:28]
    input_grad_out, total_ref, col_new_ref, row_new_ref, second_new_ref, sums_ref = refs[28:34]
    groups = ("ffn", "out", "qkv", "vec")
    kinds = ("own", "one_x", "one_y", "two_y", "two_x", "from_z")
    held = {}
    for kind in kinds:
        for group in groups:
            held[kind, group] = refs[34 + len(held)]
    for group in groups[1:]:
        held["core", group] = refs[34 + len(held)]
    (
        input_grad,
        late_z,
        late_one_y,
        late_one_x,
        late_two_x,
        late_two_y,
        col_sum,
        col_in,
        row_sum,
        row_in,
        small,
        small_in,
        square,
        turned,
        mixed,
        back_one,
        *weights,
        low_turned,
        back_turned,
        grad_mixed,
        out_buf,
        qkv_buf,
        head_buf,
        row_buf,
        out_stage,
        qkv_stage,
        vec_stage,
        head_sums,
        table_grad_ref,
        load_sem,
        stage_sem,
        core_sem,
        local_sem,
        send_sem,
        recv_sem,
        sum_send,
        sum_recv,
        far_sem,
    ) = refs[34 + len(held) :]
    near = (mixed, low_turned, back_one, *weights)

    def far_load(at):
        return pltpu.make_async_copy(far[at], near[at], far_sem.at[at])

    here = Place(dims, tensor)
    nz, ny, nx = dims
    low = jnp.bfloat16
    own_rows = total_ref.shape[0]
    half_rows = own_rows // 2
    rows, width = input_grad.shape
    own_place = (*here.at, here.rank)
    count = len(items)

    def columns(item):
        _, start, size, _ = items[item]
        return pl.ds(start, size)

    def at_home(kind, item):
        name = items[item][0]
        group = "ffn" if name in ("one", "two") else name
        members = [at for at, other in enumerate(items) if (other[0] in ("one", "two")) == (group == "ffn")]
        members = [at for at in members if group == "ffn" or items[at][0] == group]
        return held[kind, group].at[members.index(item)]

    def phases(item):
        lengthwise = along_z(nz)[::-1]
        across = ("first", "second")
        return (*lengthwise, *across) if item in late else (*across, *lengthwise)

    def moves(item, phase):
        first, second, whole = pl.ds(0, half_rows), pl.ds(half_rows, half_rows), pl.ds(0, own_rows)
        kind = phases(item)[phase]
        own = at_home("own", item)
        found = []
        if kind in ("pair", "middle", "back"):
            pair, far, near, middle = here.line()
            outside = jnp.logical_not(middle)
            rest = (slice(None), slice(None)) if item in late else here.at[1:]
            buffer = late_z.at[late.index(item)] if item in late else at_home("from_z", item)
            z = here.at[0]
            device, sent_z, add_z, slots, sends, receives = {
                "back": (near, pl.ds(far, 2), pl.ds(far, 2), pl.ds(0, 2), outside, middle),
                "middle": (3 - z, pl.ds(far, 2), pl.ds(pair, 2), pl.ds(2, 2), middle, middle),
                "pair": (near, near, z, 4, None, None),
            }[kind]
            source = own.at[(sent_z, *rest, whole)]
            found.append((here.at_z(device), source, buffer.at[slots], (add_z, *rest), whole, sends, receives))
            return found
        if item in late:
            at = late.index(item)
            steps = {
                "all": ((0, (0,), whole, late_z.at[at]),),
                "first": ((1, (0, 1), first, late_one_y.at[at]), (2, (0, 2), second, late_one_x.at[at])),
                "second": ((2, (0, 1, 2), first, late_two_x.at[at]), (1, (0, 1, 2), second, late_two_y.at[at])),
            }[kind]
        else:
            steps = {
                "first": ((2, (2,), first, "one_x"), (1, (1,), second, "one_y")),
                "second": ((1, (1, 2), first, "two_y"), (2, (1, 2), second, "two_x")),
                "all": ((0, (0, 1, 2), whole, "from_z"),),
            }[kind]
            steps = [(*step[:3], at_home(step[3], item)) for step in steps]
        for axis, fixed, part, landing in steps:
            for step in range(1, here.size(axis)):
                target = here.moved(axis, step)
                index = tuple(target[a] if a in fixed else slice(None) for a in range(3))
                added = tuple(here.at[a] if a in fixed else slice(None) for a in range(3))
                source = own.at[(*index, part)]
                found.append((here.device(target), source, landing.at[step - 1], added, part, None, None))
        return found

    def copies(item, phase):
        found = []
        for at, (device, source, landing, added, part, sends, receives) in enumerate(moves(item, phase)):
            copy = pltpu.make_async_remote_copy(
                src_ref=source,
                dst_ref=landing,
                send_sem=send_sem.at[item, phase, at],
                recv_sem=recv_sem.at[item, phase, at],
                device_id=device,
                device_id_type=MESH,
            )
            found.append((sends, receives, copy, added, part, landing))
        return found

    def add_core(item):
        own, brought = at_home("own", item), at_home("core", item)

        def body(at, carry):
            z, y, x = at // (ny * nx), at // nx % ny, at % nx
            value = own[z, y, x]
            for step in range(tensor - 1):
                value = value + brought[step, z, y, x]
            own[z, y, x] = value
            return carry

        if tensor > 1:
            lax.fori_loop(0, nz * ny * nx, body, 0)

    def add_in(item, landing, added, part):
        own = at_home("own", item)
        sizes, starts = [], []
        for axis, at in enumerate(added):
            if isinstance(at, slice):
                sizes.append(dims[axis])
                starts.append(0)
            elif hasattr(at, "start"):
                sizes.append(at.size)
                starts.append(at.start)
            else:
                sizes.append(None)
                starts.append(at)
        loops = 1
        for size in sizes:
            loops *= size or 1

        def body(at, carry):
            place, inner, rest = [], [], at
            for size, start in reversed(list(zip(sizes, starts))):
                if size is None:
                    place.insert(0, start)
                else:
                    place.insert(0, start + rest % size)
                    inner.insert(0, rest % size)
                    rest = rest // size
            where = (*place, part)
            own[where] = own[where] + (landing[tuple(inner)] if inner else landing[...])
            return carry

        if loops == 1:
            body(0, 0)
        else:
            lax.fori_loop(0, loops, body, 0)

    def put_total(item, arrived):
        wide = columns(item)
        parts_of = {}
        for landing, part in arrived:
            parts_of.setdefault((part.start, part.size), []).append(landing)
        for (start, size), landings in parts_of.items():
            part = pl.ds(start, size)
            value = at_home("own", item)[(*here.at, part)].astype(jnp.float32)
            for landing in landings:
                value = value + landing[...].astype(jnp.float32)
            total_ref[part, wide] = value
        if items[item][0] == "vec":
            return
        for at, spans in enumerate(layout.matrices()):
            for start, size in spans:
                low_end, high_end = max(start, wide.start), min(start + size, wide.start + wide.size)
                if low_end < high_end:
                    square = total_ref[:, pl.ds(low_end, high_end - low_end)]
                    square = square * square
                    col_sum[0, :, pl.ds(low_end, high_end - low_end)] = jnp.sum(square, axis=0, keepdims=True)
                    found = jnp.sum(square, axis=1, keepdims=True)
                    row_sum[0] = row_sum[0] + jnp.where(lane == at, found, 0.0)

    sent = []
    lane = lax.broadcasted_iota(jnp.int32, (1, LANES), 1)
    row_sum[0] = jnp.zeros_like(row_sum[0])
    guarded_sent = []
    late = [at for at in LATE_ITEMS if items[at][0] in ("one", "two")]

    def exchange(kind, phase, axes, buffer, landing):
        moved = []
        for at, device in enumerate(here.peers(*axes)):
            copy = pltpu.make_async_remote_copy(
                src_ref=buffer.at[phase],
                dst_ref=landing.at[phase, at],
                send_sem=sum_send.at[kind, phase, at],
                recv_sem=sum_recv.at[kind, phase, at],
                device_id=device,
                device_id_type=MESH,
            )
            copy.start()
            moved.append(copy)
        sent.extend(moved)

        def finish():
            value = buffer[phase]
            for at, copy in enumerate(moved):
                copy.wait_recv()
                value = value + landing[phase, at]
            buffer[phase + 1] = value

        return finish

    def hand_over(item, step, source, sem):
        return pltpu.make_async_remote_copy(
            src_ref=source,
            dst_ref=at_home("core", item).at[step - 1],
            send_sem=sem,
            recv_sem=core_sem.at[item, step - 1],
            device_id=here.device(here.moved(3, step)),
            device_id_type=MESH,
        )

    arriving = {}

    def keep_own(item, value):
        at_home("own", item)[...] = value.reshape(nz, ny, nx, own_rows, value.shape[1])

    out_items = [at for at, item in enumerate(items) if item[0] == "out"]
    qkv_items = [at for at, item in enumerate(items) if item[0] == "qkv"]
    vec_item = count - 1
    per_rank = len(qkv_items)
    steps_in_all = per_rank * tensor

    def rank_at(step):
        return lax.rem(here.rank + step, tensor)

    def pair_loads(at):
        turn_at, place = divmod(at, tensor)
        pair = rank_at(place + 1) * per_rank + turn_at
        column = pl.ds(pl.multiple_of(pair * 3 * LANES, LANES), 3 * LANES)
        near = at % 2
        return pair, column, [
            pltpu.make_async_copy(
                weight_qkv.at[rank_at(place + 1), turn_at], qkv_buf.at[near], load_sem.at[0, near]
            ),
            pltpu.make_async_copy(projected.at[:, column], head_buf.at[near], load_sem.at[1, near]),
        ]

    def out_task():
        fetch = [
            pltpu.make_async_copy(weight_out.at[rank, 0], out_buf.at[rank], load_sem.at[2, 0])
            for rank in range(tensor)
        ]
        for copy in fetch:
            copy.start()
        far_load(2).wait()
        turn(back_one, back_turned)
        far_load(0).wait()
        for copy in pair_loads(0)[2]:
            copy.start()
        size = out_stage.shape[5]
        item = out_items[0]
        for step in range(1, tensor + 1):
            column = pl.ds(pl.multiple_of(rank_at(step) * size, LANES), size)
            value = dot(back_turned[...], mixed[:, column]).astype(low)
            if step < tensor:
                out_stage[step - 1] = value.reshape(nz, ny, nx, own_rows, size)
                copy = hand_over(item, step, out_stage.at[step - 1], stage_sem.at[item, step - 1])
                copy.start()
                sent.append(copy)
                arriving.setdefault(item, []).append(copy)
            else:
                keep_own(item, value)
        for copy in fetch:
            copy.wait()
        for rank in range(tensor):
            weight = out_buf[rank].reshape(width, size)
            grad_mixed[:, pl.ds(rank * size, size)] = dot(back_one[...], weight).astype(low)
        far_load(1).wait()

    def state_task():
        def fill(refs, other):
            square[...] = jnp.full_like(square, other)
            base = 0
            for ref in refs:
                square[pl.ds(base, ref.shape[0]), :] = ref[...]
                base += ref.shape[0]
            return square[...].T

        for at in range(3, 7):
            far_load(at).wait()
        turned[0] = fill(row_states, 1.0)
        turned[1] = fill((second_ref,), 1.0)
        turned[2] = fill((vector_ref,), 0.0)

    staged = {}

    def pair_task(at):
        turn_at, place = divmod(at, tensor)
        pair, column, loads = pair_loads(at)
        for copy in loads:
            copy.wait()
        if at + 1 < steps_in_all:
            for copy in pair_loads(at + 1)[2]:
                copy.start()
        near = at % 2
        grads = grad_mixed[:, pl.ds(pl.multiple_of(pair * LANES, LANES), LANES)]
        value = attend_pair_back(head_buf[near], bias_ref[...], grads)
        head_sums[:, column] = jnp.sum(value.astype(jnp.float32), axis=0, keepdims=True)
        weight = qkv_buf[near].reshape(width, 3 * LANES)
        term = dot(value, weight, CONTRACT_LAST)
        if at == 0:
            input_grad[...] = term
        else:
            input_grad[...] += term
        item = qkv_items[turn_at]
        mine = place + 1 == tensor
        if not mine and 0 in staged:
            staged[0].wait_send()
        grad = dot(low_turned[...], value).astype(low)
        if mine:
            keep_own(item, grad)
        else:
            qkv_stage[...] = grad.reshape(nz, ny, nx, own_rows, 3 * LANES)
        if not mine:
            copy = hand_over(item, place + 1, qkv_stage, stage_sem.at[item, place])
            copy.start()
            staged[0] = copy
            arriving.setdefault(item, []).append(copy)

    def grad_store():
        return pltpu.make_async_copy(input_grad, input_grad_out, far_sem.at[7])

    def last_task():
        step_rows = row_buf.shape[2]

        def fetch(at):
            near = lax.rem(at, 2)
            part = pl.ds(pl.multiple_of(at * step_rows, step_rows), step_rows)
            return [
                pltpu.make_async_copy(source.at[part, :], row_buf.at[which, near], load_sem.at[which, near])
                for which, source in enumerate((input_ref, middle_ref))
            ]

        for copy in fetch(0):
            copy.start()

        def body(at, sums):
            for copy in fetch(at):
                copy.wait()

            @pl.when(at + 1 < rows // step_rows)
            def _():
                for copy in fetch(at + 1):
                    copy.start()

            near = lax.rem(at, 2)
            part = pl.ds(pl.multiple_of(at * step_rows, step_rows), step_rows)
            normed, inverse = norm_rows(row_buf[0, near])
            grad_low = input_grad[part, :]
            scaled = grad_low * table[0:1, :]
            first = jnp.mean(scaled, axis=1, keepdims=True)
            second = jnp.mean(scaled * normed, axis=1, keepdims=True)
            input_grad[part, :] = row_buf[1, near] + inverse * (scaled - first - normed * second)
            terms = (grad_low * normed, grad_low)
            return tuple(old + jnp.sum(term, axis=0, keepdims=True) for old, term in zip(sums, terms))

        zero = jnp.zeros((1, width), jnp.float32)
        found = lax.fori_loop(0, rows // step_rows, body, (zero, zero))
        grad_store().start()
        table_grad_ref[...] = jnp.zeros_like(table_grad_ref)
        for at in range(2):
            table_grad_ref[at : at + 1, :] = found[at]
        for pair in range(width // LANES):
            for kind, row in ((0, 2), (2, 3)):
                table_grad_ref[row : row + 1, pl.ds(pair * LANES, LANES)] = head_sums[
                    :, pl.ds((pair * 3 + kind) * LANES, LANES)
                ]
        for at, row in enumerate((4, 5, 6, VEC - 1)):
            table_grad_ref[row : row + 1, :] = vec_sums[at : at + 1, :]
        for at in range(VEC - 8):
            table_grad_ref[7 + at : 8 + at, :] = pre_sums[:, pl.ds(at * width, width)]
        value = table_grad_ref[...].T.astype(low)
        vec_stage[...] = value.reshape(nz, ny, nx, own_rows, LANES)
        for step in range(1, tensor):
            copy = hand_over(vec_item, step, vec_stage, stage_sem.at[vec_item, step - 1])
            copy.start()
            sent.append(copy)
            arriving.setdefault(vec_item, []).append(copy)
        keep_own(vec_item, value)

    for at in (2, 0, 1, 3, 4, 5, 6):
        far_load(at).start()
    here.barrier(((0, 3), (1, 2)))
    local = {}
    for item, (name, _, _, source) in enumerate(items):
        if name in ("one", "two"):
            array = sum_one if name == "one" else sum_two
            copy = pltpu.make_async_copy(
                array.at[source], at_home("own", item), local_sem.at[item]
            )
            copy.start()
            local[item] = copy

    def advance(item, phase):
        last = len(phases(item))
        if phase > 0:
            arrived = []
            for _, receives, copy, added, part, landing in copies(item, phase - 1):

                def take(copy=copy, landing=landing, added=added, part=part):
                    copy.wait_recv()
                    if phase < last:
                        add_in(item, landing, added, part)

                guarded(receives, take)
                arrived.append((landing, part))
            if phase == last:
                put_total(item, arrived)
        elif item in local:
            local[item].wait()
        else:
            for copy in arriving.get(item, ()):
                copy.wait_recv()
            add_core(item)
        if phase < last:
            for sends, _, copy, *_ in copies(item, phase):
                guarded(sends, copy.start)
                guarded_sent.append((sends, copy))

    steps = Steps()
    owner = {item: ("out", 0) for item in out_items}
    owner |= {item: ("pair", tensor * (at + 1) - 1) for at, item in enumerate(qkv_items)}
    owner[vec_item] = ("last", 0)
    for item, (name, _, size, _) in enumerate(items):
        share = size / layout.total * UNIT
        across = ny * nx if item in late else 1
        along = 1 if item in late else nz
        lengths = {
            "pair": (share * across, "end"),
            "middle": (share * across * 2, "middle"),
            "back": (share * across * 2, "end"),
            "all": (share * across * nz, "end"),
            "first": (share * along, "xy"),
            "second": (share * along / 2, "xy"),
        }
        if item in late:
            lengths |= {"first": (share, "xy"), "second": (share / 2, "xy")}
        early = item not in owner
        kinds = phases(item)
        for phase in range(len(kinds) + 1):
            after = [("copy", item, phase - 1)] if phase else []
            waits = [(item, phase - 1)] if phase else []
            if phase == 0 and early and item >= DEPTH + len(late):
                after = [("copy", item - DEPTH, 1)]
            if phase == 0 and not early:
                after, waits = [owner[item]], [("core", owner[item])]
            starts = []
            if phase < len(kinds):
                length, link = lengths[kinds[phase]]
                starts = [((item, phase), link, length)]
            steps.add(
                ("copy", item, phase),
                functools.partial(advance, item, phase),
                PUMP * (1.5 if phase == 1 else 1.0),
                (0.5 if phase == 0 and early else 0.0),
                after,
                waits,
                starts,
            )
    steps.add(("state", 0), state_task, 1.0, 2.0)
    steps.add(("out", 0), out_task, 8.0, 1.0, (), (), [(("core", ("out", 0)), "core", CORE_UNIT / 12)])
    for at in range(steps_in_all):
        after = [("pair", at - 1) if at else ("out", 0)]
        starts = [(("core", ("pair", at)), "core", CORE_UNIT / 24)]
        steps.add(("pair", at), functools.partial(pair_task, at), 6.0, 1.0, after, (), starts)
    steps.add(
        ("last", 0), last_task, 4.0, 1.0, [("pair", steps_in_all - 1)], (), [(("core", ("last", 0)), "core", 1.0)]
    )
    steps.run()
    sent.extend(staged.values())

    decay_rate = 1.0 - STEP ** (-0.8)
    keep_old = 1.0 - decay_rate
    long = layout.sizes["one"] * tensor
    matrices = layout.matrices()
    finish_row = exchange(0, 0, (3,), row_sum, row_in)
    finish_col = exchange(1, 0, (0,), col_sum, col_in)
    vec_start = layout.start["vec"]
    table_grad = total_ref[:, pl.ds(vec_start, LANES)]
    second_new = decay_rate * turned[1] + keep_old * (table_grad * table_grad + EPS_ONE)
    second_new_ref[...] = second_new
    vector_update = table_grad * lax.rsqrt(second_new)
    vector_sums = jnp.sum(vector_update * vector_update, axis=0, keepdims=True) / tensor
    vector_weight = jnp.sum(turned[2] * turned[2], axis=0, keepdims=True) / tensor
    weight_sums = [total_of(jnp.sum(weights[0][...] * weights[0][...], axis=0))]
    weight_sums += [total_of(ref[...] * ref[...]) for ref in weights[1:]]
    finish_row()
    row_counts = pick([jnp.full((1, 1), 1.0 / size, jnp.float32) for size in (width, width, width, width, long, long)], lane)
    row_new = decay_rate * turned[0] + keep_old * (row_sum[1] * row_counts + EPS_ONE)
    row_new_ref[...] = row_new
    finish_col()
    exchange(1, 1, (1, 2), col_sum, col_in)()
    for at, spans in enumerate(matrices):
        for place, (start, size) in enumerate(spans):
            if at < 3:
                old = col_states[0][at : at + 1, pl.ds(place * LANES, LANES)]
            else:
                old = col_states[at - 2][...]
            fresh = keep_old * (col_sum[2, :, pl.ds(start, size)] / width + EPS_ONE)
            col_new_ref[:, pl.ds(start, size)] = decay_rate * old + fresh
    ratios = []
    means = []
    for at, spans in enumerate(matrices):
        row_at = row_new[:, at : at + 1]
        ratio = 0.0
        for start, size in spans:
            value = total_ref[:, pl.ds(start, size)]
            col_at = col_new_ref[:, pl.ds(start, size)]
            ratio = ratio + total_of(value * value / (row_at * col_at))
        ratios.append(ratio)
        if at in (3, 5):
            means.append(jnp.sum(col_at, axis=1, keepdims=True) / (nz * ny * nx))
        else:
            means.append(jnp.sum(row_at, axis=0, keepdims=True) / tensor)
    small[0] = jnp.concatenate(
        [pick(ratios + means + weight_sums, lane), vector_sums, vector_weight, jnp.zeros((5, LANES), jnp.float32)], axis=0
    )
    exchange(2, 0, (0, 3), small, small_in)()
    exchange(2, 1, (1, 2), small, small_in)()
    sums_ref[...] = small[2]
    grad_store().wait()
    for copy in sent:
        copy.wait_send()
    for condition, copy in guarded_sent:
        guarded(condition, copy.wait_send)


def backward(dims, tensor, layout, large, near, weights, states):
    rows, width = large[-1].shape
    own_rows = width // (dims[0] * dims[1] * dims[2])
    half_rows = own_rows // 2
    columns = layout.columns
    items = []
    for block in range(layout.sizes["one"] // BLOCK):
        for name in ("two", "one"):
            items.append((name, layout.start[name] + block * BLOCK, BLOCK, block))
    items.append(("out", layout.start["out"], columns, 0))
    for start in range(0, 3 * columns, 3 * LANES):
        items.append(("qkv", layout.start["qkv"] + start, 3 * LANES, start))
    items.append(("vec", layout.start["vec"], LANES, 0))
    nz, ny, nx = dims
    peers = max(1, nz - 1, ny + nx - 2)
    group = max(1, nz * tensor - 1, ny * nx - 1)
    others = max(1, tensor - 1)
    offset = layout.total
    late = max(1, len(LATE_ITEMS))
    line = 5 if nz == 4 else nz - 1
    groups = (
        (2 * layout.sizes["one"] // BLOCK, BLOCK),
        (1, columns),
        (columns // LANES, 3 * LANES),
        (1, LANES),
    )
    leads = (
        (nz, ny, nx, own_rows),
        (nx - 1, nz, ny, half_rows),
        (ny - 1, nz, nx, half_rows),
        (ny - 1, nz, half_rows),
        (nx - 1, nz, half_rows),
        (line, own_rows),
    )
    low, full = jnp.bfloat16, jnp.float32
    anywhere = pl.BlockSpec(memory_space=pl.ANY)
    inside = pl.BlockSpec(memory_space=pltpu.VMEM)

    def hold(*shape):
        return pltpu.VMEM(tuple(max(1, size) for size in shape), low)

    sums = offset - LANES
    count = len(items)
    return pl.pallas_call(
        functools.partial(backward_kernel, dims, tensor, tuple(items), layout),
        name="backward",
        out_shape=[
            jax.ShapeDtypeStruct((rows, width), full),
            jax.ShapeDtypeStruct((own_rows, offset), full),
            jax.ShapeDtypeStruct((1, sums), full),
            jax.ShapeDtypeStruct((own_rows, LANES), full),
            jax.ShapeDtypeStruct((own_rows, LANES), full),
            jax.ShapeDtypeStruct((8, LANES), full),
        ],
        in_specs=[anywhere] * len(large) + [inside] * len(near) + [anywhere] * 4 + [inside] * len(states),
        out_specs=[anywhere] + [inside] * 5,
        scratch_shapes=[
            *(hold(number, *lead, size) for lead in leads for number, size in groups),
            *(hold(number, others, nz, ny, nx, own_rows, size) for number, size in groups[1:]),
            pltpu.VMEM((rows, width), full),
            hold(late, line, ny, nx, own_rows, BLOCK),
            hold(late, ny - 1, nx, half_rows, BLOCK),
            hold(late, nx - 1, ny, half_rows, BLOCK),
            hold(late, nx - 1, half_rows, BLOCK),
            hold(late, ny - 1, half_rows, BLOCK),
            pltpu.VMEM((3, 1, sums), full),
            pltpu.VMEM((2, max(1, nz - 1, ny * nx - 1), 1, sums), full),
            pltpu.VMEM((2, own_rows, LANES), full),
            pltpu.VMEM((1, others, own_rows, LANES), full),
            pltpu.VMEM((3, 8, LANES), full),
            pltpu.VMEM((2, group, 8, LANES), full),
            pltpu.VMEM((LANES, own_rows), full),
            pltpu.VMEM((3, own_rows, LANES), full),
            *[hold(rows, width)] * 2,
            *(pltpu.VMEM(weight.shape, full) for weight in weights),
            hold(width, rows),
            hold(width, rows),
            hold(rows, width),
            hold(tensor, *dims, own_rows, columns),
            hold(2, *dims, own_rows, 3 * LANES),
            hold(2, rows, 3 * LANES),
            pltpu.VMEM((2, 2, LANES // 2, width), full),
            hold(others, *dims, own_rows, columns),
            hold(*dims, own_rows, 3 * LANES),
            hold(*dims, own_rows, LANES),
            pltpu.VMEM((1, 3 * width), full),
            pltpu.VMEM((LANES, width), full),
            pltpu.SemaphoreType.DMA((3, 2)),
            pltpu.SemaphoreType.DMA((count, others)),
            pltpu.SemaphoreType.DMA((count, others)),
            pltpu.SemaphoreType.DMA((count,)),
            pltpu.SemaphoreType.DMA((count, 5, peers)),
            pltpu.SemaphoreType.DMA((count, 5, peers)),
            pltpu.SemaphoreType.DMA((3, 2, group)),
            pltpu.SemaphoreType.DMA((3, 2, group)),
            pltpu.SemaphoreType.DMA((8,)),
        ],
        compiler_params=pltpu.CompilerParams(
            collective_id=1, has_side_effects=True, vmem_limit_bytes=63 << 20
        ),
    )(*large, *near, *weights, *states)


def update_kernel(layout, width, long, *refs):
    block_in, grad_in = refs[:2]
    far = refs[2:12]
    block_out, input_grad = refs[12:14]
    own_qkv, own_out, own_one, own_two, own_table = refs[14:19]
    new_qkv, new_out, new_one, new_two, new_vectors, second_new = refs[19:25]
    qkv_row, qkv_col, out_row, out_col, one_row, one_col, two_row, two_col = refs[25:33]
    near, passing, sem = refs[33:43], refs[43:45], refs[45]
    loads = [
        pltpu.make_async_copy(source, target, sem.at[at])
        for at, (source, target) in enumerate(zip((*far, block_in, grad_in), (*near, *passing)))
    ]
    long_copies = [
        pltpu.make_async_copy(source, target, sem.at[12 + at])
        for at, (source, target) in enumerate(zip(passing, (block_out, input_grad)))
    ]
    for copy in loads:
        copy.start()
    for copy in loads:
        copy.wait()
    for copy in long_copies:
        copy.start()
    total_ref, col_ref, row_ref, second_ref, sums_ref, vector_ref = near[:6]
    weights = near[6:]
    lane = lax.broadcasted_iota(jnp.int32, (1, LANES), 1)

    def at(index):
        return sums_ref[0:1, index : index + 1]

    lengths = (width, width, width, width, width, long)
    means = [at(6 + m) / lengths[m] for m in range(6)]
    squares = [means[m] * at(m) for m in range(6)]
    squares = [squares[0] + squares[1] + squares[2], *squares[3:]]
    entries = (3 * width * width, width * width, width * long, width * long)
    step_size = []
    for m in range(4):
        damping = 1.0 / jnp.maximum(1.0, jnp.sqrt(squares[m] / entries[m] + 1e-06) / CLIP_LEVEL)
        step_size.append(LEARN_RATE * jnp.sqrt(at(12 + m) / entries[m] + 1e-06) * damping)
    spread = [(m, place, *span) for m, spans in enumerate(layout.matrices()) for place, span in enumerate(spans)]
    for m, place, start, size in spread:
        grad = total_ref[:, pl.ds(start, size)]
        col = col_ref[:, pl.ds(start, size)]
        step = step_size[max(0, m - 2)] * grad * lax.rsqrt(row_ref[:, m : m + 1] * col / means[m])
        if m < 3:
            part = slice(place * LANES, (place + 1) * LANES)
            own_qkv[m, :, part] = grad
            new_qkv[m, :, part] = weights[0][m, :, part] - step
            qkv_col[m : m + 1, part] = col
        else:
            own, new, state = (
                (own_out, new_out, out_row),
                (own_one, new_one, one_col),
                (own_two, new_two, two_row),
            )[m - 3]
            own[...] = grad
            new[...] = weights[m - 2][...] - step
            state[...] = col
    row_flat = row_ref[...].T
    qkv_row[...] = row_flat[0:3]
    out_col[...] = row_flat[3:4]
    one_row[...] = row_flat[4:5]
    two_col[...] = row_flat[5:6]

    wide = (lane >= 7) & (lane < VEC - 1)
    counts = jnp.where(wide, float(long), float(width))

    def grouped(values):
        inside = jnp.sum(jnp.where(wide, values, 0.0), axis=1, keepdims=True)
        return jnp.where(wide, inside, values)

    table_grad = total_ref[:, pl.ds(layout.start["vec"], LANES)]
    update = table_grad * lax.rsqrt(second_ref[...])
    norm = jnp.sqrt(grouped(sums_ref[1:2, :]) / counts + 1e-06)
    size = jnp.sqrt(grouped(sums_ref[2:3, :]) / counts + 1e-06)
    change = LEARN_RATE * size / jnp.maximum(1.0, norm / CLIP_LEVEL) * update
    own_table[...] = table_grad.T[:VEC]
    new_vectors[...] = vector_ref[...] - change.T[:VEC]
    second_new[...] = second_ref[...].T[:VEC]
    for copy in long_copies:
        copy.wait()


def update_weights(layout, width, long, columns, hidden, rows, results, values, vectors, weights):
    full = jnp.float32
    shapes = [
        *(result.shape for result in results),
        (3, rows, columns),
        (rows, columns),
        (rows, hidden),
        (rows, hidden),
        (VEC, rows),
        (3, rows, columns),
        (rows, columns),
        (rows, hidden),
        (rows, hidden),
        (VEC, rows),
        (VEC, rows),
        (3, rows),
        (3, columns),
        (1, columns),
        (1, rows),
        (1, rows),
        (1, hidden),
        (1, hidden),
        (1, rows),
    ]
    far = (*values, vectors, *weights)
    anywhere = pl.BlockSpec(memory_space=pl.ANY)
    inside = pl.BlockSpec(memory_space=pltpu.VMEM)
    return pl.pallas_call(
        functools.partial(update_kernel, layout, width, long),
        name="update_weights",
        out_shape=[jax.ShapeDtypeStruct(shape, full) for shape in shapes],
        in_specs=[anywhere] * (2 + len(far)),
        out_specs=[anywhere] * 2 + [inside] * (len(shapes) - 2),
        scratch_shapes=[
            *(pltpu.VMEM(array.shape, full) for array in (*far, *results)),
            pltpu.SemaphoreType.DMA((4 + len(far),)),
        ],
        compiler_params=pltpu.CompilerParams(vmem_limit_bytes=63 << 20),
    )(*results, *far)


def on_device(
    inputs,
    cotangent,
    token_mask,
    w_qkv,
    w_out,
    w_fc1,
    w_fc2,
    vectors,
    qkv_row,
    qkv_col,
    out_row,
    out_col,
    fc1_row,
    fc1_col,
    fc2_row,
    fc2_col,
    vec_second,
):
    tensor_count = lax.axis_size("tensor")
    dims = grid_of(lax.axis_size("fsdp"))
    width = inputs.shape[1]
    own_rows, columns = w_qkv.shape[1:]
    hidden = w_fc1.shape[1]
    weights = (w_qkv, w_out.T, w_fc1, w_fc2.T)
    (
        weight_qkv,
        _,
        weight_out,
        *_,
        block_out,
        grad_middle,
        back_one,
        mixed_rows,
        low_turned,
        projected,
        grad_one,
        grad_two,
        table,
        vec_sums,
        pre_sums,
        bias_column,
    ) = forward(dims, tensor_count, inputs, cotangent, token_mask, vectors, weights)
    layout = Layout(columns, hidden, ("two", "one", "out", "qkv", "vec"))
    row_states = (qkv_row, out_col[None], fc1_row[None], fc2_col[None])
    col_states = (qkv_col, out_row[None], fc1_col[None], fc2_row[None])
    input_grad, *values = backward(
        dims,
        tensor_count,
        layout,
        (
            grad_two,
            grad_one,
            weight_qkv,
            weight_out,
            projected,
            inputs,
            grad_middle,
            mixed_rows,
            low_turned,
            back_one,
        ),
        (bias_column, table, vec_sums, pre_sums),
        weights,
        (*row_states, *col_states, vec_second, vectors),
    )
    outs = update_weights(
        layout, width, FF, columns, hidden, own_rows, (block_out, input_grad), values, vectors, weights
    )
    outs = [out.reshape(-1) if out.shape[0] == 1 else out for out in outs]
    for at in (3, 5, 8, 10):
        outs[at] = outs[at].T
    return (*outs[:12], *outs[13:], outs[12])


def solution(mesh):
    in_specs = (
        P(("fsdp", "tensor"), None),
        P(("fsdp", "tensor"), None),
        P("fsdp", None),
        P(None, "fsdp", "tensor"),
        P("tensor", "fsdp"),
        P("fsdp", "tensor"),
        P("tensor", "fsdp"),
        P(None, "fsdp"),
        P(None, "fsdp"),
        P(None, "tensor"),
        P("tensor"),
        P("fsdp"),
        P("fsdp"),
        P("tensor"),
        P("tensor"),
        P("fsdp"),
        P(None, "fsdp"),
    )
    out_specs = (
        P(("fsdp", "tensor"), None),
        P(("fsdp", "tensor"), None),
        P(None, "fsdp", "tensor"),
        P("tensor", "fsdp"),
        P("fsdp", "tensor"),
        P("tensor", "fsdp"),
        P(None, "fsdp"),
        P(None, "fsdp", "tensor"),
        P("tensor", "fsdp"),
        P("fsdp", "tensor"),
        P("tensor", "fsdp"),
        P(None, "fsdp"),
        P(None, "fsdp"),
        P(None, "tensor"),
        P("tensor"),
        P("fsdp"),
        P("fsdp"),
        P("tensor"),
        P("tensor"),
        P("fsdp"),
        P(None, "fsdp"),
    )
    return jax.shard_map(
        on_device, mesh=mesh, in_specs=in_specs, out_specs=out_specs, check_vma=False
    )
```

```python
import functools

import jax
import jax.numpy as jnp
from jax import lax
from jax.experimental import pallas as pl
from jax.experimental.pallas import tpu as pltpu
from jax.sharding import PartitionSpec as P

HEAD_DIM = 64
FF = 4096
STEP = 20
VEC = 12
LANES = 128

EPS_NORM = 1e-05
EPS_ONE = 1e-30
CLIP_LEVEL = 1.0
LEARN_RATE = 0.5
MESH = pl.DeviceIdType.MESH
LOG2E = 1.4426950408889634
CONTRACT_LAST = (((1,), (1,)), ((), ()))


def grid_of(count):
    return {16: (4, 2, 2), 32: (2, 4, 4)}.get(count, (count, 1, 1))


class Place:
    def __init__(self, dims, tensor):
        self.dims = dims
        self.tensor = tensor
        fsdp = lax.axis_index("fsdp")
        _, ny, nx = dims
        self.at = (fsdp // (ny * nx), (fsdp // nx) % ny, fsdp % nx)
        self.rank = lax.axis_index("tensor")

    def moved(self, axis, step):
        place = list(self.at) + [self.rank]
        size = (*self.dims, self.tensor)[axis]
        place[axis] = lax.rem(place[axis] + step + size, size)
        return tuple(place)

    def device(self, place):
        z, y, x, rank = place
        return {"fsdp": (z * self.dims[1] + y) * self.dims[2] + x, "tensor": rank}

    def size(self, axis):
        return (*self.dims, self.tensor)[axis]

    def line(self):
        z = self.at[0]
        pair = z // 2 * 2
        middle = (z == 1) | (z == 2)
        return pair, 2 - pair, z + 1 - 2 * (z % 2), middle

    def at_z(self, z):
        return self.device((z, self.at[1], self.at[2], self.rank))

    def peers(self, *axes):
        places = [()]
        for axis in axes:
            places = [(*steps, step) for steps in places for step in range(self.size(axis))]
        found = []
        for steps in places[1:]:
            place = list(self.at) + [self.rank]
            for axis, step in zip(axes, steps):
                place[axis] = lax.rem(place[axis] + step, self.size(axis))
            found.append(self.device(tuple(place)))
        return found

    def barrier(self, groups):
        sem = pltpu.get_barrier_semaphore()
        count = 0
        for axes in groups:
            for device in self.peers(*axes):
                pl.semaphore_signal(sem, inc=1, device_id=device, device_id_type=MESH)
                count += 1
        if count:
            pl.semaphore_wait(sem, count)


def norm_rows(values):
    average = jnp.mean(values, axis=1, keepdims=True)
    center = values - average
    inverse = lax.rsqrt(jnp.mean(center * center, axis=1, keepdims=True) + EPS_NORM)
    return center * inverse, inverse


def dot(left, right, dims=(((1,), (0,)), ((), ()))):
    return lax.dot_general(left, right, dims, preferred_element_type=jnp.float32)


def turn(source, target):
    for start in range(0, source.shape[1], LANES):
        target[pl.ds(start, LANES), :] = source[:, pl.ds(start, LANES)].T


def attend_pair(heads, bias):
    mixed = []
    for head in range(2):
        query, key, value = (
            heads[:, kind * LANES + head * HEAD_DIM : kind * LANES + (head + 1) * HEAD_DIM] for kind in range(3)
        )
        scores = dot(query, key, CONTRACT_LAST) * (HEAD_DIM ** (-0.5) * LOG2E) + bias
        raised = jnp.exp2(scores - jnp.max(scores, axis=1, keepdims=True))
        summed = jnp.sum(raised, axis=1, keepdims=True)
        attention = (raised * (1.0 / summed)).astype(jnp.bfloat16)
        mixed.append(dot(attention, value).astype(jnp.bfloat16))
    return jnp.concatenate(mixed, axis=1)


def guarded(condition, run):
    if condition is None:
        run()
    else:
        pl.when(condition)(run)


def along_z(count):
    return ("pair", "mid", "back") if count == 4 else ("all",)


class Steps:
    def __init__(self):
        self.steps = {}

    def add(self, name, run, time, rank, after=(), waits=(), starts=()):
        self.steps[name] = (run, time, rank, tuple(after), tuple(waits), tuple(starts))

    def arrange(self):
        now, free, arrival, done, order = 0.0, {}, {}, set(), []
        left = list(self.steps)
        while left:
            best, soonest = None, None
            for name in left:
                _, time, rank, after, waits, _ = self.steps[name]
                if any(other not in done for other in after) or any(wait not in arrival for wait in waits):
                    continue
                ready = max([arrival[wait] for wait in waits], default=0.0)
                if ready <= now:
                    if best is None or rank < self.steps[best][2]:
                        best = name
                elif soonest is None or ready < soonest:
                    soonest = ready
            if best is None:
                now = soonest
                continue
            _, time, _, _, _, starts = self.steps[best]
            now += time
            for transfer, link, length in starts:
                begin = max(now, free.get(link, 0.0))
                free[link] = begin + length
                arrival[transfer] = begin + length + LATENCY
            done.add(best)
            left.remove(best)
            order.append(best)
        return order, now

    def run(self):
        for name in self.arrange()[0]:
            self.steps[name][0]()


class Gather:
    def __init__(self, here, pack_ref, outs, parts, local_sem, send_sem, recv_sem):
        self.here = here
        self.pack = pack_ref
        self.outs = outs
        self.rows = pack_ref.shape[0]
        self.parts = parts
        self.late = [len(parts) - at for at in LATE_PARTS if at < len(parts)]
        self.sems = (local_sem, send_sem, recv_sem)
        self.own = (*here.at, here.rank)
        self.sent = []

    def region(self, item, part, place, free):
        out, _, chunk, _ = self.parts[item]
        index = tuple(slice(None) if a in free else place[a] for a in range(3))
        lead = () if chunk is None else (place[3], chunk)
        return self.outs[out].at[(*lead, *index, part)]

    def shard(self, item, part):
        _, offset, _, size = self.parts[item]
        return self.pack.at[part, pl.ds(offset, size)]

    def phases(self, item):
        lengthwise = along_z(self.here.dims[0]) if self.parts[item][0] in (3, 4) else ("all",)
        across = ("first", "second")
        order = (*across, *lengthwise) if item in self.late else (*lengthwise, *across)
        return order if self.parts[item][2] is None else (*order, "core")

    def moves(self, item, phase):
        here, own = self.here, self.own
        kind = self.phases(item)[phase]
        late = item in self.late
        whole, half = pl.ds(0, self.rows), self.rows // 2
        first, second = pl.ds(0, half), pl.ds(half, half)
        found = []
        if kind in ("pair", "mid", "back"):
            free = (1, 2) if late else ()
            pair, far, near, middle = here.line()

            def blocks(z):
                return self.region(item, whole, (z, *own[1:]), free)

            if kind == "pair":
                sent = self.shard(item, whole) if phase == 0 else blocks(own[0])
                found.append((here.at_z(near), sent, blocks(own[0]), blocks(near), None, None))
            elif kind == "mid":
                pairs = blocks(pl.ds(pair, 2))
                found.append((here.at_z(3 - own[0]), pairs, pairs, blocks(pl.ds(far, 2)), middle, middle))
            else:
                pairs = blocks(pl.ds(far, 2))
                outside = jnp.logical_not(middle)
                found.append((here.at_z(near), pairs, pairs, pairs, middle, outside))
            return found
        before = () if late else (0,)
        steps = {
            "all": ((0, (1, 2) if late else (), whole),),
            "first": ((2, before, first), (1, before, second))
            if late
            else ((1, before, first), (2, before, second)),
            "second": ((1, (*before, 2), first), (2, (*before, 1), second))
            if late
            else ((2, (*before, 1), first), (1, (*before, 2), second)),
            "core": ((3, (0, 1, 2), whole),),
        }[kind]
        for axis, free, part in steps:
            for step in range(1, here.size(axis)):
                place = self.region(item, part, own, free)
                sent = self.shard(item, part) if phase == 0 else place
                landed = self.region(item, part, here.moved(axis, -step), free)
                found.append((here.device(here.moved(axis, step)), sent, place, landed, None, None))
        return found

    def copies(self, item, phase, landing):
        found = []
        for at, (device, sent, place, landed, sends, receives) in enumerate(self.moves(item, phase)):
            copy = pltpu.make_async_remote_copy(
                src_ref=landed if landing else sent,
                dst_ref=landed if landing else place,
                send_sem=self.sems[1].at[item, phase, at],
                recv_sem=self.sems[2].at[item, phase, at],
                device_id=device,
                device_id_type=MESH,
            )
            found.append((receives if landing else sends, copy))
        return found

    def keep(self, item):
        whole = pl.ds(0, self.rows)
        return pltpu.make_async_copy(
            self.shard(item, whole), self.region(item, whole, self.own, ()), self.sems[0].at[item]
        )

    def advance(self, item, phase):
        if phase:
            for condition, copy in self.copies(item, phase - 1, True):
                guarded(condition, copy.wait_recv)
        if phase == 0:
            self.keep(item).start()
        if phase == 1:
            self.keep(item).wait()
        if phase < len(self.phases(item)):
            for condition, copy in self.copies(item, phase, False):
                guarded(condition, copy.start)
                self.sent.append((condition, copy))

    def finish(self):
        for condition, copy in self.sent:
            guarded(condition, copy.wait_send)


BLOCK = 512
DEPTH = 3
LATENCY = 1.5
UNIT = 20.0
CORE_UNIT = 40.0
LATE_PARTS = (6,)
LATE_ITEMS = (0, 1, 2)
PUMP = 0.4


def forward_kernel(dims, tensor, parts, tasks, *refs):
    input_ref, top_ref, mask_ref, vector_ref = refs[:4]
    own_weights = refs[4:8]
    outs, land = refs[8:13], refs[13:15]
    weight_qkv, weight_vec, weight_out, weight_one, weight_two = outs
    far = refs[15:20]
    projected, grad_one, grad_two, table, vec_sums, pre_sums, bias_column = refs[20:27]
    (
        block_out,
        grad_middle,
        back_one,
        mixed,
        low_one,
        low_turned,
        pack,
        keep_ref,
        square,
        vec_buf,
        qkv_buf,
        head_stage,
        out_buf,
        one_buf,
        two_buf,
        low_two,
        low_two_turned,
        back_two,
        back_two_turned,
        grad_low_two,
        hidden_bias,
        head_bias,
        one_stage,
        two_stage,
        one_keep,
        two_keep,
        other,
        active,
        grad_pre,
        load_sem,
        store_sem,
        keep_sem,
        head_sem,
        land_sem,
        far_sem,
        local_sem,
        send_sem,
        recv_sem,
    ) = refs[27:]
    near = (block_out, grad_middle, back_one, mixed, low_turned)

    def far_store(at):
        return pltpu.make_async_copy(near[at], far[at], far_sem.at[at])

    here = Place(dims, tensor)
    gather = Gather(here, pack, outs, parts, local_sem, send_sem, recv_sem)
    rows, width = input_ref.shape
    own_rows = pack.shape[0]
    per_rank = weight_qkv.shape[1]
    low = jnp.bfloat16
    step_rows = LANES

    def fill_pack():
        base = 0
        for pair in range(per_rank):
            for kind in range(3):
                part = own_weights[0][kind, :, pl.ds(pair * LANES, LANES)]
                pack[:, pl.ds(base, LANES)] = part.astype(low)
                base += LANES
        square[...] = jnp.zeros_like(square)
        square[pl.ds(0, VEC), :] = vector_ref[...]
        pack[:, pl.ds(base, LANES)] = square[...].T.astype(low)
        base += LANES
        for ref in own_weights[1:]:
            pack[:, pl.ds(base, ref.shape[1])] = ref[...].astype(low)
            base += ref.shape[1]

    def mask_row():
        return mask_ref[pl.ds(here.rank, 1), :].astype(jnp.float32)

    def mask_bias(keep):
        return jnp.where(keep > 0.0, 0.0, -1e30)

    def first_masks():
        turned = jnp.broadcast_to(mask_row(), (LANES, rows)).T
        keep_ref[...] = turned[:, 0:1]
        bias_column[...] = mask_bias(turned[:, 0:1])

    def row_steps(body, carry):
        return lax.fori_loop(
            0, rows // step_rows, lambda at, c: body(pl.ds(pl.multiple_of(at * step_rows, step_rows), step_rows), c), carry
        )

    def load(source, buffer, sem):
        return pltpu.make_async_copy(source, buffer, sem)

    def first_norm():
        first_masks()
        copy = load(weight_vec, vec_buf, load_sem.at[7])
        copy.start()
        copy.wait()
        whole = vec_buf[...].reshape(width, LANES).astype(jnp.float32).T
        table[...] = whole[:16]
        for at in range(VEC - 8):
            hidden_bias[:, pl.ds(at * width, width)] = whole[7 + at : 8 + at]
        for pair in range(width // LANES):
            for kind, row in ((0, 2), (2, 3)):
                head_bias[:, pl.ds((pair * 3 + kind) * LANES, LANES)] = whole[
                    row : row + 1, pair * LANES : (pair + 1) * LANES
                ]
            head_bias[:, pl.ds((pair * 3 + 1) * LANES, LANES)] = jnp.zeros((1, LANES), jnp.float32)

        def body(part, carry):
            normed, _ = norm_rows(input_ref[part, :])
            low_one[part, :] = (normed * table[0:1, :] + table[1:2, :]).astype(low)
            back_two[part, :] = (top_ref[part, :].astype(jnp.float32) * keep_ref[part, :]).astype(low)
            return carry

        row_steps(body, 0)
        turn(back_two, back_two_turned)

    def head_store(pair, slot):
        column = pl.ds(pl.multiple_of(pair * 3 * LANES, LANES), 3 * LANES)
        return pltpu.make_async_copy(head_stage.at[slot], projected.at[:, column], head_sem.at[slot])

    def turn_first():
        turn(low_one, low_turned)
        far_store(4).start()

    def pair_of(at):
        turn_at, place = divmod(at, tensor)
        return lax.rem(here.rank + place, tensor) * per_rank + turn_at

    def head_load(at):
        turn_at, place = divmod(at, tensor)
        source = weight_qkv.at[lax.rem(here.rank + place, tensor), turn_at]
        return load(source, qkv_buf.at[at % 2], load_sem.at[at % 2])

    def heads(at):
        head_load(at).wait()
        pair = pair_of(at)
        slot = at % 2
        column = pl.ds(pl.multiple_of(pair * 3 * LANES, LANES), 3 * LANES)
        weight = qkv_buf[slot].reshape(width, 3 * LANES)
        value = (dot(low_one[...], weight) + head_bias[:, column]).astype(low)
        if at > 1:
            head_store(pair, slot).wait()
        head_stage[slot] = value
        head_store(pair, slot).start()
        mixed[:, pl.ds(pl.multiple_of(pair * LANES, LANES), LANES)] = attend_pair(value, mask_bias(mask_row()))

    def out_load():
        return [
            load(weight_out.at[rank, 0], out_buf.at[rank], load_sem.at[2]) for rank in range(tensor)
        ]

    def second_norm():
        far_store(3).start()
        for copy in out_load():
            copy.wait()
        columns = width // tensor
        for rank in range(tensor):
            weight = out_buf[rank].reshape(width, columns)
            term = dot(mixed[:, pl.ds(rank * columns, columns)], weight, CONTRACT_LAST)
            if rank == 0:
                grad_middle[...] = term
            else:
                grad_middle[...] += term

        def body(part, carry):
            middle = input_ref[part, :] + (grad_middle[part, :] + table[4:5, :]) * keep_ref[part, :]
            grad_middle[part, :] = middle
            normed, _ = norm_rows(middle)
            low_two[part, :] = (normed * table[5:6, :] + table[6:7, :]).astype(low)
            return carry

        row_steps(body, 0)
        turn(low_two, low_two_turned)

    stages = (one_stage, two_stage)
    keeps = (one_keep, two_keep)

    def hand_over(at):
        chunk, place = divmod(at, tensor)
        target = (*here.at, lax.rem(here.rank + place + 1, tensor))
        return [
            pltpu.make_async_remote_copy(
                src_ref=stages[which].at[at % 2],
                dst_ref=land[which].at[place, chunk],
                send_sem=store_sem.at[which, at % 2],
                recv_sem=land_sem.at[which, place, chunk],
                device_id=here.device(target),
                device_id_type=MESH,
            )
            for which in range(2)
        ]

    def keep_store(chunk):
        return [
            pltpu.make_async_copy(
                keeps[which].at[chunk % 2],
                out.at[chunk],
                keep_sem.at[which, chunk % 2],
            )
            for which, out in enumerate((grad_one, grad_two))
        ]

    def hidden_column(at):
        chunk, place = divmod(at, tensor)
        base = (lax.rem(here.rank + place + 1, tensor) * weight_one.shape[1] + chunk) * BLOCK
        return pl.ds(pl.multiple_of(base, LANES), BLOCK)

    def hidden_load(at):
        chunk, place = divmod(at, tensor)
        rank = lax.rem(here.rank + place + 1, tensor)
        return [
            load(source.at[rank, chunk], buffer.at[at % 2], load_sem.at[3 + 2 * which + at % 2])
            for which, (source, buffer) in enumerate(((weight_one, one_buf), (weight_two, two_buf)))
        ]

    staged = {}

    def hidden(at):
        chunk, place = divmod(at, tensor)
        column = hidden_column(at)
        for copy in hidden_load(at):
            copy.wait()
        half = rows // 2
        bias = hidden_bias[:, column]

        def body(turn_at, total):
            part = pl.ds(pl.multiple_of(turn_at * half, half), half)
            one = one_buf[at % 2].reshape(width, BLOCK)
            two = two_buf[at % 2].reshape(width, BLOCK)
            preact = dot(low_two[part, :], one) + bias
            gate = jax.nn.sigmoid(1.702 * preact)
            value = (preact * gate).astype(low)
            active[part, :] = value
            derivative = gate + 1.702 * preact * gate * (1.0 - gate)
            grad = (dot(back_two[part, :], two) * derivative).astype(low)
            grad_pre[part, :] = grad
            if at == 0:
                block_out[part, :] = dot(value, two, CONTRACT_LAST)
                grad_low_two[part, :] = dot(grad, one, CONTRACT_LAST)
            else:
                block_out[part, :] += dot(value, two, CONTRACT_LAST)
                grad_low_two[part, :] += dot(grad, one, CONTRACT_LAST)
            return total + jnp.sum(grad.astype(jnp.float32), axis=0, keepdims=True)

        pre_sums[:, column] = lax.fori_loop(0, 2, body, jnp.zeros((1, BLOCK), jnp.float32))
        mine = place == tensor - 1
        if mine:
            targets = [ref.at[chunk % 2] for ref in keeps]
            if chunk > 1:
                for copy in keep_store(chunk):
                    copy.wait()
        else:
            targets = [ref.at[at % 2] for ref in stages]
            for copy in staged.pop(at % 2, ()):
                copy.wait_send()
        for target, left, right in (
            (targets[0], low_two_turned, grad_pre),
            (targets[1], back_two_turned, active),
        ):
            target[...] = dot(left[...], right[...]).astype(low).reshape(*target.shape)
        if not mine:
            staged[at % 2] = hand_over(at)
            for copy in staged[at % 2]:
                copy.start()

    def combine(chunk):
        for place in range(tensor - 1):
            for which, copy in enumerate(hand_over(chunk * tensor + place)):
                copy.wait_recv()
                fetch = load(land[which].at[place, chunk], other, load_sem.at[7])
                fetch.start()
                fetch.wait()
                keeps[which][chunk % 2] = keeps[which][chunk % 2] + other[...]
        for copy in keep_store(chunk):
            copy.start()

    def last_norm():
        def body(part, sums):
            middle = grad_middle[part, :]
            keep = keep_ref[part, :]
            top = top_ref[part, :].astype(jnp.float32)
            block_out[part, :] = middle + (block_out[part, :] + table[VEC - 1 : VEC, :]) * keep
            normed, inverse = norm_rows(middle)
            grad_low = grad_low_two[part, :]
            scaled = grad_low * table[5:6, :]
            first = jnp.mean(scaled, axis=1, keepdims=True)
            second = jnp.mean(scaled * normed, axis=1, keepdims=True)
            grad = top + inverse * (scaled - first - normed * second)
            grad_middle[part, :] = grad
            masked = grad * keep
            back_one[part, :] = masked.astype(low)
            terms = (masked, grad_low * normed, grad_low, top * keep)
            return tuple(old + jnp.sum(term, axis=0, keepdims=True) for old, term in zip(sums, terms))

        zero = jnp.zeros((1, width), jnp.float32)
        for at, value in enumerate(row_steps(body, (zero,) * 4)):
            vec_sums[at : at + 1, :] = value
        for at in range(3):
            far_store(at).start()

    fill_pack()
    here.barrier(((0,), (1,), (2,), (3,)))
    steps = Steps()
    whole = sum(part[3] for part in parts)
    nz, ny, nx = dims

    def lengths(item, phase):
        share = parts[item][3] / whole * UNIT
        across = ny * nx if item in gather.late else 1
        along = 1 if item in gather.late else nz
        return {
            "pair": (share * across, "end"),
            "mid": (share * across * 2, "mid"),
            "back": (share * across * 2, "end"),
            "all": (share * across * nz, "end"),
            "first": (share * along / 2, "xy"),
            "second": (share * along, "xy"),
            "core": (share * CORE_UNIT / UNIT, "core"),
        }[gather.phases(item)[phase]]

    for item, part in enumerate(parts):
        phases = len(gather.phases(item))
        for phase in range(phases + 1):
            after = [("copy", item, phase - 1)] if phase else []
            if phase == 0 and item >= DEPTH and item not in gather.late:
                after = [("copy", item - DEPTH, 1)]
            if item in gather.late:
                if phase == 0:
                    after = [("copy", DEPTH, 1)]
                if phase == 2:
                    after += [("copy", other, 1) for other in range(min(len(parts), item + 3)) if other not in gather.late]
            length, link = lengths(item, min(phase, phases - 1))
            steps.add(
                ("copy", item, phase),
                functools.partial(gather.advance, item, phase),
                PUMP,
                0.5 if phase == 0 else 0.0,
                after,
                [(item, phase - 1)] if phase else [],
                [((item, phase), link, length)] if phase < phases else [],
            )

    def landed(items):
        return [("copy", item, len(gather.phases(item))) for item in items]

    def start(copies):
        for copy in copies:
            copy.start()

    previous = None
    head_count, block_count = per_rank * tensor, FF // BLOCK
    for name, at, items in tasks:
        after = landed(items) + ([previous] if previous else [])
        begin, run, time = {
            "norm": (None, first_norm, 4.0),
            "turn": (None, turn_first, 1.5),
            "heads": (lambda at=at: head_load(at).start(), lambda at=at: heads(at), 3.0),
            "out": (lambda: start(out_load()), second_norm, 5.0),
            "hidden": (lambda at=at: start(hidden_load(at)), lambda at=at: hidden(at), 5.5),
        }[name]
        if begin is not None:
            first = landed(items)
            if at > 1:
                first.append((name, at - 2))
            steps.add(("load", name, at), begin, 0.1, 0.2, first)
            after.append(("load", name, at))
        mine = name == "hidden" and at % tensor == tensor - 1
        chunk = at // tensor
        if mine and chunk > 1:
            after.append(("combine", chunk - 2))
        starts = []
        if name == "hidden" and not mine:
            starts = [(("hand", at), "core", CORE_UNIT / len(parts))]
        steps.add((name, at), run, time, 1.0, after, (), starts)
        if mine:
            waits = [("hand", chunk * tensor + place) for place in range(tensor - 1)]
            steps.add(
                ("combine", chunk), functools.partial(combine, chunk), 2.0, 0.8, [(name, at)], waits
            )
        previous = (name, at)
    steps.add(("last", 0), last_norm, 4.0, 0.9, [previous])
    steps.run()
    for at in range(5):
        far_store(at).wait()
    for slot in range(min(2, head_count)):
        head_store(0, slot).wait()
    for chunk in range(min(2, block_count // tensor)):
        for copy in keep_store(chunk):
            copy.wait()
    for copies in staged.values():
        for copy in copies:
            copy.wait_send()
    gather.finish()


def forward(dims, tensor, inputs, cotangent, token_mask, vectors, weights):
    own_rows, columns = weights[0].shape[1:]
    hidden = weights[2].shape[1]
    rows, width = inputs.shape
    low, full = jnp.bfloat16, jnp.float32
    widths = (3 * columns, LANES, columns, hidden, hidden)
    offsets = [sum(widths[:at]) for at in range(5)]
    per_rank = columns // LANES
    parts = [(1, offsets[1], None, LANES)]
    tasks = [("norm", 0, (0,)), ("turn", 0, (0,))]
    for at in range(per_rank):
        size = 3 * LANES
        parts.append((0, offsets[0] + at * size, at, size))
        tasks += [("heads", at * tensor + place, (len(parts) - 1,)) for place in range(tensor)]
    tasks.append(("out", 0, (len(parts),)))
    parts.append((2, offsets[2], 0, columns))
    for block in range(hidden // BLOCK):
        needed = (len(parts), len(parts) + 1)
        parts += [(which, offsets[which] + block * BLOCK, block, BLOCK) for which in (3, 4)]
        tasks += [("hidden", block * tensor + place, needed) for place in range(tensor)]
    count = len(parts)
    peers = max(1, dims[0] - 1, dims[1] + dims[2] - 2, tensor - 1)
    anywhere = pl.BlockSpec(memory_space=pl.ANY)
    inside = pl.BlockSpec(memory_space=pltpu.VMEM)
    block = (*dims, own_rows, BLOCK)
    chunks = hidden // BLOCK

    def shape(kind, *size):
        return jax.ShapeDtypeStruct(size, kind)

    return pl.pallas_call(
        functools.partial(forward_kernel, dims, tensor, tuple(parts), tuple(tasks)),
        name="forward",
        out_shape=[
            shape(low, tensor, per_rank, *dims, own_rows, 3 * LANES),
            shape(low, *dims, own_rows, LANES),
            shape(low, tensor, 1, *dims, own_rows, columns),
            *[shape(low, tensor, chunks, *block)] * 2,
            *[shape(low, max(1, tensor - 1), chunks, *block)] * 2,
            shape(full, rows, width),
            shape(full, rows, width),
            *[shape(low, rows, width)] * 2,
            shape(low, width, rows),
            shape(low, rows, 3 * width),
            *[shape(low, chunks, *block)] * 2,
            shape(full, 16, width),
            shape(full, 8, width),
            shape(full, 1, hidden * tensor),
            shape(full, rows, 1),
        ],
        in_specs=[inside] * 8,
        out_specs=[anywhere] * 15 + [inside] * 4,
        scratch_shapes=[
            pltpu.VMEM((rows, width), full),
            pltpu.VMEM((rows, width), full),
            *[pltpu.VMEM((rows, width), low)] * 3,
            pltpu.VMEM((width, rows), low),
            pltpu.VMEM((own_rows, sum(widths)), low),
            pltpu.VMEM((rows, 1), full),
            pltpu.VMEM((LANES, own_rows), full),
            pltpu.VMEM((*dims, own_rows, LANES), low),
            pltpu.VMEM((2, *dims, own_rows, 3 * LANES), low),
            pltpu.VMEM((2, rows, 3 * LANES), low),
            pltpu.VMEM((tensor, *dims, own_rows, columns), low),
            pltpu.VMEM((2, *block), low),
            pltpu.VMEM((2, *block), low),
            pltpu.VMEM((rows, width), low),
            pltpu.VMEM((width, rows), low),
            pltpu.VMEM((rows, width), low),
            pltpu.VMEM((width, rows), low),
            pltpu.VMEM((rows, width), full),
            pltpu.VMEM((1, hidden * tensor), full),
            pltpu.VMEM((1, 3 * width), full),
            pltpu.VMEM((2, *block), low),
            pltpu.VMEM((2, *block), low),
            pltpu.VMEM((2, *block), low),
            pltpu.VMEM((2, *block), low),
            pltpu.VMEM(block, low),
            pltpu.VMEM((rows, BLOCK), low),
            pltpu.VMEM((rows, BLOCK), low),
            pltpu.SemaphoreType.DMA((8,)),
            pltpu.SemaphoreType.DMA((2, 2)),
            pltpu.SemaphoreType.DMA((2, 2)),
            pltpu.SemaphoreType.DMA((2,)),
            pltpu.SemaphoreType.DMA((2, max(1, tensor - 1), chunks)),
            pltpu.SemaphoreType.DMA((5,)),
            pltpu.SemaphoreType.DMA((count,)),
            pltpu.SemaphoreType.DMA((count, 6, peers)),
            pltpu.SemaphoreType.DMA((count, 6, peers)),
        ],
        compiler_params=pltpu.CompilerParams(
            collective_id=0, has_side_effects=True, vmem_limit_bytes=62 << 20
        ),
    )(inputs, cotangent, token_mask, vectors, *weights)


class Layout:
    def __init__(self, columns, hidden, order):
        sizes = {"qkv": 3 * columns, "out": columns, "one": hidden, "two": hidden, "vec": LANES}
        self.order = order
        self.sizes = sizes
        self.start = {}
        at = 0
        for name in order:
            self.start[name] = at
            at += sizes[name]
        self.total = at
        self.columns = columns

    def span(self, name):
        return (self.start[name], self.sizes[name])

    def matrices(self):
        base = self.start["qkv"]
        pairs = range(self.columns // LANES)
        spans = [[(base + (pair * 3 + at) * LANES, LANES) for pair in pairs] for at in range(3)]
        return spans + [[self.span(name)] for name in ("out", "one", "two")]


def pick(values, lane):
    row = jnp.zeros((1, LANES), jnp.float32)
    for at, value in enumerate(values):
        row = jnp.where(lane == at, value, row)
    return row


def total_of(values):
    return jnp.sum(jnp.sum(values, axis=1, keepdims=True), axis=0, keepdims=True)


def attend_pair_back(heads, bias, grads):
    parts = ([], [], [])
    for head in range(2):
        query, key, value = (
            heads[:, kind * LANES + head * HEAD_DIM : kind * LANES + (head + 1) * HEAD_DIM] for kind in range(3)
        )
        grad = grads[:, head * HEAD_DIM : (head + 1) * HEAD_DIM]
        scores = dot(key, query, CONTRACT_LAST) * (HEAD_DIM ** (-0.5) * LOG2E) + bias
        raised = jnp.exp2(scores - jnp.max(scores, axis=0, keepdims=True))
        attention = raised * (1.0 / jnp.sum(raised, axis=0, keepdims=True))
        grad_value = dot(attention.astype(jnp.bfloat16), grad)
        grad_attention = dot(value, grad, CONTRACT_LAST)
        weighted = jnp.sum(attention * grad_attention, axis=0, keepdims=True)
        grad_scores = (attention * (grad_attention - weighted) * HEAD_DIM ** (-0.5)).astype(jnp.bfloat16)
        grad_key = dot(grad_scores, query)
        grad_query = dot(key.T, grad_scores).T
        for kind, part in enumerate((grad_query, grad_key, grad_value)):
            parts[kind].append(part.astype(jnp.bfloat16))
    return jnp.concatenate([piece for kind in parts for piece in kind], axis=1)


def backward_kernel(dims, tensor, items, layout, *refs):
    (
        sum_two,
        sum_one,
        weight_qkv,
        weight_out,
        projected,
        input_ref,
        middle_ref,
        *far,
        bias_ref,
        table,
        vec_sums,
        pre_sums,
    ) = refs[:14]
    far = (*far, *refs[14:18])
    row_states, col_states = refs[18:22], refs[22:26]
    second_ref, vector_ref = refs[26:28]
    input_grad_out, total_ref, col_new_ref, row_new_ref, second_new_ref, sums_ref = refs[28:34]
    groups = ("ffn", "out", "qkv", "vec")
    kinds = ("own", "one_x", "one_y", "two_y", "two_x", "from_z")
    held = {}
    for kind in kinds:
        for group in groups:
            held[kind, group] = refs[34 + len(held)]
    for group in groups[1:]:
        held["core", group] = refs[34 + len(held)]
    (
        input_grad,
        late_z,
        late_one_y,
        late_one_x,
        late_two_x,
        late_two_y,
        col_sum,
        col_in,
        row_sum,
        row_in,
        small,
        small_in,
        square,
        turned,
        mixed,
        back_one,
        *weights,
        low_turned,
        back_turned,
        grad_mixed,
        out_buf,
        qkv_buf,
        head_buf,
        row_buf,
        out_stage,
        qkv_stage,
        vec_stage,
        head_sums,
        table_grad_ref,
        load_sem,
        stage_sem,
        core_sem,
        local_sem,
        send_sem,
        recv_sem,
        sum_send,
        sum_recv,
        far_sem,
    ) = refs[34 + len(held) :]
    near = (mixed, low_turned, back_one, *weights)

    def far_load(at):
        return pltpu.make_async_copy(far[at], near[at], far_sem.at[at])

    here = Place(dims, tensor)
    nz, ny, nx = dims
    low = jnp.bfloat16
    own_rows = total_ref.shape[0]
    half_rows = own_rows // 2
    rows, width = input_grad.shape
    own_place = (*here.at, here.rank)
    count = len(items)

    def columns(item):
        _, start, size, _ = items[item]
        return pl.ds(start, size)

    def at_home(kind, item):
        name = items[item][0]
        if name in ("one", "two"):
            members = [at for at, other in enumerate(items) if other[0] in ("one", "two")]
            if kind != "own":
                members = [at for at in members if at not in late]
            return held[kind, "ffn"].at[members.index(item)]
        members = [at for at, other in enumerate(items) if other[0] == name]
        return held[kind, name].at[members.index(item)]

    def phases(item):
        lengthwise = along_z(nz)[::-1]
        across = ("first", "second")
        return (*lengthwise, *across) if item in late else (*across, *lengthwise)

    def moves(item, phase):
        first, second, whole = pl.ds(0, half_rows), pl.ds(half_rows, half_rows), pl.ds(0, own_rows)
        kind = phases(item)[phase]
        own = at_home("own", item)
        found = []
        if kind in ("pair", "mid", "back"):
            pair, far, near, middle = here.line()
            outside = jnp.logical_not(middle)
            rest = (slice(None), slice(None)) if item in late else here.at[1:]
            buffer = late_z.at[late.index(item)] if item in late else at_home("from_z", item)
            z = here.at[0]
            device, sent_z, add_z, slots, sends, receives = {
                "back": (near, pl.ds(far, 2), pl.ds(far, 2), pl.ds(0, 2), outside, middle),
                "mid": (3 - z, pl.ds(far, 2), pl.ds(pair, 2), pl.ds(2, 2), middle, middle),
                "pair": (near, near, z, 4, None, None),
            }[kind]
            source = own.at[(sent_z, *rest, whole)]
            found.append((here.at_z(device), source, buffer.at[slots], (add_z, *rest), whole, sends, receives))
            return found
        if item in late:
            at = late.index(item)
            steps = {
                "all": ((0, (0,), whole, late_z.at[at]),),
                "first": ((1, (0, 1), first, late_one_y.at[at]), (2, (0, 2), second, late_one_x.at[at])),
                "second": ((2, (0, 1, 2), first, late_two_x.at[at]), (1, (0, 1, 2), second, late_two_y.at[at])),
            }[kind]
        else:
            steps = {
                "first": ((2, (2,), first, "one_x"), (1, (1,), second, "one_y")),
                "second": ((1, (1, 2), first, "two_y"), (2, (1, 2), second, "two_x")),
                "all": ((0, (0, 1, 2), whole, "from_z"),),
            }[kind]
            steps = [(*step[:3], at_home(step[3], item)) for step in steps]
        for axis, fixed, part, landing in steps:
            for step in range(1, here.size(axis)):
                target = here.moved(axis, step)
                index = tuple(target[a] if a in fixed else slice(None) for a in range(3))
                added = tuple(here.at[a] if a in fixed else slice(None) for a in range(3))
                source = own.at[(*index, part)]
                found.append((here.device(target), source, landing.at[step - 1], added, part, None, None))
        return found

    def copies(item, phase):
        found = []
        for at, (device, source, landing, added, part, sends, receives) in enumerate(moves(item, phase)):
            copy = pltpu.make_async_remote_copy(
                src_ref=source,
                dst_ref=landing,
                send_sem=send_sem.at[item, phase, at],
                recv_sem=recv_sem.at[item, phase, at],
                device_id=device,
                device_id_type=MESH,
            )
            found.append((sends, receives, copy, added, part, landing))
        return found

    def add_core(item):
        own, brought = at_home("own", item), at_home("core", item)

        def body(at, carry):
            z, y, x = at // (ny * nx), at // nx % ny, at % nx
            value = own[z, y, x]
            for step in range(tensor - 1):
                value = value + brought[step, z, y, x]
            own[z, y, x] = value
            return carry

        if tensor > 1:
            lax.fori_loop(0, nz * ny * nx, body, 0)

    def add_in(item, landing, added, part):
        own = at_home("own", item)
        sizes, starts = [], []
        for axis, at in enumerate(added):
            if isinstance(at, slice):
                sizes.append(dims[axis])
                starts.append(0)
            elif hasattr(at, "start"):
                sizes.append(at.size)
                starts.append(at.start)
            else:
                sizes.append(None)
                starts.append(at)
        loops = 1
        for size in sizes:
            loops *= size or 1

        def body(at, carry):
            place, inner, rest = [], [], at
            for size, start in reversed(list(zip(sizes, starts))):
                if size is None:
                    place.insert(0, start)
                else:
                    place.insert(0, start + rest % size)
                    inner.insert(0, rest % size)
                    rest = rest // size
            where = (*place, part)
            own[where] = own[where] + (landing[tuple(inner)] if inner else landing[...])
            return carry

        if loops == 1:
            body(0, 0)
        else:
            lax.fori_loop(0, loops, body, 0)

    def put_total(item, arrived):
        wide = columns(item)
        parts_of = {}
        for landing, part in arrived:
            parts_of.setdefault((part.start, part.size), []).append(landing)
        for (start, size), landings in parts_of.items():
            part = pl.ds(start, size)
            value = at_home("own", item)[(*here.at, part)].astype(jnp.float32)
            for landing in landings:
                value = value + landing[...].astype(jnp.float32)
            total_ref[part, wide] = value
        if items[item][0] == "vec":
            return
        for at, spans in enumerate(layout.matrices()):
            for start, size in spans:
                low_end, high_end = max(start, wide.start), min(start + size, wide.start + wide.size)
                if low_end < high_end:
                    square = total_ref[:, pl.ds(low_end, high_end - low_end)]
                    square = square * square
                    col_sum[0, :, pl.ds(low_end, high_end - low_end)] = jnp.sum(square, axis=0, keepdims=True)
                    found = jnp.sum(square, axis=1, keepdims=True)
                    row_sum[0] = row_sum[0] + jnp.where(lane == at, found, 0.0)

    sent = []
    lane = lax.broadcasted_iota(jnp.int32, (1, LANES), 1)
    row_sum[0] = jnp.zeros_like(row_sum[0])
    guarded_sent = []
    late = [at for at in LATE_ITEMS if items[at][0] in ("one", "two")]

    def exchange(kind, phase, axes, buffer, landing):
        moved = []
        for at, device in enumerate(here.peers(*axes)):
            copy = pltpu.make_async_remote_copy(
                src_ref=buffer.at[phase],
                dst_ref=landing.at[phase, at],
                send_sem=sum_send.at[kind, phase, at],
                recv_sem=sum_recv.at[kind, phase, at],
                device_id=device,
                device_id_type=MESH,
            )
            copy.start()
            moved.append(copy)
        sent.extend(moved)

        def finish():
            value = buffer[phase]
            for at, copy in enumerate(moved):
                copy.wait_recv()
                value = value + landing[phase, at]
            buffer[phase + 1] = value

        return finish

    def hand_over(item, step, source, sem):
        return pltpu.make_async_remote_copy(
            src_ref=source,
            dst_ref=at_home("core", item).at[step - 1],
            send_sem=sem,
            recv_sem=core_sem.at[item, step - 1],
            device_id=here.device(here.moved(3, step)),
            device_id_type=MESH,
        )

    arriving = {}

    def keep_own(item, value):
        at_home("own", item)[...] = value.reshape(nz, ny, nx, own_rows, value.shape[1])

    out_items = [at for at, item in enumerate(items) if item[0] == "out"]
    qkv_items = [at for at, item in enumerate(items) if item[0] == "qkv"]
    vec_item = count - 1
    per_rank = len(qkv_items)
    steps_in_all = per_rank * tensor

    def rank_at(step):
        return lax.rem(here.rank + step, tensor)

    def pair_loads(at):
        turn_at, place = divmod(at, tensor)
        pair = rank_at(place + 1) * per_rank + turn_at
        column = pl.ds(pl.multiple_of(pair * 3 * LANES, LANES), 3 * LANES)
        near = at % 2
        return pair, column, [
            pltpu.make_async_copy(
                weight_qkv.at[rank_at(place + 1), turn_at], qkv_buf.at[near], load_sem.at[0, near]
            ),
            pltpu.make_async_copy(projected.at[:, column], head_buf.at[near], load_sem.at[1, near]),
        ]

    def out_task():
        fetch = [
            pltpu.make_async_copy(weight_out.at[rank, 0], out_buf.at[rank], load_sem.at[2, 0])
            for rank in range(tensor)
        ]
        for copy in fetch:
            copy.start()
        far_load(2).wait()
        turn(back_one, back_turned)
        far_load(0).wait()
        for copy in pair_loads(0)[2]:
            copy.start()
        size = out_stage.shape[5]
        item = out_items[0]
        for step in range(1, tensor + 1):
            column = pl.ds(pl.multiple_of(rank_at(step) * size, LANES), size)
            value = dot(back_turned[...], mixed[:, column]).astype(low)
            if step < tensor:
                out_stage[step - 1] = value.reshape(nz, ny, nx, own_rows, size)
                copy = hand_over(item, step, out_stage.at[step - 1], stage_sem.at[item, step - 1])
                copy.start()
                sent.append(copy)
                arriving.setdefault(item, []).append(copy)
            else:
                keep_own(item, value)
        for copy in fetch:
            copy.wait()
        for rank in range(tensor):
            weight = out_buf[rank].reshape(width, size)
            grad_mixed[:, pl.ds(rank * size, size)] = dot(back_one[...], weight).astype(low)
        far_load(1).wait()

    def state_task():
        def fill(refs, other):
            square[...] = jnp.full_like(square, other)
            base = 0
            for ref in refs:
                square[pl.ds(base, ref.shape[0]), :] = ref[...]
                base += ref.shape[0]
            return square[...].T

        for at in range(3, 7):
            far_load(at).wait()
        turned[0] = fill(row_states, 1.0)
        turned[1] = fill((second_ref,), 1.0)
        turned[2] = fill((vector_ref,), 0.0)

    staged = {}

    def pair_task(at):
        turn_at, place = divmod(at, tensor)
        pair, column, loads = pair_loads(at)
        for copy in loads:
            copy.wait()
        if at + 1 < steps_in_all:
            for copy in pair_loads(at + 1)[2]:
                copy.start()
        near = at % 2
        grads = grad_mixed[:, pl.ds(pl.multiple_of(pair * LANES, LANES), LANES)]
        value = attend_pair_back(head_buf[near], bias_ref[...], grads)
        head_sums[:, column] = jnp.sum(value.astype(jnp.float32), axis=0, keepdims=True)
        weight = qkv_buf[near].reshape(width, 3 * LANES)
        term = dot(value, weight, CONTRACT_LAST)
        if at == 0:
            input_grad[...] = term
        else:
            input_grad[...] += term
        item = qkv_items[turn_at]
        mine = place + 1 == tensor
        if not mine and 0 in staged:
            staged[0].wait_send()
        grad = dot(low_turned[...], value).astype(low)
        if mine:
            keep_own(item, grad)
        else:
            qkv_stage[...] = grad.reshape(nz, ny, nx, own_rows, 3 * LANES)
        if not mine:
            copy = hand_over(item, place + 1, qkv_stage, stage_sem.at[item, place])
            copy.start()
            staged[0] = copy
            arriving.setdefault(item, []).append(copy)

    def grad_store():
        return pltpu.make_async_copy(input_grad, input_grad_out, far_sem.at[7])

    def last_task():
        step_rows = row_buf.shape[2]

        def fetch(at):
            near = lax.rem(at, 2)
            part = pl.ds(pl.multiple_of(at * step_rows, step_rows), step_rows)
            return [
                pltpu.make_async_copy(source.at[part, :], row_buf.at[which, near], load_sem.at[which, near])
                for which, source in enumerate((input_ref, middle_ref))
            ]

        for copy in fetch(0):
            copy.start()

        def body(at, sums):
            for copy in fetch(at):
                copy.wait()

            @pl.when(at + 1 < rows // step_rows)
            def _():
                for copy in fetch(at + 1):
                    copy.start()

            near = lax.rem(at, 2)
            part = pl.ds(pl.multiple_of(at * step_rows, step_rows), step_rows)
            normed, inverse = norm_rows(row_buf[0, near])
            grad_low = input_grad[part, :]
            scaled = grad_low * table[0:1, :]
            first = jnp.mean(scaled, axis=1, keepdims=True)
            second = jnp.mean(scaled * normed, axis=1, keepdims=True)
            input_grad[part, :] = row_buf[1, near] + inverse * (scaled - first - normed * second)
            terms = (grad_low * normed, grad_low)
            return tuple(old + jnp.sum(term, axis=0, keepdims=True) for old, term in zip(sums, terms))

        zero = jnp.zeros((1, width), jnp.float32)
        found = lax.fori_loop(0, rows // step_rows, body, (zero, zero))
        grad_store().start()
        table_grad_ref[...] = jnp.zeros_like(table_grad_ref)
        for at in range(2):
            table_grad_ref[at : at + 1, :] = found[at]
        for pair in range(width // LANES):
            for kind, row in ((0, 2), (2, 3)):
                table_grad_ref[row : row + 1, pl.ds(pair * LANES, LANES)] = head_sums[
                    :, pl.ds((pair * 3 + kind) * LANES, LANES)
                ]
        for at, row in enumerate((4, 5, 6, VEC - 1)):
            table_grad_ref[row : row + 1, :] = vec_sums[at : at + 1, :]
        for at in range(VEC - 8):
            table_grad_ref[7 + at : 8 + at, :] = pre_sums[:, pl.ds(at * width, width)]
        value = table_grad_ref[...].T.astype(low)
        vec_stage[...] = value.reshape(nz, ny, nx, own_rows, LANES)
        for step in range(1, tensor):
            copy = hand_over(vec_item, step, vec_stage, stage_sem.at[vec_item, step - 1])
            copy.start()
            sent.append(copy)
            arriving.setdefault(vec_item, []).append(copy)
        keep_own(vec_item, value)

    for at in (2, 0, 1, 3, 4, 5, 6):
        far_load(at).start()
    here.barrier(((0, 3), (1, 2)))
    local = {}
    for item, (name, _, _, source) in enumerate(items):
        if name in ("one", "two"):
            array = sum_one if name == "one" else sum_two
            copy = pltpu.make_async_copy(
                array.at[source], at_home("own", item), local_sem.at[item]
            )
            copy.start()
            local[item] = copy

    def advance(item, phase):
        last = len(phases(item))
        if phase > 0:
            arrived = []
            for _, receives, copy, added, part, landing in copies(item, phase - 1):

                def take(copy=copy, landing=landing, added=added, part=part):
                    copy.wait_recv()
                    if phase < last:
                        add_in(item, landing, added, part)

                guarded(receives, take)
                arrived.append((landing, part))
            if phase == last:
                put_total(item, arrived)
        elif item in local:
            local[item].wait()
        else:
            for copy in arriving.get(item, ()):
                copy.wait_recv()
            add_core(item)
        if phase < last:
            for sends, _, copy, *_ in copies(item, phase):
                guarded(sends, copy.start)
                guarded_sent.append((sends, copy))

    steps = Steps()
    owner = {item: ("out", 0) for item in out_items}
    owner |= {item: ("pair", tensor * (at + 1) - 1) for at, item in enumerate(qkv_items)}
    owner[vec_item] = ("last", 0)
    for item, (name, _, size, _) in enumerate(items):
        share = size / layout.total * UNIT
        across = ny * nx if item in late else 1
        along = 1 if item in late else nz
        lengths = {
            "pair": (share * across, "end"),
            "mid": (share * across * 2, "mid"),
            "back": (share * across * 2, "end"),
            "all": (share * across * nz, "end"),
            "first": (share * along, "xy"),
            "second": (share * along / 2, "xy"),
        }
        if item in late:
            lengths |= {"first": (share, "xy"), "second": (share / 2, "xy")}
        early = item not in owner
        kinds = phases(item)
        for phase in range(len(kinds) + 1):
            after = [("copy", item, phase - 1)] if phase else []
            waits = [(item, phase - 1)] if phase else []
            if phase == 0 and early and item >= DEPTH + len(late):
                after = [("copy", item - DEPTH, 1)]
            if phase == 0 and not early:
                after, waits = [owner[item]], [("core", owner[item])]
            starts = []
            if phase < len(kinds):
                length, link = lengths[kinds[phase]]
                starts = [((item, phase), link, length)]
            steps.add(
                ("copy", item, phase),
                functools.partial(advance, item, phase),
                PUMP * (1.5 if phase == 1 else 1.0),
                (0.5 if phase == 0 and early else 0.0),
                after,
                waits,
                starts,
            )
    steps.add(("state", 0), state_task, 1.0, 2.0)
    steps.add(("out", 0), out_task, 8.0, 1.0, (), (), [(("core", ("out", 0)), "core", CORE_UNIT / 12)])
    for at in range(steps_in_all):
        after = [("pair", at - 1) if at else ("out", 0)]
        starts = [(("core", ("pair", at)), "core", CORE_UNIT / 24)]
        steps.add(("pair", at), functools.partial(pair_task, at), 6.0, 1.0, after, (), starts)
    steps.add(
        ("last", 0), last_task, 4.0, 1.0, [("pair", steps_in_all - 1)], (), [(("core", ("last", 0)), "core", 1.0)]
    )
    steps.run()
    sent.extend(staged.values())

    decay_rate = 1.0 - STEP ** (-0.8)
    keep_old = 1.0 - decay_rate
    long = layout.sizes["one"] * tensor
    matrices = layout.matrices()
    finish_row = exchange(0, 0, (3,), row_sum, row_in)
    finish_col = exchange(1, 0, (0,), col_sum, col_in)
    vec_start = layout.start["vec"]
    table_grad = total_ref[:, pl.ds(vec_start, LANES)]
    second_new = decay_rate * turned[1] + keep_old * (table_grad * table_grad + EPS_ONE)
    second_new_ref[...] = second_new
    vector_update = table_grad * lax.rsqrt(second_new)
    vector_sums = jnp.sum(vector_update * vector_update, axis=0, keepdims=True) / tensor
    vector_weight = jnp.sum(turned[2] * turned[2], axis=0, keepdims=True) / tensor
    weight_sums = [total_of(jnp.sum(weights[0][...] * weights[0][...], axis=0))]
    weight_sums += [total_of(ref[...] * ref[...]) for ref in weights[1:]]
    finish_row()
    row_counts = pick([jnp.full((1, 1), 1.0 / size, jnp.float32) for size in (width, width, width, width, long, long)], lane)
    row_new = decay_rate * turned[0] + keep_old * (row_sum[1] * row_counts + EPS_ONE)
    row_new_ref[...] = row_new
    finish_col()
    exchange(1, 1, (1, 2), col_sum, col_in)()
    for at, spans in enumerate(matrices):
        for place, (start, size) in enumerate(spans):
            if at < 3:
                old = col_states[0][at : at + 1, pl.ds(place * LANES, LANES)]
            else:
                old = col_states[at - 2][...]
            fresh = keep_old * (col_sum[2, :, pl.ds(start, size)] / width + EPS_ONE)
            col_new_ref[:, pl.ds(start, size)] = decay_rate * old + fresh
    ratios = []
    means = []
    for at, spans in enumerate(matrices):
        row_at = row_new[:, at : at + 1]
        ratio = 0.0
        for start, size in spans:
            value = total_ref[:, pl.ds(start, size)]
            col_at = col_new_ref[:, pl.ds(start, size)]
            ratio = ratio + total_of(value * value / (row_at * col_at))
        ratios.append(ratio)
        if at in (3, 5):
            means.append(jnp.sum(col_at, axis=1, keepdims=True) / (nz * ny * nx))
        else:
            means.append(jnp.sum(row_at, axis=0, keepdims=True) / tensor)
    small[0] = jnp.concatenate(
        [pick(ratios + means + weight_sums, lane), vector_sums, vector_weight, jnp.zeros((5, LANES), jnp.float32)], axis=0
    )
    exchange(2, 0, (0, 3), small, small_in)()
    exchange(2, 1, (1, 2), small, small_in)()
    sums_ref[...] = small[2]
    grad_store().wait()
    for copy in sent:
        copy.wait_send()
    for condition, copy in guarded_sent:
        guarded(condition, copy.wait_send)


def backward(dims, tensor, layout, large, near, weights, states):
    rows, width = large[-1].shape
    own_rows = width // (dims[0] * dims[1] * dims[2])
    half_rows = own_rows // 2
    columns = layout.columns
    items = []
    for block in range(layout.sizes["one"] // BLOCK):
        for name in ("two", "one"):
            items.append((name, layout.start[name] + block * BLOCK, BLOCK, block))
    items.append(("out", layout.start["out"], columns, 0))
    for start in range(0, 3 * columns, 3 * LANES):
        items.append(("qkv", layout.start["qkv"] + start, 3 * LANES, start))
    items.append(("vec", layout.start["vec"], LANES, 0))
    nz, ny, nx = dims
    peers = max(1, nz - 1, ny + nx - 2)
    group = max(1, nz * tensor - 1, ny * nx - 1)
    others = max(1, tensor - 1)
    offset = layout.total
    late = max(1, len(LATE_ITEMS))
    line = 5 if nz == 4 else nz - 1
    groups = (
        (2 * layout.sizes["one"] // BLOCK, BLOCK),
        (1, columns),
        (columns // LANES, 3 * LANES),
        (1, LANES),
    )
    leads = (
        (nz, ny, nx, own_rows),
        (nx - 1, nz, ny, half_rows),
        (ny - 1, nz, nx, half_rows),
        (ny - 1, nz, half_rows),
        (nx - 1, nz, half_rows),
        (line, own_rows),
    )
    low, full = jnp.bfloat16, jnp.float32
    anywhere = pl.BlockSpec(memory_space=pl.ANY)
    inside = pl.BlockSpec(memory_space=pltpu.VMEM)

    def hold(*shape):
        return pltpu.VMEM(tuple(max(1, size) for size in shape), low)

    sums = offset - LANES
    count = len(items)
    return pl.pallas_call(
        functools.partial(backward_kernel, dims, tensor, tuple(items), layout),
        name="backward",
        out_shape=[
            jax.ShapeDtypeStruct((rows, width), full),
            jax.ShapeDtypeStruct((own_rows, offset), full),
            jax.ShapeDtypeStruct((1, sums), full),
            jax.ShapeDtypeStruct((own_rows, LANES), full),
            jax.ShapeDtypeStruct((own_rows, LANES), full),
            jax.ShapeDtypeStruct((8, LANES), full),
        ],
        in_specs=[anywhere] * len(large) + [inside] * len(near) + [anywhere] * 4 + [inside] * len(states),
        out_specs=[anywhere] + [inside] * 5,
        scratch_shapes=[
            *(
                hold(number if lead is leads[0] or at else number - late, *lead, size)
                for lead in leads
                for at, (number, size) in enumerate(groups)
            ),
            *(hold(number, others, nz, ny, nx, own_rows, size) for number, size in groups[1:]),
            pltpu.VMEM((rows, width), full),
            hold(late, line, ny, nx, own_rows, BLOCK),
            hold(late, ny - 1, nx, half_rows, BLOCK),
            hold(late, nx - 1, ny, half_rows, BLOCK),
            hold(late, nx - 1, half_rows, BLOCK),
            hold(late, ny - 1, half_rows, BLOCK),
            pltpu.VMEM((3, 1, sums), full),
            pltpu.VMEM((2, max(1, nz - 1, ny * nx - 1), 1, sums), full),
            pltpu.VMEM((2, own_rows, LANES), full),
            pltpu.VMEM((1, others, own_rows, LANES), full),
            pltpu.VMEM((3, 8, LANES), full),
            pltpu.VMEM((2, group, 8, LANES), full),
            pltpu.VMEM((LANES, own_rows), full),
            pltpu.VMEM((3, own_rows, LANES), full),
            *[hold(rows, width)] * 2,
            *(pltpu.VMEM(weight.shape, full) for weight in weights),
            hold(width, rows),
            hold(width, rows),
            hold(rows, width),
            hold(tensor, *dims, own_rows, columns),
            hold(2, *dims, own_rows, 3 * LANES),
            hold(2, rows, 3 * LANES),
            pltpu.VMEM((2, 2, LANES // 2, width), full),
            hold(others, *dims, own_rows, columns),
            hold(*dims, own_rows, 3 * LANES),
            hold(*dims, own_rows, LANES),
            pltpu.VMEM((1, 3 * width), full),
            pltpu.VMEM((LANES, width), full),
            pltpu.SemaphoreType.DMA((3, 2)),
            pltpu.SemaphoreType.DMA((count, others)),
            pltpu.SemaphoreType.DMA((count, others)),
            pltpu.SemaphoreType.DMA((count,)),
            pltpu.SemaphoreType.DMA((count, 5, peers)),
            pltpu.SemaphoreType.DMA((count, 5, peers)),
            pltpu.SemaphoreType.DMA((3, 2, group)),
            pltpu.SemaphoreType.DMA((3, 2, group)),
            pltpu.SemaphoreType.DMA((8,)),
        ],
        compiler_params=pltpu.CompilerParams(
            collective_id=1, has_side_effects=True, vmem_limit_bytes=63 << 20
        ),
    )(*large, *near, *weights, *states)


def update_kernel(layout, width, long, *refs):
    block_in, grad_in = refs[:2]
    far = refs[2:12]
    block_out, input_grad = refs[12:14]
    own_qkv, own_out, own_one, own_two, own_table = refs[14:19]
    new_qkv, new_out, new_one, new_two, new_vectors, second_new = refs[19:25]
    qkv_row, qkv_col, out_row, out_col, one_row, one_col, two_row, two_col = refs[25:33]
    near, passing, sem = refs[33:43], refs[43:45], refs[45]
    loads = [
        pltpu.make_async_copy(source, target, sem.at[at])
        for at, (source, target) in enumerate(zip((*far, block_in, grad_in), (*near, *passing)))
    ]
    later = loads[len(far) :]
    long_copies = [
        pltpu.make_async_copy(source, target, sem.at[12 + at])
        for at, (source, target) in enumerate(zip(passing, (block_out, input_grad)))
    ]
    for copy in loads:
        copy.start()
    for copy in loads[: len(far)]:
        copy.wait()
    total_ref, col_ref, row_ref, second_ref, sums_ref, vector_ref = near[:6]
    weights = near[6:]
    lane = lax.broadcasted_iota(jnp.int32, (1, LANES), 1)

    def at(index):
        return sums_ref[0:1, index : index + 1]

    lengths = (width, width, width, width, width, long)
    means = [at(6 + m) / lengths[m] for m in range(6)]
    squares = [means[m] * at(m) for m in range(6)]
    squares = [squares[0] + squares[1] + squares[2], *squares[3:]]
    entries = (3 * width * width, width * width, width * long, width * long)
    step_size = []
    for m in range(4):
        damping = 1.0 / jnp.maximum(1.0, jnp.sqrt(squares[m] / entries[m] + 1e-06) / CLIP_LEVEL)
        step_size.append(LEARN_RATE * jnp.sqrt(at(12 + m) / entries[m] + 1e-06) * damping)
    spread = [(m, place, *span) for m, spans in enumerate(layout.matrices()) for place, span in enumerate(spans)]
    for m, place, start, size in spread:
        if m == 3:
            for load, store in zip(later, long_copies):
                load.wait()
                store.start()
        grad = total_ref[:, pl.ds(start, size)]
        col = col_ref[:, pl.ds(start, size)]
        step = step_size[max(0, m - 2)] * grad * lax.rsqrt(row_ref[:, m : m + 1] * col / means[m])
        if m < 3:
            part = slice(place * LANES, (place + 1) * LANES)
            own_qkv[m, :, part] = grad
            new_qkv[m, :, part] = weights[0][m, :, part] - step
            qkv_col[m : m + 1, part] = col
        else:
            own, new, state = (
                (own_out, new_out, out_row),
                (own_one, new_one, one_col),
                (own_two, new_two, two_row),
            )[m - 3]
            own[...] = grad
            new[...] = weights[m - 2][...] - step
            state[...] = col
    row_flat = row_ref[...].T
    qkv_row[...] = row_flat[0:3]
    out_col[...] = row_flat[3:4]
    one_row[...] = row_flat[4:5]
    two_col[...] = row_flat[5:6]

    wide = (lane >= 7) & (lane < VEC - 1)
    counts = jnp.where(wide, float(long), float(width))

    def grouped(values):
        inside = jnp.sum(jnp.where(wide, values, 0.0), axis=1, keepdims=True)
        return jnp.where(wide, inside, values)

    table_grad = total_ref[:, pl.ds(layout.start["vec"], LANES)]
    update = table_grad * lax.rsqrt(second_ref[...])
    norm = jnp.sqrt(grouped(sums_ref[1:2, :]) / counts + 1e-06)
    size = jnp.sqrt(grouped(sums_ref[2:3, :]) / counts + 1e-06)
    change = LEARN_RATE * size / jnp.maximum(1.0, norm / CLIP_LEVEL) * update
    own_table[...] = table_grad.T[:VEC]
    new_vectors[...] = vector_ref[...] - change.T[:VEC]
    second_new[...] = second_ref[...].T[:VEC]
    for copy in long_copies:
        copy.wait()


def update_weights(layout, width, long, columns, hidden, rows, results, values, vectors, weights):
    full = jnp.float32
    shapes = [
        *(result.shape for result in results),
        (3, rows, columns),
        (rows, columns),
        (rows, hidden),
        (rows, hidden),
        (VEC, rows),
        (3, rows, columns),
        (rows, columns),
        (rows, hidden),
        (rows, hidden),
        (VEC, rows),
        (VEC, rows),
        (3, rows),
        (3, columns),
        (1, columns),
        (1, rows),
        (1, rows),
        (1, hidden),
        (1, hidden),
        (1, rows),
    ]
    far = (*values, vectors, *weights)
    anywhere = pl.BlockSpec(memory_space=pl.ANY)
    inside = pl.BlockSpec(memory_space=pltpu.VMEM)
    return pl.pallas_call(
        functools.partial(update_kernel, layout, width, long),
        name="update_weights",
        out_shape=[jax.ShapeDtypeStruct(shape, full) for shape in shapes],
        in_specs=[anywhere] * (2 + len(far)),
        out_specs=[anywhere] * 2 + [inside] * (len(shapes) - 2),
        scratch_shapes=[
            *(pltpu.VMEM(array.shape, full) for array in (*far, *results)),
            pltpu.SemaphoreType.DMA((4 + len(far),)),
        ],
        compiler_params=pltpu.CompilerParams(vmem_limit_bytes=63 << 20),
    )(*results, *far)


def on_device(
    inputs,
    cotangent,
    token_mask,
    w_qkv,
    w_out,
    w_fc1,
    w_fc2,
    vectors,
    qkv_row,
    qkv_col,
    out_row,
    out_col,
    fc1_row,
    fc1_col,
    fc2_row,
    fc2_col,
    vec_second,
):
    tensor_count = lax.axis_size("tensor")
    dims = grid_of(lax.axis_size("fsdp"))
    width = inputs.shape[1]
    own_rows, columns = w_qkv.shape[1:]
    hidden = w_fc1.shape[1]
    weights = (w_qkv, w_out.T, w_fc1, w_fc2.T)
    (
        weight_qkv,
        _,
        weight_out,
        *_,
        block_out,
        grad_middle,
        back_one,
        mixed_rows,
        low_turned,
        projected,
        grad_one,
        grad_two,
        table,
        vec_sums,
        pre_sums,
        bias_column,
    ) = forward(dims, tensor_count, inputs, cotangent, token_mask, vectors, weights)
    layout = Layout(columns, hidden, ("two", "one", "out", "qkv", "vec"))
    row_states = (qkv_row, out_col[None], fc1_row[None], fc2_col[None])
    col_states = (qkv_col, out_row[None], fc1_col[None], fc2_row[None])
    input_grad, *values = backward(
        dims,
        tensor_count,
        layout,
        (
            grad_two,
            grad_one,
            weight_qkv,
            weight_out,
            projected,
            inputs,
            grad_middle,
            mixed_rows,
            low_turned,
            back_one,
        ),
        (bias_column, table, vec_sums, pre_sums),
        weights,
        (*row_states, *col_states, vec_second, vectors),
    )
    outs = update_weights(
        layout, width, FF, columns, hidden, own_rows, (block_out, input_grad), values, vectors, weights
    )
    outs = [out.reshape(-1) if out.shape[0] == 1 else out for out in outs]
    for at in (3, 5, 8, 10):
        outs[at] = outs[at].T
    return (*outs[:12], *outs[13:], outs[12])


def solution(mesh):
    in_specs = (
        P(("fsdp", "tensor"), None),
        P(("fsdp", "tensor"), None),
        P("fsdp", None),
        P(None, "fsdp", "tensor"),
        P("tensor", "fsdp"),
        P("fsdp", "tensor"),
        P("tensor", "fsdp"),
        P(None, "fsdp"),
        P(None, "fsdp"),
        P(None, "tensor"),
        P("tensor"),
        P("fsdp"),
        P("fsdp"),
        P("tensor"),
        P("tensor"),
        P("fsdp"),
        P(None, "fsdp"),
    )
    out_specs = (
        P(("fsdp", "tensor"), None),
        P(("fsdp", "tensor"), None),
        P(None, "fsdp", "tensor"),
        P("tensor", "fsdp"),
        P("fsdp", "tensor"),
        P("tensor", "fsdp"),
        P(None, "fsdp"),
        P(None, "fsdp", "tensor"),
        P("tensor", "fsdp"),
        P("fsdp", "tensor"),
        P("tensor", "fsdp"),
        P(None, "fsdp"),
        P(None, "fsdp"),
        P(None, "tensor"),
        P("tensor"),
        P("fsdp"),
        P("fsdp"),
        P("tensor"),
        P("tensor"),
        P("fsdp"),
        P(None, "fsdp"),
    )
    return jax.shard_map(
        on_device, mesh=mesh, in_specs=in_specs, out_specs=out_specs, check_vma=False
    )
```

```python
import functools

import jax
import jax.numpy as jnp
from jax import lax
from jax.experimental import pallas as pl
from jax.experimental.pallas import tpu as pltpu
from jax.sharding import PartitionSpec as P

HEAD_DIM = 64
FF = 4096
STEP = 20
VEC = 12
LANES = 128

EPS_NORM = 1e-05
EPS_ONE = 1e-30
CLIP_LEVEL = 1.0
LEARN_RATE = 0.5
MESH = pl.DeviceIdType.MESH
LOG2E = 1.4426950408889634
CONTRACT_LAST = (((1,), (1,)), ((), ()))


def grid_of(count):
    return {16: (4, 2, 2), 32: (2, 4, 4)}.get(count, (count, 1, 1))


class Place:
    def __init__(self, dims, tensor):
        self.dims = dims
        self.tensor = tensor
        fsdp = lax.axis_index("fsdp")
        _, ny, nx = dims
        self.at = (fsdp // (ny * nx), (fsdp // nx) % ny, fsdp % nx)
        self.rank = lax.axis_index("tensor")

    def moved(self, axis, step):
        place = list(self.at) + [self.rank]
        size = (*self.dims, self.tensor)[axis]
        place[axis] = lax.rem(place[axis] + step + size, size)
        return tuple(place)

    def device(self, place):
        z, y, x, rank = place
        return {"fsdp": (z * self.dims[1] + y) * self.dims[2] + x, "tensor": rank}

    def size(self, axis):
        return (*self.dims, self.tensor)[axis]

    def line(self):
        z = self.at[0]
        pair = z // 2 * 2
        middle = (z == 1) | (z == 2)
        return pair, 2 - pair, z + 1 - 2 * (z % 2), middle

    def at_z(self, z):
        return self.device((z, self.at[1], self.at[2], self.rank))

    def peers(self, *axes):
        places = [()]
        for axis in axes:
            places = [(*steps, step) for steps in places for step in range(self.size(axis))]
        found = []
        for steps in places[1:]:
            place = list(self.at) + [self.rank]
            for axis, step in zip(axes, steps):
                place[axis] = lax.rem(place[axis] + step, self.size(axis))
            found.append(self.device(tuple(place)))
        return found

    def barrier(self, groups):
        sem = pltpu.get_barrier_semaphore()
        count = 0
        for axes in groups:
            for device in self.peers(*axes):
                pl.semaphore_signal(sem, inc=1, device_id=device, device_id_type=MESH)
                count += 1
        if count:
            pl.semaphore_wait(sem, count)


def norm_rows(values):
    average = jnp.mean(values, axis=1, keepdims=True)
    center = values - average
    inverse = lax.rsqrt(jnp.mean(center * center, axis=1, keepdims=True) + EPS_NORM)
    return center * inverse, inverse


def dot(left, right, dims=(((1,), (0,)), ((), ()))):
    return lax.dot_general(left, right, dims, preferred_element_type=jnp.float32)


def turn(source, target):
    for start in range(0, source.shape[1], LANES):
        target[pl.ds(start, LANES), :] = source[:, pl.ds(start, LANES)].T


def attend_pair(heads, bias):
    mixed = []
    for head in range(2):
        query, key, value = (
            heads[:, kind * LANES + head * HEAD_DIM : kind * LANES + (head + 1) * HEAD_DIM] for kind in range(3)
        )
        scores = dot(query, key, CONTRACT_LAST) * (HEAD_DIM ** (-0.5) * LOG2E) + bias
        raised = jnp.exp2(scores - jnp.max(scores, axis=1, keepdims=True))
        summed = jnp.sum(raised, axis=1, keepdims=True)
        attention = (raised * (1.0 / summed)).astype(jnp.bfloat16)
        mixed.append(dot(attention, value).astype(jnp.bfloat16))
    return jnp.concatenate(mixed, axis=1)


def guarded(condition, run):
    if condition is None:
        run()
    else:
        pl.when(condition)(run)


def along_z(count):
    return ("pair", "mid", "back") if count == 4 else ("all",)


class Steps:
    def __init__(self):
        self.steps = {}

    def add(self, name, run, time, rank, after=(), waits=(), starts=()):
        self.steps[name] = (run, time, rank, tuple(after), tuple(waits), tuple(starts))

    def arrange(self):
        now, free, arrival, done, order = 0.0, {}, {}, set(), []
        left = list(self.steps)
        while left:
            best, soonest = None, None
            for name in left:
                _, time, rank, after, waits, _ = self.steps[name]
                if any(other not in done for other in after) or any(wait not in arrival for wait in waits):
                    continue
                ready = max([arrival[wait] for wait in waits], default=0.0)
                if ready <= now:
                    if best is None or rank < self.steps[best][2]:
                        best = name
                elif soonest is None or ready < soonest:
                    soonest = ready
            if best is None:
                now = soonest
                continue
            _, time, _, _, _, starts = self.steps[best]
            now += time
            for transfer, link, length in starts:
                begin = max(now, free.get(link, 0.0))
                free[link] = begin + length
                arrival[transfer] = begin + length + LATENCY
            done.add(best)
            left.remove(best)
            order.append(best)
        return order, now

    def run(self):
        for name in self.arrange()[0]:
            self.steps[name][0]()


class Gather:
    def __init__(self, here, pack_ref, outs, parts, local_sem, send_sem, recv_sem):
        self.here = here
        self.pack = pack_ref
        self.outs = outs
        self.rows = pack_ref.shape[0]
        self.parts = parts
        self.late = [len(parts) - at for at in LATE_PARTS if at < len(parts)]
        self.sems = (local_sem, send_sem, recv_sem)
        self.own = (*here.at, here.rank)
        self.sent = []

    def region(self, item, part, place, free):
        out, _, chunk, _ = self.parts[item]
        index = tuple(slice(None) if a in free else place[a] for a in range(3))
        lead = () if chunk is None else (place[3], chunk)
        return self.outs[out].at[(*lead, *index, part)]

    def shard(self, item, part):
        _, offset, _, size = self.parts[item]
        return self.pack.at[part, pl.ds(offset, size)]

    def phases(self, item):
        lengthwise = ("all",)
        across = ("first", "second")
        order = (*across, *lengthwise) if item in self.late else (*lengthwise, *across)
        return order if self.parts[item][2] is None else (*order, "core")

    def moves(self, item, phase):
        here, own = self.here, self.own
        kind = self.phases(item)[phase]
        late = item in self.late
        whole, half = pl.ds(0, self.rows), self.rows // 2
        first, second = pl.ds(0, half), pl.ds(half, half)
        found = []
        if kind in ("pair", "mid", "back"):
            free = (1, 2) if late else ()
            pair, far, near, middle = here.line()

            def blocks(z):
                return self.region(item, whole, (z, *own[1:]), free)

            if kind == "pair":
                sent = self.shard(item, whole) if phase == 0 else blocks(own[0])
                found.append((here.at_z(near), sent, blocks(own[0]), blocks(near), None, None))
            elif kind == "mid":
                pairs = blocks(pl.ds(pair, 2))
                found.append((here.at_z(3 - own[0]), pairs, pairs, blocks(pl.ds(far, 2)), middle, middle))
            else:
                pairs = blocks(pl.ds(far, 2))
                outside = jnp.logical_not(middle)
                found.append((here.at_z(near), pairs, pairs, pairs, middle, outside))
            return found
        before = () if late else (0,)
        steps = {
            "all": ((0, (1, 2) if late else (), whole),),
            "first": ((2, before, first), (1, before, second))
            if late
            else ((1, before, first), (2, before, second)),
            "second": ((1, (*before, 2), first), (2, (*before, 1), second))
            if late
            else ((2, (*before, 1), first), (1, (*before, 2), second)),
            "core": ((3, (0, 1, 2), whole),),
        }[kind]
        for axis, free, part in steps:
            for step in range(1, here.size(axis)):
                place = self.region(item, part, own, free)
                sent = self.shard(item, part) if phase == 0 else place
                landed = self.region(item, part, here.moved(axis, -step), free)
                found.append((here.device(here.moved(axis, step)), sent, place, landed, None, None))
        return found

    def copies(self, item, phase, landing):
        found = []
        for at, (device, sent, place, landed, sends, receives) in enumerate(self.moves(item, phase)):
            copy = pltpu.make_async_remote_copy(
                src_ref=landed if landing else sent,
                dst_ref=landed if landing else place,
                send_sem=self.sems[1].at[item, phase, at],
                recv_sem=self.sems[2].at[item, phase, at],
                device_id=device,
                device_id_type=MESH,
            )
            found.append((receives if landing else sends, copy))
        return found

    def keep(self, item):
        whole = pl.ds(0, self.rows)
        return pltpu.make_async_copy(
            self.shard(item, whole), self.region(item, whole, self.own, ()), self.sems[0].at[item]
        )

    def advance(self, item, phase):
        if phase:
            for condition, copy in self.copies(item, phase - 1, True):
                guarded(condition, copy.wait_recv)
        if phase == 0:
            self.keep(item).start()
        if phase == 1:
            self.keep(item).wait()
        if phase < len(self.phases(item)):
            for condition, copy in self.copies(item, phase, False):
                guarded(condition, copy.start)
                self.sent.append((condition, copy))

    def finish(self):
        for condition, copy in self.sent:
            guarded(condition, copy.wait_send)


BLOCK = 512
DEPTH = 3
LATENCY = 1.5
UNIT = 20.0
CORE_UNIT = 40.0
LATE_PARTS = (3,)
LATE_ITEMS = (0, 1, 2)
PUMP = 0.4


def forward_kernel(dims, tensor, parts, tasks, *refs):
    input_ref, top_ref, mask_ref, vector_ref = refs[:4]
    own_weights = refs[4:8]
    outs, land = refs[8:13], refs[13:15]
    weight_qkv, weight_vec, weight_out, weight_one, weight_two = outs
    far = refs[15:20]
    projected, grad_one, grad_two, table, vec_sums, pre_sums, bias_column = refs[20:27]
    (
        block_out,
        grad_middle,
        back_one,
        mixed,
        low_one,
        low_turned,
        pack,
        keep_ref,
        square,
        vec_buf,
        qkv_buf,
        head_stage,
        out_buf,
        one_buf,
        two_buf,
        low_two,
        low_two_turned,
        back_two,
        back_two_turned,
        grad_low_two,
        hidden_bias,
        head_bias,
        one_stage,
        two_stage,
        one_keep,
        two_keep,
        other,
        active,
        grad_pre,
        load_sem,
        store_sem,
        keep_sem,
        head_sem,
        land_sem,
        far_sem,
        local_sem,
        send_sem,
        recv_sem,
    ) = refs[27:]
    near = (block_out, grad_middle, back_one, mixed, low_turned)

    def far_store(at):
        return pltpu.make_async_copy(near[at], far[at], far_sem.at[at])

    here = Place(dims, tensor)
    gather = Gather(here, pack, outs, parts, local_sem, send_sem, recv_sem)
    rows, width = input_ref.shape
    own_rows = pack.shape[0]
    per_rank = weight_qkv.shape[1]
    low = jnp.bfloat16
    step_rows = LANES

    def fill_pack():
        base = 0
        for pair in range(per_rank):
            for kind in range(3):
                part = own_weights[0][kind, :, pl.ds(pair * LANES, LANES)]
                pack[:, pl.ds(base, LANES)] = part.astype(low)
                base += LANES
        square[...] = jnp.zeros_like(square)
        square[pl.ds(0, VEC), :] = vector_ref[...]
        pack[:, pl.ds(base, LANES)] = square[...].T.astype(low)
        base += LANES
        for ref in own_weights[1:]:
            pack[:, pl.ds(base, ref.shape[1])] = ref[...].astype(low)
            base += ref.shape[1]

    def mask_row():
        return mask_ref[pl.ds(here.rank, 1), :].astype(jnp.float32)

    def mask_bias(keep):
        return jnp.where(keep > 0.0, 0.0, -1e30)

    def first_masks():
        turned = jnp.broadcast_to(mask_row(), (LANES, rows)).T
        keep_ref[...] = turned[:, 0:1]
        bias_column[...] = mask_bias(turned[:, 0:1])

    def row_steps(body, carry):
        return lax.fori_loop(
            0, rows // step_rows, lambda at, c: body(pl.ds(pl.multiple_of(at * step_rows, step_rows), step_rows), c), carry
        )

    def load(source, buffer, sem):
        return pltpu.make_async_copy(source, buffer, sem)

    def first_norm():
        first_masks()
        copy = load(weight_vec, vec_buf, load_sem.at[7])
        copy.start()
        copy.wait()
        whole = vec_buf[...].reshape(width, LANES).astype(jnp.float32).T
        table[...] = whole[:16]
        for at in range(VEC - 8):
            hidden_bias[:, pl.ds(at * width, width)] = whole[7 + at : 8 + at]
        for pair in range(width // LANES):
            for kind, row in ((0, 2), (2, 3)):
                head_bias[:, pl.ds((pair * 3 + kind) * LANES, LANES)] = whole[
                    row : row + 1, pair * LANES : (pair + 1) * LANES
                ]
            head_bias[:, pl.ds((pair * 3 + 1) * LANES, LANES)] = jnp.zeros((1, LANES), jnp.float32)

        def body(part, carry):
            normed, _ = norm_rows(input_ref[part, :])
            low_one[part, :] = (normed * table[0:1, :] + table[1:2, :]).astype(low)
            back_two[part, :] = (top_ref[part, :].astype(jnp.float32) * keep_ref[part, :]).astype(low)
            return carry

        row_steps(body, 0)
        turn(back_two, back_two_turned)

    def head_store(pair, slot):
        column = pl.ds(pl.multiple_of(pair * 3 * LANES, LANES), 3 * LANES)
        return pltpu.make_async_copy(head_stage.at[slot], projected.at[:, column], head_sem.at[slot])

    def turn_first():
        turn(low_one, low_turned)
        far_store(4).start()

    def pair_of(at):
        turn_at, place = divmod(at, tensor)
        return lax.rem(here.rank + place, tensor) * per_rank + turn_at

    def head_load(at):
        turn_at, place = divmod(at, tensor)
        source = weight_qkv.at[lax.rem(here.rank + place, tensor), turn_at]
        return load(source, qkv_buf.at[at % 2], load_sem.at[at % 2])

    def heads(at):
        head_load(at).wait()
        pair = pair_of(at)
        slot = at % 2
        column = pl.ds(pl.multiple_of(pair * 3 * LANES, LANES), 3 * LANES)
        weight = qkv_buf[slot].reshape(width, 3 * LANES)
        value = (dot(low_one[...], weight) + head_bias[:, column]).astype(low)
        if at > 1:
            head_store(pair, slot).wait()
        head_stage[slot] = value
        head_store(pair, slot).start()
        mixed[:, pl.ds(pl.multiple_of(pair * LANES, LANES), LANES)] = attend_pair(value, mask_bias(mask_row()))

    def out_load():
        return [
            load(weight_out.at[rank, 0], out_buf.at[rank], load_sem.at[2]) for rank in range(tensor)
        ]

    def second_norm():
        far_store(3).start()
        for copy in out_load():
            copy.wait()
        columns = width // tensor
        for rank in range(tensor):
            weight = out_buf[rank].reshape(width, columns)
            term = dot(mixed[:, pl.ds(rank * columns, columns)], weight, CONTRACT_LAST)
            if rank == 0:
                grad_middle[...] = term
            else:
                grad_middle[...] += term

        def body(part, carry):
            middle = input_ref[part, :] + (grad_middle[part, :] + table[4:5, :]) * keep_ref[part, :]
            grad_middle[part, :] = middle
            normed, _ = norm_rows(middle)
            low_two[part, :] = (normed * table[5:6, :] + table[6:7, :]).astype(low)
            return carry

        row_steps(body, 0)
        turn(low_two, low_two_turned)

    stages = (one_stage, two_stage)
    keeps = (one_keep, two_keep)

    def hand_over(at):
        chunk, place = divmod(at, tensor)
        target = (*here.at, lax.rem(here.rank + place + 1, tensor))
        return [
            pltpu.make_async_remote_copy(
                src_ref=stages[which].at[at % 2],
                dst_ref=land[which].at[place, chunk],
                send_sem=store_sem.at[which, at % 2],
                recv_sem=land_sem.at[which, place, chunk],
                device_id=here.device(target),
                device_id_type=MESH,
            )
            for which in range(2)
        ]

    def keep_store(chunk):
        return [
            pltpu.make_async_copy(
                keeps[which].at[chunk % 2],
                out.at[chunk],
                keep_sem.at[which, chunk % 2],
            )
            for which, out in enumerate((grad_one, grad_two))
        ]

    def hidden_column(at):
        chunk, place = divmod(at, tensor)
        base = (lax.rem(here.rank + place + 1, tensor) * weight_one.shape[1] + chunk) * BLOCK
        return pl.ds(pl.multiple_of(base, LANES), BLOCK)

    def hidden_load(at):
        chunk, place = divmod(at, tensor)
        rank = lax.rem(here.rank + place + 1, tensor)
        return [
            load(source.at[rank, chunk], buffer.at[at % 2], load_sem.at[3 + 2 * which + at % 2])
            for which, (source, buffer) in enumerate(((weight_one, one_buf), (weight_two, two_buf)))
        ]

    staged = {}

    def hidden(at):
        chunk, place = divmod(at, tensor)
        column = hidden_column(at)
        for copy in hidden_load(at):
            copy.wait()
        half = rows // 2
        bias = hidden_bias[:, column]

        def body(turn_at, total):
            part = pl.ds(pl.multiple_of(turn_at * half, half), half)
            one = one_buf[at % 2].reshape(width, BLOCK)
            two = two_buf[at % 2].reshape(width, BLOCK)
            preact = dot(low_two[part, :], one) + bias
            gate = jax.nn.sigmoid(1.702 * preact)
            value = (preact * gate).astype(low)
            active[part, :] = value
            derivative = gate + 1.702 * preact * gate * (1.0 - gate)
            grad = (dot(back_two[part, :], two) * derivative).astype(low)
            grad_pre[part, :] = grad
            if at == 0:
                block_out[part, :] = dot(value, two, CONTRACT_LAST)
                grad_low_two[part, :] = dot(grad, one, CONTRACT_LAST)
            else:
                block_out[part, :] += dot(value, two, CONTRACT_LAST)
                grad_low_two[part, :] += dot(grad, one, CONTRACT_LAST)
            return total + jnp.sum(grad.astype(jnp.float32), axis=0, keepdims=True)

        pre_sums[:, column] = lax.fori_loop(0, 2, body, jnp.zeros((1, BLOCK), jnp.float32))
        mine = place == tensor - 1
        if mine:
            targets = [ref.at[chunk % 2] for ref in keeps]
            if chunk > 1:
                for copy in keep_store(chunk):
                    copy.wait()
        else:
            targets = [ref.at[at % 2] for ref in stages]
            for copy in staged.pop(at % 2, ()):
                copy.wait_send()
        for target, left, right in (
            (targets[0], low_two_turned, grad_pre),
            (targets[1], back_two_turned, active),
        ):
            target[...] = dot(left[...], right[...]).astype(low).reshape(*target.shape)
        if not mine:
            staged[at % 2] = hand_over(at)
            for copy in staged[at % 2]:
                copy.start()

    def fetch(chunk, place):
        for which, copy in enumerate(hand_over(chunk * tensor + place)):
            copy.wait_recv()
            load(land[which].at[place, chunk], other.at[which], load_sem.at[7]).start()

    def combine(chunk):
        for place in range(tensor - 1):
            if place:
                fetch(chunk, place)
            for which in range(2):
                load(land[which].at[place, chunk], other.at[which], load_sem.at[7]).wait()
            for which in range(2):
                keeps[which][chunk % 2] = keeps[which][chunk % 2] + other[which]
        for copy in keep_store(chunk):
            copy.start()

    def last_norm():
        def body(part, sums):
            middle = grad_middle[part, :]
            keep = keep_ref[part, :]
            top = top_ref[part, :].astype(jnp.float32)
            block_out[part, :] = middle + (block_out[part, :] + table[VEC - 1 : VEC, :]) * keep
            normed, inverse = norm_rows(middle)
            grad_low = grad_low_two[part, :]
            scaled = grad_low * table[5:6, :]
            first = jnp.mean(scaled, axis=1, keepdims=True)
            second = jnp.mean(scaled * normed, axis=1, keepdims=True)
            grad = top + inverse * (scaled - first - normed * second)
            grad_middle[part, :] = grad
            masked = grad * keep
            back_one[part, :] = masked.astype(low)
            terms = (masked, grad_low * normed, grad_low, top * keep)
            return tuple(old + jnp.sum(term, axis=0, keepdims=True) for old, term in zip(sums, terms))

        zero = jnp.zeros((1, width), jnp.float32)
        for at, value in enumerate(row_steps(body, (zero,) * 4)):
            vec_sums[at : at + 1, :] = value
        for at in range(3):
            far_store(at).start()

    fill_pack()
    here.barrier(((0,), (1,), (2,), (3,)))
    steps = Steps()
    whole = sum(part[3] for part in parts)
    nz, ny, nx = dims

    def lengths(item, phase):
        share = parts[item][3] / whole * UNIT
        across = ny * nx if item in gather.late else 1
        along = 1 if item in gather.late else nz
        return {
            "pair": (share * across, "end"),
            "mid": (share * across * 2, "mid"),
            "back": (share * across * 2, "end"),
            "all": (share * across * nz, "end"),
            "first": (share * along / 2, "xy"),
            "second": (share * along, "xy"),
            "core": (share * CORE_UNIT / UNIT, "core"),
        }[gather.phases(item)[phase]]

    for item, part in enumerate(parts):
        phases = len(gather.phases(item))
        for phase in range(phases + 1):
            after = [("copy", item, phase - 1)] if phase else []
            if phase == 0 and item >= DEPTH and item not in gather.late:
                after = [("copy", item - DEPTH, 1)]
            if item in gather.late:
                if phase == 0:
                    after = [("copy", DEPTH, 1)]
                if phase == 2:
                    after += [("copy", other, 1) for other in range(min(len(parts), item + 3)) if other not in gather.late]
            length, link = lengths(item, min(phase, phases - 1))
            steps.add(
                ("copy", item, phase),
                functools.partial(gather.advance, item, phase),
                PUMP,
                0.5 if phase == 0 else 0.0,
                after,
                [(item, phase - 1)] if phase else [],
                [((item, phase), link, length)] if phase < phases else [],
            )

    def landed(items):
        return [("copy", item, len(gather.phases(item))) for item in items]

    def start(copies):
        for copy in copies:
            copy.start()

    previous = None
    head_count, block_count = per_rank * tensor, FF // BLOCK
    for name, at, items in tasks:
        after = landed(items) + ([previous] if previous else [])
        begin, run, time = {
            "norm": (None, first_norm, 4.0),
            "turn": (None, turn_first, 1.5),
            "heads": (lambda at=at: head_load(at).start(), lambda at=at: heads(at), 3.0),
            "out": (lambda: start(out_load()), second_norm, 5.0),
            "hidden": (lambda at=at: start(hidden_load(at)), lambda at=at: hidden(at), 5.5),
        }[name]
        if begin is not None:
            first = landed(items)
            if at > 1:
                first.append((name, at - 2))
            steps.add(("load", name, at), begin, 0.1, 0.2, first)
            after.append(("load", name, at))
        mine = name == "hidden" and at % tensor == tensor - 1
        chunk = at // tensor
        if mine and chunk > 1:
            after.append(("sum", chunk - 2))
        starts = []
        if name == "hidden" and not mine:
            starts = [(("hand", at), "core", CORE_UNIT / len(parts))]
        steps.add((name, at), run, time, 1.0, after, (), starts)
        if mine:
            waits = [("hand", chunk * tensor + place) for place in range(tensor - 1)]
            if waits:
                before = [(name, at)] + ([("sum", chunk - 1)] if chunk else [])
                steps.add(("fetch", chunk), functools.partial(fetch, chunk, 0), 0.2, 0.3, before, waits, [(("got", chunk), "hbm", 1.0)])
                after, waits = [("fetch", chunk)], [("got", chunk)]
            else:
                after = [(name, at)]
            steps.add(("sum", chunk), functools.partial(combine, chunk), 0.8, 0.8, after, waits)
        previous = (name, at)
    steps.add(("last", 0), last_norm, 4.0, 0.9, [previous])
    steps.run()
    for at in range(5):
        far_store(at).wait()
    for slot in range(min(2, head_count)):
        head_store(0, slot).wait()
    for chunk in range(min(2, block_count // tensor)):
        for copy in keep_store(chunk):
            copy.wait()
    for copies in staged.values():
        for copy in copies:
            copy.wait_send()
    gather.finish()


def forward(dims, tensor, inputs, cotangent, token_mask, vectors, weights):
    own_rows, columns = weights[0].shape[1:]
    hidden = weights[2].shape[1]
    rows, width = inputs.shape
    low, full = jnp.bfloat16, jnp.float32
    widths = (3 * columns, LANES, columns, hidden, hidden)
    offsets = [sum(widths[:at]) for at in range(5)]
    per_rank = columns // LANES
    parts = [(1, offsets[1], None, LANES)]
    tasks = [("norm", 0, (0,)), ("turn", 0, (0,))]
    for at in range(per_rank):
        size = 3 * LANES
        parts.append((0, offsets[0] + at * size, at, size))
        tasks += [("heads", at * tensor + place, (len(parts) - 1,)) for place in range(tensor)]
    tasks.append(("out", 0, (len(parts),)))
    parts.append((2, offsets[2], 0, columns))
    for block in range(hidden // BLOCK):
        needed = (len(parts), len(parts) + 1)
        parts += [(which, offsets[which] + block * BLOCK, block, BLOCK) for which in (3, 4)]
        tasks += [("hidden", block * tensor + place, needed) for place in range(tensor)]
    count = len(parts)
    peers = max(1, dims[0] - 1, dims[1] + dims[2] - 2, tensor - 1)
    anywhere = pl.BlockSpec(memory_space=pl.ANY)
    inside = pl.BlockSpec(memory_space=pltpu.VMEM)
    block = (*dims, own_rows, BLOCK)
    chunks = hidden // BLOCK

    def shape(kind, *size):
        return jax.ShapeDtypeStruct(size, kind)

    return pl.pallas_call(
        functools.partial(forward_kernel, dims, tensor, tuple(parts), tuple(tasks)),
        name="forward",
        out_shape=[
            shape(low, tensor, per_rank, *dims, own_rows, 3 * LANES),
            shape(low, *dims, own_rows, LANES),
            shape(low, tensor, 1, *dims, own_rows, columns),
            *[shape(low, tensor, chunks, *block)] * 2,
            *[shape(low, max(1, tensor - 1), chunks, *block)] * 2,
            shape(full, rows, width),
            shape(full, rows, width),
            *[shape(low, rows, width)] * 2,
            shape(low, width, rows),
            shape(low, rows, 3 * width),
            *[shape(low, chunks, *block)] * 2,
            shape(full, 16, width),
            shape(full, 8, width),
            shape(full, 1, hidden * tensor),
            shape(full, rows, 1),
        ],
        in_specs=[inside] * 8,
        out_specs=[anywhere] * 15 + [inside] * 4,
        scratch_shapes=[
            pltpu.VMEM((rows, width), full),
            pltpu.VMEM((rows, width), full),
            *[pltpu.VMEM((rows, width), low)] * 3,
            pltpu.VMEM((width, rows), low),
            pltpu.VMEM((own_rows, sum(widths)), low),
            pltpu.VMEM((rows, 1), full),
            pltpu.VMEM((LANES, own_rows), full),
            pltpu.VMEM((*dims, own_rows, LANES), low),
            pltpu.VMEM((2, *dims, own_rows, 3 * LANES), low),
            pltpu.VMEM((2, rows, 3 * LANES), low),
            pltpu.VMEM((tensor, *dims, own_rows, columns), low),
            pltpu.VMEM((2, *block), low),
            pltpu.VMEM((2, *block), low),
            pltpu.VMEM((rows, width), low),
            pltpu.VMEM((width, rows), low),
            pltpu.VMEM((rows, width), low),
            pltpu.VMEM((width, rows), low),
            pltpu.VMEM((rows, width), full),
            pltpu.VMEM((1, hidden * tensor), full),
            pltpu.VMEM((1, 3 * width), full),
            pltpu.VMEM((2, *block), low),
            pltpu.VMEM((2, *block), low),
            pltpu.VMEM((2, *block), low),
            pltpu.VMEM((2, *block), low),
            pltpu.VMEM((2, *block), low),
            pltpu.VMEM((rows, BLOCK), low),
            pltpu.VMEM((rows, BLOCK), low),
            pltpu.SemaphoreType.DMA((8,)),
            pltpu.SemaphoreType.DMA((2, 2)),
            pltpu.SemaphoreType.DMA((2, 2)),
            pltpu.SemaphoreType.DMA((2,)),
            pltpu.SemaphoreType.DMA((2, max(1, tensor - 1), chunks)),
            pltpu.SemaphoreType.DMA((5,)),
            pltpu.SemaphoreType.DMA((count,)),
            pltpu.SemaphoreType.DMA((count, 6, peers)),
            pltpu.SemaphoreType.DMA((count, 6, peers)),
        ],
        compiler_params=pltpu.CompilerParams(
            collective_id=0, has_side_effects=True, vmem_limit_bytes=62 << 20
        ),
    )(inputs, cotangent, token_mask, vectors, *weights)


class Layout:
    def __init__(self, columns, hidden, order):
        sizes = {"qkv": 3 * columns, "out": columns, "one": hidden, "two": hidden, "vec": LANES}
        self.order = order
        self.sizes = sizes
        self.start = {}
        at = 0
        for name in order:
            self.start[name] = at
            at += sizes[name]
        self.total = at
        self.columns = columns

    def span(self, name):
        return (self.start[name], self.sizes[name])

    def matrices(self):
        base = self.start["qkv"]
        pairs = range(self.columns // LANES)
        spans = [[(base + (pair * 3 + at) * LANES, LANES) for pair in pairs] for at in range(3)]
        return spans + [[self.span(name)] for name in ("out", "one", "two")]


def pick(values, lane):
    row = jnp.zeros((1, LANES), jnp.float32)
    for at, value in enumerate(values):
        row = jnp.where(lane == at, value, row)
    return row


def total_of(values):
    return jnp.sum(jnp.sum(values, axis=1, keepdims=True), axis=0, keepdims=True)


def attend_pair_back(heads, bias, grads):
    parts = ([], [], [])
    for head in range(2):
        query, key, value = (
            heads[:, kind * LANES + head * HEAD_DIM : kind * LANES + (head + 1) * HEAD_DIM] for kind in range(3)
        )
        grad = grads[:, head * HEAD_DIM : (head + 1) * HEAD_DIM]
        scores = dot(key, query, CONTRACT_LAST) * (HEAD_DIM ** (-0.5) * LOG2E) + bias
        raised = jnp.exp2(scores - jnp.max(scores, axis=0, keepdims=True))
        attention = raised * (1.0 / jnp.sum(raised, axis=0, keepdims=True))
        grad_value = dot(attention.astype(jnp.bfloat16), grad)
        grad_attention = dot(value, grad, CONTRACT_LAST)
        weighted = jnp.sum(attention * grad_attention, axis=0, keepdims=True)
        grad_scores = (attention * (grad_attention - weighted) * HEAD_DIM ** (-0.5)).astype(jnp.bfloat16)
        grad_key = dot(grad_scores, query)
        grad_query = dot(key.T, grad_scores).T
        for kind, part in enumerate((grad_query, grad_key, grad_value)):
            parts[kind].append(part.astype(jnp.bfloat16))
    return jnp.concatenate([piece for kind in parts for piece in kind], axis=1)


def backward_kernel(dims, tensor, items, layout, *refs):
    (
        sum_two,
        sum_one,
        weight_qkv,
        weight_out,
        projected,
        input_ref,
        middle_ref,
        *far,
        bias_ref,
        table,
        vec_sums,
        pre_sums,
    ) = refs[:14]
    far = (*far, *refs[14:18])
    row_states, col_states = refs[18:22], refs[22:26]
    second_ref, vector_ref = refs[26:28]
    input_grad_out, total_ref, col_new_ref, row_new_ref, second_new_ref, sums_ref = refs[28:34]
    groups = ("ffn", "out", "qkv", "vec")
    kinds = ("own", "one_x", "one_y", "two_y", "two_x", "from_z")
    held = {}
    for kind in kinds:
        for group in groups:
            held[kind, group] = refs[34 + len(held)]
    for group in groups[1:]:
        held["core", group] = refs[34 + len(held)]
    (
        input_grad,
        late_z,
        late_one_y,
        late_one_x,
        late_two_x,
        late_two_y,
        col_sum,
        col_in,
        row_sum,
        row_in,
        small,
        small_in,
        square,
        turned,
        mixed,
        back_one,
        *weights,
        low_turned,
        back_turned,
        grad_mixed,
        out_buf,
        qkv_buf,
        head_buf,
        row_buf,
        out_stage,
        qkv_stage,
        vec_stage,
        head_sums,
        table_grad_ref,
        load_sem,
        stage_sem,
        core_sem,
        local_sem,
        send_sem,
        recv_sem,
        sum_send,
        sum_recv,
        far_sem,
    ) = refs[34 + len(held) :]
    near = (mixed, low_turned, back_one, *weights)

    def far_load(at):
        return pltpu.make_async_copy(far[at], near[at], far_sem.at[at])

    here = Place(dims, tensor)
    nz, ny, nx = dims
    low = jnp.bfloat16
    own_rows = total_ref.shape[0]
    half_rows = own_rows // 2
    rows, width = input_grad.shape
    own_place = (*here.at, here.rank)
    count = len(items)

    def columns(item):
        _, start, size, _ = items[item]
        return pl.ds(start, size)

    def at_home(kind, item):
        name = items[item][0]
        if name in ("one", "two"):
            members = [at for at, other in enumerate(items) if other[0] in ("one", "two")]
            if kind != "own":
                members = [at for at in members if at not in late]
            return held[kind, "ffn"].at[members.index(item)]
        members = [at for at, other in enumerate(items) if other[0] == name]
        return held[kind, name].at[members.index(item)]

    def phases(item):
        lengthwise = along_z(nz)[::-1]
        across = ("first", "second")
        return (*lengthwise, *across) if item in late else (*across, *lengthwise)

    def moves(item, phase):
        first, second, whole = pl.ds(0, half_rows), pl.ds(half_rows, half_rows), pl.ds(0, own_rows)
        kind = phases(item)[phase]
        own = at_home("own", item)
        found = []
        if kind in ("pair", "mid", "back"):
            pair, far, near, middle = here.line()
            outside = jnp.logical_not(middle)
            rest = (slice(None), slice(None)) if item in late else here.at[1:]
            buffer = late_z.at[late.index(item)] if item in late else at_home("from_z", item)
            z = here.at[0]
            device, sent_z, add_z, slots, sends, receives = {
                "back": (near, pl.ds(far, 2), pl.ds(far, 2), pl.ds(0, 2), outside, middle),
                "mid": (3 - z, pl.ds(far, 2), pl.ds(pair, 2), pl.ds(2, 2), middle, middle),
                "pair": (near, near, z, 4, None, None),
            }[kind]
            source = own.at[(sent_z, *rest, whole)]
            found.append((here.at_z(device), source, buffer.at[slots], (add_z, *rest), whole, sends, receives))
            return found
        if item in late:
            at = late.index(item)
            steps = {
                "all": ((0, (0,), whole, late_z.at[at]),),
                "first": ((1, (0, 1), first, late_one_y.at[at]), (2, (0, 2), second, late_one_x.at[at])),
                "second": ((2, (0, 1, 2), first, late_two_x.at[at]), (1, (0, 1, 2), second, late_two_y.at[at])),
            }[kind]
        else:
            steps = {
                "first": ((2, (2,), first, "one_x"), (1, (1,), second, "one_y")),
                "second": ((1, (1, 2), first, "two_y"), (2, (1, 2), second, "two_x")),
                "all": ((0, (0, 1, 2), whole, "from_z"),),
            }[kind]
            steps = [(*step[:3], at_home(step[3], item)) for step in steps]
        for axis, fixed, part, landing in steps:
            for step in range(1, here.size(axis)):
                target = here.moved(axis, step)
                index = tuple(target[a] if a in fixed else slice(None) for a in range(3))
                added = tuple(here.at[a] if a in fixed else slice(None) for a in range(3))
                source = own.at[(*index, part)]
                found.append((here.device(target), source, landing.at[step - 1], added, part, None, None))
        return found

    def copies(item, phase):
        found = []
        for at, (device, source, landing, added, part, sends, receives) in enumerate(moves(item, phase)):
            copy = pltpu.make_async_remote_copy(
                src_ref=source,
                dst_ref=landing,
                send_sem=send_sem.at[item, phase, at],
                recv_sem=recv_sem.at[item, phase, at],
                device_id=device,
                device_id_type=MESH,
            )
            found.append((sends, receives, copy, added, part, landing))
        return found

    def add_core(item):
        own, brought = at_home("own", item), at_home("core", item)

        def body(at, carry):
            z, y, x = at // (ny * nx), at // nx % ny, at % nx
            value = own[z, y, x]
            for step in range(tensor - 1):
                value = value + brought[step, z, y, x]
            own[z, y, x] = value
            return carry

        if tensor > 1:
            lax.fori_loop(0, nz * ny * nx, body, 0)

    def add_in(item, landing, added, part):
        own = at_home("own", item)
        sizes, starts = [], []
        for axis, at in enumerate(added):
            if isinstance(at, slice):
                sizes.append(dims[axis])
                starts.append(0)
            elif hasattr(at, "start"):
                sizes.append(at.size)
                starts.append(at.start)
            else:
                sizes.append(None)
                starts.append(at)
        loops = 1
        for size in sizes:
            loops *= size or 1

        def body(at, carry):
            place, inner, rest = [], [], at
            for size, start in reversed(list(zip(sizes, starts))):
                if size is None:
                    place.insert(0, start)
                else:
                    place.insert(0, start + rest % size)
                    inner.insert(0, rest % size)
                    rest = rest // size
            where = (*place, part)
            own[where] = own[where] + (landing[tuple(inner)] if inner else landing[...])
            return carry

        if loops == 1:
            body(0, 0)
        else:
            lax.fori_loop(0, loops, body, 0)

    def put_total(item, arrived):
        wide = columns(item)
        parts_of = {}
        for landing, part in arrived:
            parts_of.setdefault((part.start, part.size), []).append(landing)
        for (start, size), landings in parts_of.items():
            part = pl.ds(start, size)
            value = at_home("own", item)[(*here.at, part)].astype(jnp.float32)
            for landing in landings:
                value = value + landing[...].astype(jnp.float32)
            total_ref[part, wide] = value
        if items[item][0] == "vec":
            return
        for at, spans in enumerate(layout.matrices()):
            for start, size in spans:
                low_end, high_end = max(start, wide.start), min(start + size, wide.start + wide.size)
                if low_end < high_end:
                    square = total_ref[:, pl.ds(low_end, high_end - low_end)]
                    square = square * square
                    col_sum[0, :, pl.ds(low_end, high_end - low_end)] = jnp.sum(square, axis=0, keepdims=True)
                    found = jnp.sum(square, axis=1, keepdims=True)
                    row_sum[0] = row_sum[0] + jnp.where(lane == at, found, 0.0)

    sent = []
    lane = lax.broadcasted_iota(jnp.int32, (1, LANES), 1)
    row_sum[0] = jnp.zeros_like(row_sum[0])
    guarded_sent = []
    late = [at for at in LATE_ITEMS if items[at][0] in ("one", "two")]

    def exchange(kind, phase, axes, buffer, landing):
        moved = []
        for at, device in enumerate(here.peers(*axes)):
            copy = pltpu.make_async_remote_copy(
                src_ref=buffer.at[phase],
                dst_ref=landing.at[phase, at],
                send_sem=sum_send.at[kind, phase, at],
                recv_sem=sum_recv.at[kind, phase, at],
                device_id=device,
                device_id_type=MESH,
            )
            copy.start()
            moved.append(copy)
        sent.extend(moved)

        def finish():
            value = buffer[phase]
            for at, copy in enumerate(moved):
                copy.wait_recv()
                value = value + landing[phase, at]
            buffer[phase + 1] = value

        return finish

    def hand_over(item, step, source, sem):
        return pltpu.make_async_remote_copy(
            src_ref=source,
            dst_ref=at_home("core", item).at[step - 1],
            send_sem=sem,
            recv_sem=core_sem.at[item, step - 1],
            device_id=here.device(here.moved(3, step)),
            device_id_type=MESH,
        )

    arriving = {}

    def keep_own(item, value):
        at_home("own", item)[...] = value.reshape(nz, ny, nx, own_rows, value.shape[1])

    out_items = [at for at, item in enumerate(items) if item[0] == "out"]
    qkv_items = [at for at, item in enumerate(items) if item[0] == "qkv"]
    vec_item = count - 1
    per_rank = len(qkv_items)
    steps_in_all = per_rank * tensor

    def rank_at(step):
        return lax.rem(here.rank + step, tensor)

    def pair_loads(at):
        turn_at, place = divmod(at, tensor)
        pair = rank_at(place + 1) * per_rank + turn_at
        column = pl.ds(pl.multiple_of(pair * 3 * LANES, LANES), 3 * LANES)
        near = at % 2
        return pair, column, [
            pltpu.make_async_copy(
                weight_qkv.at[rank_at(place + 1), turn_at], qkv_buf.at[near], load_sem.at[0, near]
            ),
            pltpu.make_async_copy(projected.at[:, column], head_buf.at[near], load_sem.at[1, near]),
        ]

    def out_task():
        fetch = [
            pltpu.make_async_copy(weight_out.at[rank, 0], out_buf.at[rank], load_sem.at[2, 0])
            for rank in range(tensor)
        ]
        for copy in fetch:
            copy.start()
        far_load(2).wait()
        turn(back_one, back_turned)
        far_load(0).wait()
        for copy in pair_loads(0)[2]:
            copy.start()
        size = out_stage.shape[5]
        item = out_items[0]
        for step in range(1, tensor + 1):
            column = pl.ds(pl.multiple_of(rank_at(step) * size, LANES), size)
            value = dot(back_turned[...], mixed[:, column]).astype(low)
            if step < tensor:
                out_stage[step - 1] = value.reshape(nz, ny, nx, own_rows, size)
                copy = hand_over(item, step, out_stage.at[step - 1], stage_sem.at[item, step - 1])
                copy.start()
                sent.append(copy)
                arriving.setdefault(item, []).append(copy)
            else:
                keep_own(item, value)
        for copy in fetch:
            copy.wait()
        for rank in range(tensor):
            weight = out_buf[rank].reshape(width, size)
            grad_mixed[:, pl.ds(rank * size, size)] = dot(back_one[...], weight).astype(low)
        far_load(1).wait()

    def state_task():
        def fill(refs, other):
            square[...] = jnp.full_like(square, other)
            base = 0
            for ref in refs:
                square[pl.ds(base, ref.shape[0]), :] = ref[...]
                base += ref.shape[0]
            return square[...].T

        for at in range(3, 7):
            far_load(at).wait()
        turned[0] = fill(row_states, 1.0)
        turned[1] = fill((second_ref,), 1.0)
        turned[2] = fill((vector_ref,), 0.0)

    staged = {}

    def pair_task(at):
        turn_at, place = divmod(at, tensor)
        pair, column, loads = pair_loads(at)
        for copy in loads:
            copy.wait()
        if at + 1 < steps_in_all:
            for copy in pair_loads(at + 1)[2]:
                copy.start()
        near = at % 2
        grads = grad_mixed[:, pl.ds(pl.multiple_of(pair * LANES, LANES), LANES)]
        value = attend_pair_back(head_buf[near], bias_ref[...], grads)
        head_sums[:, column] = jnp.sum(value.astype(jnp.float32), axis=0, keepdims=True)
        weight = qkv_buf[near].reshape(width, 3 * LANES)
        term = dot(value, weight, CONTRACT_LAST)
        if at == 0:
            input_grad[...] = term
        else:
            input_grad[...] += term
        item = qkv_items[turn_at]
        mine = place + 1 == tensor
        if not mine and 0 in staged:
            staged[0].wait_send()
        grad = dot(low_turned[...], value).astype(low)
        if mine:
            keep_own(item, grad)
        else:
            qkv_stage[...] = grad.reshape(nz, ny, nx, own_rows, 3 * LANES)
        if not mine:
            copy = hand_over(item, place + 1, qkv_stage, stage_sem.at[item, place])
            copy.start()
            staged[0] = copy
            arriving.setdefault(item, []).append(copy)

    def grad_store():
        return pltpu.make_async_copy(input_grad, input_grad_out, far_sem.at[7])

    def last_task():
        step_rows = row_buf.shape[2]

        def fetch(at):
            near = lax.rem(at, 2)
            part = pl.ds(pl.multiple_of(at * step_rows, step_rows), step_rows)
            return [
                pltpu.make_async_copy(source.at[part, :], row_buf.at[which, near], load_sem.at[which, near])
                for which, source in enumerate((input_ref, middle_ref))
            ]

        for copy in fetch(0):
            copy.start()

        def body(at, sums):
            for copy in fetch(at):
                copy.wait()

            @pl.when(at + 1 < rows // step_rows)
            def _():
                for copy in fetch(at + 1):
                    copy.start()

            near = lax.rem(at, 2)
            part = pl.ds(pl.multiple_of(at * step_rows, step_rows), step_rows)
            normed, inverse = norm_rows(row_buf[0, near])
            grad_low = input_grad[part, :]
            scaled = grad_low * table[0:1, :]
            first = jnp.mean(scaled, axis=1, keepdims=True)
            second = jnp.mean(scaled * normed, axis=1, keepdims=True)
            input_grad[part, :] = row_buf[1, near] + inverse * (scaled - first - normed * second)
            terms = (grad_low * normed, grad_low)
            return tuple(old + jnp.sum(term, axis=0, keepdims=True) for old, term in zip(sums, terms))

        zero = jnp.zeros((1, width), jnp.float32)
        found = lax.fori_loop(0, rows // step_rows, body, (zero, zero))
        grad_store().start()
        table_grad_ref[...] = jnp.zeros_like(table_grad_ref)
        for at in range(2):
            table_grad_ref[at : at + 1, :] = found[at]
        for pair in range(width // LANES):
            for kind, row in ((0, 2), (2, 3)):
                table_grad_ref[row : row + 1, pl.ds(pair * LANES, LANES)] = head_sums[
                    :, pl.ds((pair * 3 + kind) * LANES, LANES)
                ]
        for at, row in enumerate((4, 5, 6, VEC - 1)):
            table_grad_ref[row : row + 1, :] = vec_sums[at : at + 1, :]
        for at in range(VEC - 8):
            table_grad_ref[7 + at : 8 + at, :] = pre_sums[:, pl.ds(at * width, width)]
        value = table_grad_ref[...].T.astype(low)
        vec_stage[...] = value.reshape(nz, ny, nx, own_rows, LANES)
        for step in range(1, tensor):
            copy = hand_over(vec_item, step, vec_stage, stage_sem.at[vec_item, step - 1])
            copy.start()
            sent.append(copy)
            arriving.setdefault(vec_item, []).append(copy)
        keep_own(vec_item, value)

    for at in (2, 0, 1, 3, 4, 5, 6):
        far_load(at).start()
    here.barrier(((0, 3), (1, 2)))
    local = {}
    for item, (name, _, _, source) in enumerate(items):
        if name in ("one", "two"):
            array = sum_one if name == "one" else sum_two
            copy = pltpu.make_async_copy(
                array.at[source], at_home("own", item), local_sem.at[item]
            )
            copy.start()
            local[item] = copy

    def advance(item, phase):
        last = len(phases(item))
        if phase > 0:
            arrived = []
            for _, receives, copy, added, part, landing in copies(item, phase - 1):

                def take(copy=copy, landing=landing, added=added, part=part):
                    copy.wait_recv()
                    if phase < last:
                        add_in(item, landing, added, part)

                guarded(receives, take)
                arrived.append((landing, part))
            if phase == last:
                put_total(item, arrived)
        elif item in local:
            local[item].wait()
        else:
            for copy in arriving.get(item, ()):
                copy.wait_recv()
            add_core(item)
        if phase < last:
            for sends, _, copy, *_ in copies(item, phase):
                guarded(sends, copy.start)
                guarded_sent.append((sends, copy))

    steps = Steps()
    owner = {item: ("out", 0) for item in out_items}
    owner |= {item: ("pair", tensor * (at + 1) - 1) for at, item in enumerate(qkv_items)}
    owner[vec_item] = ("last", 0)
    for item, (name, _, size, _) in enumerate(items):
        share = size / layout.total * UNIT
        across = ny * nx if item in late else 1
        along = 1 if item in late else nz
        lengths = {
            "pair": (share * across, "end"),
            "mid": (share * across * 2, "mid"),
            "back": (share * across * 2, "end"),
            "all": (share * across * nz, "end"),
            "first": (share * along, "xy"),
            "second": (share * along / 2, "xy"),
        }
        if item in late:
            lengths |= {"first": (share, "xy"), "second": (share / 2, "xy")}
        early = item not in owner
        kinds = phases(item)
        for phase in range(len(kinds) + 1):
            after = [("copy", item, phase - 1)] if phase else []
            waits = [(item, phase - 1)] if phase else []
            if phase == 0 and early and item >= DEPTH + len(late):
                after = [("copy", item - DEPTH, 1)]
            if phase == 0 and not early:
                after, waits = [owner[item]], [("core", owner[item])]
            starts = []
            if phase < len(kinds):
                length, link = lengths[kinds[phase]]
                starts = [((item, phase), link, length)]
            steps.add(
                ("copy", item, phase),
                functools.partial(advance, item, phase),
                PUMP * (1.5 if phase == 1 else 1.0),
                (0.5 if phase == 0 and early else 0.0),
                after,
                waits,
                starts,
            )
    steps.add(("state", 0), state_task, 1.0, 2.0)
    steps.add(("out", 0), out_task, 8.0, 1.0, (), (), [(("core", ("out", 0)), "core", CORE_UNIT / 12)])
    for at in range(steps_in_all):
        after = [("pair", at - 1) if at else ("out", 0)]
        starts = [(("core", ("pair", at)), "core", CORE_UNIT / 24)]
        steps.add(("pair", at), functools.partial(pair_task, at), 6.0, 1.0, after, (), starts)
    steps.add(
        ("last", 0), last_task, 4.0, 1.0, [("pair", steps_in_all - 1)], (), [(("core", ("last", 0)), "core", 1.0)]
    )
    steps.run()
    sent.extend(staged.values())

    decay_rate = 1.0 - STEP ** (-0.8)
    keep_old = 1.0 - decay_rate
    long = layout.sizes["one"] * tensor
    matrices = layout.matrices()
    finish_row = exchange(0, 0, (3,), row_sum, row_in)
    finish_col = exchange(1, 0, (0,), col_sum, col_in)
    vec_start = layout.start["vec"]
    table_grad = total_ref[:, pl.ds(vec_start, LANES)]
    second_new = decay_rate * turned[1] + keep_old * (table_grad * table_grad + EPS_ONE)
    second_new_ref[...] = second_new
    vector_update = table_grad * lax.rsqrt(second_new)
    vector_sums = jnp.sum(vector_update * vector_update, axis=0, keepdims=True) / tensor
    vector_weight = jnp.sum(turned[2] * turned[2], axis=0, keepdims=True) / tensor
    weight_sums = [total_of(jnp.sum(weights[0][...] * weights[0][...], axis=0))]
    weight_sums += [total_of(ref[...] * ref[...]) for ref in weights[1:]]
    finish_row()
    row_counts = pick([jnp.full((1, 1), 1.0 / size, jnp.float32) for size in (width, width, width, width, long, long)], lane)
    row_new = decay_rate * turned[0] + keep_old * (row_sum[1] * row_counts + EPS_ONE)
    row_new_ref[...] = row_new
    finish_col()
    exchange(1, 1, (1, 2), col_sum, col_in)()
    for at, spans in enumerate(matrices):
        for place, (start, size) in enumerate(spans):
            if at < 3:
                old = col_states[0][at : at + 1, pl.ds(place * LANES, LANES)]
            else:
                old = col_states[at - 2][...]
            fresh = keep_old * (col_sum[2, :, pl.ds(start, size)] / width + EPS_ONE)
            col_new_ref[:, pl.ds(start, size)] = decay_rate * old + fresh
    ratios = []
    means = []
    for at, spans in enumerate(matrices):
        row_at = row_new[:, at : at + 1]
        ratio = 0.0
        for start, size in spans:
            value = total_ref[:, pl.ds(start, size)]
            col_at = col_new_ref[:, pl.ds(start, size)]
            ratio = ratio + total_of(value * value / (row_at * col_at))
        ratios.append(ratio)
        if at in (3, 5):
            means.append(jnp.sum(col_at, axis=1, keepdims=True) / (nz * ny * nx))
        else:
            means.append(jnp.sum(row_at, axis=0, keepdims=True) / tensor)
    small[0] = jnp.concatenate(
        [pick(ratios + means + weight_sums, lane), vector_sums, vector_weight, jnp.zeros((5, LANES), jnp.float32)], axis=0
    )
    exchange(2, 0, (0, 3), small, small_in)()
    exchange(2, 1, (1, 2), small, small_in)()
    sums_ref[...] = small[2]
    grad_store().wait()
    for copy in sent:
        copy.wait_send()
    for condition, copy in guarded_sent:
        guarded(condition, copy.wait_send)


def backward(dims, tensor, layout, large, near, weights, states):
    rows, width = large[-1].shape
    own_rows = width // (dims[0] * dims[1] * dims[2])
    half_rows = own_rows // 2
    columns = layout.columns
    items = []
    for block in range(layout.sizes["one"] // BLOCK):
        for name in ("two", "one"):
            items.append((name, layout.start[name] + block * BLOCK, BLOCK, block))
    items.append(("out", layout.start["out"], columns, 0))
    for start in range(0, 3 * columns, 3 * LANES):
        items.append(("qkv", layout.start["qkv"] + start, 3 * LANES, start))
    items.append(("vec", layout.start["vec"], LANES, 0))
    nz, ny, nx = dims
    peers = max(1, nz - 1, ny + nx - 2)
    group = max(1, nz * tensor - 1, ny * nx - 1)
    others = max(1, tensor - 1)
    offset = layout.total
    late = max(1, len(LATE_ITEMS))
    line = 5 if nz == 4 else nz - 1
    groups = (
        (2 * layout.sizes["one"] // BLOCK, BLOCK),
        (1, columns),
        (columns // LANES, 3 * LANES),
        (1, LANES),
    )
    leads = (
        (nz, ny, nx, own_rows),
        (nx - 1, nz, ny, half_rows),
        (ny - 1, nz, nx, half_rows),
        (ny - 1, nz, half_rows),
        (nx - 1, nz, half_rows),
        (line, own_rows),
    )
    low, full = jnp.bfloat16, jnp.float32
    anywhere = pl.BlockSpec(memory_space=pl.ANY)
    inside = pl.BlockSpec(memory_space=pltpu.VMEM)

    def hold(*shape):
        return pltpu.VMEM(tuple(max(1, size) for size in shape), low)

    sums = offset - LANES
    count = len(items)
    return pl.pallas_call(
        functools.partial(backward_kernel, dims, tensor, tuple(items), layout),
        name="backward",
        out_shape=[
            jax.ShapeDtypeStruct((rows, width), full),
            jax.ShapeDtypeStruct((own_rows, offset), full),
            jax.ShapeDtypeStruct((1, sums), full),
            jax.ShapeDtypeStruct((own_rows, LANES), full),
            jax.ShapeDtypeStruct((own_rows, LANES), full),
            jax.ShapeDtypeStruct((8, LANES), full),
        ],
        in_specs=[anywhere] * len(large) + [inside] * len(near) + [anywhere] * 4 + [inside] * len(states),
        out_specs=[anywhere] + [inside] * 5,
        scratch_shapes=[
            *(
                hold(number if lead is leads[0] or at else number - late, *lead, size)
                for lead in leads
                for at, (number, size) in enumerate(groups)
            ),
            *(hold(number, others, nz, ny, nx, own_rows, size) for number, size in groups[1:]),
            pltpu.VMEM((rows, width), full),
            hold(late, line, ny, nx, own_rows, BLOCK),
            hold(late, ny - 1, nx, half_rows, BLOCK),
            hold(late, nx - 1, ny, half_rows, BLOCK),
            hold(late, nx - 1, half_rows, BLOCK),
            hold(late, ny - 1, half_rows, BLOCK),
            pltpu.VMEM((3, 1, sums), full),
            pltpu.VMEM((2, max(1, nz - 1, ny * nx - 1), 1, sums), full),
            pltpu.VMEM((2, own_rows, LANES), full),
            pltpu.VMEM((1, others, own_rows, LANES), full),
            pltpu.VMEM((3, 8, LANES), full),
            pltpu.VMEM((2, group, 8, LANES), full),
            pltpu.VMEM((LANES, own_rows), full),
            pltpu.VMEM((3, own_rows, LANES), full),
            *[hold(rows, width)] * 2,
            *(pltpu.VMEM(weight.shape, full) for weight in weights),
            hold(width, rows),
            hold(width, rows),
            hold(rows, width),
            hold(tensor, *dims, own_rows, columns),
            hold(2, *dims, own_rows, 3 * LANES),
            hold(2, rows, 3 * LANES),
            pltpu.VMEM((2, 2, LANES // 2, width), full),
            hold(others, *dims, own_rows, columns),
            hold(*dims, own_rows, 3 * LANES),
            hold(*dims, own_rows, LANES),
            pltpu.VMEM((1, 3 * width), full),
            pltpu.VMEM((LANES, width), full),
            pltpu.SemaphoreType.DMA((3, 2)),
            pltpu.SemaphoreType.DMA((count, others)),
            pltpu.SemaphoreType.DMA((count, others)),
            pltpu.SemaphoreType.DMA((count,)),
            pltpu.SemaphoreType.DMA((count, 5, peers)),
            pltpu.SemaphoreType.DMA((count, 5, peers)),
            pltpu.SemaphoreType.DMA((3, 2, group)),
            pltpu.SemaphoreType.DMA((3, 2, group)),
            pltpu.SemaphoreType.DMA((8,)),
        ],
        compiler_params=pltpu.CompilerParams(
            collective_id=1, has_side_effects=True, vmem_limit_bytes=63 << 20
        ),
    )(*large, *near, *weights, *states)


def update_kernel(layout, width, long, *refs):
    block_in, grad_in = refs[:2]
    far = refs[2:12]
    block_out, input_grad = refs[12:14]
    own_qkv, own_out, own_one, own_two, own_table = refs[14:19]
    new_qkv, new_out, new_one, new_two, new_vectors, second_new = refs[19:25]
    qkv_row, qkv_col, out_row, out_col, one_row, one_col, two_row, two_col = refs[25:33]
    near, passing, sem = refs[33:43], refs[43:45], refs[45]
    loads = [
        pltpu.make_async_copy(source, target, sem.at[at])
        for at, (source, target) in enumerate(zip((*far, block_in, grad_in), (*near, *passing)))
    ]
    later = loads[len(far) :]
    long_copies = [
        pltpu.make_async_copy(source, target, sem.at[12 + at])
        for at, (source, target) in enumerate(zip(passing, (block_out, input_grad)))
    ]
    for copy in loads:
        copy.start()
    for copy in loads[: len(far)]:
        copy.wait()
    total_ref, col_ref, row_ref, second_ref, sums_ref, vector_ref = near[:6]
    weights = near[6:]
    lane = lax.broadcasted_iota(jnp.int32, (1, LANES), 1)

    def at(index):
        return sums_ref[0:1, index : index + 1]

    lengths = (width, width, width, width, width, long)
    means = [at(6 + m) / lengths[m] for m in range(6)]
    squares = [means[m] * at(m) for m in range(6)]
    squares = [squares[0] + squares[1] + squares[2], *squares[3:]]
    entries = (3 * width * width, width * width, width * long, width * long)
    step_size = []
    for m in range(4):
        damping = 1.0 / jnp.maximum(1.0, jnp.sqrt(squares[m] / entries[m] + 1e-06) / CLIP_LEVEL)
        step_size.append(LEARN_RATE * jnp.sqrt(at(12 + m) / entries[m] + 1e-06) * damping)
    spread = [(m, place, *span) for m, spans in enumerate(layout.matrices()) for place, span in enumerate(spans)]
    for m, place, start, size in spread:
        if m == 3:
            for load, store in zip(later, long_copies):
                load.wait()
                store.start()
        grad = total_ref[:, pl.ds(start, size)]
        col = col_ref[:, pl.ds(start, size)]
        step = step_size[max(0, m - 2)] * grad * lax.rsqrt(row_ref[:, m : m + 1] * col / means[m])
        if m < 3:
            part = slice(place * LANES, (place + 1) * LANES)
            own_qkv[m, :, part] = grad
            new_qkv[m, :, part] = weights[0][m, :, part] - step
            qkv_col[m : m + 1, part] = col
        else:
            own, new, state = (
                (own_out, new_out, out_row),
                (own_one, new_one, one_col),
                (own_two, new_two, two_row),
            )[m - 3]
            own[...] = grad
            new[...] = weights[m - 2][...] - step
            state[...] = col
    row_flat = row_ref[...].T
    qkv_row[...] = row_flat[0:3]
    out_col[...] = row_flat[3:4]
    one_row[...] = row_flat[4:5]
    two_col[...] = row_flat[5:6]

    wide = (lane >= 7) & (lane < VEC - 1)
    counts = jnp.where(wide, float(long), float(width))

    def grouped(values):
        inside = jnp.sum(jnp.where(wide, values, 0.0), axis=1, keepdims=True)
        return jnp.where(wide, inside, values)

    table_grad = total_ref[:, pl.ds(layout.start["vec"], LANES)]
    update = table_grad * lax.rsqrt(second_ref[...])
    norm = jnp.sqrt(grouped(sums_ref[1:2, :]) / counts + 1e-06)
    size = jnp.sqrt(grouped(sums_ref[2:3, :]) / counts + 1e-06)
    change = LEARN_RATE * size / jnp.maximum(1.0, norm / CLIP_LEVEL) * update
    own_table[...] = table_grad.T[:VEC]
    new_vectors[...] = vector_ref[...] - change.T[:VEC]
    second_new[...] = second_ref[...].T[:VEC]
    for copy in long_copies:
        copy.wait()


def update_weights(layout, width, long, columns, hidden, rows, results, values, vectors, weights):
    full = jnp.float32
    shapes = [
        *(result.shape for result in results),
        (3, rows, columns),
        (rows, columns),
        (rows, hidden),
        (rows, hidden),
        (VEC, rows),
        (3, rows, columns),
        (rows, columns),
        (rows, hidden),
        (rows, hidden),
        (VEC, rows),
        (VEC, rows),
        (3, rows),
        (3, columns),
        (1, columns),
        (1, rows),
        (1, rows),
        (1, hidden),
        (1, hidden),
        (1, rows),
    ]
    far = (*values, vectors, *weights)
    anywhere = pl.BlockSpec(memory_space=pl.ANY)
    inside = pl.BlockSpec(memory_space=pltpu.VMEM)
    return pl.pallas_call(
        functools.partial(update_kernel, layout, width, long),
        name="update",
        out_shape=[jax.ShapeDtypeStruct(shape, full) for shape in shapes],
        in_specs=[anywhere] * (2 + len(far)),
        out_specs=[anywhere] * 2 + [inside] * (len(shapes) - 2),
        scratch_shapes=[
            *(pltpu.VMEM(array.shape, full) for array in (*far, *results)),
            pltpu.SemaphoreType.DMA((4 + len(far),)),
        ],
        compiler_params=pltpu.CompilerParams(vmem_limit_bytes=63 << 20),
    )(*results, *far)


def on_device(
    inputs,
    cotangent,
    token_mask,
    w_qkv,
    w_out,
    w_fc1,
    w_fc2,
    vectors,
    qkv_row,
    qkv_col,
    out_row,
    out_col,
    fc1_row,
    fc1_col,
    fc2_row,
    fc2_col,
    vec_second,
):
    tensor_count = lax.axis_size("tensor")
    dims = grid_of(lax.axis_size("fsdp"))
    width = inputs.shape[1]
    own_rows, columns = w_qkv.shape[1:]
    hidden = w_fc1.shape[1]
    weights = (w_qkv, w_out.T, w_fc1, w_fc2.T)
    (
        weight_qkv,
        _,
        weight_out,
        *_,
        block_out,
        grad_middle,
        back_one,
        mixed_rows,
        low_turned,
        projected,
        grad_one,
        grad_two,
        table,
        vec_sums,
        pre_sums,
        bias_column,
    ) = forward(dims, tensor_count, inputs, cotangent, token_mask, vectors, weights)
    layout = Layout(columns, hidden, ("two", "one", "out", "qkv", "vec"))
    row_states = (qkv_row, out_col[None], fc1_row[None], fc2_col[None])
    col_states = (qkv_col, out_row[None], fc1_col[None], fc2_row[None])
    input_grad, *values = backward(
        dims,
        tensor_count,
        layout,
        (
            grad_two,
            grad_one,
            weight_qkv,
            weight_out,
            projected,
            inputs,
            grad_middle,
            mixed_rows,
            low_turned,
            back_one,
        ),
        (bias_column, table, vec_sums, pre_sums),
        weights,
        (*row_states, *col_states, vec_second, vectors),
    )
    outs = update_weights(
        layout, width, FF, columns, hidden, own_rows, (block_out, input_grad), values, vectors, weights
    )
    outs = [out.reshape(-1) if out.shape[0] == 1 else out for out in outs]
    for at in (3, 5, 8, 10):
        outs[at] = outs[at].T
    return (*outs[:12], *outs[13:], outs[12])


def solution(mesh):
    in_specs = (
        P(("fsdp", "tensor"), None),
        P(("fsdp", "tensor"), None),
        P("fsdp", None),
        P(None, "fsdp", "tensor"),
        P("tensor", "fsdp"),
        P("fsdp", "tensor"),
        P("tensor", "fsdp"),
        P(None, "fsdp"),
        P(None, "fsdp"),
        P(None, "tensor"),
        P("tensor"),
        P("fsdp"),
        P("fsdp"),
        P("tensor"),
        P("tensor"),
        P("fsdp"),
        P(None, "fsdp"),
    )
    out_specs = (
        P(("fsdp", "tensor"), None),
        P(("fsdp", "tensor"), None),
        P(None, "fsdp", "tensor"),
        P("tensor", "fsdp"),
        P("fsdp", "tensor"),
        P("tensor", "fsdp"),
        P(None, "fsdp"),
        P(None, "fsdp", "tensor"),
        P("tensor", "fsdp"),
        P("fsdp", "tensor"),
        P("tensor", "fsdp"),
        P(None, "fsdp"),
        P(None, "fsdp"),
        P(None, "tensor"),
        P("tensor"),
        P("fsdp"),
        P("fsdp"),
        P("tensor"),
        P("tensor"),
        P("fsdp"),
        P(None, "fsdp"),
    )
    return jax.shard_map(
        on_device, mesh=mesh, in_specs=in_specs, out_specs=out_specs, check_vma=False
    )
```

```python
import functools

import jax
import jax.numpy as jnp
from jax import lax
from jax.experimental import pallas as pl
from jax.experimental.pallas import tpu as pltpu
from jax.sharding import PartitionSpec as P

HEAD_DIM = 64
FF = 4096
STEP = 20
VEC = 12
LANES = 128

EPS_NORM = 1e-05
EPS_ONE = 1e-30
CLIP_LEVEL = 1.0
LEARN_RATE = 0.5
MESH = pl.DeviceIdType.MESH
LOG2E = 1.4426950408889634
CONTRACT_LAST = (((1,), (1,)), ((), ()))


def grid_of(count):
    return {16: (4, 2, 2), 32: (2, 4, 4)}.get(count, (count, 1, 1))


class Place:
    def __init__(self, dims, tensor):
        self.dims = dims
        self.tensor = tensor
        fsdp = lax.axis_index("fsdp")
        _, ny, nx = dims
        self.at = (fsdp // (ny * nx), (fsdp // nx) % ny, fsdp % nx)
        self.rank = lax.axis_index("tensor")

    def moved(self, axis, step):
        place = list(self.at) + [self.rank]
        size = (*self.dims, self.tensor)[axis]
        place[axis] = lax.rem(place[axis] + step + size, size)
        return tuple(place)

    def device(self, place):
        z, y, x, rank = place
        return {"fsdp": (z * self.dims[1] + y) * self.dims[2] + x, "tensor": rank}

    def size(self, axis):
        return (*self.dims, self.tensor)[axis]

    def line(self):
        z = self.at[0]
        pair = z // 2 * 2
        middle = (z == 1) | (z == 2)
        return pair, 2 - pair, z + 1 - 2 * (z % 2), middle

    def at_z(self, z):
        return self.device((z, self.at[1], self.at[2], self.rank))

    def peers(self, *axes):
        places = [()]
        for axis in axes:
            places = [(*steps, step) for steps in places for step in range(self.size(axis))]
        found = []
        for steps in places[1:]:
            place = list(self.at) + [self.rank]
            for axis, step in zip(axes, steps):
                place[axis] = lax.rem(place[axis] + step, self.size(axis))
            found.append(self.device(tuple(place)))
        return found

    def barrier(self, groups):
        sem = pltpu.get_barrier_semaphore()
        count = 0
        for axes in groups:
            for device in self.peers(*axes):
                pl.semaphore_signal(sem, inc=1, device_id=device, device_id_type=MESH)
                count += 1
        if count:
            pl.semaphore_wait(sem, count)


def norm_rows(values):
    average = jnp.mean(values, axis=1, keepdims=True)
    center = values - average
    inverse = lax.rsqrt(jnp.mean(center * center, axis=1, keepdims=True) + EPS_NORM)
    return center * inverse, inverse


def dot(left, right, dims=(((1,), (0,)), ((), ()))):
    return lax.dot_general(left, right, dims, preferred_element_type=jnp.float32)


def turn(source, target):
    for start in range(0, source.shape[1], LANES):
        target[pl.ds(start, LANES), :] = source[:, pl.ds(start, LANES)].T


def attend_pair(heads, bias):
    mixed = []
    for head in range(2):
        query, key, value = (
            heads[:, kind * LANES + head * HEAD_DIM : kind * LANES + (head + 1) * HEAD_DIM] for kind in range(3)
        )
        scores = dot(query, key, CONTRACT_LAST) * (HEAD_DIM ** (-0.5) * LOG2E) + bias
        raised = jnp.exp2(scores - jnp.max(scores, axis=1, keepdims=True))
        summed = jnp.sum(raised, axis=1, keepdims=True)
        attention = (raised * (1.0 / summed)).astype(jnp.bfloat16)
        mixed.append(dot(attention, value).astype(jnp.bfloat16))
    return jnp.concatenate(mixed, axis=1)


def guarded(condition, run):
    if condition is None:
        run()
    else:
        pl.when(condition)(run)


def along_z(count):
    return ("pair", "mid", "back") if count == 4 else ("all",)


class Steps:
    def __init__(self):
        self.steps = {}

    def add(self, name, run, time, rank, after=(), waits=(), starts=()):
        self.steps[name] = (run, time, rank, tuple(after), tuple(waits), tuple(starts))

    def arrange(self):
        now, free, arrival, done, order = 0.0, {}, {}, set(), []
        left = list(self.steps)
        while left:
            best, soonest = None, None
            for name in left:
                _, time, rank, after, waits, _ = self.steps[name]
                if any(other not in done for other in after) or any(wait not in arrival for wait in waits):
                    continue
                ready = max([arrival[wait] for wait in waits], default=0.0)
                if ready <= now:
                    if best is None or rank < self.steps[best][2]:
                        best = name
                elif soonest is None or ready < soonest:
                    soonest = ready
            if best is None:
                now = soonest
                continue
            _, time, _, _, _, starts = self.steps[best]
            now += time
            for transfer, link, length in starts:
                begin = max(now, free.get(link, 0.0))
                free[link] = begin + length
                arrival[transfer] = begin + length + LATENCY
            done.add(best)
            left.remove(best)
            order.append(best)
        return order, now

    def run(self):
        for name in self.arrange()[0]:
            self.steps[name][0]()


class Gather:
    def __init__(self, here, pack_ref, outs, parts, local_sem, send_sem, recv_sem):
        self.here = here
        self.pack = pack_ref
        self.outs = outs
        self.rows = pack_ref.shape[0]
        self.parts = parts
        self.late = [len(parts) - at for at in LATE_PARTS if at < len(parts)]
        self.sems = (local_sem, send_sem, recv_sem)
        self.own = (*here.at, here.rank)
        self.sent = []

    def region(self, item, part, place, free):
        out, _, chunk, _ = self.parts[item]
        index = tuple(slice(None) if a in free else place[a] for a in range(3))
        lead = () if chunk is None else (place[3], chunk)
        return self.outs[out].at[(*lead, *index, part)]

    def shard(self, item, part):
        _, offset, _, size = self.parts[item]
        return self.pack.at[part, pl.ds(offset, size)]

    def phases(self, item):
        lengthwise = ("all",)
        across = ("first", "second")
        order = (*across, *lengthwise) if item in self.late else (*lengthwise, *across)
        return order if self.parts[item][2] is None else (*order, "core")

    def moves(self, item, phase):
        here, own = self.here, self.own
        kind = self.phases(item)[phase]
        late = item in self.late
        whole, half = pl.ds(0, self.rows), self.rows // 2
        first, second = pl.ds(0, half), pl.ds(half, half)
        found = []
        if kind in ("pair", "mid", "back"):
            free = (1, 2) if late else ()
            pair, far, near, middle = here.line()

            def blocks(z):
                return self.region(item, whole, (z, *own[1:]), free)

            if kind == "pair":
                sent = self.shard(item, whole) if phase == 0 else blocks(own[0])
                found.append((here.at_z(near), sent, blocks(own[0]), blocks(near), None, None))
            elif kind == "mid":
                pairs = blocks(pl.ds(pair, 2))
                found.append((here.at_z(3 - own[0]), pairs, pairs, blocks(pl.ds(far, 2)), middle, middle))
            else:
                pairs = blocks(pl.ds(far, 2))
                outside = jnp.logical_not(middle)
                found.append((here.at_z(near), pairs, pairs, pairs, middle, outside))
            return found
        before = () if late else (0,)
        steps = {
            "all": ((0, (1, 2) if late else (), whole),),
            "first": ((2, before, first), (1, before, second))
            if late
            else ((1, before, first), (2, before, second)),
            "second": ((1, (*before, 2), first), (2, (*before, 1), second))
            if late
            else ((2, (*before, 1), first), (1, (*before, 2), second)),
            "core": ((3, (0, 1, 2), whole),),
        }[kind]
        for axis, free, part in steps:
            for step in range(1, here.size(axis)):
                place = self.region(item, part, own, free)
                sent = self.shard(item, part) if phase == 0 else place
                landed = self.region(item, part, here.moved(axis, -step), free)
                found.append((here.device(here.moved(axis, step)), sent, place, landed, None, None))
        return found

    def copies(self, item, phase, landing):
        found = []
        for at, (device, sent, place, landed, sends, receives) in enumerate(self.moves(item, phase)):
            copy = pltpu.make_async_remote_copy(
                src_ref=landed if landing else sent,
                dst_ref=landed if landing else place,
                send_sem=self.sems[1].at[item, phase, at],
                recv_sem=self.sems[2].at[item, phase, at],
                device_id=device,
                device_id_type=MESH,
            )
            found.append((receives if landing else sends, copy))
        return found

    def keep(self, item):
        whole = pl.ds(0, self.rows)
        return pltpu.make_async_copy(
            self.shard(item, whole), self.region(item, whole, self.own, ()), self.sems[0].at[item]
        )

    def advance(self, item, phase):
        if phase:
            for condition, copy in self.copies(item, phase - 1, True):
                guarded(condition, copy.wait_recv)
        if phase == 0:
            self.keep(item).start()
        if phase == 1:
            self.keep(item).wait()
        if phase < len(self.phases(item)):
            for condition, copy in self.copies(item, phase, False):
                guarded(condition, copy.start)
                self.sent.append((condition, copy))

    def finish(self):
        for condition, copy in self.sent:
            guarded(condition, copy.wait_send)


BLOCK = 512
DEPTH = 3
LATENCY = 1.5
UNIT = 20.0
CORE_UNIT = 40.0
LATE_PARTS = (3,)
LATE_ITEMS = (0, 1, 2)
PUMP = 0.4


def forward_kernel(dims, tensor, parts, tasks, *refs):
    input_ref, top_ref, mask_ref, vector_ref = refs[:4]
    own_weights = refs[4:8]
    outs, land = refs[8:13], refs[13:15]
    weight_qkv, weight_vec, weight_out, weight_one, weight_two = outs
    far = refs[15:20]
    projected, grad_one, grad_two, table, vec_sums, pre_sums, bias_column = refs[20:27]
    (
        block_out,
        grad_middle,
        back_one,
        mixed,
        low_one,
        low_turned,
        pack,
        keep_ref,
        square,
        vec_buf,
        qkv_buf,
        head_stage,
        out_buf,
        one_buf,
        two_buf,
        low_two,
        low_two_turned,
        back_two,
        back_two_turned,
        grad_low_two,
        hidden_bias,
        head_bias,
        one_stage,
        two_stage,
        one_keep,
        two_keep,
        other,
        active,
        grad_pre,
        load_sem,
        store_sem,
        keep_sem,
        head_sem,
        land_sem,
        far_sem,
        local_sem,
        send_sem,
        recv_sem,
    ) = refs[27:]
    near = (block_out, grad_middle, back_one, mixed, low_turned)

    def far_store(at):
        return pltpu.make_async_copy(near[at], far[at], far_sem.at[at])

    here = Place(dims, tensor)
    gather = Gather(here, pack, outs, parts, local_sem, send_sem, recv_sem)
    rows, width = input_ref.shape
    own_rows = pack.shape[0]
    per_rank = weight_qkv.shape[1]
    low = jnp.bfloat16
    step_rows = LANES

    def fill_pack():
        base = 0
        for pair in range(per_rank):
            for kind in range(3):
                part = own_weights[0][kind, :, pl.ds(pair * LANES, LANES)]
                pack[:, pl.ds(base, LANES)] = part.astype(low)
                base += LANES
        square[...] = jnp.zeros_like(square)
        square[pl.ds(0, VEC), :] = vector_ref[...]
        pack[:, pl.ds(base, LANES)] = square[...].T.astype(low)
        base += LANES
        for ref in own_weights[1:]:
            pack[:, pl.ds(base, ref.shape[1])] = ref[...].astype(low)
            base += ref.shape[1]

    def mask_row():
        return mask_ref[pl.ds(here.rank, 1), :].astype(jnp.float32)

    def mask_bias(keep):
        return jnp.where(keep > 0.0, 0.0, -1e30)

    def first_masks():
        turned = jnp.broadcast_to(mask_row(), (LANES, rows)).T
        keep_ref[...] = turned[:, 0:1]
        bias_column[...] = mask_bias(turned[:, 0:1])

    def row_steps(body, carry):
        return lax.fori_loop(
            0, rows // step_rows, lambda at, c: body(pl.ds(pl.multiple_of(at * step_rows, step_rows), step_rows), c), carry
        )

    def load(source, buffer, sem):
        return pltpu.make_async_copy(source, buffer, sem)

    def first_norm():
        first_masks()
        copy = load(weight_vec, vec_buf, load_sem.at[7])
        copy.start()
        copy.wait()
        whole = vec_buf[...].reshape(width, LANES).astype(jnp.float32).T
        table[...] = whole[:16]
        for at in range(VEC - 8):
            hidden_bias[:, pl.ds(at * width, width)] = whole[7 + at : 8 + at]
        for pair in range(width // LANES):
            for kind, row in ((0, 2), (2, 3)):
                head_bias[:, pl.ds((pair * 3 + kind) * LANES, LANES)] = whole[
                    row : row + 1, pair * LANES : (pair + 1) * LANES
                ]
            head_bias[:, pl.ds((pair * 3 + 1) * LANES, LANES)] = jnp.zeros((1, LANES), jnp.float32)

        def body(part, carry):
            normed, _ = norm_rows(input_ref[part, :])
            low_one[part, :] = (normed * table[0:1, :] + table[1:2, :]).astype(low)
            back_two[part, :] = (top_ref[part, :].astype(jnp.float32) * keep_ref[part, :]).astype(low)
            return carry

        row_steps(body, 0)
        turn(back_two, back_two_turned)

    def head_store(pair, slot):
        column = pl.ds(pl.multiple_of(pair * 3 * LANES, LANES), 3 * LANES)
        return pltpu.make_async_copy(head_stage.at[slot], projected.at[:, column], head_sem.at[slot])

    def turn_first():
        turn(low_one, low_turned)
        far_store(4).start()

    def pair_of(at):
        turn_at, place = divmod(at, tensor)
        return lax.rem(here.rank + place, tensor) * per_rank + turn_at

    def head_load(at):
        turn_at, place = divmod(at, tensor)
        source = weight_qkv.at[lax.rem(here.rank + place, tensor), turn_at]
        return load(source, qkv_buf.at[at % 2], load_sem.at[at % 2])

    def heads(at):
        head_load(at).wait()
        pair = pair_of(at)
        slot = at % 2
        column = pl.ds(pl.multiple_of(pair * 3 * LANES, LANES), 3 * LANES)
        weight = qkv_buf[slot].reshape(width, 3 * LANES)
        value = (dot(low_one[...], weight) + head_bias[:, column]).astype(low)
        if at > 1:
            head_store(pair, slot).wait()
        head_stage[slot] = value
        head_store(pair, slot).start()
        mixed[:, pl.ds(pl.multiple_of(pair * LANES, LANES), LANES)] = attend_pair(value, mask_bias(mask_row()))

    def out_load():
        return [
            load(weight_out.at[rank, 0], out_buf.at[rank], load_sem.at[2]) for rank in range(tensor)
        ]

    def second_norm():
        far_store(3).start()
        for copy in out_load():
            copy.wait()
        columns = width // tensor
        for rank in range(tensor):
            weight = out_buf[rank].reshape(width, columns)
            term = dot(mixed[:, pl.ds(rank * columns, columns)], weight, CONTRACT_LAST)
            if rank == 0:
                grad_middle[...] = term
            else:
                grad_middle[...] += term

        def body(part, carry):
            middle = input_ref[part, :] + (grad_middle[part, :] + table[4:5, :]) * keep_ref[part, :]
            grad_middle[part, :] = middle
            normed, _ = norm_rows(middle)
            low_two[part, :] = (normed * table[5:6, :] + table[6:7, :]).astype(low)
            return carry

        row_steps(body, 0)
        turn(low_two, low_two_turned)

    stages = (one_stage, two_stage)
    keeps = (one_keep, two_keep)

    def hand_over(at):
        chunk, place = divmod(at, tensor)
        target = (*here.at, lax.rem(here.rank + place + 1, tensor))
        return [
            pltpu.make_async_remote_copy(
                src_ref=stages[which].at[at % 2],
                dst_ref=land[which].at[place, chunk],
                send_sem=store_sem.at[which, at % 2],
                recv_sem=land_sem.at[which, place, chunk],
                device_id=here.device(target),
                device_id_type=MESH,
            )
            for which in range(2)
        ]

    def keep_store(chunk):
        return [
            pltpu.make_async_copy(
                keeps[which].at[chunk % 2],
                out.at[chunk],
                keep_sem.at[which, chunk % 2],
            )
            for which, out in enumerate((grad_one, grad_two))
        ]

    def hidden_column(at):
        chunk, place = divmod(at, tensor)
        base = (lax.rem(here.rank + place + 1, tensor) * weight_one.shape[1] + chunk) * BLOCK
        return pl.ds(pl.multiple_of(base, LANES), BLOCK)

    def hidden_load(at):
        chunk, place = divmod(at, tensor)
        rank = lax.rem(here.rank + place + 1, tensor)
        return [
            load(source.at[rank, chunk], buffer.at[at % 2], load_sem.at[3 + 2 * which + at % 2])
            for which, (source, buffer) in enumerate(((weight_one, one_buf), (weight_two, two_buf)))
        ]

    staged = {}

    def hidden(at):
        chunk, place = divmod(at, tensor)
        column = hidden_column(at)
        for copy in hidden_load(at):
            copy.wait()
        half = rows // 2
        bias = hidden_bias[:, column]

        def body(turn_at, total):
            part = pl.ds(pl.multiple_of(turn_at * half, half), half)
            one = one_buf[at % 2].reshape(width, BLOCK)
            two = two_buf[at % 2].reshape(width, BLOCK)
            preact = dot(low_two[part, :], one) + bias
            gate = jax.nn.sigmoid(1.702 * preact)
            value = (preact * gate).astype(low)
            active[part, :] = value
            derivative = gate + 1.702 * preact * gate * (1.0 - gate)
            grad = (dot(back_two[part, :], two) * derivative).astype(low)
            grad_pre[part, :] = grad
            if at == 0:
                block_out[part, :] = dot(value, two, CONTRACT_LAST)
                grad_low_two[part, :] = dot(grad, one, CONTRACT_LAST)
            else:
                block_out[part, :] += dot(value, two, CONTRACT_LAST)
                grad_low_two[part, :] += dot(grad, one, CONTRACT_LAST)
            return total + jnp.sum(grad.astype(jnp.float32), axis=0, keepdims=True)

        pre_sums[:, column] = lax.fori_loop(0, 2, body, jnp.zeros((1, BLOCK), jnp.float32))
        mine = place == tensor - 1
        if mine:
            targets = [ref.at[chunk % 2] for ref in keeps]
            if chunk > 1:
                for copy in keep_store(chunk):
                    copy.wait()
        else:
            targets = [ref.at[at % 2] for ref in stages]
            for copy in staged.pop(at % 2, ()):
                copy.wait_send()
        for target, left, right in (
            (targets[0], low_two_turned, grad_pre),
            (targets[1], back_two_turned, active),
        ):
            target[...] = dot(left[...], right[...]).astype(low).reshape(*target.shape)
        if not mine:
            staged[at % 2] = hand_over(at)
            for copy in staged[at % 2]:
                copy.start()

    def fetch(chunk, place):
        for which, copy in enumerate(hand_over(chunk * tensor + place)):
            copy.wait_recv()
            load(land[which].at[place, chunk], other.at[which], load_sem.at[7]).start()

    def combine(chunk):
        for place in range(tensor - 1):
            if place:
                fetch(chunk, place)
            for which in range(2):
                load(land[which].at[place, chunk], other.at[which], load_sem.at[7]).wait()
            for which in range(2):
                keeps[which][chunk % 2] = keeps[which][chunk % 2] + other[which]
        for copy in keep_store(chunk):
            copy.start()

    def last_norm():
        def body(part, sums):
            middle = grad_middle[part, :]
            keep = keep_ref[part, :]
            top = top_ref[part, :].astype(jnp.float32)
            block_out[part, :] = middle + (block_out[part, :] + table[VEC - 1 : VEC, :]) * keep
            normed, inverse = norm_rows(middle)
            grad_low = grad_low_two[part, :]
            scaled = grad_low * table[5:6, :]
            first = jnp.mean(scaled, axis=1, keepdims=True)
            second = jnp.mean(scaled * normed, axis=1, keepdims=True)
            grad = top + inverse * (scaled - first - normed * second)
            grad_middle[part, :] = grad
            masked = grad * keep
            back_one[part, :] = masked.astype(low)
            terms = (masked, grad_low * normed, grad_low, top * keep)
            return tuple(old + jnp.sum(term, axis=0, keepdims=True) for old, term in zip(sums, terms))

        zero = jnp.zeros((1, width), jnp.float32)
        for at, value in enumerate(row_steps(body, (zero,) * 4)):
            vec_sums[at : at + 1, :] = value
        for at in range(3):
            far_store(at).start()

    fill_pack()
    here.barrier(((0,), (1,), (2,), (3,)))
    steps = Steps()
    whole = sum(part[3] for part in parts)
    nz, ny, nx = dims

    def lengths(item, phase):
        share = parts[item][3] / whole * UNIT
        across = ny * nx if item in gather.late else 1
        along = 1 if item in gather.late else nz
        return {
            "pair": (share * across, "end"),
            "mid": (share * across * 2, "mid"),
            "back": (share * across * 2, "end"),
            "all": (share * across * nz, "end"),
            "first": (share * along / 2, "xy"),
            "second": (share * along, "xy"),
            "core": (share * CORE_UNIT / UNIT, "core"),
        }[gather.phases(item)[phase]]

    for item, part in enumerate(parts):
        phases = len(gather.phases(item))
        for phase in range(phases + 1):
            after = [("copy", item, phase - 1)] if phase else []
            if phase == 0 and item >= DEPTH and item not in gather.late:
                after = [("copy", item - DEPTH, 1)]
            if item in gather.late:
                if phase == 0:
                    after = [("copy", DEPTH, 1)]
                if phase == 2:
                    after += [("copy", other, 1) for other in range(min(len(parts), item + 3)) if other not in gather.late]
            length, link = lengths(item, min(phase, phases - 1))
            steps.add(
                ("copy", item, phase),
                functools.partial(gather.advance, item, phase),
                PUMP,
                0.5 if phase == 0 else 0.0,
                after,
                [(item, phase - 1)] if phase else [],
                [((item, phase), link, length)] if phase < phases else [],
            )

    def landed(items):
        return [("copy", item, len(gather.phases(item))) for item in items]

    def start(copies):
        for copy in copies:
            copy.start()

    previous = None
    head_count, block_count = per_rank * tensor, FF // BLOCK
    for name, at, items in tasks:
        after = landed(items) + ([previous] if previous else [])
        begin, run, time = {
            "norm": (None, first_norm, 4.0),
            "turn": (None, turn_first, 1.5),
            "heads": (lambda at=at: head_load(at).start(), lambda at=at: heads(at), 3.0),
            "out": (lambda: start(out_load()), second_norm, 5.0),
            "hidden": (lambda at=at: start(hidden_load(at)), lambda at=at: hidden(at), 5.5),
        }[name]
        if begin is not None:
            first = landed(items)
            if at > 1:
                first.append((name, at - 2))
            steps.add(("load", name, at), begin, 0.1, 0.2, first)
            after.append(("load", name, at))
        mine = name == "hidden" and at % tensor == tensor - 1
        chunk = at // tensor
        if mine and chunk > 1:
            after.append(("sum", chunk - 2))
        starts = []
        if name == "hidden" and not mine:
            starts = [(("hand", at), "core", CORE_UNIT / len(parts))]
        steps.add((name, at), run, time, 1.0, after, (), starts)
        if mine:
            waits = [("hand", chunk * tensor + place) for place in range(tensor - 1)]
            if waits:
                before = [(name, at)] + ([("sum", chunk - 1)] if chunk else [])
                steps.add(("fetch", chunk), functools.partial(fetch, chunk, 0), 0.2, 0.3, before, waits, [(("got", chunk), "hbm", 1.0)])
                after, waits = [("fetch", chunk)], [("got", chunk)]
            else:
                after = [(name, at)]
            steps.add(("sum", chunk), functools.partial(combine, chunk), 0.8, 0.8, after, waits)
        previous = (name, at)
    steps.add(("last", 0), last_norm, 4.0, 0.9, [previous])
    steps.run()
    for at in range(5):
        far_store(at).wait()
    for slot in range(min(2, head_count)):
        head_store(0, slot).wait()
    for chunk in range(min(2, block_count // tensor)):
        for copy in keep_store(chunk):
            copy.wait()
    for copies in staged.values():
        for copy in copies:
            copy.wait_send()
    gather.finish()


def forward(dims, tensor, inputs, cotangent, token_mask, vectors, weights):
    own_rows, columns = weights[0].shape[1:]
    hidden = weights[2].shape[1]
    rows, width = inputs.shape
    low, full = jnp.bfloat16, jnp.float32
    widths = (3 * columns, LANES, columns, hidden, hidden)
    offsets = [sum(widths[:at]) for at in range(5)]
    per_rank = columns // LANES
    parts = [(1, offsets[1], None, LANES)]
    tasks = [("norm", 0, (0,)), ("turn", 0, (0,))]
    for at in range(per_rank):
        size = 3 * LANES
        parts.append((0, offsets[0] + at * size, at, size))
        tasks += [("heads", at * tensor + place, (len(parts) - 1,)) for place in range(tensor)]
    tasks.append(("out", 0, (len(parts),)))
    parts.append((2, offsets[2], 0, columns))
    for block in range(hidden // BLOCK):
        needed = (len(parts), len(parts) + 1)
        parts += [(which, offsets[which] + block * BLOCK, block, BLOCK) for which in (3, 4)]
        tasks += [("hidden", block * tensor + place, needed) for place in range(tensor)]
    count = len(parts)
    peers = max(1, dims[0] - 1, dims[1] + dims[2] - 2, tensor - 1)
    anywhere = pl.BlockSpec(memory_space=pl.ANY)
    inside = pl.BlockSpec(memory_space=pltpu.VMEM)
    block = (*dims, own_rows, BLOCK)
    chunks = hidden // BLOCK

    def shape(kind, *size):
        return jax.ShapeDtypeStruct(size, kind)

    return pl.pallas_call(
        functools.partial(forward_kernel, dims, tensor, tuple(parts), tuple(tasks)),
        name="forward",
        out_shape=[
            shape(low, tensor, per_rank, *dims, own_rows, 3 * LANES),
            shape(low, *dims, own_rows, LANES),
            shape(low, tensor, 1, *dims, own_rows, columns),
            *[shape(low, tensor, chunks, *block)] * 2,
            *[shape(low, max(1, tensor - 1), chunks, *block)] * 2,
            shape(full, rows, width),
            shape(full, rows, width),
            *[shape(low, rows, width)] * 2,
            shape(low, width, rows),
            shape(low, rows, 3 * width),
            *[shape(low, chunks, *block)] * 2,
            shape(full, 16, width),
            shape(full, 8, width),
            shape(full, 1, hidden * tensor),
            shape(full, rows, 1),
        ],
        in_specs=[inside] * 8,
        out_specs=[anywhere] * 15 + [inside] * 4,
        scratch_shapes=[
            pltpu.VMEM((rows, width), full),
            pltpu.VMEM((rows, width), full),
            *[pltpu.VMEM((rows, width), low)] * 3,
            pltpu.VMEM((width, rows), low),
            pltpu.VMEM((own_rows, sum(widths)), low),
            pltpu.VMEM((rows, 1), full),
            pltpu.VMEM((LANES, own_rows), full),
            pltpu.VMEM((*dims, own_rows, LANES), low),
            pltpu.VMEM((2, *dims, own_rows, 3 * LANES), low),
            pltpu.VMEM((2, rows, 3 * LANES), low),
            pltpu.VMEM((tensor, *dims, own_rows, columns), low),
            pltpu.VMEM((2, *block), low),
            pltpu.VMEM((2, *block), low),
            pltpu.VMEM((rows, width), low),
            pltpu.VMEM((width, rows), low),
            pltpu.VMEM((rows, width), low),
            pltpu.VMEM((width, rows), low),
            pltpu.VMEM((rows, width), full),
            pltpu.VMEM((1, hidden * tensor), full),
            pltpu.VMEM((1, 3 * width), full),
            pltpu.VMEM((2, *block), low),
            pltpu.VMEM((2, *block), low),
            pltpu.VMEM((2, *block), low),
            pltpu.VMEM((2, *block), low),
            pltpu.VMEM((2, *block), low),
            pltpu.VMEM((rows, BLOCK), low),
            pltpu.VMEM((rows, BLOCK), low),
            pltpu.SemaphoreType.DMA((8,)),
            pltpu.SemaphoreType.DMA((2, 2)),
            pltpu.SemaphoreType.DMA((2, 2)),
            pltpu.SemaphoreType.DMA((2,)),
            pltpu.SemaphoreType.DMA((2, max(1, tensor - 1), chunks)),
            pltpu.SemaphoreType.DMA((5,)),
            pltpu.SemaphoreType.DMA((count,)),
            pltpu.SemaphoreType.DMA((count, 6, peers)),
            pltpu.SemaphoreType.DMA((count, 6, peers)),
        ],
        compiler_params=pltpu.CompilerParams(
            collective_id=0, has_side_effects=True, vmem_limit_bytes=62 << 20
        ),
    )(inputs, cotangent, token_mask, vectors, *weights)


class Layout:
    def __init__(self, columns, hidden, order):
        sizes = {"qkv": 3 * columns, "out": columns, "one": hidden, "two": hidden, "vec": LANES}
        self.order = order
        self.sizes = sizes
        self.start = {}
        at = 0
        for name in order:
            self.start[name] = at
            at += sizes[name]
        self.total = at
        self.columns = columns

    def span(self, name):
        return (self.start[name], self.sizes[name])

    def matrices(self):
        base = self.start["qkv"]
        pairs = range(self.columns // LANES)
        spans = [[(base + (pair * 3 + at) * LANES, LANES) for pair in pairs] for at in range(3)]
        return spans + [[self.span(name)] for name in ("out", "one", "two")]


def pick(values, lane):
    row = jnp.zeros((1, LANES), jnp.float32)
    for at, value in enumerate(values):
        row = jnp.where(lane == at, value, row)
    return row


def total_of(values):
    return jnp.sum(jnp.sum(values, axis=1, keepdims=True), axis=0, keepdims=True)


def attend_pair_back(heads, bias, grads):
    parts = ([], [], [])
    for head in range(2):
        query, key, value = (
            heads[:, kind * LANES + head * HEAD_DIM : kind * LANES + (head + 1) * HEAD_DIM] for kind in range(3)
        )
        grad = grads[:, head * HEAD_DIM : (head + 1) * HEAD_DIM]
        scores = dot(key, query, CONTRACT_LAST) * (HEAD_DIM ** (-0.5) * LOG2E) + bias
        raised = jnp.exp2(scores - jnp.max(scores, axis=0, keepdims=True))
        attention = raised * (1.0 / jnp.sum(raised, axis=0, keepdims=True))
        grad_value = dot(attention.astype(jnp.bfloat16), grad)
        grad_attention = dot(value, grad, CONTRACT_LAST)
        weighted = jnp.sum(attention * grad_attention, axis=0, keepdims=True)
        grad_scores = (attention * (grad_attention - weighted) * HEAD_DIM ** (-0.5)).astype(jnp.bfloat16)
        grad_key = dot(grad_scores, query)
        grad_query = dot(key.T, grad_scores).T
        for kind, part in enumerate((grad_query, grad_key, grad_value)):
            parts[kind].append(part.astype(jnp.bfloat16))
    return jnp.concatenate([piece for kind in parts for piece in kind], axis=1)


def backward_kernel(dims, tensor, items, layout, *refs):
    (
        sum_two,
        sum_one,
        weight_qkv,
        weight_out,
        projected,
        input_ref,
        middle_ref,
        *far,
        bias_ref,
        table,
        vec_sums,
        pre_sums,
    ) = refs[:14]
    far = (*far, *refs[14:18])
    row_states, col_states = refs[18:22], refs[22:26]
    second_ref, vector_ref = refs[26:28]
    input_grad_out, total_ref, col_new_ref, row_new_ref, second_new_ref, sums_ref = refs[28:34]
    groups = ("ffn", "out", "qkv", "vec")
    kinds = ("own", "one_x", "one_y", "two_y", "two_x", "from_z")
    held = {}
    for kind in kinds:
        for group in groups:
            held[kind, group] = refs[34 + len(held)]
    for group in groups[1:]:
        held["core", group] = refs[34 + len(held)]
    (
        input_grad,
        late_z,
        late_one_y,
        late_one_x,
        late_two_x,
        late_two_y,
        col_sum,
        col_in,
        row_sum,
        row_in,
        small,
        small_in,
        square,
        turned,
        mixed,
        back_one,
        *weights,
        low_turned,
        back_turned,
        grad_mixed,
        out_buf,
        qkv_buf,
        head_buf,
        row_buf,
        out_stage,
        qkv_stage,
        vec_stage,
        head_sums,
        table_grad_ref,
        load_sem,
        stage_sem,
        core_sem,
        local_sem,
        send_sem,
        recv_sem,
        sum_send,
        sum_recv,
        far_sem,
    ) = refs[34 + len(held) :]
    near = (mixed, low_turned, back_one, *weights)

    def far_load(at):
        return pltpu.make_async_copy(far[at], near[at], far_sem.at[at])

    here = Place(dims, tensor)
    nz, ny, nx = dims
    low = jnp.bfloat16
    own_rows = total_ref.shape[0]
    half_rows = own_rows // 2
    rows, width = input_grad.shape
    own_place = (*here.at, here.rank)
    count = len(items)

    def columns(item):
        _, start, size, _ = items[item]
        return pl.ds(start, size)

    def at_home(kind, item):
        name = items[item][0]
        if name in ("one", "two"):
            members = [at for at, other in enumerate(items) if other[0] in ("one", "two")]
            if kind != "own":
                members = [at for at in members if at not in late]
            return held[kind, "ffn"].at[members.index(item)]
        members = [at for at, other in enumerate(items) if other[0] == name]
        return held[kind, name].at[members.index(item)]

    def phases(item):
        lengthwise = along_z(nz)[::-1] if item in late else ("all",)
        across = ("first", "second")
        return (*lengthwise, *across) if item in late else (*across, *lengthwise)

    def moves(item, phase):
        first, second, whole = pl.ds(0, half_rows), pl.ds(half_rows, half_rows), pl.ds(0, own_rows)
        kind = phases(item)[phase]
        own = at_home("own", item)
        found = []
        if kind in ("pair", "mid", "back"):
            pair, far, near, middle = here.line()
            outside = jnp.logical_not(middle)
            rest = (slice(None), slice(None)) if item in late else here.at[1:]
            buffer = late_z.at[late.index(item)] if item in late else at_home("from_z", item)
            z = here.at[0]
            device, sent_z, add_z, slots, sends, receives = {
                "back": (near, pl.ds(far, 2), pl.ds(far, 2), pl.ds(0, 2), outside, middle),
                "mid": (3 - z, pl.ds(far, 2), pl.ds(pair, 2), pl.ds(2, 2), middle, middle),
                "pair": (near, near, z, 4, None, None),
            }[kind]
            source = own.at[(sent_z, *rest, whole)]
            found.append((here.at_z(device), source, buffer.at[slots], (add_z, *rest), whole, sends, receives))
            return found
        if item in late:
            at = late.index(item)
            steps = {
                "all": ((0, (0,), whole, late_z.at[at]),),
                "first": ((1, (0, 1), first, late_one_y.at[at]), (2, (0, 2), second, late_one_x.at[at])),
                "second": ((2, (0, 1, 2), first, late_two_x.at[at]), (1, (0, 1, 2), second, late_two_y.at[at])),
            }[kind]
        else:
            steps = {
                "first": ((2, (2,), first, "one_x"), (1, (1,), second, "one_y")),
                "second": ((1, (1, 2), first, "two_y"), (2, (1, 2), second, "two_x")),
                "all": ((0, (0, 1, 2), whole, "from_z"),),
            }[kind]
            steps = [(*step[:3], at_home(step[3], item)) for step in steps]
        for axis, fixed, part, landing in steps:
            for step in range(1, here.size(axis)):
                target = here.moved(axis, step)
                index = tuple(target[a] if a in fixed else slice(None) for a in range(3))
                added = tuple(here.at[a] if a in fixed else slice(None) for a in range(3))
                source = own.at[(*index, part)]
                found.append((here.device(target), source, landing.at[step - 1], added, part, None, None))
        return found

    def copies(item, phase):
        found = []
        for at, (device, source, landing, added, part, sends, receives) in enumerate(moves(item, phase)):
            copy = pltpu.make_async_remote_copy(
                src_ref=source,
                dst_ref=landing,
                send_sem=send_sem.at[item, phase, at],
                recv_sem=recv_sem.at[item, phase, at],
                device_id=device,
                device_id_type=MESH,
            )
            found.append((sends, receives, copy, added, part, landing))
        return found

    def add_core(item):
        own, brought = at_home("own", item), at_home("core", item)

        def body(at, carry):
            z, y, x = at // (ny * nx), at // nx % ny, at % nx
            value = own[z, y, x]
            for step in range(tensor - 1):
                value = value + brought[step, z, y, x]
            own[z, y, x] = value
            return carry

        if tensor > 1:
            lax.fori_loop(0, nz * ny * nx, body, 0)

    def add_in(item, landing, added, part):
        own = at_home("own", item)
        sizes, starts = [], []
        for axis, at in enumerate(added):
            if isinstance(at, slice):
                sizes.append(dims[axis])
                starts.append(0)
            elif hasattr(at, "start"):
                sizes.append(at.size)
                starts.append(at.start)
            else:
                sizes.append(None)
                starts.append(at)
        loops = 1
        for size in sizes:
            loops *= size or 1

        def body(at, carry):
            place, inner, rest = [], [], at
            for size, start in reversed(list(zip(sizes, starts))):
                if size is None:
                    place.insert(0, start)
                else:
                    place.insert(0, start + rest % size)
                    inner.insert(0, rest % size)
                    rest = rest // size
            where = (*place, part)
            own[where] = own[where] + (landing[tuple(inner)] if inner else landing[...])
            return carry

        if loops == 1:
            body(0, 0)
        else:
            lax.fori_loop(0, loops, body, 0)

    def put_total(item, arrived):
        wide = columns(item)
        parts_of = {}
        for landing, part in arrived:
            parts_of.setdefault((part.start, part.size), []).append(landing)
        for (start, size), landings in parts_of.items():
            part = pl.ds(start, size)
            value = at_home("own", item)[(*here.at, part)].astype(jnp.float32)
            for landing in landings:
                value = value + landing[...].astype(jnp.float32)
            total_ref[part, wide] = value
        if items[item][0] == "vec":
            return
        for at, spans in enumerate(layout.matrices()):
            for start, size in spans:
                low_end, high_end = max(start, wide.start), min(start + size, wide.start + wide.size)
                if low_end < high_end:
                    square = total_ref[:, pl.ds(low_end, high_end - low_end)]
                    square = square * square
                    col_sum[0, :, pl.ds(low_end, high_end - low_end)] = jnp.sum(square, axis=0, keepdims=True)
                    found = jnp.sum(square, axis=1, keepdims=True)
                    row_sum[0] = row_sum[0] + jnp.where(lane == at, found, 0.0)

    sent = []
    lane = lax.broadcasted_iota(jnp.int32, (1, LANES), 1)
    row_sum[0] = jnp.zeros_like(row_sum[0])
    guarded_sent = []
    late = [at for at in LATE_ITEMS if items[at][0] in ("one", "two")]

    def exchange(kind, phase, axes, buffer, landing):
        moved = []
        for at, device in enumerate(here.peers(*axes)):
            copy = pltpu.make_async_remote_copy(
                src_ref=buffer.at[phase],
                dst_ref=landing.at[phase, at],
                send_sem=sum_send.at[kind, phase, at],
                recv_sem=sum_recv.at[kind, phase, at],
                device_id=device,
                device_id_type=MESH,
            )
            copy.start()
            moved.append(copy)
        sent.extend(moved)

        def finish():
            value = buffer[phase]
            for at, copy in enumerate(moved):
                copy.wait_recv()
                value = value + landing[phase, at]
            buffer[phase + 1] = value

        return finish

    def hand_over(item, step, source, sem):
        return pltpu.make_async_remote_copy(
            src_ref=source,
            dst_ref=at_home("core", item).at[step - 1],
            send_sem=sem,
            recv_sem=core_sem.at[item, step - 1],
            device_id=here.device(here.moved(3, step)),
            device_id_type=MESH,
        )

    arriving = {}

    def keep_own(item, value):
        at_home("own", item)[...] = value.reshape(nz, ny, nx, own_rows, value.shape[1])

    out_items = [at for at, item in enumerate(items) if item[0] == "out"]
    qkv_items = [at for at, item in enumerate(items) if item[0] == "qkv"]
    vec_item = count - 1
    per_rank = len(qkv_items)
    steps_in_all = per_rank * tensor

    def rank_at(step):
        return lax.rem(here.rank + step, tensor)

    def pair_loads(at):
        turn_at, place = divmod(at, tensor)
        pair = rank_at(place + 1) * per_rank + turn_at
        column = pl.ds(pl.multiple_of(pair * 3 * LANES, LANES), 3 * LANES)
        near = at % 2
        return pair, column, [
            pltpu.make_async_copy(
                weight_qkv.at[rank_at(place + 1), turn_at], qkv_buf.at[near], load_sem.at[0, near]
            ),
            pltpu.make_async_copy(projected.at[:, column], head_buf.at[near], load_sem.at[1, near]),
        ]

    def out_task():
        fetch = [
            pltpu.make_async_copy(weight_out.at[rank, 0], out_buf.at[rank], load_sem.at[2, 0])
            for rank in range(tensor)
        ]
        for copy in fetch:
            copy.start()
        far_load(2).wait()
        turn(back_one, back_turned)
        far_load(0).wait()
        for copy in pair_loads(0)[2]:
            copy.start()
        size = out_stage.shape[5]
        item = out_items[0]
        for step in range(1, tensor + 1):
            column = pl.ds(pl.multiple_of(rank_at(step) * size, LANES), size)
            value = dot(back_turned[...], mixed[:, column]).astype(low)
            if step < tensor:
                out_stage[step - 1] = value.reshape(nz, ny, nx, own_rows, size)
                copy = hand_over(item, step, out_stage.at[step - 1], stage_sem.at[item, step - 1])
                copy.start()
                sent.append(copy)
                arriving.setdefault(item, []).append(copy)
            else:
                keep_own(item, value)
        for copy in fetch:
            copy.wait()
        for rank in range(tensor):
            weight = out_buf[rank].reshape(width, size)
            grad_mixed[:, pl.ds(rank * size, size)] = dot(back_one[...], weight).astype(low)
        far_load(1).wait()

    def state_task():
        def fill(refs, other):
            square[...] = jnp.full_like(square, other)
            base = 0
            for ref in refs:
                square[pl.ds(base, ref.shape[0]), :] = ref[...]
                base += ref.shape[0]
            return square[...].T

        for at in range(3, 7):
            far_load(at).wait()
        turned[0] = fill(row_states, 1.0)
        turned[1] = fill((second_ref,), 1.0)
        turned[2] = fill((vector_ref,), 0.0)

    staged = {}

    def pair_task(at):
        turn_at, place = divmod(at, tensor)
        pair, column, loads = pair_loads(at)
        for copy in loads:
            copy.wait()
        if at + 1 < steps_in_all:
            for copy in pair_loads(at + 1)[2]:
                copy.start()
        near = at % 2
        grads = grad_mixed[:, pl.ds(pl.multiple_of(pair * LANES, LANES), LANES)]
        value = attend_pair_back(head_buf[near], bias_ref[...], grads)
        head_sums[:, column] = jnp.sum(value.astype(jnp.float32), axis=0, keepdims=True)
        weight = qkv_buf[near].reshape(width, 3 * LANES)
        term = dot(value, weight, CONTRACT_LAST)
        if at == 0:
            input_grad[...] = term
        else:
            input_grad[...] += term
        item = qkv_items[turn_at]
        mine = place + 1 == tensor
        if not mine and 0 in staged:
            staged[0].wait_send()
        grad = dot(low_turned[...], value).astype(low)
        if mine:
            keep_own(item, grad)
        else:
            qkv_stage[...] = grad.reshape(nz, ny, nx, own_rows, 3 * LANES)
        if not mine:
            copy = hand_over(item, place + 1, qkv_stage, stage_sem.at[item, place])
            copy.start()
            staged[0] = copy
            arriving.setdefault(item, []).append(copy)

    def grad_store():
        return pltpu.make_async_copy(input_grad, input_grad_out, far_sem.at[7])

    def last_task():
        step_rows = row_buf.shape[2]

        def fetch(at):
            near = lax.rem(at, 2)
            part = pl.ds(pl.multiple_of(at * step_rows, step_rows), step_rows)
            return [
                pltpu.make_async_copy(source.at[part, :], row_buf.at[which, near], load_sem.at[which, near])
                for which, source in enumerate((input_ref, middle_ref))
            ]

        for copy in fetch(0):
            copy.start()

        def body(at, sums):
            for copy in fetch(at):
                copy.wait()

            @pl.when(at + 1 < rows // step_rows)
            def _():
                for copy in fetch(at + 1):
                    copy.start()

            near = lax.rem(at, 2)
            part = pl.ds(pl.multiple_of(at * step_rows, step_rows), step_rows)
            normed, inverse = norm_rows(row_buf[0, near])
            grad_low = input_grad[part, :]
            scaled = grad_low * table[0:1, :]
            first = jnp.mean(scaled, axis=1, keepdims=True)
            second = jnp.mean(scaled * normed, axis=1, keepdims=True)
            input_grad[part, :] = row_buf[1, near] + inverse * (scaled - first - normed * second)
            terms = (grad_low * normed, grad_low)
            return tuple(old + jnp.sum(term, axis=0, keepdims=True) for old, term in zip(sums, terms))

        zero = jnp.zeros((1, width), jnp.float32)
        found = lax.fori_loop(0, rows // step_rows, body, (zero, zero))
        grad_store().start()
        table_grad_ref[...] = jnp.zeros_like(table_grad_ref)
        for at in range(2):
            table_grad_ref[at : at + 1, :] = found[at]
        for pair in range(width // LANES):
            for kind, row in ((0, 2), (2, 3)):
                table_grad_ref[row : row + 1, pl.ds(pair * LANES, LANES)] = head_sums[
                    :, pl.ds((pair * 3 + kind) * LANES, LANES)
                ]
        for at, row in enumerate((4, 5, 6, VEC - 1)):
            table_grad_ref[row : row + 1, :] = vec_sums[at : at + 1, :]
        for at in range(VEC - 8):
            table_grad_ref[7 + at : 8 + at, :] = pre_sums[:, pl.ds(at * width, width)]
        value = table_grad_ref[...].T.astype(low)
        vec_stage[...] = value.reshape(nz, ny, nx, own_rows, LANES)
        for step in range(1, tensor):
            copy = hand_over(vec_item, step, vec_stage, stage_sem.at[vec_item, step - 1])
            copy.start()
            sent.append(copy)
            arriving.setdefault(vec_item, []).append(copy)
        keep_own(vec_item, value)

    for at in (2, 0, 1, 3, 4, 5, 6):
        far_load(at).start()
    here.barrier(((0, 3), (1, 2)))
    local = {}
    for item, (name, _, _, source) in enumerate(items):
        if name in ("one", "two"):
            array = sum_one if name == "one" else sum_two
            copy = pltpu.make_async_copy(
                array.at[source], at_home("own", item), local_sem.at[item]
            )
            copy.start()
            local[item] = copy

    def advance(item, phase):
        last = len(phases(item))
        if phase > 0:
            arrived = []
            for _, receives, copy, added, part, landing in copies(item, phase - 1):

                def take(copy=copy, landing=landing, added=added, part=part):
                    copy.wait_recv()
                    if phase < last:
                        add_in(item, landing, added, part)

                guarded(receives, take)
                arrived.append((landing, part))
            if phase == last:
                put_total(item, arrived)
        elif item in local:
            local[item].wait()
        else:
            for copy in arriving.get(item, ()):
                copy.wait_recv()
            add_core(item)
        if phase < last:
            for sends, _, copy, *_ in copies(item, phase):
                guarded(sends, copy.start)
                guarded_sent.append((sends, copy))

    steps = Steps()
    owner = {item: ("out", 0) for item in out_items}
    owner |= {item: ("pair", tensor * (at + 1) - 1) for at, item in enumerate(qkv_items)}
    owner[vec_item] = ("last", 0)
    for item, (name, _, size, _) in enumerate(items):
        share = size / layout.total * UNIT
        across = ny * nx if item in late else 1
        along = 1 if item in late else nz
        lengths = {
            "pair": (share * across, "end"),
            "mid": (share * across * 2, "mid"),
            "back": (share * across * 2, "end"),
            "all": (share * across * nz, "end"),
            "first": (share * along, "xy"),
            "second": (share * along / 2, "xy"),
        }
        if item in late:
            lengths |= {"first": (share, "xy"), "second": (share / 2, "xy")}
        early = item not in owner
        kinds = phases(item)
        for phase in range(len(kinds) + 1):
            after = [("copy", item, phase - 1)] if phase else []
            waits = [(item, phase - 1)] if phase else []
            if phase == 0 and early and item >= DEPTH + len(late):
                after = [("copy", item - DEPTH, 1)]
            if phase == 0 and not early:
                after, waits = [owner[item]], [("core", owner[item])]
            starts = []
            if phase < len(kinds):
                length, link = lengths[kinds[phase]]
                starts = [((item, phase), link, length)]
            steps.add(
                ("copy", item, phase),
                functools.partial(advance, item, phase),
                PUMP * (1.5 if phase == 1 else 1.0),
                (0.5 if phase == 0 and early else 0.0),
                after,
                waits,
                starts,
            )
    steps.add(("state", 0), state_task, 1.0, 2.0)
    steps.add(("out", 0), out_task, 8.0, 1.0, (), (), [(("core", ("out", 0)), "core", CORE_UNIT / 12)])
    for at in range(steps_in_all):
        after = [("pair", at - 1) if at else ("out", 0)]
        starts = [(("core", ("pair", at)), "core", CORE_UNIT / 24)]
        steps.add(("pair", at), functools.partial(pair_task, at), 6.0, 1.0, after, (), starts)
    steps.add(
        ("last", 0), last_task, 4.0, 1.0, [("pair", steps_in_all - 1)], (), [(("core", ("last", 0)), "core", 1.0)]
    )
    steps.run()
    sent.extend(staged.values())

    decay_rate = 1.0 - STEP ** (-0.8)
    keep_old = 1.0 - decay_rate
    long = layout.sizes["one"] * tensor
    matrices = layout.matrices()
    finish_row = exchange(0, 0, (3,), row_sum, row_in)
    finish_col = exchange(1, 0, (0,), col_sum, col_in)
    vec_start = layout.start["vec"]
    table_grad = total_ref[:, pl.ds(vec_start, LANES)]
    second_new = decay_rate * turned[1] + keep_old * (table_grad * table_grad + EPS_ONE)
    second_new_ref[...] = second_new
    vector_update = table_grad * lax.rsqrt(second_new)
    vector_sums = jnp.sum(vector_update * vector_update, axis=0, keepdims=True) / tensor
    vector_weight = jnp.sum(turned[2] * turned[2], axis=0, keepdims=True) / tensor
    weight_sums = [total_of(jnp.sum(weights[0][...] * weights[0][...], axis=0))]
    weight_sums += [total_of(ref[...] * ref[...]) for ref in weights[1:]]
    finish_row()
    row_counts = pick([jnp.full((1, 1), 1.0 / size, jnp.float32) for size in (width, width, width, width, long, long)], lane)
    row_new = decay_rate * turned[0] + keep_old * (row_sum[1] * row_counts + EPS_ONE)
    row_new_ref[...] = row_new
    finish_col()
    exchange(1, 1, (1, 2), col_sum, col_in)()
    for at, spans in enumerate(matrices):
        for place, (start, size) in enumerate(spans):
            if at < 3:
                old = col_states[0][at : at + 1, pl.ds(place * LANES, LANES)]
            else:
                old = col_states[at - 2][...]
            fresh = keep_old * (col_sum[2, :, pl.ds(start, size)] / width + EPS_ONE)
            col_new_ref[:, pl.ds(start, size)] = decay_rate * old + fresh
    ratios = []
    means = []
    for at, spans in enumerate(matrices):
        row_at = row_new[:, at : at + 1]
        ratio = 0.0
        for start, size in spans:
            value = total_ref[:, pl.ds(start, size)]
            col_at = col_new_ref[:, pl.ds(start, size)]
            ratio = ratio + total_of(value * value / (row_at * col_at))
        ratios.append(ratio)
        if at in (3, 5):
            means.append(jnp.sum(col_at, axis=1, keepdims=True) / (nz * ny * nx))
        else:
            means.append(jnp.sum(row_at, axis=0, keepdims=True) / tensor)
    small[0] = jnp.concatenate(
        [pick(ratios + means + weight_sums, lane), vector_sums, vector_weight, jnp.zeros((5, LANES), jnp.float32)], axis=0
    )
    exchange(2, 0, (0, 3), small, small_in)()
    exchange(2, 1, (1, 2), small, small_in)()
    sums_ref[...] = small[2]
    grad_store().wait()
    for copy in sent:
        copy.wait_send()
    for condition, copy in guarded_sent:
        guarded(condition, copy.wait_send)


def backward(dims, tensor, layout, large, near, weights, states):
    rows, width = large[-1].shape
    own_rows = width // (dims[0] * dims[1] * dims[2])
    half_rows = own_rows // 2
    columns = layout.columns
    items = []
    for block in range(layout.sizes["one"] // BLOCK):
        for name in ("two", "one"):
            items.append((name, layout.start[name] + block * BLOCK, BLOCK, block))
    items.append(("out", layout.start["out"], columns, 0))
    for start in range(0, 3 * columns, 3 * LANES):
        items.append(("qkv", layout.start["qkv"] + start, 3 * LANES, start))
    items.append(("vec", layout.start["vec"], LANES, 0))
    nz, ny, nx = dims
    peers = max(1, nz - 1, ny + nx - 2)
    group = max(1, nz * tensor - 1, ny * nx - 1)
    others = max(1, tensor - 1)
    offset = layout.total
    late = max(1, len(LATE_ITEMS))
    line = 5 if nz == 4 else nz - 1
    groups = (
        (2 * layout.sizes["one"] // BLOCK, BLOCK),
        (1, columns),
        (columns // LANES, 3 * LANES),
        (1, LANES),
    )
    leads = (
        (nz, ny, nx, own_rows),
        (nx - 1, nz, ny, half_rows),
        (ny - 1, nz, nx, half_rows),
        (ny - 1, nz, half_rows),
        (nx - 1, nz, half_rows),
        (nz - 1, own_rows),
    )
    low, full = jnp.bfloat16, jnp.float32
    anywhere = pl.BlockSpec(memory_space=pl.ANY)
    inside = pl.BlockSpec(memory_space=pltpu.VMEM)

    def hold(*shape):
        return pltpu.VMEM(tuple(max(1, size) for size in shape), low)

    sums = offset - LANES
    count = len(items)
    return pl.pallas_call(
        functools.partial(backward_kernel, dims, tensor, tuple(items), layout),
        name="backward",
        out_shape=[
            jax.ShapeDtypeStruct((rows, width), full),
            jax.ShapeDtypeStruct((own_rows, offset), full),
            jax.ShapeDtypeStruct((1, sums), full),
            jax.ShapeDtypeStruct((own_rows, LANES), full),
            jax.ShapeDtypeStruct((own_rows, LANES), full),
            jax.ShapeDtypeStruct((8, LANES), full),
        ],
        in_specs=[anywhere] * len(large) + [inside] * len(near) + [anywhere] * 4 + [inside] * len(states),
        out_specs=[anywhere] + [inside] * 5,
        scratch_shapes=[
            *(
                hold(number if lead is leads[0] or at else number - late, *lead, size)
                for lead in leads
                for at, (number, size) in enumerate(groups)
            ),
            *(hold(number, others, nz, ny, nx, own_rows, size) for number, size in groups[1:]),
            pltpu.VMEM((rows, width), full),
            hold(late, line, ny, nx, own_rows, BLOCK),
            hold(late, ny - 1, nx, half_rows, BLOCK),
            hold(late, nx - 1, ny, half_rows, BLOCK),
            hold(late, nx - 1, half_rows, BLOCK),
            hold(late, ny - 1, half_rows, BLOCK),
            pltpu.VMEM((3, 1, sums), full),
            pltpu.VMEM((2, max(1, nz - 1, ny * nx - 1), 1, sums), full),
            pltpu.VMEM((2, own_rows, LANES), full),
            pltpu.VMEM((1, others, own_rows, LANES), full),
            pltpu.VMEM((3, 8, LANES), full),
            pltpu.VMEM((2, group, 8, LANES), full),
            pltpu.VMEM((LANES, own_rows), full),
            pltpu.VMEM((3, own_rows, LANES), full),
            *[hold(rows, width)] * 2,
            *(pltpu.VMEM(weight.shape, full) for weight in weights),
            hold(width, rows),
            hold(width, rows),
            hold(rows, width),
            hold(tensor, *dims, own_rows, columns),
            hold(2, *dims, own_rows, 3 * LANES),
            hold(2, rows, 3 * LANES),
            pltpu.VMEM((2, 2, LANES // 2, width), full),
            hold(others, *dims, own_rows, columns),
            hold(*dims, own_rows, 3 * LANES),
            hold(*dims, own_rows, LANES),
            pltpu.VMEM((1, 3 * width), full),
            pltpu.VMEM((LANES, width), full),
            pltpu.SemaphoreType.DMA((3, 2)),
            pltpu.SemaphoreType.DMA((count, others)),
            pltpu.SemaphoreType.DMA((count, others)),
            pltpu.SemaphoreType.DMA((count,)),
            pltpu.SemaphoreType.DMA((count, 5, peers)),
            pltpu.SemaphoreType.DMA((count, 5, peers)),
            pltpu.SemaphoreType.DMA((3, 2, group)),
            pltpu.SemaphoreType.DMA((3, 2, group)),
            pltpu.SemaphoreType.DMA((8,)),
        ],
        compiler_params=pltpu.CompilerParams(
            collective_id=1, has_side_effects=True, vmem_limit_bytes=63 << 20
        ),
    )(*large, *near, *weights, *states)


def update_kernel(layout, width, long, *refs):
    block_in, grad_in = refs[:2]
    far = refs[2:12]
    block_out, input_grad = refs[12:14]
    own_qkv, own_out, own_one, own_two, own_table = refs[14:19]
    new_qkv, new_out, new_one, new_two, new_vectors, second_new = refs[19:25]
    qkv_row, qkv_col, out_row, out_col, one_row, one_col, two_row, two_col = refs[25:33]
    near, passing, sem = refs[33:43], refs[43:45], refs[45]
    loads = [
        pltpu.make_async_copy(source, target, sem.at[at])
        for at, (source, target) in enumerate(zip((*far, block_in, grad_in), (*near, *passing)))
    ]
    later = loads[len(far) :]
    long_copies = [
        pltpu.make_async_copy(source, target, sem.at[12 + at])
        for at, (source, target) in enumerate(zip(passing, (block_out, input_grad)))
    ]
    for copy in loads:
        copy.start()
    for copy in loads[: len(far)]:
        copy.wait()
    total_ref, col_ref, row_ref, second_ref, sums_ref, vector_ref = near[:6]
    weights = near[6:]
    lane = lax.broadcasted_iota(jnp.int32, (1, LANES), 1)

    def at(index):
        return sums_ref[0:1, index : index + 1]

    lengths = (width, width, width, width, width, long)
    means = [at(6 + m) / lengths[m] for m in range(6)]
    squares = [means[m] * at(m) for m in range(6)]
    squares = [squares[0] + squares[1] + squares[2], *squares[3:]]
    entries = (3 * width * width, width * width, width * long, width * long)
    step_size = []
    for m in range(4):
        damping = 1.0 / jnp.maximum(1.0, jnp.sqrt(squares[m] / entries[m] + 1e-06) / CLIP_LEVEL)
        step_size.append(LEARN_RATE * jnp.sqrt(at(12 + m) / entries[m] + 1e-06) * damping)
    spread = [(m, place, *span) for m, spans in enumerate(layout.matrices()) for place, span in enumerate(spans)]
    for m, place, start, size in spread:
        if m == 3:
            for load, store in zip(later, long_copies):
                load.wait()
                store.start()
        grad = total_ref[:, pl.ds(start, size)]
        col = col_ref[:, pl.ds(start, size)]
        step = step_size[max(0, m - 2)] * grad * lax.rsqrt(row_ref[:, m : m + 1] * col / means[m])
        if m < 3:
            part = slice(place * LANES, (place + 1) * LANES)
            own_qkv[m, :, part] = grad
            new_qkv[m, :, part] = weights[0][m, :, part] - step
            qkv_col[m : m + 1, part] = col
        else:
            own, new, state = (
                (own_out, new_out, out_row),
                (own_one, new_one, one_col),
                (own_two, new_two, two_row),
            )[m - 3]
            own[...] = grad
            new[...] = weights[m - 2][...] - step
            state[...] = col
    row_flat = row_ref[...].T
    qkv_row[...] = row_flat[0:3]
    out_col[...] = row_flat[3:4]
    one_row[...] = row_flat[4:5]
    two_col[...] = row_flat[5:6]

    wide = (lane >= 7) & (lane < VEC - 1)
    counts = jnp.where(wide, float(long), float(width))

    def grouped(values):
        inside = jnp.sum(jnp.where(wide, values, 0.0), axis=1, keepdims=True)
        return jnp.where(wide, inside, values)

    table_grad = total_ref[:, pl.ds(layout.start["vec"], LANES)]
    update = table_grad * lax.rsqrt(second_ref[...])
    norm = jnp.sqrt(grouped(sums_ref[1:2, :]) / counts + 1e-06)
    size = jnp.sqrt(grouped(sums_ref[2:3, :]) / counts + 1e-06)
    change = LEARN_RATE * size / jnp.maximum(1.0, norm / CLIP_LEVEL) * update
    own_table[...] = table_grad.T[:VEC]
    new_vectors[...] = vector_ref[...] - change.T[:VEC]
    second_new[...] = second_ref[...].T[:VEC]
    for copy in long_copies:
        copy.wait()


def update_weights(layout, width, long, columns, hidden, rows, results, values, vectors, weights):
    full = jnp.float32
    shapes = [
        *(result.shape for result in results),
        (3, rows, columns),
        (rows, columns),
        (rows, hidden),
        (rows, hidden),
        (VEC, rows),
        (3, rows, columns),
        (rows, columns),
        (rows, hidden),
        (rows, hidden),
        (VEC, rows),
        (VEC, rows),
        (3, rows),
        (3, columns),
        (1, columns),
        (1, rows),
        (1, rows),
        (1, hidden),
        (1, hidden),
        (1, rows),
    ]
    far = (*values, vectors, *weights)
    anywhere = pl.BlockSpec(memory_space=pl.ANY)
    inside = pl.BlockSpec(memory_space=pltpu.VMEM)
    return pl.pallas_call(
        functools.partial(update_kernel, layout, width, long),
        name="update",
        out_shape=[jax.ShapeDtypeStruct(shape, full) for shape in shapes],
        in_specs=[anywhere] * (2 + len(far)),
        out_specs=[anywhere] * 2 + [inside] * (len(shapes) - 2),
        scratch_shapes=[
            *(pltpu.VMEM(array.shape, full) for array in (*far, *results)),
            pltpu.SemaphoreType.DMA((4 + len(far),)),
        ],
        compiler_params=pltpu.CompilerParams(vmem_limit_bytes=63 << 20),
    )(*results, *far)


def on_device(
    inputs,
    cotangent,
    token_mask,
    w_qkv,
    w_out,
    w_fc1,
    w_fc2,
    vectors,
    qkv_row,
    qkv_col,
    out_row,
    out_col,
    fc1_row,
    fc1_col,
    fc2_row,
    fc2_col,
    vec_second,
):
    tensor_count = lax.axis_size("tensor")
    dims = grid_of(lax.axis_size("fsdp"))
    width = inputs.shape[1]
    own_rows, columns = w_qkv.shape[1:]
    hidden = w_fc1.shape[1]
    weights = (w_qkv, w_out.T, w_fc1, w_fc2.T)
    (
        weight_qkv,
        _,
        weight_out,
        *_,
        block_out,
        grad_middle,
        back_one,
        mixed_rows,
        low_turned,
        projected,
        grad_one,
        grad_two,
        table,
        vec_sums,
        pre_sums,
        bias_column,
    ) = forward(dims, tensor_count, inputs, cotangent, token_mask, vectors, weights)
    layout = Layout(columns, hidden, ("two", "one", "out", "qkv", "vec"))
    row_states = (qkv_row, out_col[None], fc1_row[None], fc2_col[None])
    col_states = (qkv_col, out_row[None], fc1_col[None], fc2_row[None])
    input_grad, *values = backward(
        dims,
        tensor_count,
        layout,
        (
            grad_two,
            grad_one,
            weight_qkv,
            weight_out,
            projected,
            inputs,
            grad_middle,
            mixed_rows,
            low_turned,
            back_one,
        ),
        (bias_column, table, vec_sums, pre_sums),
        weights,
        (*row_states, *col_states, vec_second, vectors),
    )
    outs = update_weights(
        layout, width, FF, columns, hidden, own_rows, (block_out, input_grad), values, vectors, weights
    )
    outs = [out.reshape(-1) if out.shape[0] == 1 else out for out in outs]
    for at in (3, 5, 8, 10):
        outs[at] = outs[at].T
    return (*outs[:12], *outs[13:], outs[12])


def solution(mesh):
    in_specs = (
        P(("fsdp", "tensor"), None),
        P(("fsdp", "tensor"), None),
        P("fsdp", None),
        P(None, "fsdp", "tensor"),
        P("tensor", "fsdp"),
        P("fsdp", "tensor"),
        P("tensor", "fsdp"),
        P(None, "fsdp"),
        P(None, "fsdp"),
        P(None, "tensor"),
        P("tensor"),
        P("fsdp"),
        P("fsdp"),
        P("tensor"),
        P("tensor"),
        P("fsdp"),
        P(None, "fsdp"),
    )
    out_specs = (
        P(("fsdp", "tensor"), None),
        P(("fsdp", "tensor"), None),
        P(None, "fsdp", "tensor"),
        P("tensor", "fsdp"),
        P("fsdp", "tensor"),
        P("tensor", "fsdp"),
        P(None, "fsdp"),
        P(None, "fsdp", "tensor"),
        P("tensor", "fsdp"),
        P("fsdp", "tensor"),
        P("tensor", "fsdp"),
        P(None, "fsdp"),
        P(None, "fsdp"),
        P(None, "tensor"),
        P("tensor"),
        P("fsdp"),
        P("fsdp"),
        P("tensor"),
        P("tensor"),
        P("fsdp"),
        P(None, "fsdp"),
    )
    return jax.shard_map(
        on_device, mesh=mesh, in_specs=in_specs, out_specs=out_specs, check_vma=False
    )
```
